32 devices in a mesh: box: 8 (over z, y), orb: 4 (over x, core).
Axes of the slice: x: 2, y: 2, z: 4, core: 2. Of those that a mesh axis runs over, the one named last changes fastest.
Arguments:
- orbitals: bfloat16 [16, 1000, 1536], P('box', None, 'orb'), may hold values from -0.0546875 to 0.0546875
- potential: float32 [16, 1000], P('box'), may hold values from -3 to 1
- deriv_blocks: bfloat16 [3, 10, 10], replicated, may hold values from -1 to 1
- levels: int32 [16], P('box'), may hold values from 0 to 2
- box_counts: int32 [8], P('box'), may hold values from 1 to 2, as said below
- neighbours: int32 [16, 3, 2], P('box'), may hold values from -1 to 15, as said below
Outputs:
- fock: float32 [1536, 1536], P('box', 'orb')
- correlation: float32 [1536, 1536], P('box', 'orb')
- inverse_root: float32 [1536, 1536], P('box', 'orb')
The draws below stay inside these ranges and needn't reach their ends.
Inputs may be any that keep to these rules, and one draw needn't show every extreme that they name: Each index of box holds box_counts of live slots, which are its first slots; the counts sum to 12, and some index holds 2. `neighbours`: an entry is -1 or the global slot of a live slot, other than the slot itself, on the same index of box or on the index just before or just after it; every entry of a non-live slot is -1.
All inputs are finite; a program needn't handle non-finite values.
Results may differ from the reference program's by a relative error of at most 0.0012.
Values may be sent and summed in bfloat16 or wider, within the bound.
No kernel may reach another device: no remote copies, remote signals or barrier semaphores. Data moves between devices by JAX's collectives and lax.ppermute only.
A program may use at most 128 MiB of HBM per device.

```python
import jax
import jax.numpy as jnp
from jax import lax

ORBITAL_COUNT = 1536
SCALING_PER_DIM = 10
SLOTS_PER_INDEX = 2
TOTAL_BOX_SLOTS = 16
LIVE_BOX_TOTAL = 12


def layout_helper(key):
    base_key = jax.random.fold_in(key, 7331)
    key_rank, key_shift, key_selection, key_boundary = jax.random.split(base_key, 4)
    device_list = TOTAL_BOX_SLOTS // SLOTS_PER_INDEX
    ordering = jax.random.permutation(key_rank, device_list)
    count_list = jnp.where(ordering < device_list // 2, SLOTS_PER_INDEX, 1).astype(jnp.int32)
    slot_position_index = jnp.arange(TOTAL_BOX_SLOTS, dtype=jnp.int32)
    owner_dev = slot_position_index // SLOTS_PER_INDEX
    within_dev = slot_position_index % SLOTS_PER_INDEX
    offset_amount = jax.random.randint(key_shift, (TOTAL_BOX_SLOTS, 3, 2), -1, 2).astype(jnp.int32)
    dir_index = jnp.arange(3, dtype=jnp.int32)[None, :, None]
    side_index = jnp.arange(2, dtype=jnp.int32)[None, None, :]
    forced_boxes = (within_dev[:, None, None] == 0) & (dir_index == 0)
    offset_amount = jnp.where(forced_boxes, 2 * side_index - 1, offset_amount)
    target = owner_dev[:, None, None] + offset_amount
    inside = (target >= 0) & (target < device_list)
    target_device = jnp.clip(target, 0, device_list - 1)
    selected_boxes = jax.random.randint(key_selection, (TOTAL_BOX_SLOTS, 3, 2), 0, SLOTS_PER_INDEX).astype(jnp.int32) % count_list[target_device]
    boundary_edge = (jax.random.randint(key_boundary, (TOTAL_BOX_SLOTS, 3, 2), 0, 6) == 0) & jnp.logical_not(forced_boxes)
    self_ref = (offset_amount == 0) & (selected_boxes == within_dev[:, None, None])
    is_live = within_dev < count_list[owner_dev]
    accepted = inside & is_live[:, None, None] & jnp.logical_not(self_ref) & jnp.logical_not(boundary_edge)
    neighbour_slots = jnp.where(accepted, target_device * SLOTS_PER_INDEX + selected_boxes, -1).astype(jnp.int32)
    return (count_list, neighbour_slots)


def draw_box_counts(key, part):
    count_list, neighbour_slots = layout_helper(key)
    return count_list


def draw_neighbours(key, part):
    count_list, neighbour_slots = layout_helper(key)
    return neighbour_slots


def with_ends(drawn, key, least, top_value):
    longest = drawn.shape.index(max(drawn.shape))
    spots = []
    for shift in (0, 1):
        where = [jax.random.randint(jax.random.fold_in(key, axis), (), 0, length) for axis, length in enumerate(drawn.shape)]
        where[longest] = (where[longest] + shift) % drawn.shape[longest]
        spots.append(tuple(where))
    return drawn.at[spots[0]].set(least).at[spots[1]].set(top_value)


def block_scale(rng, dims, cuts, low, top_value):
    loudness, own = 1.0, jax.random.fold_in(rng, 6)
    for position, shards_of in cuts:
        heights = jnp.exp(jax.random.uniform(jax.random.fold_in(own, position), (shards_of,), jnp.float32, low / len(cuts), top_value / len(cuts)))
        loudness = loudness * jnp.repeat(heights, dims[position] // shards_of).reshape([-1 if axis == position else 1 for axis in range(len(dims))])
    return loudness


def gaussian(key, shape, spread, bound, cuts=(), kind=jnp.bfloat16):
    array = jax.random.normal(key, shape, jnp.float32) * spread
    if len(cuts) > 0:
        array = block_scale(key, shape, cuts, -0.22, 0.18) * array
    return jnp.clip(array, min=-bound, max=bound).astype(kind)


def setup_inputs(seed: int = 0) -> dict:
    key_of = jax.random.split(jax.random.key(seed), 7)
    return {
        "orbitals": gaussian(key_of[0], (TOTAL_BOX_SLOTS, SCALING_PER_DIM ** 3, ORBITAL_COUNT), (1.0 / (SCALING_PER_DIM ** 3 * LIVE_BOX_TOTAL) ** 0.5), 0.0546875, ((0, 8), (2, 4))),
        "potential": jnp.clip(-3.0 + 4.0 * jax.random.uniform(key_of[1], (TOTAL_BOX_SLOTS, SCALING_PER_DIM ** 3), jnp.float32) ** block_scale(key_of[1], (TOTAL_BOX_SLOTS, SCALING_PER_DIM ** 3), ((0, 8),), -0.2, 0.2), -3.0, 1.0),
        "deriv_blocks": gaussian(key_of[2], (3, SCALING_PER_DIM, SCALING_PER_DIM), (3 * SCALING_PER_DIM) ** -0.5, 1.0),
        "levels": with_ends(jax.random.randint(key_of[3], (TOTAL_BOX_SLOTS,), 0, 3), jax.random.fold_in(key_of[3], 1), 0, 2).astype(jnp.int32),
        "box_counts": draw_box_counts(jax.random.fold_in(key_of[6], 71), 0),
        "neighbours": draw_neighbours(jax.random.fold_in(key_of[6], 71), 0),
    }


def contract(left, right):
    return lax.dot_general(left, right, (((0,), (0,)), ((), ())), preferred_element_type=jnp.float32)


def highest(left, right):
    return jnp.dot(left, right, precision=lax.Precision.HIGHEST, preferred_element_type=jnp.float32)


def reference(orbitals, potential, deriv_blocks, levels, box_counts, neighbours):
    cube_edge_length = SCALING_PER_DIM
    coefficient_count = SCALING_PER_DIM ** 3
    slot_position_index = jnp.arange(TOTAL_BOX_SLOTS, dtype=jnp.int32)
    is_live = (slot_position_index % SLOTS_PER_INDEX) < box_counts[slot_position_index // SLOTS_PER_INDEX]
    active_boxes = jnp.where(is_live[:, None, None], orbitals, jnp.zeros((), jnp.bfloat16))
    padded = jnp.concatenate([jnp.zeros((1, coefficient_count, ORBITAL_COUNT), jnp.bfloat16), active_boxes], axis=0)
    blocks = deriv_blocks.astype(jnp.float32)
    level_scale = jnp.where(levels == 0, 0.5, jnp.where(levels == 1, 1.0, 2.0)).astype(jnp.float32)
    einsum_forms = ["ij,sjbco->sibco", "ij,sajco->saico", "ij,sabjo->sabio"]
    cube_shape_tuple = (TOTAL_BOX_SLOTS, cube_edge_length, cube_edge_length, cube_edge_length, ORBITAL_COUNT)
    kinetic = jnp.zeros((ORBITAL_COUNT, ORBITAL_COUNT), jnp.float32)
    for direction in range(3):
        lower_side = padded[(neighbours[:, direction, 0] + 1).astype(jnp.int32)].reshape(cube_shape_tuple)
        upper_side = padded[(neighbours[:, direction, 1] + 1).astype(jnp.int32)].reshape(cube_shape_tuple)
        middle = active_boxes.reshape(cube_shape_tuple)
        form = einsum_forms[direction]
        raw_sum = jnp.einsum(form, blocks[0], lower_side.astype(jnp.float32))
        raw_sum = raw_sum + jnp.einsum(form, blocks[1], middle.astype(jnp.float32))
        raw_sum = raw_sum + jnp.einsum(form, blocks[2], upper_side.astype(jnp.float32))
        derivative_matrix = (level_scale[:, None, None, None, None] * raw_sum).astype(jnp.bfloat16)
        derivative_matrix = derivative_matrix.reshape(TOTAL_BOX_SLOTS * coefficient_count, ORBITAL_COUNT)
        kinetic = kinetic + contract(derivative_matrix, derivative_matrix)
    flattened_active = active_boxes.reshape(TOTAL_BOX_SLOTS * coefficient_count, ORBITAL_COUNT)
    weighted_values = (potential[:, :, None] * active_boxes.astype(jnp.float32)).astype(jnp.bfloat16)
    weighted_values = weighted_values.reshape(TOTAL_BOX_SLOTS * coefficient_count, ORBITAL_COUNT)
    correlation = contract(flattened_active, flattened_active)
    fock = 0.5 * kinetic + contract(flattened_active, weighted_values)
    identity = jnp.eye(ORBITAL_COUNT, dtype=jnp.float32)
    first_turn = 1.5 * identity - 0.5 * correlation
    scaled_root = highest(correlation, first_turn)
    mixed_term = highest(first_turn, scaled_root)
    second_turn = 1.5 * identity - 0.5 * mixed_term
    inverse_root = highest(second_turn, first_turn)
    return fock, correlation, inverse_root
```

```python
import functools

import jax
import jax.numpy as jnp
from jax import lax
from jax.experimental import pallas as pl
from jax.experimental.pallas import tpu as pltpu
from jax.sharding import Mesh, PartitionSpec as P

PAIR = 2
ROWS = 16
BOX = ("lvl", "pair")
f32, bf16 = jnp.float32, jnp.bfloat16


def swap(value, axis, bit):
    count = lax.axis_size(axis)
    return lax.ppermute(value, axis, [(i, i ^ bit) for i in range(count)])


def shift(value, axis, step):
    count = lax.axis_size(axis)
    return lax.ppermute(value, axis, [(i, i + step) for i in range(count) if 0 <= i + step < count])


def turn(value, axis, step):
    count = lax.axis_size(axis)
    return lax.ppermute(value, axis, [(i, (i + step) % count) for i in range(count)])


def contract(left, right):
    return lax.dot_general(left, right, (((0,), (0,)), ((), ())), preferred_element_type=f32)


def matmul(left, right):
    return jnp.dot(left, right, preferred_element_type=f32)


def kinetic_kernel(edge, slots, table, scale, *refs):
    parts, (pot, fwd_in, fwd_out, back_in, back_out), outs, scratch = refs[:6], refs[6:11], refs[11:14], refs[14:]
    high, low, fix = outs
    x, rounded, left_over, total, total_fix = scratch
    square = edge * edge
    padded = x.shape[2]
    own = PAIR * slots
    width = x.shape[3]
    x[...] = jnp.zeros_like(x)
    total[...] = jnp.zeros_like(total)
    total_fix[...] = jnp.zeros_like(total_fix)
    for place, part in enumerate(parts):
        for slot in range(slots):
            for i in range(edge):
                x[place * slots + slot, i, :square, :] = part[slot, i * square : (i + 1) * square, :]
    chunks = padded // ROWS

    def per_slot(s, carry):
        @pl.when(table[s, 0] >= 0)
        def _():
            own_scale = scale[s]
            for a in range(3):
                source = [table[s, 1 + 3 * a + k] for k in range(3)]

                def forward(i, carry):
                    if a == 0:
                        rows = pl.ds(pl.multiple_of(i * ROWS, ROWS), ROWS)
                        block = jnp.concatenate(
                            [x[t, :, rows, :].reshape(edge * ROWS, width) for t in source], axis=0
                        )
                        exact = own_scale * matmul(fwd_out[...], block)
                        exact = exact.reshape(edge, ROWS, width)
                        value = exact.astype(bf16)
                        rounded[:, rows, :] = value
                        left_over[:, rows, :] = (value.astype(f32) - exact).astype(bf16)
                    else:
                        block = jnp.concatenate([x[t, i] for t in source], axis=0)
                        exact = own_scale * matmul(fwd_in[a - 1], block)
                        value = exact.astype(bf16)
                        rounded[i] = value
                        left_over[i] = (value.astype(f32) - exact).astype(bf16)
                    return carry

                lax.fori_loop(0, chunks if a == 0 else edge, forward, 0)
                for k in range(3):
                    target = source[k]

                    @pl.when(target < own)
                    def _():
                        half = 0.5 * own_scale

                        def back(i, carry):
                            for field, sum_ref in ((rounded, total), (left_over, total_fix)):
                                if a == 0:
                                    rows = pl.ds(pl.multiple_of(i * ROWS, ROWS), ROWS)
                                    term = matmul(back_out[k], field[:, rows, :].reshape(edge * ROWS, width))
                                    sum_ref[target, :, rows, :] += half * term.reshape(edge, ROWS, width)
                                else:
                                    sum_ref[target, i] += half * matmul(back_in[a - 1, k], field[i])
                            return carry

                        lax.fori_loop(0, chunks if a == 0 else edge, back, 0)

        return carry

    lax.fori_loop(0, table.shape[0], per_slot, 0)
    for t in range(own):
        for i in range(edge):
            rows = slice(i * square, (i + 1) * square)
            weighted = (pot[t, rows, :] * x[t, i, :square, :].astype(f32)).astype(bf16).astype(f32)
            whole = total[t, i, :square, :] + weighted
            top = whole.astype(bf16)
            high[t, rows, :] = top
            low[t, rows, :] = (whole - top.astype(f32)).astype(bf16)
            fix[t, rows, :] = total_fix[t, i, :square, :].astype(bf16)


def kinetic(parts, pot, deriv_blocks, table, scale):
    slots, coefficients, width = parts[0].shape
    edge = deriv_blocks.shape[1]
    square = edge * edge
    padded = -(-square // ROWS) * ROWS
    own = PAIR * slots
    blocks = deriv_blocks.astype(f32)
    eye = jnp.eye(edge, dtype=f32)
    grow = ((0, 0), (0, padded - square), (0, padded - square))
    inner = jnp.stack(
        [
            jnp.pad(jnp.einsum("kij,ab->kiajb", blocks, eye).reshape(3, square, square), grow),
            jnp.pad(jnp.einsum("kij,ab->kaibj", blocks, eye).reshape(3, square, square), grow),
        ]
    )
    outer = jnp.einsum("kij,ab->kiajb", blocks, jnp.eye(ROWS, dtype=f32)).reshape(3, edge * ROWS, edge * ROWS)
    fwd_in = jnp.moveaxis(inner, 1, 2).reshape(2, padded, 3 * padded).astype(bf16)
    fwd_out = jnp.moveaxis(outer, 0, 1).reshape(edge * ROWS, 3 * edge * ROWS).astype(bf16)
    back_in = jnp.swapaxes(inner, 2, 3).astype(bf16)
    back_out = jnp.swapaxes(outer, 1, 2).astype(bf16)
    vmem = pl.BlockSpec(memory_space=pltpu.VMEM)
    smem = pl.BlockSpec(memory_space=pltpu.SMEM)
    out = jax.ShapeDtypeStruct((own, coefficients, width), bf16)
    return pl.pallas_call(
        functools.partial(kinetic_kernel, edge, slots),
        out_shape=(out, out, out),
        in_specs=[smem, smem] + [vmem] * 11,
        out_specs=(vmem, vmem, vmem),
        scratch_shapes=[
            pltpu.VMEM((6 * slots + 1, edge, padded, width), bf16),
            pltpu.VMEM((edge, padded, width), bf16),
            pltpu.VMEM((edge, padded, width), bf16),
            pltpu.VMEM((own, edge, padded, width), f32),
            pltpu.VMEM((own, edge, padded, width), f32),
        ],
        compiler_params=pltpu.CompilerParams(vmem_limit_bytes=48 * 1024 * 1024),
        cost_estimate=pl.CostEstimate(flops=10**10, bytes_accessed=20 * 10**6, transcendentals=0),
    )(table, scale, *parts, pot, fwd_in, fwd_out, back_in, back_out)


def gather_orb(block):
    blocks = [block]
    bit = lax.axis_size("orb") // 2
    found = {0: block}
    while bit:
        found.update({q ^ bit: swap(value, "orb", bit) for q, value in list(found.items())})
        bit //= 2
    return [found[q] for q in range(lax.axis_size("orb"))]


def body(orbitals, potential, deriv_blocks, levels, box_counts, neighbours):
    slots, coefficients, own_width = orbitals.shape
    level, pair, orb = lax.axis_index("lvl"), lax.axis_index("pair"), lax.axis_index("orb")
    level_count, orb_count = lax.axis_size("lvl"), lax.axis_size("orb")
    half = own_width // PAIR
    all_width = own_width * orb_count
    first = pair == 0

    live = jnp.arange(slots, dtype=jnp.int32) < box_counts[0]
    active = jnp.where(live[:, None, None], orbitals, jnp.zeros((), bf16))

    facts = jnp.concatenate(
        [neighbours.reshape(slots, 6), levels[:, None], live.astype(jnp.int32)[:, None]], axis=1
    )
    facts = lax.all_gather(facts, BOX, axis=0, tiled=True)
    other_pot = swap(potential, "pair", 1)

    mine = jnp.where(first, active[:, :, :half], active[:, :, half:])
    theirs = jnp.where(first, active[:, :, half:], active[:, :, :half])
    beside = swap(theirs, "pair", 1)
    beside_rest = swap(mine, "pair", 1)
    parts = [mine, beside]
    for step in (1, -1):
        parts += [shift(mine, "lvl", step), shift(beside, "lvl", step)]

    left_own = gather_orb(active)
    beside_all = jnp.concatenate(
        [jnp.where(first, beside, beside_rest), jnp.where(first, beside_rest, beside)], axis=2
    )
    left_beside = gather_orb(beside_all)

    box_of_level = level * PAIR
    ids = jnp.concatenate(
        [
            (box_of_level + pair) * slots + jnp.arange(slots),
            (box_of_level + 1 - pair) * slots + jnp.arange(slots),
            (box_of_level - 1) * slots + jnp.arange(slots),
            (box_of_level + PAIR) * slots + jnp.arange(slots),
        ]
    ).astype(jnp.int32)
    there = (ids >= 0) & (ids < facts.shape[0])
    chosen = facts[jnp.clip(ids, 0, facts.shape[0] - 1)]

    def place(slot_id):
        box = slot_id // slots
        apart = box // PAIR - level
        base = jnp.where(apart == 0, 0, jnp.where(apart < 0, 2, 4))
        where = (base + (box % PAIR != pair)) * slots + slot_id % slots
        return jnp.where(slot_id >= 0, where, 6 * slots)

    near = place(chosen[:, :6])
    self_place = place(ids)
    table = [jnp.where(there & (chosen[:, 7] > 0), self_place, -1)]
    for a in range(3):
        table += [near[:, 2 * a], self_place, near[:, 2 * a + 1]]
    table = jnp.stack(table, axis=1).astype(jnp.int32)
    level_of = chosen[:, 6]
    scale = jnp.where(level_of == 0, 0.5, jnp.where(level_of == 1, 1.0, 2.0)).astype(f32)
    pot = jnp.concatenate([potential, other_pot])[:, :, None]

    flat = lambda block: block.reshape(slots * coefficients, block.shape[-1])
    groups = range(orb_count)

    def chunk_of(blocks, target):
        if level_count == orb_count:
            return lax.dynamic_index_in_dim(blocks, orb ^ target, keepdims=False)
        ordered = jnp.stack([lax.dynamic_index_in_dim(blocks, orb ^ j, keepdims=False) for j in groups])
        ordered = ordered.reshape(level_count, all_width // level_count, blocks.shape[-1])
        return lax.dynamic_index_in_dim(ordered, target, keepdims=False)

    def sum_levels(blocks, kind):
        total = chunk_of(blocks, level)
        for step in range(1, level_count):
            sent = chunk_of(blocks, (level + step) % level_count).astype(kind)
            total = total + turn(sent, "lvl", step).astype(f32)
        return total

    def own_rows(strip):
        rows = strip.shape[0] // PAIR
        kept = jnp.where(first, strip[:rows], strip[rows:])
        got = swap(jnp.where(first, strip[rows:], strip[:rows]), "pair", 1)
        return jnp.concatenate([jnp.where(first, kept, got), jnp.where(first, got, kept)], axis=1)

    correlation_blocks = jnp.stack(
        [contract(flat(left_own[q]), flat(mine)) + contract(flat(left_beside[q]), flat(beside)) for q in groups]
    )
    strip = sum_levels(correlation_blocks, f32)
    correlation = own_rows(strip)

    high, low, fix = kinetic(parts, pot, deriv_blocks, table, scale)
    right = jnp.concatenate([high, low, fix], axis=2).reshape(PAIR, slots * coefficients, 3 * half)
    fock_blocks = jnp.stack(
        [contract(flat(left_own[q]), right[0]) + contract(flat(left_beside[q]), right[1]) for q in groups]
    )
    fock_strip = sum_levels(fock_blocks[:, :, :half] + fock_blocks[:, :, half : 2 * half], f32)
    fock = own_rows(fock_strip)
    fix_blocks = fock_blocks[:, :, 2 * half :]
    if level_count == orb_count:
        fix_total = jnp.zeros((own_width, half), f32)
        for step in range(orb_count):
            to = [
                (z * orb_count + o, o * orb_count + (z + step) % orb_count)
                for z in range(level_count)
                for o in groups
            ]
            sent = lax.dynamic_index_in_dim(fix_blocks, orb ^ ((level + step) % orb_count), keepdims=False)
            fix_total = fix_total + lax.ppermute(sent.astype(bf16), ("lvl", "orb"), to).astype(f32)
        fix_own = fix_total.T
    else:
        ordered = jnp.stack([lax.dynamic_index_in_dim(fix_blocks, orb ^ j, keepdims=False) for j in groups])
        ordered = lax.psum(ordered.reshape(all_width, half).astype(bf16), "lvl")
        whole = lax.all_gather(ordered, ("orb", "pair"), axis=1, tiled=True)
        rows = fock.shape[0]
        mine_rows = lax.dynamic_slice_in_dim(whole, (level * PAIR + pair) * rows, rows, axis=1)
        fix_own = lax.dynamic_slice_in_dim(mine_rows, orb * own_width, own_width, axis=0).astype(f32).T
    fock = fock + fix_own

    def identity(rows, row0, cols, col0):
        row_ids = row0 + jnp.arange(rows, dtype=jnp.int32)
        col_ids = col0 + jnp.arange(cols, dtype=jnp.int32)
        return (row_ids[:, None] == col_ids[None, :]).astype(f32)

    block_rows = correlation.shape[0]
    row0, col0 = (level * PAIR + pair) * block_rows, orb * own_width
    eye = identity(block_rows, row0, own_width, col0)
    offset = correlation - eye
    gathered = lax.all_gather(offset.astype(bf16), BOX + ("orb",), axis=0, tiled=False)
    whole = gathered.reshape(level_count * PAIR, orb_count, block_rows, own_width)
    whole = jnp.swapaxes(whole, 1, 2).reshape(all_width, all_width)
    rows_of = lax.dynamic_slice_in_dim(whole, row0, block_rows, axis=0)
    cols_of = lax.dynamic_slice_in_dim(whole, col0, own_width, axis=1)
    row_square = matmul(rows_of, whole)
    col_square = matmul(whole, cols_of)
    own_square = lax.dynamic_slice_in_dim(row_square, col0, own_width, axis=1)
    left = (rows_of.astype(f32) - 0.25 * row_square).astype(bf16)
    right_side = (0.25 * (cols_of.astype(f32) - col_square)).astype(bf16)
    inverse_root = eye - 0.5 * offset + 0.125 * own_square + matmul(left, right_side)
    return fock, correlation, inverse_root


def solution(mesh):
    levels = mesh.shape["box"] // PAIR
    split = Mesh(mesh.devices.reshape(levels, PAIR, mesh.shape["orb"]), ("lvl", "pair", "orb"))
    in_specs = (P(BOX, None, "orb"), P(BOX, None), P(), P(BOX), P(BOX), P(BOX, None, None))
    out_specs = (P(BOX, "orb"),) * 3
    return jax.shard_map(body, mesh=split, in_specs=in_specs, out_specs=out_specs, check_vma=False)
```

```python
import functools

import jax
import jax.numpy as jnp
import numpy as np
from jax import lax
from jax.experimental import pallas as pl
from jax.experimental.pallas import tpu as pltpu
from jax.sharding import Mesh, PartitionSpec as P

PAIR = 2
ROWS = 16
BOX = ("lvl", "pair")
f32, bf16 = jnp.float32, jnp.bfloat16


def swap(value, axis, bit):
    count = lax.axis_size(axis)
    return lax.ppermute(value, axis, [(i, i ^ bit) for i in range(count)])


def shift(value, axis, step):
    count = lax.axis_size(axis)
    return lax.ppermute(value, axis, [(i, i + step) for i in range(count) if 0 <= i + step < count])


def contract(left, right):
    return lax.dot_general(left, right, (((0,), (0,)), ((), ())), preferred_element_type=f32)


def matmul(left, right):
    return jnp.dot(left, right, preferred_element_type=f32)


def spread(value, axis, bits):
    return jnp.stack([swap(value, axis, bit) if bit else value for bit in bits])


def kinetic_kernel(edge, slots, table, scale, *refs):
    parts, (pot, fwd_in, fwd_out, back_in, back_out), out = refs[:6], refs[6:11], refs[11]
    raw, x, rounded, left_over, total, total_fix, sems = refs[12:]
    square = edge * edge
    own = PAIR * slots
    width = x.shape[3]
    copies = [pltpu.make_async_copy(part, raw.at[place], sems.at[place]) for place, part in enumerate(parts)]
    for copy in copies:
        copy.start()
    x[...] = jnp.zeros_like(x)
    total[...] = jnp.zeros_like(total)
    total_fix[...] = jnp.zeros_like(total_fix)
    for copy in copies:
        copy.wait()

    def lay_out(place, carry):
        for slot in range(slots):
            for i in range(edge):
                x[place * slots + slot, i, :square, :] = raw[place, slot, i * square : (i + 1) * square, :]
        return carry

    lax.fori_loop(0, len(parts), lay_out, 0)
    chunks = -(-square // ROWS)

    def per_slot(s, carry):
        @pl.when(table[s, 0] >= 0)
        def _():
            own_scale = scale[s]
            for a in range(3):
                source = [table[s, 1 + 3 * a + k] for k in range(3)]
                for i in range(chunks if a == 0 else edge):
                    if a == 0:
                        rows = slice(i * ROWS, (i + 1) * ROWS)
                        block = jnp.concatenate([x[t, :, rows, :].reshape(edge * ROWS, width) for t in source], axis=0)
                        exact = (own_scale * matmul(fwd_out[...], block)).reshape(edge, ROWS, width)
                        value = exact.astype(bf16)
                        rounded[:, rows, :] = value
                        left_over[:, rows, :] = (value.astype(f32) - exact).astype(bf16)
                    else:
                        block = jnp.concatenate([x[t, i] for t in source], axis=0)
                        exact = own_scale * matmul(fwd_in[a - 1], block)
                        value = exact.astype(bf16)
                        rounded[i] = value
                        left_over[i] = (value.astype(f32) - exact).astype(bf16)
                half = 0.5 * own_scale
                for k in range(3):
                    target = source[k]

                    @pl.when(target < own)
                    def _():
                        for i in range(chunks if a == 0 else edge):
                            for field, sum_ref in ((rounded, total), (left_over, total_fix)):
                                if a == 0:
                                    rows = slice(i * ROWS, (i + 1) * ROWS)
                                    term = matmul(back_out[k], field[:, rows, :].reshape(edge * ROWS, width))
                                    sum_ref[target, :, rows, :] += half * term.reshape(edge, ROWS, width)
                                else:
                                    sum_ref[target, i] += half * matmul(back_in[a - 1, k], field[i])

        return carry

    lax.fori_loop(0, table.shape[0], per_slot, 0)

    def finish(t, carry):
        for i in range(edge):
            rows = slice(i * square, (i + 1) * square)
            exact = pot[t, rows, :] * x[t, i, :square, :].astype(f32)
            lost = exact.astype(bf16).astype(f32) - exact
            whole = total[t, i, :square, :] + exact
            top = whole.astype(bf16)
            low = (whole - top.astype(f32)).astype(bf16)
            fix = (total_fix[t, i, :square, :] + lost).astype(bf16)
            out[t, rows, :] = jnp.concatenate([top, low, fix], axis=1)
        return carry

    lax.fori_loop(0, own, finish, 0)


def block_matrices(deriv_blocks):
    edge = deriv_blocks.shape[1]
    square = edge * edge
    padded = -(-square // ROWS) * ROWS
    ids = np.arange(padded)
    slow = ((ids[:, None] // edge) == np.arange(edge)).astype(np.float32)
    fast = (((ids[:, None] % edge) == np.arange(edge)) & (ids[:, None] < square)).astype(np.float32)
    ids = np.arange(edge * ROWS)
    outer = ((ids[:, None] // ROWS) == np.arange(edge)).astype(np.float32)
    within = ((ids[:, None] % ROWS) == np.arange(ROWS)).astype(np.float32)
    stacked = jnp.moveaxis(deriv_blocks, 0, 1).reshape(edge, 3 * edge)
    forward, backward = [], []
    for spot, mask in ((slow, fast), (fast, slow), (outer, within)):
        same = mask @ mask.T
        spread_out = np.kron(np.eye(3, dtype=np.float32), spot.T)
        spot_b, same_b = jnp.asarray(spot, bf16), jnp.asarray(same, f32)
        wide = matmul(matmul(spot_b, stacked).astype(bf16), jnp.asarray(spread_out, bf16))
        forward.append((wide * jnp.tile(same_b, (1, 3))).astype(bf16))
        turned = jnp.einsum("ri,kji->krj", spot_b, deriv_blocks, preferred_element_type=f32).astype(bf16)
        turned = jnp.einsum("krj,cj->krc", turned, spot_b, preferred_element_type=f32)
        backward.append((turned * same_b).astype(bf16))
    return jnp.stack(forward[:2]), forward[2], jnp.stack(backward[:2]), backward[2]


def kinetic(parts, pot, matrices, table, scale, edge):
    slots, coefficients, width = parts[0].shape
    padded = matrices[0].shape[1]
    own = PAIR * slots
    vmem = pl.BlockSpec(memory_space=pltpu.VMEM)
    smem = pl.BlockSpec(memory_space=pltpu.SMEM)
    anywhere = pl.BlockSpec(memory_space=pl.ANY)
    return pl.pallas_call(
        functools.partial(kinetic_kernel, edge, slots),
        out_shape=jax.ShapeDtypeStruct((own, coefficients, 3 * width), bf16),
        in_specs=[smem, smem] + [anywhere] * 6 + [vmem] * 5,
        out_specs=vmem,
        scratch_shapes=[
            pltpu.VMEM((6, slots, coefficients, width), bf16),
            pltpu.VMEM((6 * slots + 1, edge, padded, width), bf16),
            pltpu.VMEM((edge, padded, width), bf16),
            pltpu.VMEM((edge, padded, width), bf16),
            pltpu.VMEM((own, edge, padded, width), f32),
            pltpu.VMEM((own, edge, padded, width), f32),
            pltpu.SemaphoreType.DMA((6,)),
        ],
        compiler_params=pltpu.CompilerParams(vmem_limit_bytes=48 * 1024 * 1024),
        cost_estimate=pl.CostEstimate(flops=2 * 10**10, bytes_accessed=40 * 10**6, transcendentals=0),
    )(table, scale, *parts, pot, *matrices)


def body(orbitals, potential, deriv_blocks, levels, box_counts, neighbours):
    slots, coefficients, own_width = orbitals.shape
    edge = deriv_blocks.shape[1]
    level, pair, orb = lax.axis_index("lvl"), lax.axis_index("pair"), lax.axis_index("orb")
    level_count, orb_count = lax.axis_size("lvl"), lax.axis_size("orb")
    half = own_width // PAIR
    all_width = own_width * orb_count
    box_rows = all_width // (level_count * PAIR)
    first = pair == 0
    groups = range(orb_count)
    square_grid = level_count == orb_count and orb_count & (orb_count - 1) == 0 and box_rows == half

    live = jnp.arange(slots, dtype=jnp.int32) < box_counts[0]
    active = jnp.where(live[:, None, None], orbitals, jnp.zeros((), bf16))

    mine = jnp.where(first, active[:, :, :half], active[:, :, half:])
    theirs = jnp.where(first, active[:, :, half:], active[:, :, :half])
    facts = jnp.concatenate(
        [neighbours.reshape(slots, 6), levels[:, None], live.astype(jnp.int32)[:, None]], axis=1
    )
    beside = swap(theirs, "pair", 1)
    far = {q: swap(active, "orb", q) for q in groups if q and q % 2 == 0}
    lower, upper = shift(mine, "lvl", 1), shift(mine, "lvl", -1)
    beside_rest = swap(mine, "pair", 1)
    near_active = swap(active, "orb", 1)
    both_facts = jnp.stack([facts, swap(facts, "pair", 1)])
    other_pot = swap(potential, "pair", 1)
    lower_facts, upper_facts = shift(both_facts, "lvl", 1), shift(both_facts, "lvl", -1)
    lower_beside, upper_beside = shift(beside, "lvl", 1), shift(beside, "lvl", -1)

    box_of_level = level * PAIR
    slot_ids = jnp.arange(slots, dtype=jnp.int32)
    ids = jnp.concatenate(
        [
            (box_of_level + pair) * slots + slot_ids,
            (box_of_level + 1 - pair) * slots + slot_ids,
            (box_of_level - 1) * slots + slot_ids,
            (box_of_level + PAIR) * slots + slot_ids,
        ]
    ).astype(jnp.int32)
    there = (ids >= 0) & (ids < level_count * PAIR * slots)
    chosen = jnp.concatenate(
        [
            both_facts[0],
            both_facts[1],
            jnp.where(first, lower_facts[1], lower_facts[0]),
            jnp.where(first, upper_facts[0], upper_facts[1]),
        ]
    )

    def place(slot_id):
        box = slot_id // slots
        apart = box // PAIR - level
        base = jnp.where(apart == 0, 0, jnp.where(apart < 0, 2, 4))
        where = (base + (box % PAIR != pair)) * slots + slot_id % slots
        return jnp.where(slot_id >= 0, where, 6 * slots)

    near = place(chosen[:, :6])
    self_place = place(ids)
    table = [jnp.where(there & (chosen[:, 7] > 0), self_place, -1)]
    for a in range(3):
        table += [near[:, 2 * a], self_place, near[:, 2 * a + 1]]
    table = jnp.stack(table, axis=1).astype(jnp.int32)
    level_of = chosen[:, 6]
    scale = jnp.where(level_of == 0, 0.5, jnp.where(level_of == 1, 1.0, 2.0)).astype(f32)
    pot = jnp.concatenate([potential, other_pot])[:, :, None]
    matrices = block_matrices(deriv_blocks)

    far, beside_rest, lower, upper, near_active, table, scale, pot, matrices = lax.optimization_barrier(
        (far, beside_rest, lower, upper, near_active, table, scale, pot, matrices)
    )
    beside_all = jnp.concatenate(
        [jnp.where(first, beside, beside_rest), jnp.where(first, beside_rest, beside)], axis=2
    )
    cut = slots // 2
    far_beside = {
        q: jnp.concatenate([swap(beside_all[:cut], "orb", q), swap(far[q][cut:], "pair", 1)]) for q in far
    }
    left_own = {0: active, 1: near_active, **far}
    left_beside = {0: beside_all, 1: swap(beside_all, "orb", 1), **far_beside}
    for q in far:
        left_own[q + 1] = swap(far[q], "orb", 1)
        left_beside[q + 1] = swap(far_beside[q], "orb", 1)
    parts = [mine, beside, lower, lower_beside, upper, upper_beside]
    flat = lambda block: block.reshape(slots * coefficients, block.shape[-1])

    def row_blocks(right_own, right_beside):
        return jnp.stack(
            [
                contract(flat(right_own), flat(left_own[q])) + contract(flat(right_beside), flat(left_beside[q]))
                for q in groups
            ]
        )

    def block(blocks, q):
        return lax.dynamic_index_in_dim(blocks, q, keepdims=False)

    def natural(blocks):
        return jnp.concatenate([block(blocks, orb ^ j) for j in groups], axis=1)

    def deliver(blocks, kind):
        if not square_grid:
            strip = lax.psum(natural(blocks), "lvl")
            strip = lax.all_gather(strip, ("orb", "pair"), axis=0, tiled=True)
            strip = lax.dynamic_slice_in_dim(strip, (level * PAIR + pair) * box_rows, box_rows, axis=0)
            return lax.dynamic_slice_in_dim(strip, orb * own_width, own_width, axis=1)
        total = 0.0
        for step in range(level_count):
            to = [
                (z * orb_count + o, o * orb_count + (z ^ step)) for z in range(level_count) for o in groups
            ]
            sent = block(blocks, orb ^ level ^ step).astype(kind)
            total = total + lax.ppermute(sent, ("lvl", "orb"), to).astype(f32)
        return total

    def deliver_turned(blocks):
        sums = []
        for over in range(PAIR):
            total = 0.0
            for step in range(level_count):
                wide = block(blocks, orb ^ level ^ step)
                to_first = (pair ^ over) == 0
                sent = jnp.where(to_first, wide[:, :half], wide[:, half:]).astype(bf16)
                to = [
                    (z * PAIR + y, (z ^ step) * PAIR + (y ^ over)) for z in range(level_count) for y in range(PAIR)
                ]
                if step or over:
                    sent = lax.ppermute(sent, BOX, to)
                total = total + sent.astype(f32)
            sums.append(total.T)
        own, other = sums
        return jnp.concatenate([jnp.where(first, own, other), jnp.where(first, other, own)], axis=1)

    def natural_turned(blocks):
        strip = lax.psum(natural(blocks), "lvl")
        everywhere = lax.all_gather(strip, "pair", axis=0, tiled=True)
        rows = lax.dynamic_slice_in_dim(everywhere, (level * PAIR + pair) * box_rows, box_rows, axis=1)
        return rows.T

    def identity(rows, row0, cols, col0):
        row_ids = row0 + jnp.arange(rows, dtype=jnp.int32)
        col_ids = col0 + jnp.arange(cols, dtype=jnp.int32)
        return (row_ids[:, None] == col_ids[None, :]).astype(f32)

    offset_blocks = row_blocks(mine, beside)
    offset_blocks = offset_blocks.at[0].add(-identity(half, pair * half, own_width, 0) / level_count)
    offset = deliver(offset_blocks, bf16)
    row0, col0 = (level * PAIR + pair) * box_rows, orb * own_width
    eye = identity(box_rows, row0, own_width, col0)
    correlation = offset + eye

    right = kinetic(parts, pot, matrices, table, scale, edge)
    fock_blocks = row_blocks(right[:slots], right[slots:])
    fock = deliver(fock_blocks[:, :half] + fock_blocks[:, half : 2 * half], f32)
    fix = fock_blocks[:, 2 * half :]
    fock = fock + (deliver_turned(fix) if square_grid else natural_turned(fix))

    small = offset.astype(bf16)
    if square_grid:
        levels_of, far_of = range(level_count), range(0, orb_count, 2)
        top, low = small[: box_rows // 2], small[box_rows // 2 :]
        top = spread(spread(spread(spread(top, "lvl", levels_of), "pair", (0, 1)), "orb", far_of), "orb", (0, 1))
        low = spread(spread(spread(spread(low, "orb", far_of), "lvl", levels_of), "pair", (0, 1)), "orb", (0, 1))
        top = jnp.transpose(top, (3, 2, 4, 1, 0, 5))
        low = jnp.transpose(low, (2, 1, 4, 3, 0, 5))
        whole = jnp.stack([top, low], axis=2).reshape(all_width, all_width)
        rows_of, cols_of = whole[:box_rows], whole[:, :own_width]
        apart = level ^ orb

        def to_row_order(strip):
            pieces = []
            for z in levels_of:
                piece = lax.dynamic_slice_in_dim(strip, (apart ^ z) * own_width, own_width, axis=1)
                turned = jnp.concatenate([piece[:, half:], piece[:, :half]], axis=1)
                pieces.append(jnp.where(first, piece, turned))
            return jnp.concatenate(pieces, axis=1)

        def to_col_order(strip):
            pieces = []
            for q in groups:
                piece = lax.dynamic_slice_in_dim(strip, (apart ^ q) * own_width, own_width, axis=0)
                turned = jnp.concatenate([piece[half:], piece[:half]], axis=0)
                pieces.append(jnp.where(first, piece, turned))
            return jnp.concatenate(pieces, axis=0)

        own_square_at = lambda strip: strip[:, :own_width]
    else:
        gathered = lax.all_gather(small, "orb", axis=1, tiled=True)
        whole = lax.all_gather(gathered, BOX, axis=0, tiled=True)
        rows_of = lax.dynamic_slice_in_dim(whole, row0, box_rows, axis=0)
        cols_of = lax.dynamic_slice_in_dim(whole, col0, own_width, axis=1)
        to_row_order = to_col_order = lambda strip: strip
        own_square_at = lambda strip: lax.dynamic_slice_in_dim(strip, col0, own_width, axis=1)
    row_square = matmul(to_row_order(rows_of), whole)
    col_square = matmul(whole, to_col_order(cols_of))
    left = to_row_order((rows_of.astype(f32) - 0.25 * row_square).astype(bf16))
    right_side = (0.25 * (cols_of.astype(f32) - col_square)).astype(bf16)
    inverse_root = eye - 0.5 * offset + 0.125 * own_square_at(row_square) + matmul(left, right_side)
    return fock, correlation, inverse_root


def solution(mesh):
    levels = mesh.shape["box"] // PAIR
    split = Mesh(mesh.devices.reshape(levels, PAIR, mesh.shape["orb"]), ("lvl", "pair", "orb"))
    in_specs = (P(BOX, None, "orb"), P(BOX, None), P(), P(BOX), P(BOX), P(BOX, None, None))
    out_specs = (P(BOX, "orb"),) * 3
    return jax.shard_map(body, mesh=split, in_specs=in_specs, out_specs=out_specs, check_vma=False)
```

```python
import functools

import jax
import jax.numpy as jnp
import numpy as np
from jax import lax
from jax.experimental import pallas as pl
from jax.experimental.pallas import tpu as pltpu
from jax.sharding import Mesh, PartitionSpec as P

PAIR = 2
ROWS = 16
BOX = ("lvl", "pair")
f32, bf16 = jnp.float32, jnp.bfloat16


def swap(value, axis, bit):
    count = lax.axis_size(axis)
    return lax.ppermute(value, axis, [(i, i ^ bit) for i in range(count)])


def shift(value, axis, step):
    count = lax.axis_size(axis)
    return lax.ppermute(value, axis, [(i, i + step) for i in range(count) if 0 <= i + step < count])


def contract(left, right):
    return lax.dot_general(left, right, (((0,), (0,)), ((), ())), preferred_element_type=f32)


def matmul(left, right):
    return jnp.dot(left, right, preferred_element_type=f32)


def spread(value, axis, bits):
    return jnp.stack([swap(value, axis, bit) if bit else value for bit in bits])


def params(mebibytes):
    return pltpu.CompilerParams(vmem_limit_bytes=mebibytes * 1024 * 1024)


def pack_kernel(meta, orbitals, facts, active, mine, theirs):
    slots, coefficients, width = orbitals.shape
    half, fold = width // PAIR, coefficients // 2
    first = meta[0] == 0
    for slot in range(slots):
        keep = slot < meta[1]
        for part in range(2):
            rows = slice(part * fold, (part + 1) * fold)
            here = orbitals[slot, rows, :]
            here = jnp.where(keep, here, jnp.zeros_like(here))
            active[slot, rows, :] = here
            low, high = here[:, :half], here[:, half:]
            lanes = slice(part * half, (part + 1) * half)
            mine[slot, :fold, lanes] = jnp.where(first, low, high)
            theirs[slot, :fold, lanes] = jnp.where(first, high, low)
        for out in (mine, theirs):
            out[slot, fold:, :] = jnp.broadcast_to(facts[slot : slot + 1, :], (out.shape[1] - fold, width)).astype(bf16)


def pack(meta, orbitals, facts):
    slots, coefficients, width = orbitals.shape
    fold = coefficients // 2
    padded = (fold // ROWS + 1) * ROWS
    vmem = pl.BlockSpec(memory_space=pltpu.VMEM)
    packed = jax.ShapeDtypeStruct((slots, padded, width), bf16)
    return pl.pallas_call(
        pack_kernel,
        out_shape=(jax.ShapeDtypeStruct(orbitals.shape, bf16), packed, packed),
        in_specs=[pl.BlockSpec(memory_space=pltpu.SMEM), vmem, vmem],
        out_specs=(vmem, vmem, vmem),
        compiler_params=params(24),
        name="pack",
    )(meta, orbitals, facts)


def load_left(lefts, held, sems):
    copies = [pltpu.make_async_copy(left, held.at[i], sems.at[i]) for i, left in enumerate(lefts)]
    for copy in copies:
        copy.start()
    return copies


def correlation_kernel(levels, meta, *refs):
    lefts, out, held, turned, sems = refs[:-4], refs[-4], refs[-3], refs[-2], refs[-1]
    copies = load_left(lefts, held, sems)
    groups = len(lefts) // 2
    half, width = out.shape[1:]
    first, apart = meta[0] == 0, meta[1]
    for copy in copies:
        copy.wait()
    for side in range(2):
        own = held[side * groups]
        turned[side] = jnp.where(first, own[:, :half], own[:, half:]).T

    def per_group(q, carry):
        total = matmul(turned[0], held[q]) + matmul(turned[1], held[groups + q])
        rows = lax.broadcasted_iota(jnp.int32, (half, width), 0) + jnp.where(first, 0, half)
        columns = lax.broadcasted_iota(jnp.int32, (half, width), 1)
        share = jnp.where((rows == columns) & (q == 0), 1.0 / levels, 0.0)
        out[q ^ apart] = (total - share).astype(bf16)
        return carry

    lax.fori_loop(0, groups, per_group, 0)


def fock_kernel(meta, *refs):
    lefts, right, out, held, raw, turned, sems = refs[:-6], refs[-6], refs[-5], refs[-4], refs[-3], refs[-2], refs[-1]
    copies = load_left(lefts, held, sems)
    last = pltpu.make_async_copy(right, raw, sems.at[len(lefts)])
    last.start()
    groups = len(lefts) // 2
    half, width = out.shape[2:]
    apart = meta[1]
    last.wait()
    for side in range(2):
        turned[side] = raw[side].T
    for copy in copies:
        copy.wait()

    def per_group(q, carry):
        total = matmul(turned[0], held[q]) + matmul(turned[1], held[groups + q])
        main = total[:half] + total[half : 2 * half]
        top = main.astype(bf16)
        out[q ^ apart, 0] = top
        out[q ^ apart, 1] = (main - top.astype(f32)).astype(bf16)
        out[q ^ apart, 2] = total[2 * half :].astype(bf16)
        return carry

    lax.fori_loop(0, groups, per_group, 0)


def row_products(kernel, name, meta, lefts, right, shape, tall):
    depth, width = lefts[0].shape
    smem = pl.BlockSpec(memory_space=pltpu.SMEM)
    anywhere = pl.BlockSpec(memory_space=pl.ANY)
    scratch = [pltpu.VMEM((len(lefts), depth, width), bf16)]
    if right is not None:
        scratch.append(pltpu.VMEM(right.shape, bf16))
    scratch += [pltpu.VMEM((2, tall, depth), bf16), pltpu.SemaphoreType.DMA((len(lefts) + 1,))]
    operands = list(lefts) + ([] if right is None else [right])
    return pl.pallas_call(
        kernel,
        out_shape=jax.ShapeDtypeStruct(shape, bf16),
        in_specs=[smem] + [anywhere] * len(operands),
        out_specs=pl.BlockSpec(memory_space=pltpu.VMEM),
        scratch_shapes=scratch,
        compiler_params=params(40),
        cost_estimate=pl.CostEstimate(
            flops=2 * len(lefts) * depth * width * tall, bytes_accessed=2 * len(lefts) * depth * width, transcendentals=0
        ),
        name=name,
    )(meta, *operands)


def root_kernel(meta, top, low, offset, root, whole, rows_f, cols_b):
    level, pair, orb = meta[0], meta[1], meta[2]
    fine, width = top.shape[4:]
    coarse = 2 * fine
    side = whole.shape[0]
    groups = side // width
    for core in range(2):
        for far in range(top.shape[1]):
            lanes = pl.ds(pl.multiple_of((orb ^ (2 * far + core)) * width, width), width)
            for z in range(top.shape[3]):
                for y in range(PAIR):
                    start = ((level ^ z) * PAIR + (pair ^ y)) * coarse
                    whole[pl.ds(pl.multiple_of(start, fine), fine), lanes] = top[core, far, y, z]
                    whole[pl.ds(pl.multiple_of(start + fine, fine), fine), lanes] = low[core, y, z, far]
    row0 = pl.multiple_of((level * PAIR + pair) * coarse, coarse)
    own_lanes = pl.ds(pl.multiple_of(orb * width, width), width)
    rows = whole[pl.ds(row0, coarse), :]

    def across(j, carry):
        lanes = pl.ds(pl.multiple_of(j * width, width), width)
        rows_f[:, lanes] = matmul(rows, whole[:, lanes])
        return carry

    lax.fori_loop(0, groups, across, 0)
    columns = whole[:, own_lanes]

    def down(i, carry):
        here = pl.ds(pl.multiple_of(i * coarse, coarse), coarse)
        square = matmul(whole[here, :], columns)
        cols_b[here, :] = (0.25 * (whole[here, own_lanes].astype(f32) - square)).astype(bf16)
        return carry

    lax.fori_loop(0, side // coarse, down, 0)
    left = (rows.astype(f32) - 0.25 * rows_f[...]).astype(bf16)
    value = matmul(left, cols_b[...]) + 0.125 * rows_f[:, own_lanes] - 0.5 * offset[...]
    row_ids = lax.broadcasted_iota(jnp.int32, value.shape, 0) + row0
    col_ids = lax.broadcasted_iota(jnp.int32, value.shape, 1) + orb * width
    root[...] = value + jnp.where(row_ids == col_ids, 1.0, 0.0)


def root_of(meta, top, low, offset, side):
    coarse, width = offset.shape
    vmem = pl.BlockSpec(memory_space=pltpu.VMEM)
    return pl.pallas_call(
        root_kernel,
        out_shape=jax.ShapeDtypeStruct(offset.shape, f32),
        in_specs=[pl.BlockSpec(memory_space=pltpu.SMEM), vmem, vmem, vmem],
        out_specs=vmem,
        scratch_shapes=[
            pltpu.VMEM((side, side), bf16),
            pltpu.VMEM((coarse, side), f32),
            pltpu.VMEM((side, width), bf16),
        ],
        compiler_params=params(40),
        name="root",
    )(meta, top, low, offset)


def kinetic_kernel(edge, slots, table, scale, *refs):
    parts, (pot, fwd_in, fwd_out, back_in, back_out), out = refs[:6], refs[6:11], refs[11]
    raw, x, rounded, left_over, total, total_fix, sems = refs[12:]
    square = edge * edge
    own = PAIR * slots
    width = x.shape[3]
    copies = [pltpu.make_async_copy(part, raw.at[place], sems.at[place]) for place, part in enumerate(parts)]
    for copy in copies:
        copy.start()
    x[...] = jnp.zeros_like(x)
    total[...] = jnp.zeros_like(total)
    total_fix[...] = jnp.zeros_like(total_fix)
    for copy in copies:
        copy.wait()

    def lay_out(place, carry):
        for slot in range(slots):
            for i in range(edge):
                part, row = i // (edge // 2), i % (edge // 2) * square
                x[place * slots + slot, i, :square, :] = raw[
                    place, slot, row : row + square, part * width : (part + 1) * width
                ]
        return carry

    lax.fori_loop(0, len(parts), lay_out, 0)
    chunks = -(-square // ROWS)

    def per_slot(s, carry):
        @pl.when(table[s, 0] >= 0)
        def _():
            own_scale = scale[s]
            for a in range(3):
                source = [table[s, 1 + 3 * a + k] for k in range(3)]
                for i in range(chunks if a == 0 else edge):
                    if a == 0:
                        rows = slice(i * ROWS, (i + 1) * ROWS)
                        block = jnp.concatenate([x[t, :, rows, :].reshape(edge * ROWS, width) for t in source], axis=0)
                        exact = (own_scale * matmul(fwd_out[...], block)).reshape(edge, ROWS, width)
                        value = exact.astype(bf16)
                        rounded[:, rows, :] = value
                        left_over[:, rows, :] = (value.astype(f32) - exact).astype(bf16)
                    else:
                        block = jnp.concatenate([x[t, i] for t in source], axis=0)
                        exact = own_scale * matmul(fwd_in[a - 1], block)
                        value = exact.astype(bf16)
                        rounded[i] = value
                        left_over[i] = (value.astype(f32) - exact).astype(bf16)
                half = 0.5 * own_scale
                for k in range(3):
                    target = source[k]

                    @pl.when(target < own)
                    def _():
                        for i in range(chunks if a == 0 else edge):
                            for field, sum_ref in ((rounded, total), (left_over, total_fix)):
                                if a == 0:
                                    rows = slice(i * ROWS, (i + 1) * ROWS)
                                    term = matmul(back_out[k], field[:, rows, :].reshape(edge * ROWS, width))
                                    sum_ref[target, :, rows, :] += half * term.reshape(edge, ROWS, width)
                                else:
                                    sum_ref[target, i] += half * matmul(back_in[a - 1, k], field[i])

        return carry

    lax.fori_loop(0, table.shape[0], per_slot, 0)

    def finish(t, carry):
        for i in range(edge):
            rows = slice(i * square, (i + 1) * square)
            exact = pot[t, rows, :] * x[t, i, :square, :].astype(f32)
            lost = exact.astype(bf16).astype(f32) - exact
            whole = total[t, i, :square, :] + exact
            top = whole.astype(bf16)
            low = (whole - top.astype(f32)).astype(bf16)
            fix = (total_fix[t, i, :square, :] + lost).astype(bf16)
            out[t, rows, :] = jnp.concatenate([top, low, fix], axis=1)
        return carry

    lax.fori_loop(0, own, finish, 0)


def block_matrices(deriv_blocks):
    edge = deriv_blocks.shape[1]
    square = edge * edge
    padded = -(-square // ROWS) * ROWS
    ids = np.arange(padded)
    slow = ((ids[:, None] // edge) == np.arange(edge)).astype(np.float32)
    fast = (((ids[:, None] % edge) == np.arange(edge)) & (ids[:, None] < square)).astype(np.float32)
    ids = np.arange(edge * ROWS)
    outer = ((ids[:, None] // ROWS) == np.arange(edge)).astype(np.float32)
    within = ((ids[:, None] % ROWS) == np.arange(ROWS)).astype(np.float32)
    stacked = jnp.moveaxis(deriv_blocks, 0, 1).reshape(edge, 3 * edge)
    forward, backward = [], []
    for spot, mask in ((slow, fast), (fast, slow), (outer, within)):
        same = mask @ mask.T
        spread_out = np.kron(np.eye(3, dtype=np.float32), spot.T)
        spot_b, same_b = jnp.asarray(spot, bf16), jnp.asarray(same, f32)
        wide = matmul(matmul(spot_b, stacked).astype(bf16), jnp.asarray(spread_out, bf16))
        forward.append((wide * jnp.tile(same_b, (1, 3))).astype(bf16))
        turned = jnp.einsum("ri,kji->krj", spot_b, deriv_blocks, preferred_element_type=f32).astype(bf16)
        turned = jnp.einsum("krj,cj->krc", turned, spot_b, preferred_element_type=f32)
        backward.append((turned * same_b).astype(bf16))
    return jnp.stack(forward[:2]), forward[2], jnp.stack(backward[:2]), backward[2]


def kinetic(parts, pot, matrices, table, scale, edge, coefficients):
    slots, folded, lanes = parts[0].shape
    width = lanes // 2
    padded = matrices[0].shape[1]
    own = PAIR * slots
    vmem = pl.BlockSpec(memory_space=pltpu.VMEM)
    smem = pl.BlockSpec(memory_space=pltpu.SMEM)
    anywhere = pl.BlockSpec(memory_space=pl.ANY)
    return pl.pallas_call(
        functools.partial(kinetic_kernel, edge, slots),
        out_shape=jax.ShapeDtypeStruct((own, coefficients, 3 * width), bf16),
        in_specs=[smem, smem] + [anywhere] * 6 + [vmem] * 5,
        out_specs=vmem,
        scratch_shapes=[
            pltpu.VMEM((6, slots, folded, lanes), bf16),
            pltpu.VMEM((6 * slots + 1, edge, padded, width), bf16),
            pltpu.VMEM((edge, padded, width), bf16),
            pltpu.VMEM((edge, padded, width), bf16),
            pltpu.VMEM((own, edge, padded, width), f32),
            pltpu.VMEM((own, edge, padded, width), f32),
            pltpu.SemaphoreType.DMA((6,)),
        ],
        compiler_params=params(48),
        cost_estimate=pl.CostEstimate(flops=2 * 10**10, bytes_accessed=40 * 10**6, transcendentals=0),
        name="kinetic",
    )(table, scale, *parts, pot, *matrices)


def body(orbitals, potential, deriv_blocks, levels, box_counts, neighbours):
    slots, coefficients, own_width = orbitals.shape
    edge = deriv_blocks.shape[1]
    level, pair, orb = lax.axis_index("lvl"), lax.axis_index("pair"), lax.axis_index("orb")
    level_count, orb_count = lax.axis_size("lvl"), lax.axis_size("orb")
    half, fold = own_width // PAIR, coefficients // 2
    all_width = own_width * orb_count
    box_rows = all_width // (level_count * PAIR)
    first = pair == 0
    groups = range(orb_count)
    square_grid = level_count == orb_count and box_rows == half
    row0, col0 = (level * PAIR + pair) * box_rows, orb * own_width

    slot_ids = jnp.arange(slots, dtype=jnp.int32)
    own_ids = (level * PAIR + pair) * slots + slot_ids
    none = 16 * slots
    apart_ids = jnp.where(neighbours >= 0, neighbours - own_ids[:, None, None], none).reshape(slots, 6)
    live = (slot_ids < box_counts[0]).astype(jnp.int32)
    facts = jnp.concatenate([apart_ids, levels[:, None], live[:, None]], axis=1)
    wide_facts = jnp.pad(facts.astype(f32), ((0, 0), (0, own_width - facts.shape[1])))
    active, mine, theirs = pack(jnp.stack([pair, box_counts[0]]).astype(jnp.int32), orbitals, wide_facts)

    far = {q: swap(active, "orb", q) for q in groups if q and q % 2 == 0}
    beside = swap(theirs, "pair", 1)
    lower, upper = shift(mine, "lvl", 1), shift(mine, "lvl", -1)
    beside_rest = swap(mine, "pair", 1)
    later_pot, beside = lax.optimization_barrier((potential, beside))
    lower_beside, upper_beside = shift(beside, "lvl", 1), shift(beside, "lvl", -1)
    other_pot = swap(later_pot, "pair", 1)
    matrices = block_matrices(deriv_blocks)

    far, beside_rest, lower, upper, active, matrices = lax.optimization_barrier(
        (far, beside_rest, lower, upper, active, matrices)
    )

    def unfold(packed):
        return jnp.concatenate([packed[:, :fold, :half], packed[:, :fold, half:]], axis=1)

    beside_half, rest_half = unfold(beside), unfold(beside_rest)
    beside_all = jnp.concatenate(
        [jnp.where(first, beside_half, rest_half), jnp.where(first, rest_half, beside_half)], axis=2
    )
    cut = slots // 2
    far_beside = {
        q: jnp.concatenate([swap(beside_all[:cut], "orb", q), swap(far[q][cut:], "pair", 1)]) for q in far
    }
    left_own = {0: active, 1: swap(active, "orb", 1), **far}
    left_beside = {0: beside_all, 1: swap(beside_all, "orb", 1), **far_beside}
    for q in far:
        left_own[q + 1] = swap(far[q], "orb", 1)
        left_beside[q + 1] = swap(far_beside[q], "orb", 1)
    flat = lambda block: block.reshape(slots * coefficients, block.shape[-1])
    lefts = [flat(left_own[q]) for q in groups] + [flat(left_beside[q]) for q in groups]

    def facts_of(packed):
        return packed[:, fold, : facts.shape[1]].astype(f32).astype(jnp.int32)

    box_of_level = level * PAIR
    ids = jnp.concatenate(
        [
            own_ids,
            (box_of_level + 1 - pair) * slots + slot_ids,
            (box_of_level - 1) * slots + slot_ids,
            (box_of_level + PAIR) * slots + slot_ids,
        ]
    ).astype(jnp.int32)
    chosen = jnp.concatenate(
        [
            facts,
            facts_of(beside),
            jnp.where(first, facts_of(lower_beside), facts_of(lower)),
            jnp.where(first, facts_of(upper), facts_of(upper_beside)),
        ]
    )
    there = (ids >= 0) & (ids < level_count * PAIR * slots)

    def place(slot_id):
        box = slot_id // slots
        apart = box // PAIR - level
        base = jnp.where(apart == 0, 0, jnp.where(apart < 0, 2, 4))
        return (base + (box % PAIR != pair)) * slots + slot_id % slots

    distance = chosen[:, :6]
    near = jnp.where(distance < none, place(jnp.maximum(ids, 0)[:, None] + distance), 6 * slots)
    near = jnp.clip(near, 0, 6 * slots)
    self_place = place(jnp.maximum(ids, 0))
    table = [jnp.where(there & (chosen[:, 7] > 0), self_place, -1)]
    for a in range(3):
        table += [near[:, 2 * a], self_place, near[:, 2 * a + 1]]
    table = jnp.stack(table, axis=1).astype(jnp.int32)
    level_of = chosen[:, 6]
    scale = jnp.where(level_of == 0, 0.5, jnp.where(level_of == 1, 1.0, 2.0)).astype(f32)
    pot = jnp.concatenate([potential, other_pot])[:, :, None]

    def natural(blocks):
        return jnp.concatenate([lax.dynamic_index_in_dim(blocks, orb ^ j, keepdims=False) for j in groups], axis=1)

    def deliver(blocks):
        got = []
        for step in groups:
            to = [(z * orb_count + o, o * orb_count + (z ^ step)) for z in range(level_count) for o in groups]
            got.append(lax.ppermute(blocks[step], ("lvl", "orb"), to))
        return got

    def own_block(strip):
        strip = lax.all_gather(lax.psum(strip, "lvl"), ("orb", "pair"), axis=0, tiled=True)
        strip = lax.dynamic_slice_in_dim(strip, row0, box_rows, axis=0)
        return lax.dynamic_slice_in_dim(strip, col0, own_width, axis=1)

    apart = orb ^ level if square_grid else 0 * orb
    meta = jnp.stack([pair, apart]).astype(jnp.int32)

    parts = [mine, beside, lower, lower_beside, upper, upper_beside]
    right = kinetic(parts, pot, matrices, table, scale, edge, coefficients)

    shape = (orb_count, half, own_width)
    blocks = row_products(
        functools.partial(correlation_kernel, level_count), "correlation", meta, lefts, None, shape, half
    )
    if square_grid:
        offset = sum(block.astype(f32) for block in deliver(blocks))
    else:
        offset = own_block(natural(blocks).astype(f32))
    row_ids = row0 + jnp.arange(box_rows, dtype=jnp.int32)
    col_ids = col0 + jnp.arange(own_width, dtype=jnp.int32)
    correlation = offset + (row_ids[:, None] == col_ids[None, :]).astype(f32)
    small = offset.astype(bf16)

    right = right.reshape(2, slots * coefficients, 3 * half)
    shape = (orb_count, 3, half, own_width)
    blocks = row_products(fock_kernel, "fock", meta, lefts, right, shape, 3 * half)
    if square_grid:
        sums = sum(block.astype(f32) for block in deliver(blocks))
        share = sums[2].astype(bf16)
        pieces = []
        for over in range(PAIR):
            to_first = (pair ^ over) == 0
            sent = jnp.where(to_first, share[:, :half], share[:, half:])
            to = [
                ((z * PAIR + y) * orb_count + o, (o * PAIR + (y ^ over)) * orb_count + z)
                for z in range(level_count)
                for y in range(PAIR)
                for o in groups
            ]
            pieces.append(lax.ppermute(sent, BOX + ("orb",), to).astype(f32).T)
        turned = jnp.concatenate(
            [jnp.where(first, pieces[0], pieces[1]), jnp.where(first, pieces[1], pieces[0])], axis=1
        )
        fock = sums[0] + sums[1] + turned
    else:
        fock = own_block(natural(blocks[:, 0]).astype(f32) + natural(blocks[:, 1]).astype(f32))
        share = lax.all_gather(lax.psum(natural(blocks[:, 2]).astype(f32), "lvl"), "pair", axis=0, tiled=True)
        fock = fock + lax.dynamic_slice_in_dim(share, row0, box_rows, axis=1).T

    if square_grid:
        levels_of, far_of = range(level_count), range(0, orb_count, 2)
        top, low = small[: box_rows // 2], small[box_rows // 2 :]
        top = spread(spread(spread(spread(top, "lvl", levels_of), "pair", (0, 1)), "orb", far_of), "orb", (0, 1))
        low = spread(spread(spread(spread(low, "orb", far_of), "lvl", levels_of), "pair", (0, 1)), "orb", (0, 1))
        inverse_root = root_of(jnp.stack([level, pair, orb]).astype(jnp.int32), top, low, offset, all_width)
    else:
        gathered = lax.all_gather(small, "orb", axis=1, tiled=True)
        whole = lax.all_gather(gathered, BOX, axis=0, tiled=True)
        rows_of = lax.dynamic_slice_in_dim(whole, row0, box_rows, axis=0)
        cols_of = lax.dynamic_slice_in_dim(whole, col0, own_width, axis=1)
        row_square, col_square = matmul(rows_of, whole), matmul(whole, cols_of)
        left = (rows_of.astype(f32) - 0.25 * row_square).astype(bf16)
        right_side = (0.25 * (cols_of.astype(f32) - col_square)).astype(bf16)
        own_square = lax.dynamic_slice_in_dim(row_square, col0, own_width, axis=1)
        inverse_root = correlation - 1.5 * offset + 0.125 * own_square + matmul(left, right_side)
    return fock, correlation, inverse_root


def solution(mesh):
    levels = mesh.shape["box"] // PAIR
    split = Mesh(mesh.devices.reshape(levels, PAIR, mesh.shape["orb"]), ("lvl", "pair", "orb"))
    in_specs = (P(BOX, None, "orb"), P(BOX, None), P(), P(BOX), P(BOX), P(BOX, None, None))
    out_specs = (P(BOX, "orb"),) * 3
    return jax.shard_map(body, mesh=split, in_specs=in_specs, out_specs=out_specs, check_vma=False)
```

```python
import functools

import jax
import jax.numpy as jnp
import numpy as np
from jax import lax
from jax.experimental import pallas as pl
from jax.experimental.pallas import tpu as pltpu
from jax.sharding import Mesh, PartitionSpec as P

PAIR = 2
ROWS = 16
BOX = ("lvl", "pair")
f32, bf16 = jnp.float32, jnp.bfloat16


def swap(value, axis, bit):
    count = lax.axis_size(axis)
    return lax.ppermute(value, axis, [(i, i ^ bit) for i in range(count)])


def shift(value, axis, step):
    count = lax.axis_size(axis)
    return lax.ppermute(value, axis, [(i, i + step) for i in range(count) if 0 <= i + step < count])


def contract(left, right):
    return lax.dot_general(left, right, (((0,), (0,)), ((), ())), preferred_element_type=f32)


def matmul(left, right):
    return jnp.dot(left, right, preferred_element_type=f32)


def spread(value, axis, bits):
    return jnp.stack([swap(value, axis, bit) if bit else value for bit in bits])


def params(mebibytes):
    return pltpu.CompilerParams(vmem_limit_bytes=mebibytes * 1024 * 1024)


def pack_kernel(meta, orbitals, facts, active, mine, theirs):
    slots, coefficients, width = orbitals.shape
    half, fold = width // PAIR, coefficients // 2
    first = meta[0] == 0
    for slot in range(slots):
        keep = slot < meta[1]
        for part in range(2):
            rows = slice(part * fold, (part + 1) * fold)
            here = orbitals[slot, rows, :]
            here = jnp.where(keep, here, jnp.zeros_like(here))
            active[slot, rows, :] = here
            low, high = here[:, :half], here[:, half:]
            lanes = slice(part * half, (part + 1) * half)
            mine[slot, :fold, lanes] = jnp.where(first, low, high)
            theirs[slot, :fold, lanes] = jnp.where(first, high, low)
        for out in (mine, theirs):
            out[slot, fold:, :] = jnp.broadcast_to(facts[slot : slot + 1, :], (out.shape[1] - fold, width)).astype(bf16)


def pack(meta, orbitals, facts):
    slots, coefficients, width = orbitals.shape
    fold = coefficients // 2
    padded = (fold // ROWS + 1) * ROWS
    vmem = pl.BlockSpec(memory_space=pltpu.VMEM)
    packed = jax.ShapeDtypeStruct((slots, padded, width), bf16)
    return pl.pallas_call(
        pack_kernel,
        out_shape=(jax.ShapeDtypeStruct(orbitals.shape, bf16), packed, packed),
        in_specs=[pl.BlockSpec(memory_space=pltpu.SMEM), vmem, vmem],
        out_specs=(vmem, vmem, vmem),
        compiler_params=params(24),
        name="pack",
    )(meta, orbitals, facts)


def load_left(lefts, held, sems):
    copies = [pltpu.make_async_copy(left, held.at[i], sems.at[i]) for i, left in enumerate(lefts)]
    for copy in copies:
        copy.start()
    return copies


def correlation_kernel(share, meta, *refs):
    refs, (out, held, turned, sems) = refs[:-4], refs[-4:]
    groups, half, width = out.shape
    lefts, before = refs[:groups], refs[groups:]
    copies = load_left(lefts, held, sems)
    first, apart = meta[0] == 0, meta[1]
    copies[0].wait()
    own = held[0]
    turned[...] = jnp.where(first, own[:, :half], own[:, half:]).T
    for copy in copies[1:]:
        copy.wait()

    def per_group(q, carry):
        total = matmul(turned[...], held[q])
        if before:
            rows = lax.broadcasted_iota(jnp.int32, (half, width), 0) + jnp.where(first, 0, half)
            columns = lax.broadcasted_iota(jnp.int32, (half, width), 1)
            total = total + before[0][q ^ apart] - jnp.where((rows == columns) & (q == 0), share, 0.0)
        out[q ^ apart] = total.astype(out.dtype)
        return carry

    lax.fori_loop(0, groups, per_group, 0)


def box_correlation(share, meta, lefts, before, half):
    depth, width = lefts[0].shape
    vmem = pl.BlockSpec(memory_space=pltpu.VMEM)
    extra = [] if before is None else [before]
    return pl.pallas_call(
        functools.partial(correlation_kernel, share),
        out_shape=jax.ShapeDtypeStruct((len(lefts), half, width), f32 if before is None else bf16),
        in_specs=[pl.BlockSpec(memory_space=pltpu.SMEM)]
        + [pl.BlockSpec(memory_space=pl.ANY)] * len(lefts)
        + [vmem] * len(extra),
        out_specs=vmem,
        scratch_shapes=[
            pltpu.VMEM((len(lefts), depth, width), bf16),
            pltpu.VMEM((half, depth), bf16),
            pltpu.SemaphoreType.DMA((len(lefts),)),
        ],
        compiler_params=params(32),
        cost_estimate=pl.CostEstimate(
            flops=2 * len(lefts) * depth * width * half, bytes_accessed=2 * len(lefts) * depth * width, transcendentals=0
        ),
        name="correlation",
    )(meta, *lefts, *extra)


def fock_kernel(meta, *refs):
    lefts, right, out, held, raw, turned, sems = refs[:-6], refs[-6], refs[-5], refs[-4], refs[-3], refs[-2], refs[-1]
    copies = load_left(lefts, held, sems)
    last = pltpu.make_async_copy(right, raw, sems.at[len(lefts)])
    last.start()
    groups = len(lefts) // 2
    half, width = out.shape[2:]
    apart = meta[1]
    last.wait()
    for side in range(2):
        turned[side] = raw[side].T
    for copy in copies:
        copy.wait()

    def per_group(q, carry):
        total = matmul(turned[0], held[q]) + matmul(turned[1], held[groups + q])
        main = total[:half] + total[half : 2 * half]
        top = main.astype(bf16)
        out[q ^ apart, 0] = top
        out[q ^ apart, 1] = (main - top.astype(f32)).astype(bf16)
        out[q ^ apart, 2] = total[2 * half :].astype(bf16)
        return carry

    lax.fori_loop(0, groups, per_group, 0)


def fock_rows(meta, lefts, right):
    depth, width = lefts[0].shape
    tall = right.shape[-1]
    anywhere = pl.BlockSpec(memory_space=pl.ANY)
    return pl.pallas_call(
        fock_kernel,
        out_shape=jax.ShapeDtypeStruct((len(lefts) // 2, 3, tall // 3, width), bf16),
        in_specs=[pl.BlockSpec(memory_space=pltpu.SMEM)] + [anywhere] * (len(lefts) + 1),
        out_specs=pl.BlockSpec(memory_space=pltpu.VMEM),
        scratch_shapes=[
            pltpu.VMEM((len(lefts), depth, width), bf16),
            pltpu.VMEM(right.shape, bf16),
            pltpu.VMEM((2, tall, depth), bf16),
            pltpu.SemaphoreType.DMA((len(lefts) + 1,)),
        ],
        compiler_params=params(40),
        cost_estimate=pl.CostEstimate(
            flops=2 * len(lefts) * depth * width * tall, bytes_accessed=2 * len(lefts) * depth * width, transcendentals=0
        ),
        name="fock",
    )(meta, *lefts, right)


def root_kernel(meta, top, low, offset, root, whole, rows_f, cols_b):
    level, pair, orb = meta[0], meta[1], meta[2]
    coarse, width = top.shape[4:]
    side = whole.shape[0]
    groups = side // width
    for core in range(2):
        for far in range(top.shape[1]):
            lanes = pl.ds(pl.multiple_of((orb ^ (2 * far + core)) * width, width), width)
            for z in range(top.shape[3]):
                for y in range(PAIR):
                    start = ((level ^ z) * PAIR + (pair ^ y)) * coarse
                    whole[pl.ds(pl.multiple_of(start, coarse), coarse), lanes] = top[core, far, y, z]
                    start = ((level ^ (z + top.shape[3])) * PAIR + (pair ^ y)) * coarse
                    whole[pl.ds(pl.multiple_of(start, coarse), coarse), lanes] = low[core, y, far, z]
    row0 = pl.multiple_of((level * PAIR + pair) * coarse, coarse)
    own_lanes = pl.ds(pl.multiple_of(orb * width, width), width)
    rows = whole[pl.ds(row0, coarse), :]

    def across(j, carry):
        lanes = pl.ds(pl.multiple_of(j * width, width), width)
        rows_f[:, lanes] = matmul(rows, whole[:, lanes])
        return carry

    lax.fori_loop(0, groups, across, 0)
    columns = whole[:, own_lanes]

    def down(i, carry):
        here = pl.ds(pl.multiple_of(i * coarse, coarse), coarse)
        square = matmul(whole[here, :], columns)
        cols_b[here, :] = (0.25 * (whole[here, own_lanes].astype(f32) - square)).astype(bf16)
        return carry

    lax.fori_loop(0, side // coarse, down, 0)
    left = (rows.astype(f32) - 0.25 * rows_f[...]).astype(bf16)
    value = matmul(left, cols_b[...]) + 0.125 * rows_f[:, own_lanes] - 0.5 * offset[...]
    row_ids = lax.broadcasted_iota(jnp.int32, value.shape, 0) + row0
    col_ids = lax.broadcasted_iota(jnp.int32, value.shape, 1) + orb * width
    root[...] = value + jnp.where(row_ids == col_ids, 1.0, 0.0)


def root_of(meta, top, low, offset, side):
    coarse, width = offset.shape
    vmem = pl.BlockSpec(memory_space=pltpu.VMEM)
    return pl.pallas_call(
        root_kernel,
        out_shape=jax.ShapeDtypeStruct(offset.shape, f32),
        in_specs=[pl.BlockSpec(memory_space=pltpu.SMEM), vmem, vmem, vmem],
        out_specs=vmem,
        scratch_shapes=[
            pltpu.VMEM((side, side), bf16),
            pltpu.VMEM((coarse, side), f32),
            pltpu.VMEM((side, width), bf16),
        ],
        compiler_params=params(40),
        name="root",
    )(meta, top, low, offset)


def kinetic_kernel(edge, slots, table, scale, *refs):
    parts, (pot, fwd_in, fwd_out, back_in, back_out), out = refs[:6], refs[6:11], refs[11]
    raw, x, rounded, left_over, total, total_fix, sems = refs[12:]
    square = edge * edge
    own = PAIR * slots
    width = x.shape[3]
    copies = [pltpu.make_async_copy(part, raw.at[place], sems.at[place]) for place, part in enumerate(parts)]
    for copy in copies:
        copy.start()
    x[...] = jnp.zeros_like(x)
    total[...] = jnp.zeros_like(total)
    total_fix[...] = jnp.zeros_like(total_fix)
    for copy in copies:
        copy.wait()

    def lay_out(place, carry):
        for slot in range(slots):
            for i in range(edge):
                part, row = i // (edge // 2), i % (edge // 2) * square
                x[place * slots + slot, i, :square, :] = raw[
                    place, slot, row : row + square, part * width : (part + 1) * width
                ]
        return carry

    lax.fori_loop(0, len(parts), lay_out, 0)
    chunks = -(-square // ROWS)

    def per_slot(s, carry):
        @pl.when(table[s, 0] >= 0)
        def _():
            own_scale = scale[s]
            for a in range(3):
                source = [table[s, 1 + 3 * a + k] for k in range(3)]
                for i in range(chunks if a == 0 else edge):
                    if a == 0:
                        rows = slice(i * ROWS, (i + 1) * ROWS)
                        block = jnp.concatenate([x[t, :, rows, :].reshape(edge * ROWS, width) for t in source], axis=0)
                        exact = (own_scale * matmul(fwd_out[...], block)).reshape(edge, ROWS, width)
                        value = exact.astype(bf16)
                        rounded[:, rows, :] = value
                        left_over[:, rows, :] = (value.astype(f32) - exact).astype(bf16)
                    else:
                        block = jnp.concatenate([x[t, i] for t in source], axis=0)
                        exact = own_scale * matmul(fwd_in[a - 1], block)
                        value = exact.astype(bf16)
                        rounded[i] = value
                        left_over[i] = (value.astype(f32) - exact).astype(bf16)
                half = 0.5 * own_scale
                for k in range(3):
                    target = source[k]

                    @pl.when(target < own)
                    def _():
                        for i in range(chunks if a == 0 else edge):
                            for field, sum_ref in ((rounded, total), (left_over, total_fix)):
                                if a == 0:
                                    rows = slice(i * ROWS, (i + 1) * ROWS)
                                    term = matmul(back_out[k], field[:, rows, :].reshape(edge * ROWS, width))
                                    sum_ref[target, :, rows, :] += half * term.reshape(edge, ROWS, width)
                                else:
                                    sum_ref[target, i] += half * matmul(back_in[a - 1, k], field[i])

        return carry

    lax.fori_loop(0, table.shape[0], per_slot, 0)

    def finish(t, carry):
        for i in range(edge):
            rows = slice(i * square, (i + 1) * square)
            exact = pot[t, rows, :] * x[t, i, :square, :].astype(f32)
            lost = exact.astype(bf16).astype(f32) - exact
            whole = total[t, i, :square, :] + exact
            top = whole.astype(bf16)
            low = (whole - top.astype(f32)).astype(bf16)
            fix = (total_fix[t, i, :square, :] + lost).astype(bf16)
            out[t, rows, :] = jnp.concatenate([top, low, fix], axis=1)
        return carry

    lax.fori_loop(0, own, finish, 0)


def block_matrices(deriv_blocks):
    edge = deriv_blocks.shape[1]
    square = edge * edge
    padded = -(-square // ROWS) * ROWS
    ids = np.arange(padded)
    slow = ((ids[:, None] // edge) == np.arange(edge)).astype(np.float32)
    fast = (((ids[:, None] % edge) == np.arange(edge)) & (ids[:, None] < square)).astype(np.float32)
    ids = np.arange(edge * ROWS)
    outer = ((ids[:, None] // ROWS) == np.arange(edge)).astype(np.float32)
    within = ((ids[:, None] % ROWS) == np.arange(ROWS)).astype(np.float32)
    stacked = jnp.moveaxis(deriv_blocks, 0, 1).reshape(edge, 3 * edge)
    forward, backward = [], []
    for spot, mask in ((slow, fast), (fast, slow), (outer, within)):
        same = mask @ mask.T
        spread_out = np.kron(np.eye(3, dtype=np.float32), spot.T)
        spot_b, same_b = jnp.asarray(spot, bf16), jnp.asarray(same, f32)
        wide = matmul(matmul(spot_b, stacked).astype(bf16), jnp.asarray(spread_out, bf16))
        forward.append((wide * jnp.tile(same_b, (1, 3))).astype(bf16))
        turned = jnp.einsum("ri,kji->krj", spot_b, deriv_blocks, preferred_element_type=f32).astype(bf16)
        turned = jnp.einsum("krj,cj->krc", turned, spot_b, preferred_element_type=f32)
        backward.append((turned * same_b).astype(bf16))
    return jnp.stack(forward[:2]), forward[2], jnp.stack(backward[:2]), backward[2]


def kinetic(parts, pot, matrices, table, scale, edge, coefficients):
    slots, folded, lanes = parts[0].shape
    width = lanes // 2
    padded = matrices[0].shape[1]
    own = PAIR * slots
    vmem = pl.BlockSpec(memory_space=pltpu.VMEM)
    smem = pl.BlockSpec(memory_space=pltpu.SMEM)
    anywhere = pl.BlockSpec(memory_space=pl.ANY)
    return pl.pallas_call(
        functools.partial(kinetic_kernel, edge, slots),
        out_shape=jax.ShapeDtypeStruct((own, coefficients, 3 * width), bf16),
        in_specs=[smem, smem] + [anywhere] * 6 + [vmem] * 5,
        out_specs=vmem,
        scratch_shapes=[
            pltpu.VMEM((6, slots, folded, lanes), bf16),
            pltpu.VMEM((6 * slots + 1, edge, padded, width), bf16),
            pltpu.VMEM((edge, padded, width), bf16),
            pltpu.VMEM((edge, padded, width), bf16),
            pltpu.VMEM((own, edge, padded, width), f32),
            pltpu.VMEM((own, edge, padded, width), f32),
            pltpu.SemaphoreType.DMA((6,)),
        ],
        compiler_params=params(48),
        cost_estimate=pl.CostEstimate(flops=2 * 10**10, bytes_accessed=40 * 10**6, transcendentals=0),
        name="kinetic",
    )(table, scale, *parts, pot, *matrices)


def body(orbitals, potential, deriv_blocks, levels, box_counts, neighbours):
    slots, coefficients, own_width = orbitals.shape
    edge = deriv_blocks.shape[1]
    level, pair, orb = lax.axis_index("lvl"), lax.axis_index("pair"), lax.axis_index("orb")
    level_count, orb_count = lax.axis_size("lvl"), lax.axis_size("orb")
    half, fold = own_width // PAIR, coefficients // 2
    all_width = own_width * orb_count
    box_rows = all_width // (level_count * PAIR)
    first = pair == 0
    groups = range(orb_count)
    square_grid = level_count == orb_count and box_rows == half
    row0, col0 = (level * PAIR + pair) * box_rows, orb * own_width

    slot_ids = jnp.arange(slots, dtype=jnp.int32)
    own_ids = (level * PAIR + pair) * slots + slot_ids
    none = 16 * slots
    apart_ids = jnp.where(neighbours >= 0, neighbours - own_ids[:, None, None], none).reshape(slots, 6)
    live = (slot_ids < box_counts[0]).astype(jnp.int32)
    facts = jnp.concatenate([apart_ids, levels[:, None], live[:, None]], axis=1)
    wide_facts = jnp.pad(facts.astype(f32), ((0, 0), (0, own_width - facts.shape[1])))
    active, mine, theirs = pack(jnp.stack([pair, box_counts[0]]).astype(jnp.int32), orbitals, wide_facts)

    far = {q: swap(active, "orb", q) for q in groups if q and q % 2 == 0}
    beside = swap(theirs, "pair", 1)
    lower, upper = shift(mine, "lvl", 1), shift(mine, "lvl", -1)
    beside_rest = swap(mine, "pair", 1)
    later_pot, beside = lax.optimization_barrier((potential, beside))
    lower_beside, upper_beside = shift(beside, "lvl", 1), shift(beside, "lvl", -1)
    other_pot = swap(later_pot, "pair", 1)
    matrices = block_matrices(deriv_blocks)

    far, beside, beside_rest, lower, upper, lower_beside, upper_beside, other_pot, active, matrices = (
        lax.optimization_barrier(
            (far, beside, beside_rest, lower, upper, lower_beside, upper_beside, other_pot, active, matrices)
        )
    )

    def unfold(packed):
        return jnp.concatenate([packed[:, :fold, :half], packed[:, :fold, half:]], axis=1)

    beside_half, rest_half = unfold(beside), unfold(beside_rest)
    beside_all = jnp.concatenate(
        [jnp.where(first, beside_half, rest_half), jnp.where(first, rest_half, beside_half)], axis=2
    )
    cut = slots // 2
    cross = {q: (swap(beside_all[:cut], "orb", q), swap(far[q][cut:], "pair", 1)) for q in far}
    left_own = {0: active, 1: swap(active, "orb", 1), **far}
    left_beside = {0: beside_all, 1: swap(beside_all, "orb", 1)}
    for q in far:
        left_own[q + 1] = swap(far[q], "orb", 1)

    def facts_of(packed):
        return packed[:, fold, : facts.shape[1]].astype(f32).astype(jnp.int32)

    box_of_level = level * PAIR
    ids = jnp.concatenate(
        [
            own_ids,
            (box_of_level + 1 - pair) * slots + slot_ids,
            (box_of_level - 1) * slots + slot_ids,
            (box_of_level + PAIR) * slots + slot_ids,
        ]
    ).astype(jnp.int32)
    chosen = jnp.concatenate(
        [
            facts,
            facts_of(beside),
            jnp.where(first, facts_of(lower_beside), facts_of(lower)),
            jnp.where(first, facts_of(upper), facts_of(upper_beside)),
        ]
    )
    there = (ids >= 0) & (ids < level_count * PAIR * slots)

    def place(slot_id):
        box = slot_id // slots
        apart = box // PAIR - level
        base = jnp.where(apart == 0, 0, jnp.where(apart < 0, 2, 4))
        return (base + (box % PAIR != pair)) * slots + slot_id % slots

    distance = chosen[:, :6]
    near = jnp.where(distance < none, place(jnp.maximum(ids, 0)[:, None] + distance), 6 * slots)
    near = jnp.clip(near, 0, 6 * slots)
    self_place = place(jnp.maximum(ids, 0))
    table = [jnp.where(there & (chosen[:, 7] > 0), self_place, -1)]
    for a in range(3):
        table += [near[:, 2 * a], self_place, near[:, 2 * a + 1]]
    table = jnp.stack(table, axis=1).astype(jnp.int32)
    level_of = chosen[:, 6]
    scale = jnp.where(level_of == 0, 0.5, jnp.where(level_of == 1, 1.0, 2.0)).astype(f32)
    pot = jnp.concatenate([potential, other_pot])[:, :, None]

    def natural(blocks):
        return jnp.concatenate([lax.dynamic_index_in_dim(blocks, orb ^ j, keepdims=False) for j in groups], axis=1)

    def deliver(block, step):
        to = [(z * orb_count + o, o * orb_count + (z ^ step)) for z in range(level_count) for o in groups]
        return lax.ppermute(block, ("lvl", "orb"), to)

    def own_block(strip):
        strip = lax.all_gather(lax.psum(strip, "lvl"), ("orb", "pair"), axis=0, tiled=True)
        strip = lax.dynamic_slice_in_dim(strip, row0, box_rows, axis=0)
        return lax.dynamic_slice_in_dim(strip, col0, own_width, axis=1)

    apart = orb ^ level if square_grid else 0 * orb
    meta = jnp.stack([pair, apart]).astype(jnp.int32)

    parts = [mine, beside, lower, lower_beside, upper, upper_beside]
    right = kinetic(parts, pot, matrices, table, scale, edge, coefficients)

    cross, right, meta = lax.optimization_barrier((cross, right, meta))
    for q in far:
        left_beside[q] = jnp.concatenate(cross[q])
        left_beside[q + 1] = swap(left_beside[q], "orb", 1)
    flat = lambda block: block.reshape(slots * coefficients, block.shape[-1])
    lefts_own = [flat(left_own[q]) for q in groups]
    lefts_beside = [flat(left_beside[q]) for q in groups]

    share = 1.0 / level_count
    blocks = box_correlation(share, meta, lefts_own, None, half)
    blocks = box_correlation(share, meta, lefts_beside, blocks, half)
    if square_grid:
        offset = sum(deliver(blocks[step], step).astype(f32) for step in groups)
    else:
        offset = own_block(natural(blocks).astype(f32))
    row_ids = row0 + jnp.arange(box_rows, dtype=jnp.int32)
    col_ids = col0 + jnp.arange(own_width, dtype=jnp.int32)
    correlation = offset + (row_ids[:, None] == col_ids[None, :]).astype(f32)
    small = offset.astype(bf16)

    right = right.reshape(2, slots * coefficients, 3 * half)
    blocks = fock_rows(meta, lefts_own + lefts_beside, right)
    if square_grid:
        pieces = [small] + [swap(small, "lvl", z) for z in range(1, level_count)]
        early = orb_count // 2
        pieces, blocks = lax.optimization_barrier((pieces, blocks))
        far_of = range(0, orb_count, 2)
        top = jnp.stack(pieces[: level_count // 2])
        low = jnp.stack(pieces[level_count // 2 :])
        top = spread(spread(top, "pair", (0, 1)), "orb", far_of)
        low = spread(spread(low, "orb", far_of), "pair", (0, 1))
        got = [deliver(blocks[step], step) for step in range(early)]
        top, low, blocks = lax.optimization_barrier((top, low, blocks))
        got += [deliver(blocks[step], step) for step in range(early, orb_count)]
        top, low = spread(top, "orb", (0, 1)), spread(low, "orb", (0, 1))
        sums = sum(block.astype(f32) for block in got)
        share = sums[2].astype(bf16)
        pieces = []
        for over in range(PAIR):
            to_first = (pair ^ over) == 0
            sent = jnp.where(to_first, share[:, :half], share[:, half:])
            to = [
                ((z * PAIR + y) * orb_count + o, (o * PAIR + (y ^ over)) * orb_count + z)
                for z in range(level_count)
                for y in range(PAIR)
                for o in groups
            ]
            pieces.append(lax.ppermute(sent, BOX + ("orb",), to).astype(f32).T)
        turned = jnp.concatenate(
            [jnp.where(first, pieces[0], pieces[1]), jnp.where(first, pieces[1], pieces[0])], axis=1
        )
        fock = sums[0] + sums[1] + turned
    else:
        fock = own_block(natural(blocks[:, 0]).astype(f32) + natural(blocks[:, 1]).astype(f32))
        share = lax.all_gather(lax.psum(natural(blocks[:, 2]).astype(f32), "lvl"), "pair", axis=0, tiled=True)
        fock = fock + lax.dynamic_slice_in_dim(share, row0, box_rows, axis=1).T

    if square_grid:
        inverse_root = root_of(jnp.stack([level, pair, orb]).astype(jnp.int32), top, low, offset, all_width)
    else:
        gathered = lax.all_gather(small, "orb", axis=1, tiled=True)
        whole = lax.all_gather(gathered, BOX, axis=0, tiled=True)
        rows_of = lax.dynamic_slice_in_dim(whole, row0, box_rows, axis=0)
        cols_of = lax.dynamic_slice_in_dim(whole, col0, own_width, axis=1)
        row_square, col_square = matmul(rows_of, whole), matmul(whole, cols_of)
        left = (rows_of.astype(f32) - 0.25 * row_square).astype(bf16)
        right_side = (0.25 * (cols_of.astype(f32) - col_square)).astype(bf16)
        own_square = lax.dynamic_slice_in_dim(row_square, col0, own_width, axis=1)
        inverse_root = correlation - 1.5 * offset + 0.125 * own_square + matmul(left, right_side)
    return fock, correlation, inverse_root


def solution(mesh):
    levels = mesh.shape["box"] // PAIR
    split = Mesh(mesh.devices.reshape(levels, PAIR, mesh.shape["orb"]), ("lvl", "pair", "orb"))
    in_specs = (P(BOX, None, "orb"), P(BOX, None), P(), P(BOX), P(BOX), P(BOX, None, None))
    out_specs = (P(BOX, "orb"),) * 3
    return jax.shard_map(body, mesh=split, in_specs=in_specs, out_specs=out_specs, check_vma=False)
```

```python
import functools

import jax
import jax.numpy as jnp
import numpy as np
from jax import lax
from jax.experimental import pallas as pl
from jax.experimental.pallas import tpu as pltpu
from jax.sharding import Mesh, PartitionSpec as P

PAIR = 2
ROWS = 16
BOX = ("lvl", "pair")
f32, bf16 = jnp.float32, jnp.bfloat16


def swap(value, axis, bit):
    count = lax.axis_size(axis)
    return lax.ppermute(value, axis, [(i, i ^ bit) for i in range(count)])


def shift(value, axis, step):
    count = lax.axis_size(axis)
    return lax.ppermute(value, axis, [(i, i + step) for i in range(count) if 0 <= i + step < count])


def contract(left, right):
    return lax.dot_general(left, right, (((0,), (0,)), ((), ())), preferred_element_type=f32)


def matmul(left, right):
    return jnp.dot(left, right, preferred_element_type=f32)


def spread(value, axis, bits):
    return jnp.stack([swap(value, axis, bit) if bit else value for bit in bits])


def params(mebibytes):
    return pltpu.CompilerParams(vmem_limit_bytes=mebibytes * 1024 * 1024)


def pack_kernel(meta, orbitals, facts, active, mine, theirs):
    slots, coefficients, width = orbitals.shape
    half, fold = width // PAIR, coefficients // 2
    first = meta[0] == 0
    for slot in range(slots):
        keep = slot < meta[1]
        for part in range(2):
            rows = slice(part * fold, (part + 1) * fold)
            here = orbitals[slot, rows, :]
            here = jnp.where(keep, here, jnp.zeros_like(here))
            active[slot, rows, :] = here
            low, high = here[:, :half], here[:, half:]
            lanes = slice(part * half, (part + 1) * half)
            mine[slot, :fold, lanes] = jnp.where(first, low, high)
            theirs[slot, :fold, lanes] = jnp.where(first, high, low)
        for out in (mine, theirs):
            out[slot, fold:, :] = jnp.broadcast_to(facts[slot : slot + 1, :], (out.shape[1] - fold, width)).astype(bf16)


def pack(meta, orbitals, facts):
    slots, coefficients, width = orbitals.shape
    fold = coefficients // 2
    padded = (fold // ROWS + 1) * ROWS
    vmem = pl.BlockSpec(memory_space=pltpu.VMEM)
    packed = jax.ShapeDtypeStruct((slots, padded, width), bf16)
    return pl.pallas_call(
        pack_kernel,
        out_shape=(jax.ShapeDtypeStruct(orbitals.shape, bf16), packed, packed),
        in_specs=[pl.BlockSpec(memory_space=pltpu.SMEM), vmem, vmem],
        out_specs=(vmem, vmem, vmem),
        compiler_params=params(24),
        name="pack",
    )(meta, orbitals, facts)


def load_left(lefts, held, sems):
    copies = []
    for q, pieces in enumerate(lefts):
        row = 0
        for piece in pieces:
            rows, width = piece.shape
            here = held.at[row : row + rows, q * width : (q + 1) * width]
            copies.append(pltpu.make_async_copy(piece, here, sems.at[len(copies)]))
            row += rows
    for copy in copies:
        copy.start()
    return copies


def grouped(refs, counts):
    refs = list(refs)
    return [[refs.pop(0) for _ in range(count)] for count in counts]


def correlation_kernel(share, counts, meta, *refs):
    refs, (out, held, turned, sems) = refs[:-4], refs[-4:]
    groups, half, width = out.shape
    lefts, before = grouped(refs, counts), refs[sum(counts) :]
    copies = load_left(lefts, held, sems)
    first = meta[0] == 0
    for copy in copies[: counts[0]]:
        copy.wait()
    own = held[:, :width]
    turned[...] = jnp.where(first, own[:, :half], own[:, half:]).T
    for copy in copies[counts[0] :]:
        copy.wait()
    for base in range(0, groups, 2):
        wide = matmul(turned[...], held[:, base * width : (base + 2) * width])
        for q in (base, base + 1):
            total = wide[:, (q - base) * width : (q - base + 1) * width]
            if before:
                total = total + before[0][q]
                if q == 0:
                    rows = lax.broadcasted_iota(jnp.int32, (half, width), 0) + jnp.where(first, 0, half)
                    columns = lax.broadcasted_iota(jnp.int32, (half, width), 1)
                    total = total - jnp.where(rows == columns, share, 0.0)
            out[q] = total.astype(out.dtype)


def box_correlation(share, meta, lefts, before, half):
    depth, width = sum(piece.shape[0] for piece in lefts[0]), lefts[0][0].shape[1]
    counts = [len(pieces) for pieces in lefts]
    vmem = pl.BlockSpec(memory_space=pltpu.VMEM)
    extra = [] if before is None else [before]
    return pl.pallas_call(
        functools.partial(correlation_kernel, share, counts),
        out_shape=jax.ShapeDtypeStruct((len(lefts), half, width), f32 if before is None else bf16),
        in_specs=[pl.BlockSpec(memory_space=pltpu.SMEM)]
        + [pl.BlockSpec(memory_space=pl.ANY)] * sum(counts)
        + [vmem] * len(extra),
        out_specs=vmem,
        scratch_shapes=[
            pltpu.VMEM((depth, len(lefts) * width), bf16),
            pltpu.VMEM((half, depth), bf16),
            pltpu.SemaphoreType.DMA((sum(counts),)),
        ],
        compiler_params=params(32),
        cost_estimate=pl.CostEstimate(
            flops=2 * len(lefts) * depth * width * half, bytes_accessed=2 * len(lefts) * depth * width, transcendentals=0
        ),
        name="correlation",
    )(meta, *[piece for pieces in lefts for piece in pieces], *extra)


def fock_kernel(counts, *refs):
    refs, (right, out, held, raw, turned, sems, last_sems) = refs[:-7], refs[-7:]
    groups, _, half, width = out.shape
    lefts = grouped(refs, counts)
    lasts = [pltpu.make_async_copy(right.at[side], raw.at[side], last_sems.at[side]) for side in range(2)]
    for copy in lasts:
        copy.start()
    copies = []
    for side in range(2):
        blocks = lefts[side * groups : (side + 1) * groups]
        copies += load_left(blocks, held.at[side], sems.at[side])
    for side in range(2):
        lasts[side].wait()
        turned[side] = raw[side].T
    for copy in copies:
        copy.wait()

    def two_groups(j, carry):
        lanes = pl.ds(pl.multiple_of(j * 2 * width, 2 * width), 2 * width)
        total = matmul(turned[0], held[0, :, lanes]) + matmul(turned[1], held[1, :, lanes])
        main = total[:half] + total[half : 2 * half]
        top = main.astype(bf16)
        low = (main - top.astype(f32)).astype(bf16)
        fix = total[2 * half :].astype(bf16)
        for q in range(2):
            here = slice(q * width, (q + 1) * width)
            out[2 * j + q, 0], out[2 * j + q, 1], out[2 * j + q, 2] = top[:, here], low[:, here], fix[:, here]
        return carry

    lax.fori_loop(0, groups // 2, two_groups, 0)


def fock_rows(lefts, right):
    depth, width = sum(piece.shape[0] for piece in lefts[0]), lefts[0][0].shape[1]
    counts = [len(pieces) for pieces in lefts]
    groups, tall = len(lefts) // 2, right.shape[-1]
    most = max(sum(counts[:groups]), sum(counts[groups:]))
    anywhere = pl.BlockSpec(memory_space=pl.ANY)
    return pl.pallas_call(
        functools.partial(fock_kernel, counts),
        out_shape=jax.ShapeDtypeStruct((groups, 3, tall // 3, width), bf16),
        in_specs=[anywhere] * (sum(counts) + 1),
        out_specs=pl.BlockSpec(memory_space=pltpu.VMEM),
        scratch_shapes=[
            pltpu.VMEM((2, depth, groups * width), bf16),
            pltpu.VMEM(right.shape, bf16),
            pltpu.VMEM((2, tall, depth), bf16),
            pltpu.SemaphoreType.DMA((2, most)),
            pltpu.SemaphoreType.DMA((2,)),
        ],
        compiler_params=params(44),
        cost_estimate=pl.CostEstimate(
            flops=2 * len(lefts) * depth * width * tall, bytes_accessed=2 * len(lefts) * depth * width, transcendentals=0
        ),
        name="fock",
    )(*[piece for pieces in lefts for piece in pieces], right)


def root_kernel(meta, top, low, offset, root, whole, rows_f, cols_b):
    level, pair, orb = meta[0], meta[1], meta[2]
    coarse, width = top.shape[4:]
    side = whole.shape[0]
    groups = side // width
    for core in range(2):
        for far in range(top.shape[1]):
            for y in range(PAIR):
                start = ((orb ^ (2 * far + core)) * PAIR + (pair ^ y)) * coarse
                rows = pl.ds(pl.multiple_of(start, coarse), coarse)
                for z in range(top.shape[3]):
                    lanes = pl.ds(pl.multiple_of((level ^ z) * width, width), width)
                    whole[rows, lanes] = top[core, far, y, z]
                    lanes = pl.ds(pl.multiple_of((level ^ (z + top.shape[3])) * width, width), width)
                    whole[rows, lanes] = low[core, y, far, z]
    row0 = pl.multiple_of((level * PAIR + pair) * coarse, coarse)
    own_lanes = pl.ds(pl.multiple_of(orb * width, width), width)
    rows = whole[pl.ds(row0, coarse), :]

    def across(j, carry):
        lanes = pl.ds(pl.multiple_of(j * width, width), width)
        rows_f[:, lanes] = matmul(rows, whole[:, lanes])
        return carry

    lax.fori_loop(0, groups, across, 0)
    columns = whole[:, own_lanes]

    def down(i, carry):
        here = pl.ds(pl.multiple_of(i * coarse, coarse), coarse)
        square = matmul(whole[here, :], columns)
        cols_b[here, :] = (0.25 * (whole[here, own_lanes].astype(f32) - square)).astype(bf16)
        return carry

    lax.fori_loop(0, side // coarse, down, 0)
    left = (rows.astype(f32) - 0.25 * rows_f[...]).astype(bf16)
    value = matmul(left, cols_b[...]) + 0.125 * rows_f[:, own_lanes] - 0.5 * offset[...]
    row_ids = lax.broadcasted_iota(jnp.int32, value.shape, 0) + row0
    col_ids = lax.broadcasted_iota(jnp.int32, value.shape, 1) + orb * width
    root[...] = value + jnp.where(row_ids == col_ids, 1.0, 0.0)


def root_of(meta, top, low, offset, side):
    coarse, width = offset.shape
    vmem = pl.BlockSpec(memory_space=pltpu.VMEM)
    return pl.pallas_call(
        root_kernel,
        out_shape=jax.ShapeDtypeStruct(offset.shape, f32),
        in_specs=[pl.BlockSpec(memory_space=pltpu.SMEM), vmem, vmem, vmem],
        out_specs=vmem,
        scratch_shapes=[
            pltpu.VMEM((side, side), bf16),
            pltpu.VMEM((coarse, side), f32),
            pltpu.VMEM((side, width), bf16),
        ],
        compiler_params=params(40),
        name="root",
    )(meta, top, low, offset)


def kinetic_kernel(edge, slots, table, scale, *refs):
    parts, (pot, fwd_in, fwd_out, back_in, back_out), out = refs[:6], refs[6:11], refs[11]
    raw, x, rounded, left_over, total, total_fix, sems = refs[12:]
    square = edge * edge
    own = PAIR * slots
    width = x.shape[3]
    copies = [pltpu.make_async_copy(part, raw.at[place], sems.at[place]) for place, part in enumerate(parts)]
    for copy in copies:
        copy.start()
    x[...] = jnp.zeros_like(x)
    total[...] = jnp.zeros_like(total)
    total_fix[...] = jnp.zeros_like(total_fix)
    for copy in copies:
        copy.wait()

    def lay_out(place, carry):
        for slot in range(slots):
            for i in range(edge):
                part, row = i // (edge // 2), i % (edge // 2) * square
                x[place * slots + slot, i, :square, :] = raw[
                    place, slot, row : row + square, part * width : (part + 1) * width
                ]
        return carry

    lax.fori_loop(0, len(parts), lay_out, 0)
    chunks = -(-square // ROWS)

    def per_slot(s, carry):
        @pl.when(table[s, 0] >= 0)
        def _():
            own_scale = scale[s]
            for a in range(3):
                source = [table[s, 1 + 3 * a + k] for k in range(3)]
                for i in range(chunks if a == 0 else edge):
                    if a == 0:
                        rows = slice(i * ROWS, (i + 1) * ROWS)
                        block = jnp.concatenate([x[t, :, rows, :].reshape(edge * ROWS, width) for t in source], axis=0)
                        exact = (own_scale * matmul(fwd_out[...], block)).reshape(edge, ROWS, width)
                        value = exact.astype(bf16)
                        rounded[:, rows, :] = value
                        left_over[:, rows, :] = (value.astype(f32) - exact).astype(bf16)
                    else:
                        block = jnp.concatenate([x[t, i] for t in source], axis=0)
                        exact = own_scale * matmul(fwd_in[a - 1], block)
                        value = exact.astype(bf16)
                        rounded[i] = value
                        left_over[i] = (value.astype(f32) - exact).astype(bf16)
                half = 0.5 * own_scale
                for k in range(3):
                    target = source[k]

                    @pl.when(target < own)
                    def _():
                        for i in range(chunks if a == 0 else edge):
                            for field, sum_ref in ((rounded, total), (left_over, total_fix)):
                                if a == 0:
                                    rows = slice(i * ROWS, (i + 1) * ROWS)
                                    term = matmul(back_out[k], field[:, rows, :].reshape(edge * ROWS, width))
                                    sum_ref[target, :, rows, :] += half * term.reshape(edge, ROWS, width)
                                else:
                                    sum_ref[target, i] += half * matmul(back_in[a - 1, k], field[i])

        return carry

    lax.fori_loop(0, table.shape[0], per_slot, 0)

    def finish(t, carry):
        for i in range(edge):
            rows = slice(i * square, (i + 1) * square)
            weighted = (pot[t, rows, :] * x[t, i, :square, :].astype(f32)).astype(bf16)
            whole = total[t, i, :square, :] + weighted.astype(f32)
            top = whole.astype(bf16)
            low = (whole - top.astype(f32)).astype(bf16)
            fix = total_fix[t, i, :square, :].astype(bf16)
            out[t, rows, :] = jnp.concatenate([top, low, fix], axis=1)
        return carry

    lax.fori_loop(0, own, finish, 0)


def block_matrices(deriv_blocks):
    edge = deriv_blocks.shape[1]
    square = edge * edge
    padded = -(-square // ROWS) * ROWS
    ids = np.arange(padded)
    slow = ((ids[:, None] // edge) == np.arange(edge)).astype(np.float32)
    fast = (((ids[:, None] % edge) == np.arange(edge)) & (ids[:, None] < square)).astype(np.float32)
    ids = np.arange(edge * ROWS)
    outer = ((ids[:, None] // ROWS) == np.arange(edge)).astype(np.float32)
    within = ((ids[:, None] % ROWS) == np.arange(ROWS)).astype(np.float32)
    stacked = jnp.moveaxis(deriv_blocks, 0, 1).reshape(edge, 3 * edge)
    forward, backward = [], []
    for spot, mask in ((slow, fast), (fast, slow), (outer, within)):
        same = mask @ mask.T
        spread_out = np.kron(np.eye(3, dtype=np.float32), spot.T)
        spot_b, same_b = jnp.asarray(spot, bf16), jnp.asarray(same, f32)
        wide = matmul(matmul(spot_b, stacked).astype(bf16), jnp.asarray(spread_out, bf16))
        forward.append((wide * jnp.tile(same_b, (1, 3))).astype(bf16))
        turned = jnp.einsum("ri,kji->krj", spot_b, deriv_blocks, preferred_element_type=f32).astype(bf16)
        turned = jnp.einsum("krj,cj->krc", turned, spot_b, preferred_element_type=f32)
        backward.append((turned * same_b).astype(bf16))
    return jnp.stack(forward[:2]), forward[2], jnp.stack(backward[:2]), backward[2]


def kinetic(parts, pot, matrices, table, scale, edge, coefficients):
    slots, folded, lanes = parts[0].shape
    width = lanes // 2
    padded = matrices[0].shape[1]
    own = PAIR * slots
    vmem = pl.BlockSpec(memory_space=pltpu.VMEM)
    smem = pl.BlockSpec(memory_space=pltpu.SMEM)
    anywhere = pl.BlockSpec(memory_space=pl.ANY)
    return pl.pallas_call(
        functools.partial(kinetic_kernel, edge, slots),
        out_shape=jax.ShapeDtypeStruct((own, coefficients, 3 * width), bf16),
        in_specs=[smem, smem] + [anywhere] * 6 + [vmem] * 5,
        out_specs=vmem,
        scratch_shapes=[
            pltpu.VMEM((6, slots, folded, lanes), bf16),
            pltpu.VMEM((6 * slots + 1, edge, padded, width), bf16),
            pltpu.VMEM((edge, padded, width), bf16),
            pltpu.VMEM((edge, padded, width), bf16),
            pltpu.VMEM((own, edge, padded, width), f32),
            pltpu.VMEM((own, edge, padded, width), f32),
            pltpu.SemaphoreType.DMA((6,)),
        ],
        compiler_params=params(48),
        cost_estimate=pl.CostEstimate(flops=2 * 10**10, bytes_accessed=40 * 10**6, transcendentals=0),
        name="kinetic",
    )(table, scale, *parts, pot, *matrices)


def body(orbitals, potential, deriv_blocks, levels, box_counts, neighbours):
    slots, coefficients, own_width = orbitals.shape
    edge = deriv_blocks.shape[1]
    level, pair, orb = lax.axis_index("lvl"), lax.axis_index("pair"), lax.axis_index("orb")
    level_count, orb_count = lax.axis_size("lvl"), lax.axis_size("orb")
    half, fold = own_width // PAIR, coefficients // 2
    all_width = own_width * orb_count
    box_rows = all_width // (level_count * PAIR)
    first = pair == 0
    groups = range(orb_count)
    square_grid = level_count == orb_count and box_rows == half
    row0, col0 = (level * PAIR + pair) * box_rows, orb * own_width

    slot_ids = jnp.arange(slots, dtype=jnp.int32)
    own_ids = (level * PAIR + pair) * slots + slot_ids
    none = 16 * slots
    apart_ids = jnp.where(neighbours >= 0, neighbours - own_ids[:, None, None], none).reshape(slots, 6)
    live = (slot_ids < box_counts[0]).astype(jnp.int32)
    facts = jnp.concatenate([apart_ids, levels[:, None], live[:, None]], axis=1)
    wide_facts = jnp.pad(facts.astype(f32), ((0, 0), (0, own_width - facts.shape[1])))
    active, mine, theirs = pack(jnp.stack([pair, box_counts[0]]).astype(jnp.int32), orbitals, wide_facts)

    far = {q: swap(active, "orb", q) for q in groups if q and q % 2 == 0}
    beside = swap(theirs, "pair", 1)
    lower, upper = shift(mine, "lvl", 1), shift(mine, "lvl", -1)
    later_pot, later_mine, beside = lax.optimization_barrier((potential, mine, beside))
    beside_rest = swap(later_mine, "pair", 1)
    lower_beside, upper_beside = shift(beside, "lvl", 1), shift(beside, "lvl", -1)
    other_pot = swap(later_pot, "pair", 1)
    matrices = block_matrices(deriv_blocks)

    far, beside, beside_rest, lower, upper, lower_beside, upper_beside, other_pot, active, matrices = (
        lax.optimization_barrier(
            (far, beside, beside_rest, lower, upper, lower_beside, upper_beside, other_pot, active, matrices)
        )
    )

    def unfold(packed):
        return jnp.concatenate([packed[:, :fold, :half], packed[:, :fold, half:]], axis=1)

    beside_half, rest_half = unfold(beside), unfold(beside_rest)
    beside_all = jnp.concatenate(
        [jnp.where(first, beside_half, rest_half), jnp.where(first, rest_half, beside_half)], axis=2
    )
    flat = lambda block: block.reshape(-1, block.shape[-1])
    cut = -(-slots * coefficients // (2 * ROWS)) * ROWS
    cross = {q: (swap(flat(beside_all)[:cut], "orb", q), swap(flat(far[q])[cut:], "pair", 1)) for q in far}
    left_own = {0: active, 1: swap(active, "orb", 1), **far}
    left_beside = {0: beside_all, 1: swap(beside_all, "orb", 1)}
    for q in far:
        left_own[q + 1] = swap(far[q], "orb", 1)

    def facts_of(packed):
        return packed[:, fold, : facts.shape[1]].astype(f32).astype(jnp.int32)

    box_of_level = level * PAIR
    ids = jnp.concatenate(
        [
            own_ids,
            (box_of_level + 1 - pair) * slots + slot_ids,
            (box_of_level - 1) * slots + slot_ids,
            (box_of_level + PAIR) * slots + slot_ids,
        ]
    ).astype(jnp.int32)
    chosen = jnp.concatenate(
        [
            facts,
            facts_of(beside),
            jnp.where(first, facts_of(lower_beside), facts_of(lower)),
            jnp.where(first, facts_of(upper), facts_of(upper_beside)),
        ]
    )
    there = (ids >= 0) & (ids < level_count * PAIR * slots)

    def place(slot_id):
        box = slot_id // slots
        apart = box // PAIR - level
        base = jnp.where(apart == 0, 0, jnp.where(apart < 0, 2, 4))
        return (base + (box % PAIR != pair)) * slots + slot_id % slots

    distance = chosen[:, :6]
    near = jnp.where(distance < none, place(jnp.maximum(ids, 0)[:, None] + distance), 6 * slots)
    near = jnp.clip(near, 0, 6 * slots)
    self_place = place(jnp.maximum(ids, 0))
    table = [jnp.where(there & (chosen[:, 7] > 0), self_place, -1)]
    for a in range(3):
        table += [near[:, 2 * a], self_place, near[:, 2 * a + 1]]
    table = jnp.stack(table, axis=1).astype(jnp.int32)
    level_of = chosen[:, 6]
    scale = jnp.where(level_of == 0, 0.5, jnp.where(level_of == 1, 1.0, 2.0)).astype(f32)
    pot = jnp.concatenate([potential, other_pot])[:, :, None]

    def natural(blocks):
        return jnp.concatenate([lax.dynamic_index_in_dim(blocks, orb ^ j, keepdims=False) for j in groups], axis=1)

    def along_levels(blocks):
        mine_block = lambda target: lax.dynamic_index_in_dim(blocks, orb ^ target, keepdims=False)
        steps = range(1, level_count)
        return mine_block(level), [swap(mine_block(level ^ step), "lvl", step) for step in steps]

    def add(parts):
        own, got = parts
        return own.astype(f32) + sum(block.astype(f32) for block in got)

    def turned_rows(strip):
        pieces = []
        for over in range(PAIR):
            to_first = (pair ^ over) == 0
            piece = jnp.where(to_first, strip[:, :half], strip[:, half:])
            pieces.append((swap(piece, "pair", over) if over else piece).T)
        own, other = pieces
        return jnp.concatenate([jnp.where(first, own, other), jnp.where(first, other, own)], axis=1)

    def own_block(strip):
        strip = lax.all_gather(lax.psum(strip, "lvl"), ("orb", "pair"), axis=0, tiled=True)
        strip = lax.dynamic_slice_in_dim(strip, row0, box_rows, axis=0)
        return lax.dynamic_slice_in_dim(strip, col0, own_width, axis=1)

    meta = jnp.stack([pair, level, orb]).astype(jnp.int32)

    parts = [mine, beside, lower, lower_beside, upper, upper_beside]
    right = kinetic(parts, pot, matrices, table, scale, edge, coefficients)

    cross, right, meta = lax.optimization_barrier((cross, right, meta))
    lefts_own = [[flat(left_own[q])] for q in groups]
    lefts_beside = {q: [flat(block)] for q, block in left_beside.items()}
    for q in far:
        lefts_beside[q] = list(cross[q])
        lefts_beside[q + 1] = [swap(piece, "orb", 1) for piece in cross[q]]
    lefts_beside = [lefts_beside[q] for q in groups]

    share = 1.0 / level_count
    blocks = box_correlation(share, meta, lefts_own, None, half)
    blocks = box_correlation(share, meta, lefts_beside, blocks, half)
    right = right.reshape(2, slots * coefficients, 3 * half)
    fock_blocks = fock_rows(lefts_own + lefts_beside, right)
    if square_grid:
        sent = along_levels(blocks)
        sent, fock_blocks = lax.optimization_barrier((sent, fock_blocks))
        offset_turned = add(sent)
        small = offset_turned.astype(bf16)
        offset = turned_rows(offset_turned)
    else:
        offset = own_block(natural(blocks).astype(f32))
    row_ids = row0 + jnp.arange(box_rows, dtype=jnp.int32)
    col_ids = col0 + jnp.arange(own_width, dtype=jnp.int32)
    correlation = offset + (row_ids[:, None] == col_ids[None, :]).astype(f32)
    if square_grid:
        pieces = [small] + [swap(small, "lvl", z) for z in range(1, level_count)]
        pieces, fock_blocks = lax.optimization_barrier((pieces, fock_blocks))
        sent = along_levels(fock_blocks)
        far_of = range(0, orb_count, 2)
        top = jnp.stack(pieces[: level_count // 2])
        low = jnp.stack(pieces[level_count // 2 :])
        top = spread(spread(top, "pair", (0, 1)), "orb", far_of)
        low = spread(spread(low, "orb", far_of), "pair", (0, 1))
        top, low = spread(top, "orb", (0, 1)), spread(low, "orb", (0, 1))
        sums = add(sent)
        main = turned_rows(sums[0] + sums[1])
        to = [
            ((z * PAIR + y) * orb_count + o, (o * PAIR + y) * orb_count + z)
            for z in range(level_count)
            for y in range(PAIR)
            for o in groups
        ]
        fock = main + lax.ppermute(sums[2].astype(bf16), BOX + ("orb",), to).astype(f32)
    else:
        main = natural(fock_blocks[:, 0]).astype(f32) + natural(fock_blocks[:, 1]).astype(f32)
        main = lax.all_gather(lax.psum(main, "lvl"), "pair", axis=0, tiled=True)
        fock = lax.dynamic_slice_in_dim(main, row0, box_rows, axis=1).T + own_block(natural(fock_blocks[:, 2]).astype(f32))

    if square_grid:
        inverse_root = root_of(jnp.stack([level, pair, orb]).astype(jnp.int32), top, low, offset, all_width)
    else:
        gathered = lax.all_gather(offset.astype(bf16), "orb", axis=1, tiled=True)
        whole = lax.all_gather(gathered, BOX, axis=0, tiled=True)
        rows_of = lax.dynamic_slice_in_dim(whole, row0, box_rows, axis=0)
        cols_of = lax.dynamic_slice_in_dim(whole, col0, own_width, axis=1)
        row_square, col_square = matmul(rows_of, whole), matmul(whole, cols_of)
        left = (rows_of.astype(f32) - 0.25 * row_square).astype(bf16)
        right_side = (0.25 * (cols_of.astype(f32) - col_square)).astype(bf16)
        own_square = lax.dynamic_slice_in_dim(row_square, col0, own_width, axis=1)
        inverse_root = correlation - 1.5 * offset + 0.125 * own_square + matmul(left, right_side)
    return fock, correlation, inverse_root


def solution(mesh):
    levels = mesh.shape["box"] // PAIR
    split = Mesh(mesh.devices.reshape(levels, PAIR, mesh.shape["orb"]), ("lvl", "pair", "orb"))
    in_specs = (P(BOX, None, "orb"), P(BOX, None), P(), P(BOX), P(BOX), P(BOX, None, None))
    out_specs = (P(BOX, "orb"),) * 3
    return jax.shard_map(body, mesh=split, in_specs=in_specs, out_specs=out_specs, check_vma=False)
```

```python
import functools

import jax
import jax.numpy as jnp
import numpy as np
from jax import lax
from jax.experimental import pallas as pl
from jax.experimental.pallas import tpu as pltpu
from jax.sharding import Mesh, PartitionSpec as P

PAIR = 2
ROWS = 16
BOX = ("lvl", "pair")
f32, bf16 = jnp.float32, jnp.bfloat16


def swap(value, axis, bit):
    count = lax.axis_size(axis)
    return lax.ppermute(value, axis, [(i, i ^ bit) for i in range(count)])


def shift(value, axis, step):
    count = lax.axis_size(axis)
    return lax.ppermute(value, axis, [(i, i + step) for i in range(count) if 0 <= i + step < count])


def contract(left, right):
    return lax.dot_general(left, right, (((0,), (0,)), ((), ())), preferred_element_type=f32)


def matmul(left, right):
    return jnp.dot(left, right, preferred_element_type=f32)


def params(mebibytes):
    return pltpu.CompilerParams(vmem_limit_bytes=mebibytes * 1024 * 1024)


def pack_kernel(own, meta, orbitals, facts, packed, *active):
    slots, coefficients, width = orbitals.shape
    half, fold = width // PAIR, coefficients // 2
    low_half = (meta[0] == 0) == own
    for slot in range(slots):
        keep = slot < meta[1]
        for part in range(2):
            rows = slice(part * fold, (part + 1) * fold)
            here = orbitals[slot, rows, :]
            here = jnp.where(keep, here, jnp.zeros_like(here))
            if active:
                active[0][slot, rows, :] = here
            lanes = slice(part * half, (part + 1) * half)
            packed[slot, :fold, lanes] = jnp.where(low_half, here[:, :half], here[:, half:])
        rest = packed.shape[1] - fold
        packed[slot, fold:, :] = jnp.broadcast_to(facts[slot : slot + 1, :], (rest, width)).astype(bf16)


def pack(meta, orbitals, facts, own):
    slots, coefficients, width = orbitals.shape
    fold = coefficients // 2
    padded = (fold // ROWS + 1) * ROWS
    vmem = pl.BlockSpec(memory_space=pltpu.VMEM)
    shapes = [jax.ShapeDtypeStruct((slots, padded, width), bf16)]
    shapes += [jax.ShapeDtypeStruct(orbitals.shape, bf16)] * own
    return pl.pallas_call(
        functools.partial(pack_kernel, own),
        out_shape=shapes,
        in_specs=[pl.BlockSpec(memory_space=pltpu.SMEM), vmem, vmem],
        out_specs=[vmem] * len(shapes),
        compiler_params=params(24),
        name="pack",
    )(meta, orbitals, facts)


def unfold_kernel(fold, cut, meta, beside, rest, top, low):
    slots, _, width = beside.shape
    half = width // PAIR
    first = meta[0] == 0
    for slot in range(slots):
        for part in range(2):
            lanes = slice(part * half, (part + 1) * half)
            near, far = beside[slot, :fold, lanes], rest[slot, :fold, lanes]
            here = jnp.concatenate([jnp.where(first, near, far), jnp.where(first, far, near)], axis=1)
            start = (2 * slot + part) * fold
            split = min(max(cut - start, 0), fold)
            if split:
                top[start : start + split, :] = here[:split]
            if split < fold:
                low[start + split - cut : start + fold - cut, :] = here[split:]


def unfold(meta, beside, rest, fold, cut):
    slots, _, width = beside.shape
    vmem = pl.BlockSpec(memory_space=pltpu.VMEM)
    return pl.pallas_call(
        functools.partial(unfold_kernel, fold, cut),
        out_shape=[
            jax.ShapeDtypeStruct((cut, width), bf16),
            jax.ShapeDtypeStruct((2 * slots * fold - cut, width), bf16),
        ],
        in_specs=[pl.BlockSpec(memory_space=pltpu.SMEM), vmem, vmem],
        out_specs=[vmem, vmem],
        compiler_params=params(24),
        name="unfold",
    )(meta, beside, rest)


def load_left(lefts, held, sems):
    copies = []
    for q, pieces in enumerate(lefts):
        row = 0
        for piece in pieces:
            rows, width = piece.shape
            here = held.at[row : row + rows, q * width : (q + 1) * width]
            copies.append(pltpu.make_async_copy(piece, here, sems.at[len(copies)]))
            row += rows
    for copy in copies:
        copy.start()
    return copies


def grouped(refs, counts):
    refs = list(refs)
    return [[refs.pop(0) for _ in range(count)] for count in counts]


def correlation_kernel(share, counts, meta, *refs):
    refs, (out, held, turned, sems) = refs[:-4], refs[-4:]
    groups, half, width = out.shape
    lefts, before = grouped(refs, counts), refs[sum(counts) :]
    copies = load_left(lefts, held, sems)
    first = meta[0] == 0
    for copy in copies[: counts[0]]:
        copy.wait()
    own = held[:, :width]
    turned[...] = jnp.where(first, own[:, :half], own[:, half:]).T
    for copy in copies[counts[0] :]:
        copy.wait()
    for base in range(0, groups, 2):
        wide = matmul(turned[...], held[:, base * width : (base + 2) * width])
        for q in (base, base + 1):
            total = wide[:, (q - base) * width : (q - base + 1) * width]
            if before:
                total = total + before[0][q]
                if q == 0:
                    rows = lax.broadcasted_iota(jnp.int32, (half, width), 0) + jnp.where(first, 0, half)
                    columns = lax.broadcasted_iota(jnp.int32, (half, width), 1)
                    total = total - jnp.where(rows == columns, share, 0.0)
            out[q] = total.astype(out.dtype)


def box_correlation(share, meta, lefts, before, half):
    depth, width = sum(piece.shape[0] for piece in lefts[0]), lefts[0][0].shape[1]
    counts = [len(pieces) for pieces in lefts]
    vmem = pl.BlockSpec(memory_space=pltpu.VMEM)
    extra = [] if before is None else [before]
    return pl.pallas_call(
        functools.partial(correlation_kernel, share, counts),
        out_shape=jax.ShapeDtypeStruct((len(lefts), half, width), f32 if before is None else bf16),
        in_specs=[pl.BlockSpec(memory_space=pltpu.SMEM)]
        + [pl.BlockSpec(memory_space=pl.ANY)] * sum(counts)
        + [vmem] * len(extra),
        out_specs=vmem,
        scratch_shapes=[
            pltpu.VMEM((depth, len(lefts) * width), bf16),
            pltpu.VMEM((half, depth), bf16),
            pltpu.SemaphoreType.DMA((sum(counts),)),
        ],
        compiler_params=params(32),
        cost_estimate=pl.CostEstimate(
            flops=2 * len(lefts) * depth * width * half, bytes_accessed=2 * len(lefts) * depth * width, transcendentals=0
        ),
        name="correlation",
    )(meta, *[piece for pieces in lefts for piece in pieces], *extra)


def fock_kernel(counts, *refs):
    refs, (right, out, held, raw, turned, sems, last_sems) = refs[:-7], refs[-7:]
    groups, _, half, width = out.shape
    lefts = grouped(refs, counts)
    lasts = [pltpu.make_async_copy(right.at[side], raw.at[side], last_sems.at[side]) for side in range(2)]
    for copy in lasts:
        copy.start()
    copies = []
    for side in range(2):
        blocks = lefts[side * groups : (side + 1) * groups]
        copies += load_left(blocks, held.at[side], sems.at[side])
    for side in range(2):
        lasts[side].wait()
        turned[side] = raw[side].T
    for copy in copies:
        copy.wait()

    def two_groups(j, carry):
        lanes = pl.ds(pl.multiple_of(j * 2 * width, 2 * width), 2 * width)
        total = matmul(turned[0], held[0, :, lanes]) + matmul(turned[1], held[1, :, lanes])
        main = total[:half] + total[half : 2 * half]
        top = main.astype(bf16)
        low = (main - top.astype(f32)).astype(bf16)
        fix = total[2 * half :].astype(bf16)
        for q in range(2):
            here = slice(q * width, (q + 1) * width)
            out[2 * j + q, 0], out[2 * j + q, 1], out[2 * j + q, 2] = top[:, here], low[:, here], fix[:, here]
        return carry

    lax.fori_loop(0, groups // 2, two_groups, 0)


def fock_rows(lefts, right):
    depth, width = sum(piece.shape[0] for piece in lefts[0]), lefts[0][0].shape[1]
    counts = [len(pieces) for pieces in lefts]
    groups, tall = len(lefts) // 2, right.shape[-1]
    most = max(sum(counts[:groups]), sum(counts[groups:]))
    anywhere = pl.BlockSpec(memory_space=pl.ANY)
    return pl.pallas_call(
        functools.partial(fock_kernel, counts),
        out_shape=jax.ShapeDtypeStruct((groups, 3, tall // 3, width), bf16),
        in_specs=[anywhere] * (sum(counts) + 1),
        out_specs=pl.BlockSpec(memory_space=pltpu.VMEM),
        scratch_shapes=[
            pltpu.VMEM((2, depth, groups * width), bf16),
            pltpu.VMEM(right.shape, bf16),
            pltpu.VMEM((2, tall, depth), bf16),
            pltpu.SemaphoreType.DMA((2, most)),
            pltpu.SemaphoreType.DMA((2,)),
        ],
        compiler_params=params(44),
        cost_estimate=pl.CostEstimate(
            flops=2 * len(lefts) * depth * width * tall, bytes_accessed=2 * len(lefts) * depth * width, transcendentals=0
        ),
        name="fock",
    )(*[piece for pieces in lefts for piece in pieces], right)


def root_kernel(levels, meta, *refs):
    pieces, (offset, root, whole, rows_f, cols_b) = refs[:-5], refs[-5:]
    level, pair, orb = meta[0], meta[1], meta[2]
    coarse, width = offset.shape
    side = whole.shape[0]
    groups = side // width
    for piece, (z, y, q) in zip(pieces, piece_places(levels, groups)):
        for i in range(len(z)):
            start = ((orb ^ q[i]) * PAIR + (pair ^ y[i])) * coarse
            rows = pl.ds(pl.multiple_of(start, coarse), coarse)
            lanes = pl.ds(pl.multiple_of((level ^ z[i]) * width, width), width)
            whole[rows, lanes] = piece[i * coarse : (i + 1) * coarse, :]
    row0 = pl.multiple_of((level * PAIR + pair) * coarse, coarse)
    own_lanes = pl.ds(pl.multiple_of(orb * width, width), width)
    rows = whole[pl.ds(row0, coarse), :]

    def across(j, carry):
        lanes = pl.ds(pl.multiple_of(j * width, width), width)
        rows_f[:, lanes] = matmul(rows, whole[:, lanes])
        return carry

    lax.fori_loop(0, groups, across, 0)
    columns = whole[:, own_lanes]

    def down(i, carry):
        here = pl.ds(pl.multiple_of(i * coarse, coarse), coarse)
        square = matmul(whole[here, :], columns)
        cols_b[here, :] = (0.25 * (whole[here, own_lanes].astype(f32) - square)).astype(bf16)
        return carry

    lax.fori_loop(0, side // coarse, down, 0)
    left = (rows.astype(f32) - 0.25 * rows_f[...]).astype(bf16)
    value = matmul(left, cols_b[...]) + 0.125 * rows_f[:, own_lanes] - 0.5 * offset[...]
    row_ids = lax.broadcasted_iota(jnp.int32, value.shape, 0) + row0
    col_ids = lax.broadcasted_iota(jnp.int32, value.shape, 1) + orb * width
    root[...] = value + jnp.where(row_ids == col_ids, 1.0, 0.0)


def piece_places(levels, groups):
    places = []
    for core in (0, 1):
        for half in range(2):
            low = [half * levels // 2 + z for z in range(levels // 2)]
            for second in (0, 1):
                z, y, q = [], [], []
                for inner in (0, 1):
                    z += low
                    y += [second if half else inner] * len(low)
                    q += [2 * (inner if half else second) + core] * len(low)
                places.append((z, y, q))
    return places


def root_of(meta, pieces, offset, side, levels):
    coarse, width = offset.shape
    vmem = pl.BlockSpec(memory_space=pltpu.VMEM)
    return pl.pallas_call(
        functools.partial(root_kernel, levels),
        out_shape=jax.ShapeDtypeStruct(offset.shape, f32),
        in_specs=[pl.BlockSpec(memory_space=pltpu.SMEM)] + [vmem] * (len(pieces) + 1),
        out_specs=vmem,
        scratch_shapes=[
            pltpu.VMEM((side, side), bf16),
            pltpu.VMEM((coarse, side), f32),
            pltpu.VMEM((side, width), bf16),
        ],
        compiler_params=params(40),
        cost_estimate=pl.CostEstimate(flops=4 * side * side * width, bytes_accessed=4 * side * side, transcendentals=0),
        name="root",
    )(meta, *pieces, offset)


def kinetic_kernel(edge, slots, table, scale, *refs):
    parts, (pot, fwd_in, fwd_out, back_in, back_out), out = refs[:6], refs[6:11], refs[11]
    raw, x, rounded, left_over, total, total_fix, columns, sems = refs[12:]
    square = edge * edge
    own = PAIR * slots
    width = x.shape[3]
    copies = [pltpu.make_async_copy(part, raw.at[place], sems.at[place]) for place, part in enumerate(parts)]
    for copy in copies:
        copy.start()
    x[...] = jnp.zeros_like(x)
    total[...] = jnp.zeros_like(total)
    total_fix[...] = jnp.zeros_like(total_fix)
    columns[...] = pot[...].T
    for copy in copies:
        copy.wait()

    def lay_out(place, carry):
        for slot in range(slots):
            for i in range(edge):
                part, row = i // (edge // 2), i % (edge // 2) * square
                x[place * slots + slot, i, :square, :] = raw[
                    place, slot, row : row + square, part * width : (part + 1) * width
                ]
        return carry

    lax.fori_loop(0, len(parts), lay_out, 0)
    chunks = -(-square // ROWS)

    def per_slot(s, carry):
        @pl.when(table[s, 0] >= 0)
        def _():
            own_scale = scale[s]
            for a in range(3):
                source = [table[s, 1 + 3 * a + k] for k in range(3)]
                for i in range(chunks if a == 0 else edge):
                    if a == 0:
                        rows = slice(i * ROWS, (i + 1) * ROWS)
                        block = jnp.concatenate([x[t, :, rows, :].reshape(edge * ROWS, width) for t in source], axis=0)
                        exact = (own_scale * matmul(fwd_out[...], block)).reshape(edge, ROWS, width)
                        value = exact.astype(bf16)
                        rounded[:, rows, :] = value
                        left_over[:, rows, :] = (value.astype(f32) - exact).astype(bf16)
                    else:
                        block = jnp.concatenate([x[t, i] for t in source], axis=0)
                        exact = own_scale * matmul(fwd_in[a - 1], block)
                        value = exact.astype(bf16)
                        rounded[i] = value
                        left_over[i] = (value.astype(f32) - exact).astype(bf16)
                half = 0.5 * own_scale
                for k in range(3):
                    target = source[k]

                    @pl.when(target < own)
                    def _():
                        for i in range(chunks if a == 0 else edge):
                            for field, sum_ref in ((rounded, total), (left_over, total_fix)):
                                if a == 0:
                                    rows = slice(i * ROWS, (i + 1) * ROWS)
                                    term = matmul(back_out[k], field[:, rows, :].reshape(edge * ROWS, width))
                                    sum_ref[target, :, rows, :] += half * term.reshape(edge, ROWS, width)
                                else:
                                    sum_ref[target, i] += half * matmul(back_in[a - 1, k], field[i])

        return carry

    lax.fori_loop(0, table.shape[0], per_slot, 0)

    for t in range(own):
        for i in range(edge):
            rows = slice(i * square, (i + 1) * square)
            weighted = (columns[rows, t : t + 1] * x[t, i, :square, :].astype(f32)).astype(bf16)
            whole = total[t, i, :square, :] + weighted.astype(f32)
            top = whole.astype(bf16)
            low = (whole - top.astype(f32)).astype(bf16)
            fix = total_fix[t, i, :square, :].astype(bf16)
            out[t, rows, :] = jnp.concatenate([top, low, fix], axis=1)


def block_matrices(deriv_blocks):
    edge = deriv_blocks.shape[1]
    square = edge * edge
    padded = -(-square // ROWS) * ROWS
    ids = np.arange(padded)
    slow = ((ids[:, None] // edge) == np.arange(edge)).astype(np.float32)
    fast = (((ids[:, None] % edge) == np.arange(edge)) & (ids[:, None] < square)).astype(np.float32)
    ids = np.arange(edge * ROWS)
    outer = ((ids[:, None] // ROWS) == np.arange(edge)).astype(np.float32)
    within = ((ids[:, None] % ROWS) == np.arange(ROWS)).astype(np.float32)
    stacked = jnp.moveaxis(deriv_blocks, 0, 1).reshape(edge, 3 * edge)
    forward, backward = [], []
    for spot, mask in ((slow, fast), (fast, slow), (outer, within)):
        same = mask @ mask.T
        spread_out = np.kron(np.eye(3, dtype=np.float32), spot.T)
        spot_b, same_b = jnp.asarray(spot, bf16), jnp.asarray(same, f32)
        wide = matmul(matmul(spot_b, stacked).astype(bf16), jnp.asarray(spread_out, bf16))
        forward.append((wide * jnp.tile(same_b, (1, 3))).astype(bf16))
        turned = jnp.einsum("ri,kji->krj", spot_b, deriv_blocks, preferred_element_type=f32).astype(bf16)
        turned = jnp.einsum("krj,cj->krc", turned, spot_b, preferred_element_type=f32)
        backward.append((turned * same_b).astype(bf16))
    return jnp.stack(forward[:2]), forward[2], jnp.stack(backward[:2]), backward[2]


def kinetic(parts, pot, matrices, table, scale, edge, coefficients):
    slots, folded, lanes = parts[0].shape
    width = lanes // 2
    padded = matrices[0].shape[1]
    own = PAIR * slots
    vmem = pl.BlockSpec(memory_space=pltpu.VMEM)
    smem = pl.BlockSpec(memory_space=pltpu.SMEM)
    anywhere = pl.BlockSpec(memory_space=pl.ANY)
    return pl.pallas_call(
        functools.partial(kinetic_kernel, edge, slots),
        out_shape=jax.ShapeDtypeStruct((own, coefficients, 3 * width), bf16),
        in_specs=[smem, smem] + [anywhere] * 6 + [vmem] * 5,
        out_specs=vmem,
        scratch_shapes=[
            pltpu.VMEM((6, slots, folded, lanes), bf16),
            pltpu.VMEM((6 * slots + 1, edge, padded, width), bf16),
            pltpu.VMEM((edge, padded, width), bf16),
            pltpu.VMEM((edge, padded, width), bf16),
            pltpu.VMEM((own, edge, padded, width), f32),
            pltpu.VMEM((own, edge, padded, width), f32),
            pltpu.VMEM(pot.shape[::-1], f32),
            pltpu.SemaphoreType.DMA((6,)),
        ],
        compiler_params=params(48),
        cost_estimate=pl.CostEstimate(flops=2 * 10**10, bytes_accessed=40 * 10**6, transcendentals=0),
        name="kinetic",
    )(table, scale, *parts, pot, *matrices)


def body(orbitals, potential, deriv_blocks, levels, box_counts, neighbours):
    slots, coefficients, own_width = orbitals.shape
    edge = deriv_blocks.shape[1]
    level, pair, orb = lax.axis_index("lvl"), lax.axis_index("pair"), lax.axis_index("orb")
    level_count, orb_count = lax.axis_size("lvl"), lax.axis_size("orb")
    half, fold = own_width // PAIR, coefficients // 2
    all_width = own_width * orb_count
    box_rows = all_width // (level_count * PAIR)
    first = pair == 0
    groups = range(orb_count)
    square_grid = level_count == orb_count == 4 and box_rows == half
    row0, col0 = (level * PAIR + pair) * box_rows, orb * own_width

    slot_ids = jnp.arange(slots, dtype=jnp.int32)
    own_ids = (level * PAIR + pair) * slots + slot_ids
    none = 16 * slots
    apart_ids = jnp.where(neighbours >= 0, neighbours - own_ids[:, None, None], none).reshape(slots, 6)
    live = (slot_ids < box_counts[0]).astype(jnp.int32)
    facts = jnp.concatenate([apart_ids, levels[:, None], live[:, None]], axis=1)
    wide_facts = jnp.pad(facts.astype(f32), ((0, 0), (0, own_width - facts.shape[1])))
    pack_meta = jnp.stack([pair, box_counts[0]]).astype(jnp.int32)
    [theirs] = pack(pack_meta, orbitals, wide_facts, False)
    pack_meta, theirs = lax.optimization_barrier((pack_meta, theirs))
    mine, active = pack(pack_meta, orbitals, wide_facts, True)

    far = {q: swap(active, "orb", q) for q in groups if q and q % 2 == 0}
    beside = swap(theirs, "pair", 1)
    lower, upper = shift(mine, "lvl", 1), shift(mine, "lvl", -1)
    later_pot, later_mine, beside = lax.optimization_barrier((potential, mine, beside))
    beside_rest = swap(later_mine, "pair", 1)
    lower_beside, upper_beside = shift(beside, "lvl", 1), shift(beside, "lvl", -1)
    other_pot = swap(later_pot, "pair", 1)
    matrices = block_matrices(deriv_blocks)

    far, beside, beside_rest, lower, upper, lower_beside, upper_beside, other_pot, active, matrices = (
        lax.optimization_barrier(
            (far, beside, beside_rest, lower, upper, lower_beside, upper_beside, other_pot, active, matrices)
        )
    )

    flat = lambda block: block.reshape(-1, block.shape[-1])
    cut = -(-slots * coefficients // (2 * ROWS)) * ROWS
    beside_all = unfold(pack_meta, beside, beside_rest, fold, cut)
    cross = {q: [swap(beside_all[0], "orb", q), swap(flat(far[q])[cut:], "pair", 1)] for q in far}
    left_own = {0: active, 1: swap(active, "orb", 1), **far}
    left_beside = {0: beside_all, 1: [swap(piece, "orb", 1) for piece in beside_all]}
    for q in far:
        left_own[q + 1] = swap(far[q], "orb", 1)

    def facts_of(packed):
        return packed[:, fold, : facts.shape[1]].astype(f32).astype(jnp.int32)

    box_of_level = level * PAIR
    ids = jnp.concatenate(
        [
            own_ids,
            (box_of_level + 1 - pair) * slots + slot_ids,
            (box_of_level - 1) * slots + slot_ids,
            (box_of_level + PAIR) * slots + slot_ids,
        ]
    ).astype(jnp.int32)
    chosen = jnp.concatenate(
        [
            facts,
            facts_of(beside),
            jnp.where(first, facts_of(lower_beside), facts_of(lower)),
            jnp.where(first, facts_of(upper), facts_of(upper_beside)),
        ]
    )
    there = (ids >= 0) & (ids < level_count * PAIR * slots)

    def place(slot_id):
        box = slot_id // slots
        apart = box // PAIR - level
        base = jnp.where(apart == 0, 0, jnp.where(apart < 0, 2, 4))
        return (base + (box % PAIR != pair)) * slots + slot_id % slots

    distance = chosen[:, :6]
    near = jnp.where(distance < none, place(jnp.maximum(ids, 0)[:, None] + distance), 6 * slots)
    near = jnp.clip(near, 0, 6 * slots)
    self_place = place(jnp.maximum(ids, 0))
    table = [jnp.where(there & (chosen[:, 7] > 0), self_place, -1)]
    for a in range(3):
        table += [near[:, 2 * a], self_place, near[:, 2 * a + 1]]
    table = jnp.stack(table, axis=1).astype(jnp.int32)
    level_of = chosen[:, 6]
    scale = jnp.where(level_of == 0, 0.5, jnp.where(level_of == 1, 1.0, 2.0)).astype(f32)
    pot = jnp.concatenate([potential, other_pot])
    pot = jnp.pad(pot, ((0, -pot.shape[0] % 8), (0, -pot.shape[1] % 128)))

    def natural(blocks):
        return jnp.concatenate([lax.dynamic_index_in_dim(blocks, orb ^ j, keepdims=False) for j in groups], axis=1)

    def along_levels(blocks):
        mine_block = lambda target: lax.dynamic_index_in_dim(blocks, orb ^ target, keepdims=False)
        steps = range(1, level_count)
        return mine_block(level), [swap(mine_block(level ^ step), "lvl", step) for step in steps]

    def add(parts):
        own, got = parts
        return own.astype(f32) + sum(block.astype(f32) for block in got)

    def turned_rows(strip):
        pieces = []
        for over in range(PAIR):
            to_first = (pair ^ over) == 0
            piece = jnp.where(to_first, strip[:, :half], strip[:, half:])
            pieces.append((swap(piece, "pair", over) if over else piece).T)
        own, other = pieces
        return jnp.concatenate([jnp.where(first, own, other), jnp.where(first, other, own)], axis=1)

    def own_block(strip):
        strip = lax.all_gather(lax.psum(strip, "lvl"), ("orb", "pair"), axis=0, tiled=True)
        strip = lax.dynamic_slice_in_dim(strip, row0, box_rows, axis=0)
        return lax.dynamic_slice_in_dim(strip, col0, own_width, axis=1)

    meta = jnp.stack([pair, level, orb]).astype(jnp.int32)

    parts = [mine, beside, lower, lower_beside, upper, upper_beside]
    right = kinetic(parts, pot, matrices, table, scale, edge, coefficients)

    cross, right, meta = lax.optimization_barrier((cross, right, meta))
    lefts_own = [[flat(left_own[q])] for q in groups]
    lefts_beside = dict(left_beside)
    for q in far:
        lefts_beside[q] = list(cross[q])
        lefts_beside[q + 1] = [swap(piece, "orb", 1) for piece in cross[q]]
    lefts_beside = [lefts_beside[q] for q in groups]

    share = 1.0 / level_count
    blocks = box_correlation(share, meta, lefts_own, None, half)
    blocks = box_correlation(share, meta, lefts_beside, blocks, half)
    right = right.reshape(2, slots * coefficients, 3 * half)
    fock_blocks = fock_rows(lefts_own + lefts_beside, right)
    if square_grid:
        sent = along_levels(blocks)
        sent, fock_blocks = lax.optimization_barrier((sent, fock_blocks))
        offset_turned = add(sent)
        small = offset_turned.astype(bf16)
        offset = turned_rows(offset_turned)
    else:
        offset = own_block(natural(blocks).astype(f32))
    row_ids = row0 + jnp.arange(box_rows, dtype=jnp.int32)
    col_ids = col0 + jnp.arange(own_width, dtype=jnp.int32)
    correlation = offset + (row_ids[:, None] == col_ids[None, :]).astype(f32)
    if square_grid:
        pieces = [small] + [swap(small, "lvl", z) for z in range(1, level_count)]
        pieces, fock_blocks = lax.optimization_barrier((pieces, fock_blocks))
        join = functools.partial(jnp.concatenate, axis=0)
        top, low = join(pieces[: level_count // 2]), join(pieces[level_count // 2 :])
        sent = along_levels(fock_blocks)
        top, low = join([top, swap(top, "pair", 1)]), join([low, swap(low, "orb", 2)])
        pieces = [top, swap(top, "orb", 2), low, swap(low, "pair", 1)]
        pieces += [swap(piece, "orb", 1) for piece in pieces]
        pieces, sent = lax.optimization_barrier((pieces, sent))
        sums = add(sent)
        main = turned_rows(sums[0] + sums[1])
        to = [
            ((z * PAIR + y) * orb_count + o, (o * PAIR + y) * orb_count + z)
            for z in range(level_count)
            for y in range(PAIR)
            for o in groups
        ]
        fock = main + lax.ppermute(sums[2].astype(bf16), BOX + ("orb",), to).astype(f32)
    else:
        main = natural(fock_blocks[:, 0]).astype(f32) + natural(fock_blocks[:, 1]).astype(f32)
        main = lax.all_gather(lax.psum(main, "lvl"), "pair", axis=0, tiled=True)
        fock = lax.dynamic_slice_in_dim(main, row0, box_rows, axis=1).T + own_block(natural(fock_blocks[:, 2]).astype(f32))

    if square_grid:
        inverse_root = root_of(jnp.stack([level, pair, orb]).astype(jnp.int32), pieces, offset, all_width, level_count)
    else:
        gathered = lax.all_gather(offset.astype(bf16), "orb", axis=1, tiled=True)
        whole = lax.all_gather(gathered, BOX, axis=0, tiled=True)
        rows_of = lax.dynamic_slice_in_dim(whole, row0, box_rows, axis=0)
        cols_of = lax.dynamic_slice_in_dim(whole, col0, own_width, axis=1)
        row_square, col_square = matmul(rows_of, whole), matmul(whole, cols_of)
        left = (rows_of.astype(f32) - 0.25 * row_square).astype(bf16)
        right_side = (0.25 * (cols_of.astype(f32) - col_square)).astype(bf16)
        own_square = lax.dynamic_slice_in_dim(row_square, col0, own_width, axis=1)
        inverse_root = correlation - 1.5 * offset + 0.125 * own_square + matmul(left, right_side)
    return fock, correlation, inverse_root


def solution(mesh):
    levels = mesh.shape["box"] // PAIR
    split = Mesh(mesh.devices.reshape(levels, PAIR, mesh.shape["orb"]), ("lvl", "pair", "orb"))
    in_specs = (P(BOX, None, "orb"), P(BOX, None), P(), P(BOX), P(BOX), P(BOX, None, None))
    out_specs = (P(BOX, "orb"),) * 3
    return jax.shard_map(body, mesh=split, in_specs=in_specs, out_specs=out_specs, check_vma=False)
```

```python
import functools

import jax
import jax.numpy as jnp
import numpy as np
from jax import lax
from jax.experimental import pallas as pl
from jax.experimental.pallas import tpu as pltpu
from jax.sharding import Mesh, PartitionSpec as P

PAIR = 2
ROWS = 16
BOX = ("lvl", "pair")
f32, bf16 = jnp.float32, jnp.bfloat16


def swap(value, axis, bit):
    count = lax.axis_size(axis)
    return lax.ppermute(value, axis, [(i, i ^ bit) for i in range(count)])


def trade(value, axis, start):
    pairs = [(i, i + 1) for i in range(start, lax.axis_size(axis) - 1, 2)]
    return lax.ppermute(value, axis, pairs + [(b, a) for a, b in pairs])


def matmul(left, right):
    return jnp.dot(left, right, preferred_element_type=f32)


def params(mebibytes):
    return pltpu.CompilerParams(vmem_limit_bytes=mebibytes * 1024 * 1024)


def pack_kernel(own, meta, orbitals, facts, packed, *active):
    slots, coefficients, width = orbitals.shape
    half, fold = width // PAIR, coefficients // 2
    low_half = (meta[0] == 0) == own
    for slot in range(slots):
        keep = slot < meta[1]
        for part in range(2):
            rows = slice(part * fold, (part + 1) * fold)
            here = orbitals[slot, rows, :]
            here = jnp.where(keep, here, jnp.zeros_like(here))
            if active:
                active[0][slot, rows, :] = here
            lanes = slice(part * half, (part + 1) * half)
            packed[slot, :fold, lanes] = jnp.where(low_half, here[:, :half], here[:, half:])
        rest = packed.shape[1] - fold
        packed[slot, fold:, :] = jnp.broadcast_to(facts[slot : slot + 1, :], (rest, width)).astype(bf16)


def pack(meta, orbitals, facts, own):
    slots, coefficients, width = orbitals.shape
    fold = coefficients // 2
    padded = (fold // ROWS + 1) * ROWS
    vmem = pl.BlockSpec(memory_space=pltpu.VMEM)
    shapes = [jax.ShapeDtypeStruct((slots, padded, width), bf16)]
    shapes += [jax.ShapeDtypeStruct(orbitals.shape, bf16)] * own
    return pl.pallas_call(
        functools.partial(pack_kernel, own),
        out_shape=shapes,
        in_specs=[pl.BlockSpec(memory_space=pltpu.SMEM), vmem, vmem],
        out_specs=[vmem] * len(shapes),
        compiler_params=params(24),
        name="pack",
    )(meta, orbitals, facts)


def unfold_kernel(fold, meta, beside, rest, whole, top):
    slots, _, width = beside.shape
    half = width // PAIR
    first = meta[0] == 0
    for slot in range(slots):
        for part in range(2):
            lanes = slice(part * half, (part + 1) * half)
            near, far = beside[slot, :fold, lanes], rest[slot, :fold, lanes]
            start = (2 * slot + part) * fold
            here = jnp.concatenate([jnp.where(first, near, far), jnp.where(first, far, near)], axis=1)
            whole[start : start + fold, :] = here
    top[...] = whole[: top.shape[0], :]


def unfold(meta, beside, rest, fold, cut):
    slots, _, width = beside.shape
    vmem = pl.BlockSpec(memory_space=pltpu.VMEM)
    return pl.pallas_call(
        functools.partial(unfold_kernel, fold),
        out_shape=[
            jax.ShapeDtypeStruct((2 * slots * fold, width), bf16),
            jax.ShapeDtypeStruct((cut, width), bf16),
        ],
        in_specs=[pl.BlockSpec(memory_space=pltpu.SMEM), vmem, vmem],
        out_specs=[vmem, vmem],
        compiler_params=params(24),
        name="unfold",
    )(meta, beside, rest)


def load_left(lefts, held, sems):
    copies = []
    for q, pieces in enumerate(lefts):
        row = 0
        for piece in pieces:
            rows, width = piece.shape
            here = held.at[row : row + rows, q * width : (q + 1) * width]
            copies.append(pltpu.make_async_copy(piece, here, sems.at[len(copies)]))
            row += rows
    for copy in copies:
        copy.start()
    return copies


def grouped(refs, counts):
    refs = list(refs)
    return [[refs.pop(0) for _ in range(count)] for count in counts]


def correlation_kernel(share, counts, meta, *refs):
    refs, (out, held, turned, sems) = refs[:-4], refs[-4:]
    groups, half, width = out.shape
    lefts, before = grouped(refs, counts), refs[sum(counts) :]
    copies = load_left(lefts, held, sems)
    first = meta[0] == 0
    for copy in copies[: counts[0]]:
        copy.wait()
    own = held[:, :width]
    turned[...] = jnp.where(first, own[:, :half], own[:, half:]).T
    for copy in copies[counts[0] :]:
        copy.wait()
    for base in range(0, groups, 2):
        wide = matmul(turned[...], held[:, base * width : (base + 2) * width])
        for q in (base, base + 1):
            total = wide[:, (q - base) * width : (q - base + 1) * width]
            if before:
                total = total + before[0][q]
                if q == 0:
                    rows = lax.broadcasted_iota(jnp.int32, (half, width), 0) + jnp.where(first, 0, half)
                    columns = lax.broadcasted_iota(jnp.int32, (half, width), 1)
                    total = total - jnp.where(rows == columns, share, 0.0)
            out[q] = total.astype(out.dtype)


def box_correlation(share, meta, lefts, before, half):
    depth, width = sum(piece.shape[0] for piece in lefts[0]), lefts[0][0].shape[1]
    counts = [len(pieces) for pieces in lefts]
    vmem = pl.BlockSpec(memory_space=pltpu.VMEM)
    extra = [] if before is None else [before]
    return pl.pallas_call(
        functools.partial(correlation_kernel, share, counts),
        out_shape=jax.ShapeDtypeStruct((len(lefts), half, width), f32 if before is None else bf16),
        in_specs=[pl.BlockSpec(memory_space=pltpu.SMEM)]
        + [pl.BlockSpec(memory_space=pl.ANY)] * sum(counts)
        + [vmem] * len(extra),
        out_specs=vmem,
        scratch_shapes=[
            pltpu.VMEM((depth, len(lefts) * width), bf16),
            pltpu.VMEM((half, depth), bf16),
            pltpu.SemaphoreType.DMA((sum(counts),)),
        ],
        compiler_params=params(32),
        cost_estimate=pl.CostEstimate(
            flops=2 * len(lefts) * depth * width * half, bytes_accessed=2 * len(lefts) * depth * width, transcendentals=0
        ),
        name="correlation",
    )(meta, *[piece for pieces in lefts for piece in pieces], *extra)


def fock_kernel(side, counts, right, *refs):
    refs, (out, held, raw, turned, sems, last_sem) = refs[:-6], refs[-6:]
    lefts, before = grouped(refs, counts), refs[sum(counts) :]
    last = pltpu.make_async_copy(right.at[side], raw, last_sem)
    last.start()
    copies = load_left(lefts, held, sems)
    half, width = out.shape[-2] // (1 if before else 3), out.shape[-1]
    last.wait()
    turned[...] = raw[...].T
    for copy in copies:
        copy.wait()
    for base in range(0, len(lefts), 2):
        wide = matmul(turned[...], held[:, base * width : (base + 2) * width])
        for q in (base, base + 1):
            total = wide[:, (q - base) * width : (q - base + 1) * width]
            if before:
                total = total + before[0][q]
                main = total[:half] + total[half : 2 * half]
                top = main.astype(bf16)
                out[q, 0], out[q, 1] = top, (main - top.astype(f32)).astype(bf16)
                out[q, 2] = total[2 * half :].astype(bf16)
            else:
                out[q] = total


def box_fock(side, lefts, right, before):
    depth, width = sum(piece.shape[0] for piece in lefts[0]), lefts[0][0].shape[1]
    counts = [len(pieces) for pieces in lefts]
    tall = right.shape[-1]
    anywhere, vmem = pl.BlockSpec(memory_space=pl.ANY), pl.BlockSpec(memory_space=pltpu.VMEM)
    extra = [] if before is None else [before]
    out = ((len(lefts), tall, width), f32) if before is None else ((len(lefts), 3, tall // 3, width), bf16)
    return pl.pallas_call(
        functools.partial(fock_kernel, side, counts),
        out_shape=jax.ShapeDtypeStruct(*out),
        in_specs=[anywhere] * (sum(counts) + 1) + [vmem] * len(extra),
        out_specs=vmem,
        scratch_shapes=[
            pltpu.VMEM((depth, len(lefts) * width), bf16),
            pltpu.VMEM(right.shape[1:], bf16),
            pltpu.VMEM((tall, depth), bf16),
            pltpu.SemaphoreType.DMA((sum(counts),)),
            pltpu.SemaphoreType.DMA(()),
        ],
        compiler_params=params(40),
        cost_estimate=pl.CostEstimate(
            flops=2 * len(lefts) * depth * width * tall, bytes_accessed=2 * len(lefts) * depth * width, transcendentals=0
        ),
        name="fock",
    )(right, *[piece for pieces in lefts for piece in pieces], *extra)


def root_kernel(levels, meta, *refs):
    pieces, (offset, root, whole, rows_f, cols_b, sems) = refs[:-6], refs[-6:]
    level, pair, orb = meta[0], meta[1], meta[2]
    coarse, width = offset.shape
    side = whole.shape[0]
    groups = side // width
    copies = []
    for piece, (z, y, q) in zip(pieces, piece_places(levels, groups)):
        for i in range(len(z)):
            start = ((orb ^ q[i]) * PAIR + (pair ^ y[i])) * coarse
            rows = pl.ds(pl.multiple_of(start, coarse), coarse)
            lanes = pl.ds(pl.multiple_of((level ^ z[i]) * width, width), width)
            copies.append(
                pltpu.make_async_copy(
                    piece.at[i * coarse : (i + 1) * coarse], whole.at[rows, lanes], sems.at[len(copies)]
                )
            )
    for copy in copies:
        copy.start()
    for copy in copies:
        copy.wait()
    row0 = pl.multiple_of((level * PAIR + pair) * coarse, coarse)
    own_lanes = pl.ds(pl.multiple_of(orb * width, width), width)
    rows = whole[pl.ds(row0, coarse), :]

    def across(j, carry):
        lanes = pl.ds(pl.multiple_of(j * width, width), width)
        rows_f[:, lanes] = matmul(rows, whole[:, lanes])
        return carry

    lax.fori_loop(0, groups, across, 0)
    columns = whole[:, own_lanes]

    def down(i, carry):
        here = pl.ds(pl.multiple_of(i * coarse, coarse), coarse)
        square = matmul(whole[here, :], columns)
        cols_b[here, :] = (0.25 * (whole[here, own_lanes].astype(f32) - square)).astype(bf16)
        return carry

    lax.fori_loop(0, side // coarse, down, 0)
    left = (rows.astype(f32) - 0.25 * rows_f[...]).astype(bf16)
    value = matmul(left, cols_b[...]) + 0.125 * rows_f[:, own_lanes] - 0.5 * offset[...]
    row_ids = lax.broadcasted_iota(jnp.int32, value.shape, 0) + row0
    col_ids = lax.broadcasted_iota(jnp.int32, value.shape, 1) + orb * width
    root[...] = value + jnp.where(row_ids == col_ids, 1.0, 0.0)


def piece_places(levels, groups):
    places = []
    for core in (0, 1):
        for half in range(2):
            low = [half * levels // 2 + z for z in range(levels // 2)]
            for second in (0, 1):
                z, y, q = [], [], []
                for inner in (0, 1):
                    z += low
                    y += [second if half else inner] * len(low)
                    q += [2 * (inner if half else second) + core] * len(low)
                places.append((z, y, q))
    return places


def root_of(meta, pieces, offset, side, levels):
    coarse, width = offset.shape
    vmem, anywhere = pl.BlockSpec(memory_space=pltpu.VMEM), pl.BlockSpec(memory_space=pl.ANY)
    return pl.pallas_call(
        functools.partial(root_kernel, levels),
        out_shape=jax.ShapeDtypeStruct(offset.shape, f32),
        in_specs=[pl.BlockSpec(memory_space=pltpu.SMEM)] + [anywhere] * len(pieces) + [vmem],
        out_specs=vmem,
        scratch_shapes=[
            pltpu.VMEM((side, side), bf16),
            pltpu.VMEM((coarse, side), f32),
            pltpu.VMEM((side, width), bf16),
            pltpu.SemaphoreType.DMA((side // coarse * (side // width),)),
        ],
        compiler_params=params(40),
        cost_estimate=pl.CostEstimate(flops=4 * side * side * width, bytes_accessed=4 * side * side, transcendentals=0),
        name="root",
    )(meta, *pieces, offset)


def kinetic_kernel(edge, slots, table, scale, *refs):
    parts, (pot, fwd_in, fwd_out, back_in, back_mid, back_out), out = refs[:6], refs[6:12], refs[12]
    raw, x, outer, inner, total, total_fix, columns, sems = refs[13:]
    square = edge * edge
    own = PAIR * slots
    padded, width = x.shape[2:]
    copies = [pltpu.make_async_copy(part, raw.at[place], sems.at[place]) for place, part in enumerate(parts)]
    for copy in copies:
        copy.start()
    x[...] = jnp.zeros_like(x)
    total[...] = jnp.zeros_like(total)
    total_fix[...] = jnp.zeros_like(total_fix)
    columns[...] = pot[...].T
    for copy in copies:
        copy.wait()

    def lay_out(place, carry):
        for slot in range(slots):
            for i in range(edge):
                part, row = i // (edge // 2), i % (edge // 2) * square
                x[place * slots + slot, i, :square, :] = raw[
                    place, slot, row : row + square, part * width : (part + 1) * width
                ]
        return carry

    lax.fori_loop(0, len(parts), lay_out, 0)
    chunks = -(-square // ROWS)

    def per_slot(s, carry):
        @pl.when(table[s, 0] >= 0)
        def _():
            own_scale = scale[s]
            half = 0.5 * own_scale
            sums = (total, total_fix)

            def split(exact):
                exact = own_scale * exact
                value = exact.astype(bf16).astype(f32)
                return (half * value).astype(bf16), (half * (value - exact)).astype(bf16)

            sources = [[table[s, 1 + 3 * a + k] for k in range(3)] for a in range(3)]
            for i in range(chunks):
                rows = slice(i * ROWS, (i + 1) * ROWS)
                block = [x[t, :, rows, :].reshape(edge * ROWS, width) for t in sources[0]]
                fields = split(matmul(fwd_out[...], jnp.concatenate(block, axis=0)))
                for field in range(2):
                    outer[field, :, rows, :] = fields[field].reshape(edge, ROWS, width)
            for i in range(edge):
                for a in (1, 2):
                    block = jnp.concatenate([x[t, i] for t in sources[a]], axis=0)
                    fields = split(matmul(fwd_in[a - 1], block))
                    for field in range(2):
                        inner[field, i, (a - 1) * padded : a * padded, :] = fields[field]

            def back_outer(k, target):
                for i in range(chunks):
                    rows = slice(i * ROWS, (i + 1) * ROWS)
                    for field in range(2):
                        term = matmul(back_out[k], outer[field, :, rows, :].reshape(edge * ROWS, width))
                        sums[field][target, :, rows, :] += term.reshape(edge, ROWS, width)

            for k in (0, 2):
                for a in range(3):
                    target = sources[a][k]

                    @pl.when(target < own)
                    def _():
                        if a == 0:
                            back_outer(k, target)
                        else:
                            for i in range(edge):
                                for field in range(2):
                                    here = inner[field, i, (a - 1) * padded : a * padded, :]
                                    sums[field][target, i] += matmul(back_in[a - 1, k], here)

            here = sources[0][1]

            @pl.when(here < own)
            def _():
                back_outer(1, here)
                for i in range(edge):
                    for field in range(2):
                        sums[field][here, i] += matmul(back_mid[...], inner[field, i])

        return carry

    lax.fori_loop(0, table.shape[0], per_slot, 0)

    for t in range(own):
        for i in range(edge):
            rows = slice(i * square, (i + 1) * square)
            weighted = (columns[rows, t : t + 1] * x[t, i, :square, :].astype(f32)).astype(bf16)
            whole = total[t, i, :square, :] + weighted.astype(f32)
            top = whole.astype(bf16)
            low = (whole - top.astype(f32)).astype(bf16)
            fix = total_fix[t, i, :square, :].astype(bf16)
            out[t, rows, :] = jnp.concatenate([top, low, fix], axis=1)


def block_matrices(deriv_blocks):
    edge = deriv_blocks.shape[1]
    square = edge * edge
    padded = -(-square // ROWS) * ROWS
    ids = np.arange(padded)
    slow = ((ids[:, None] // edge) == np.arange(edge)).astype(np.float32)
    fast = (((ids[:, None] % edge) == np.arange(edge)) & (ids[:, None] < square)).astype(np.float32)
    ids = np.arange(edge * ROWS)
    outer = ((ids[:, None] // ROWS) == np.arange(edge)).astype(np.float32)
    within = ((ids[:, None] % ROWS) == np.arange(ROWS)).astype(np.float32)
    stacked = jnp.moveaxis(deriv_blocks, 0, 1).reshape(edge, 3 * edge)
    forward, backward = [], []
    for spot, mask in ((slow, fast), (fast, slow), (outer, within)):
        same = mask @ mask.T
        spread_out = np.kron(np.eye(3, dtype=np.float32), spot.T)
        spot_b, same_b = jnp.asarray(spot, bf16), jnp.asarray(same, f32)
        wide = matmul(matmul(spot_b, stacked).astype(bf16), jnp.asarray(spread_out, bf16))
        forward.append((wide * jnp.tile(same_b, (1, 3))).astype(bf16))
        turned = jnp.einsum("ri,kji->krj", spot_b, deriv_blocks, preferred_element_type=f32).astype(bf16)
        turned = jnp.einsum("krj,cj->krc", turned, spot_b, preferred_element_type=f32)
        backward.append((turned * same_b).astype(bf16))
    middle = jnp.concatenate([backward[0][1], backward[1][1]], axis=1)
    return jnp.stack(forward[:2]), forward[2], jnp.stack(backward[:2]), middle, backward[2]


def kinetic(parts, pot, matrices, table, scale, edge, coefficients):
    slots, folded, lanes = parts[0].shape
    width = lanes // 2
    padded = matrices[0].shape[1]
    own = PAIR * slots
    vmem = pl.BlockSpec(memory_space=pltpu.VMEM)
    smem = pl.BlockSpec(memory_space=pltpu.SMEM)
    anywhere = pl.BlockSpec(memory_space=pl.ANY)
    return pl.pallas_call(
        functools.partial(kinetic_kernel, edge, slots),
        out_shape=jax.ShapeDtypeStruct((own, coefficients, 3 * width), bf16),
        in_specs=[smem, smem] + [anywhere] * 6 + [vmem] * 6,
        out_specs=vmem,
        scratch_shapes=[
            pltpu.VMEM((6, slots, folded, lanes), bf16),
            pltpu.VMEM((6 * slots + 1, edge, padded, width), bf16),
            pltpu.VMEM((2, edge, padded, width), bf16),
            pltpu.VMEM((2, edge, 2 * padded, width), bf16),
            pltpu.VMEM((own, edge, padded, width), f32),
            pltpu.VMEM((own, edge, padded, width), f32),
            pltpu.VMEM(pot.shape[::-1], f32),
            pltpu.SemaphoreType.DMA((6,)),
        ],
        compiler_params=params(48),
        cost_estimate=pl.CostEstimate(flops=2 * 10**10, bytes_accessed=40 * 10**6, transcendentals=0),
        name="kinetic",
    )(table, scale, *parts, pot, *matrices)


def body(orbitals, potential, deriv_blocks, levels, box_counts, neighbours):
    slots, coefficients, own_width = orbitals.shape
    edge = deriv_blocks.shape[1]
    level, pair, orb = lax.axis_index("lvl"), lax.axis_index("pair"), lax.axis_index("orb")
    level_count, orb_count = lax.axis_size("lvl"), lax.axis_size("orb")
    half, fold = own_width // PAIR, coefficients // 2
    all_width = own_width * orb_count
    box_rows = all_width // (level_count * PAIR)
    first = pair == 0
    groups = range(orb_count)
    square_grid = level_count == orb_count == 4 and box_rows == half
    row0, col0 = (level * PAIR + pair) * box_rows, orb * own_width

    slot_ids = jnp.arange(slots, dtype=jnp.int32)
    own_ids = (level * PAIR + pair) * slots + slot_ids
    none = 16 * slots
    apart_ids = jnp.where(neighbours >= 0, neighbours - own_ids[:, None, None], none).reshape(slots, 6)
    live = (slot_ids < box_counts[0]).astype(jnp.int32)
    facts = jnp.concatenate([apart_ids, levels[:, None], live[:, None]], axis=1)
    wide_facts = jnp.pad(facts.astype(f32), ((0, 0), (0, own_width - facts.shape[1])))
    pack_meta = jnp.stack([pair, box_counts[0]]).astype(jnp.int32)
    [theirs] = pack(pack_meta, orbitals, wide_facts, False)
    pack_meta, theirs = lax.optimization_barrier((pack_meta, theirs))
    mine, active = pack(pack_meta, orbitals, wide_facts, True)

    far = {q: swap(active, "orb", q) for q in groups if q and q % 2 == 0}
    beside = swap(theirs, "pair", 1)
    first_mine, second_mine = trade(mine, "lvl", 0), trade(mine, "lvl", 1)
    near_active = swap(active, "orb", 1)
    later_pot, later_mine, beside = lax.optimization_barrier((potential, mine, beside))
    beside_rest = swap(later_mine, "pair", 1)
    first_beside, second_beside = trade(beside, "lvl", 0), trade(beside, "lvl", 1)

    def facts_of(packed):
        return packed[:, fold, : facts.shape[1]].astype(f32).astype(jnp.int32)

    side_facts = jnp.stack([facts_of(first_mine), facts_of(second_mine)])
    across_facts = swap(side_facts, "pair", 1)
    other_pot = swap(later_pot, "pair", 1)
    matrices = block_matrices(deriv_blocks)

    even = level % 2 == 0
    box_of_level = level * PAIR
    ids = jnp.concatenate(
        [
            own_ids,
            (box_of_level + 1 - pair) * slots + slot_ids,
            (box_of_level - 1) * slots + slot_ids,
            (box_of_level + PAIR) * slots + slot_ids,
        ]
    ).astype(jnp.int32)
    lower_own, lower_across = (jnp.where(even, both[1], both[0]) for both in (side_facts, across_facts))
    upper_own, upper_across = (jnp.where(even, both[0], both[1]) for both in (side_facts, across_facts))
    chosen = jnp.concatenate(
        [
            facts,
            facts_of(beside),
            jnp.where(first, lower_across, lower_own),
            jnp.where(first, upper_own, upper_across),
        ]
    )
    there = (ids >= 0) & (ids < level_count * PAIR * slots)

    def place(slot_id):
        box = slot_id // slots
        apart = box // PAIR - level
        base = jnp.where(apart == 0, 0, jnp.where((apart < 0) == even, 4, 2))
        return (base + (box % PAIR != pair)) * slots + slot_id % slots

    distance = chosen[:, :6]
    near = jnp.where(distance < none, place(jnp.maximum(ids, 0)[:, None] + distance), 6 * slots)
    near = jnp.clip(near, 0, 6 * slots)
    self_place = place(jnp.maximum(ids, 0))
    table = [jnp.where(there & (chosen[:, 7] > 0), self_place, -1)]
    for a in range(3):
        table += [near[:, 2 * a], self_place, near[:, 2 * a + 1]]
    table = jnp.stack(table, axis=1).astype(jnp.int32)
    level_of = chosen[:, 6]
    scale = jnp.where(level_of == 0, 0.5, jnp.where(level_of == 1, 1.0, 2.0)).astype(f32)
    pot = jnp.concatenate([potential, other_pot])
    pot = jnp.pad(pot, ((0, -pot.shape[0] % 8), (0, -pot.shape[1] % 128)))

    (far, near_active, beside, beside_rest, first_mine, second_mine, first_beside, second_beside, active, matrices) = (
        lax.optimization_barrier(
            (far, near_active, beside, beside_rest, first_mine, second_mine, first_beside, second_beside, active, matrices)
        )
    )
    table, scale, pot = lax.optimization_barrier((table, scale, pot))

    flat = lambda block: block.reshape(-1, block.shape[-1])
    cut = -(-slots * coefficients // (2 * ROWS)) * ROWS
    beside_all, beside_top = unfold(pack_meta, beside, beside_rest, fold, cut)
    cross = {q: [swap(beside_top, "orb", q), swap(flat(far[q])[cut:], "pair", 1)] for q in far}
    left_own = {0: active, 1: near_active, **far}
    left_beside = {0: [beside_all], 1: [swap(beside_all, "orb", 1)]}
    for q in far:
        left_own[q + 1] = swap(far[q], "orb", 1)

    def natural(blocks):
        return jnp.concatenate([lax.dynamic_index_in_dim(blocks, orb ^ j, keepdims=False) for j in groups], axis=1)

    def along_levels(blocks):
        mine_block = lambda target: lax.dynamic_index_in_dim(blocks, orb ^ target, keepdims=False)
        steps = range(1, level_count)
        return mine_block(level), [swap(mine_block(level ^ step), "lvl", step) for step in steps]

    def add(parts):
        own, got = parts
        return own.astype(f32) + sum(block.astype(f32) for block in got)

    def turned_rows(strip):
        pieces = []
        for over in range(PAIR):
            to_first = (pair ^ over) == 0
            piece = jnp.where(to_first, strip[:, :half], strip[:, half:])
            pieces.append((swap(piece, "pair", over) if over else piece).T)
        own, other = pieces
        return jnp.concatenate([jnp.where(first, own, other), jnp.where(first, other, own)], axis=1)

    def own_block(strip):
        strip = lax.all_gather(lax.psum(strip, "lvl"), ("orb", "pair"), axis=0, tiled=True)
        strip = lax.dynamic_slice_in_dim(strip, row0, box_rows, axis=0)
        return lax.dynamic_slice_in_dim(strip, col0, own_width, axis=1)

    meta = jnp.stack([pair, level, orb]).astype(jnp.int32)

    parts = [mine, beside, first_mine, first_beside, second_mine, second_beside]
    right = kinetic(parts, pot, matrices, table, scale, edge, coefficients)

    cross, right, meta = lax.optimization_barrier((cross, right, meta))
    lefts_own = [[flat(left_own[q])] for q in groups]
    lefts_beside = dict(left_beside)
    for q in far:
        lefts_beside[q] = list(cross[q])
        lefts_beside[q + 1] = [swap(piece, "orb", 1) for piece in cross[q]]
    lefts_beside = [lefts_beside[q] for q in groups]

    share = 1.0 / level_count
    blocks = box_correlation(share, meta, lefts_own, None, half)
    blocks = box_correlation(share, meta, lefts_beside, blocks, half)
    right = right.reshape(2, slots * coefficients, 3 * half)
    fock_part = box_fock(0, lefts_own, right, None)
    if square_grid:
        sent = along_levels(blocks)
        sent, fock_part = lax.optimization_barrier((sent, fock_part))
        offset_turned = add(sent)
        small = offset_turned.astype(bf16)
        offset = turned_rows(offset_turned)
    else:
        offset = own_block(natural(blocks).astype(f32))
    row_ids = row0 + jnp.arange(box_rows, dtype=jnp.int32)
    col_ids = col0 + jnp.arange(own_width, dtype=jnp.int32)
    correlation = offset + (row_ids[:, None] == col_ids[None, :]).astype(f32)
    fock_blocks = box_fock(1, lefts_beside, right, fock_part)
    if square_grid:
        pieces = [small] + [swap(small, "lvl", z) for z in range(1, level_count)]
        pieces, fock_blocks, offset = lax.optimization_barrier((pieces, fock_blocks, offset))
        join = functools.partial(jnp.concatenate, axis=0)
        top, low = join(pieces[: level_count // 2]), join(pieces[level_count // 2 :])
        sent = along_levels(fock_blocks)
        top, low = join([top, swap(top, "pair", 1)]), join([low, swap(low, "orb", 2)])
        pieces = [top, swap(top, "orb", 2), low, swap(low, "pair", 1)]
        pieces += [swap(piece, "orb", 1) for piece in pieces]
        root_meta = jnp.stack([level, pair, orb]).astype(jnp.int32)
        inverse_root = root_of(root_meta, pieces, offset, all_width, level_count)
        inverse_root, sent = lax.optimization_barrier((inverse_root, sent))
        sums = add(sent)
        main = turned_rows(sums[0] + sums[1])
        to = [
            ((z * PAIR + y) * orb_count + o, (o * PAIR + y) * orb_count + z)
            for z in range(level_count)
            for y in range(PAIR)
            for o in groups
        ]
        fock = main + lax.ppermute(sums[2].astype(bf16), BOX + ("orb",), to).astype(f32)
    else:
        main = natural(fock_blocks[:, 0]).astype(f32) + natural(fock_blocks[:, 1]).astype(f32)
        main = lax.all_gather(lax.psum(main, "lvl"), "pair", axis=0, tiled=True)
        fock = lax.dynamic_slice_in_dim(main, row0, box_rows, axis=1).T + own_block(natural(fock_blocks[:, 2]).astype(f32))
        gathered = lax.all_gather(offset.astype(bf16), "orb", axis=1, tiled=True)
        whole = lax.all_gather(gathered, BOX, axis=0, tiled=True)
        rows_of = lax.dynamic_slice_in_dim(whole, row0, box_rows, axis=0)
        cols_of = lax.dynamic_slice_in_dim(whole, col0, own_width, axis=1)
        row_square, col_square = matmul(rows_of, whole), matmul(whole, cols_of)
        left = (rows_of.astype(f32) - 0.25 * row_square).astype(bf16)
        right_side = (0.25 * (cols_of.astype(f32) - col_square)).astype(bf16)
        own_square = lax.dynamic_slice_in_dim(row_square, col0, own_width, axis=1)
        inverse_root = correlation - 1.5 * offset + 0.125 * own_square + matmul(left, right_side)
    return fock, correlation, inverse_root


def solution(mesh):
    levels = mesh.shape["box"] // PAIR
    split = Mesh(mesh.devices.reshape(levels, PAIR, mesh.shape["orb"]), ("lvl", "pair", "orb"))
    in_specs = (P(BOX, None, "orb"), P(BOX, None), P(), P(BOX), P(BOX), P(BOX, None, None))
    out_specs = (P(BOX, "orb"),) * 3
    return jax.shard_map(body, mesh=split, in_specs=in_specs, out_specs=out_specs, check_vma=False)
```

```python
import functools

import jax
import jax.numpy as jnp
import numpy as np
from jax import lax
from jax.experimental import pallas as pl
from jax.experimental.pallas import tpu as pltpu
from jax.sharding import Mesh, PartitionSpec as P

PAIR = 2
ROWS = 16
BOX = ("lvl", "pair")
f32, bf16 = jnp.float32, jnp.bfloat16


def swap(value, axis, bit):
    count = lax.axis_size(axis)
    return lax.ppermute(value, axis, [(i, i ^ bit) for i in range(count)])


def trade(value, axis, start):
    pairs = [(i, i + 1) for i in range(start, lax.axis_size(axis) - 1, 2)]
    return lax.ppermute(value, axis, pairs + [(b, a) for a, b in pairs])


def matmul(left, right):
    return jnp.dot(left, right, preferred_element_type=f32)


def params(mebibytes):
    return pltpu.CompilerParams(vmem_limit_bytes=mebibytes * 1024 * 1024)


def pack_kernel(own, meta, orbitals, facts, packed, *active):
    slots, coefficients, width = orbitals.shape
    half, fold = width // PAIR, coefficients // 2
    low_half = (meta[0] == 0) == own
    for slot in range(slots):
        keep = slot < meta[1]
        for part in range(2):
            rows = slice(part * fold, (part + 1) * fold)
            here = orbitals[slot, rows, :]
            here = jnp.where(keep, here, jnp.zeros_like(here))
            if active:
                active[0][slot, rows, :] = here
            lanes = slice(part * half, (part + 1) * half)
            packed[slot, :fold, lanes] = jnp.where(low_half, here[:, :half], here[:, half:])
        rest = packed.shape[1] - fold
        packed[slot, fold:, :] = jnp.broadcast_to(facts[slot : slot + 1, :], (rest, width)).astype(bf16)


def pack(meta, orbitals, facts, own):
    slots, coefficients, width = orbitals.shape
    fold = coefficients // 2
    padded = (fold // ROWS + 1) * ROWS
    vmem = pl.BlockSpec(memory_space=pltpu.VMEM)
    shapes = [jax.ShapeDtypeStruct((slots, padded, width), bf16)]
    shapes += [jax.ShapeDtypeStruct(orbitals.shape, bf16)] * own
    return pl.pallas_call(
        functools.partial(pack_kernel, own),
        out_shape=shapes,
        in_specs=[pl.BlockSpec(memory_space=pltpu.SMEM), vmem, vmem],
        out_specs=[vmem] * len(shapes),
        compiler_params=params(24),
        name="pack",
    )(meta, orbitals, facts)


def unfold_kernel(fold, meta, beside, rest, whole, top):
    slots, _, width = beside.shape
    half = width // PAIR
    first = meta[0] == 0
    for slot in range(slots):
        for part in range(2):
            lanes = slice(part * half, (part + 1) * half)
            near, far = beside[slot, :fold, lanes], rest[slot, :fold, lanes]
            start = (2 * slot + part) * fold
            here = jnp.concatenate([jnp.where(first, near, far), jnp.where(first, far, near)], axis=1)
            whole[start : start + fold, :] = here
    top[...] = whole[: top.shape[0], :]


def unfold(meta, beside, rest, fold, cut):
    slots, _, width = beside.shape
    vmem = pl.BlockSpec(memory_space=pltpu.VMEM)
    return pl.pallas_call(
        functools.partial(unfold_kernel, fold),
        out_shape=[
            jax.ShapeDtypeStruct((2 * slots * fold, width), bf16),
            jax.ShapeDtypeStruct((cut, width), bf16),
        ],
        in_specs=[pl.BlockSpec(memory_space=pltpu.SMEM), vmem, vmem],
        out_specs=[vmem, vmem],
        compiler_params=params(24),
        name="unfold",
    )(meta, beside, rest)


def load_left(lefts, held, sems):
    copies = []
    for q, pieces in enumerate(lefts):
        row = 0
        for piece in pieces:
            rows, width = piece.shape
            here = held.at[row : row + rows, q * width : (q + 1) * width]
            copies.append(pltpu.make_async_copy(piece, here, sems.at[len(copies)]))
            row += rows
    for copy in copies:
        copy.start()
    return copies


def grouped(refs, counts):
    refs = list(refs)
    return [[refs.pop(0) for _ in range(count)] for count in counts]


def correlation_kernel(share, counts, meta, *refs):
    refs, (out, held, turned, sems) = refs[:-4], refs[-4:]
    groups, half, width = out.shape
    lefts, before = grouped(refs, counts), refs[sum(counts) :]
    copies = load_left(lefts, held, sems)
    first = meta[0] == 0
    for copy in copies[: counts[0]]:
        copy.wait()
    own = held[:, :width]
    turned[...] = jnp.where(first, own[:, :half], own[:, half:]).T
    for copy in copies[counts[0] :]:
        copy.wait()
    for base in range(0, groups, 2):
        wide = matmul(turned[...], held[:, base * width : (base + 2) * width])
        for q in (base, base + 1):
            total = wide[:, (q - base) * width : (q - base + 1) * width]
            if before:
                total = total + before[0][q]
                if q == 0:
                    rows = lax.broadcasted_iota(jnp.int32, (half, width), 0) + jnp.where(first, 0, half)
                    columns = lax.broadcasted_iota(jnp.int32, (half, width), 1)
                    total = total - jnp.where(rows == columns, share, 0.0)
            out[q] = total.astype(out.dtype)


def box_correlation(share, meta, lefts, before, half):
    depth, width = sum(piece.shape[0] for piece in lefts[0]), lefts[0][0].shape[1]
    counts = [len(pieces) for pieces in lefts]
    vmem = pl.BlockSpec(memory_space=pltpu.VMEM)
    extra = [] if before is None else [before]
    return pl.pallas_call(
        functools.partial(correlation_kernel, share, counts),
        out_shape=jax.ShapeDtypeStruct((len(lefts), half, width), f32 if before is None else bf16),
        in_specs=[pl.BlockSpec(memory_space=pltpu.SMEM)]
        + [pl.BlockSpec(memory_space=pl.ANY)] * sum(counts)
        + [vmem] * len(extra),
        out_specs=vmem,
        scratch_shapes=[
            pltpu.VMEM((depth, len(lefts) * width), bf16),
            pltpu.VMEM((half, depth), bf16),
            pltpu.SemaphoreType.DMA((sum(counts),)),
        ],
        compiler_params=params(32),
        cost_estimate=pl.CostEstimate(
            flops=2 * len(lefts) * depth * width * half, bytes_accessed=2 * len(lefts) * depth * width, transcendentals=0
        ),
        name="correlation",
    )(meta, *[piece for pieces in lefts for piece in pieces], *extra)


def fock_kernel(side, counts, right, *refs):
    refs, (out, held, raw, turned, sems, last_sem) = refs[:-6], refs[-6:]
    lefts, before = grouped(refs, counts), refs[sum(counts) :]
    last = pltpu.make_async_copy(right.at[side], raw, last_sem)
    last.start()
    copies = load_left(lefts, held, sems)
    half, width = out.shape[-2] // (1 if before else 3), out.shape[-1]
    last.wait()
    turned[...] = raw[...].T
    for copy in copies:
        copy.wait()
    for base in range(0, len(lefts), 2):
        wide = matmul(turned[...], held[:, base * width : (base + 2) * width])
        for q in (base, base + 1):
            total = wide[:, (q - base) * width : (q - base + 1) * width]
            if before:
                total = total + before[0][q]
                main = total[:half] + total[half : 2 * half]
                top = main.astype(bf16)
                out[q, 0], out[q, 1] = top, (main - top.astype(f32)).astype(bf16)
                out[q, 2] = total[2 * half :].astype(bf16)
            else:
                out[q] = total


def box_fock(side, lefts, right, before):
    depth, width = sum(piece.shape[0] for piece in lefts[0]), lefts[0][0].shape[1]
    counts = [len(pieces) for pieces in lefts]
    tall = right.shape[-1]
    anywhere, vmem = pl.BlockSpec(memory_space=pl.ANY), pl.BlockSpec(memory_space=pltpu.VMEM)
    extra = [] if before is None else [before]
    out = ((len(lefts), tall, width), f32) if before is None else ((len(lefts), 3, tall // 3, width), bf16)
    return pl.pallas_call(
        functools.partial(fock_kernel, side, counts),
        out_shape=jax.ShapeDtypeStruct(*out),
        in_specs=[anywhere] * (sum(counts) + 1) + [vmem] * len(extra),
        out_specs=vmem,
        scratch_shapes=[
            pltpu.VMEM((depth, len(lefts) * width), bf16),
            pltpu.VMEM(right.shape[1:], bf16),
            pltpu.VMEM((tall, depth), bf16),
            pltpu.SemaphoreType.DMA((sum(counts),)),
            pltpu.SemaphoreType.DMA(()),
        ],
        compiler_params=params(40),
        cost_estimate=pl.CostEstimate(
            flops=2 * len(lefts) * depth * width * tall, bytes_accessed=2 * len(lefts) * depth * width, transcendentals=0
        ),
        name="fock",
    )(right, *[piece for pieces in lefts for piece in pieces], *extra)


def root_kernel(levels, meta, *refs):
    pieces, (offset, root, whole, rows_f, cols_b, sems) = refs[:-6], refs[-6:]
    level, pair, orb = meta[0], meta[1], meta[2]
    coarse, width = offset.shape
    side = whole.shape[0]
    groups = side // width
    copies = []
    for piece, (z, y, q) in zip(pieces, piece_places(levels, groups)):
        for i in range(len(z)):
            start = ((orb ^ q[i]) * PAIR + (pair ^ y[i])) * coarse
            rows = pl.ds(pl.multiple_of(start, coarse), coarse)
            lanes = pl.ds(pl.multiple_of((level ^ z[i]) * width, width), width)
            copies.append(
                pltpu.make_async_copy(
                    piece.at[i * coarse : (i + 1) * coarse], whole.at[rows, lanes], sems.at[len(copies)]
                )
            )
    for copy in copies:
        copy.start()
    for copy in copies:
        copy.wait()
    row0 = pl.multiple_of((level * PAIR + pair) * coarse, coarse)
    own_lanes = pl.ds(pl.multiple_of(orb * width, width), width)
    rows = whole[pl.ds(row0, coarse), :]

    def across(j, carry):
        lanes = pl.ds(pl.multiple_of(j * width, width), width)
        rows_f[:, lanes] = matmul(rows, whole[:, lanes])
        return carry

    lax.fori_loop(0, groups, across, 0)
    columns = whole[:, own_lanes]

    def down(i, carry):
        here = pl.ds(pl.multiple_of(i * coarse, coarse), coarse)
        square = matmul(whole[here, :], columns)
        cols_b[here, :] = (0.25 * (whole[here, own_lanes].astype(f32) - square)).astype(bf16)
        return carry

    lax.fori_loop(0, side // coarse, down, 0)
    left = (rows.astype(f32) - 0.25 * rows_f[...]).astype(bf16)
    value = matmul(left, cols_b[...]) + 0.125 * rows_f[:, own_lanes] - 0.5 * offset[...]
    row_ids = lax.broadcasted_iota(jnp.int32, value.shape, 0) + row0
    col_ids = lax.broadcasted_iota(jnp.int32, value.shape, 1) + orb * width
    root[...] = value + jnp.where(row_ids == col_ids, 1.0, 0.0)


def piece_places(levels, groups):
    places = []
    for core in (0, 1):
        for half in range(2):
            low = [half * levels // 2 + z for z in range(levels // 2)]
            for second in (0, 1):
                z, y, q = [], [], []
                for inner in (0, 1):
                    z += low
                    y += [second if half else inner] * len(low)
                    q += [2 * (inner if half else second) + core] * len(low)
                places.append((z, y, q))
    return places


def root_of(meta, pieces, offset, side, levels):
    coarse, width = offset.shape
    vmem, anywhere = pl.BlockSpec(memory_space=pltpu.VMEM), pl.BlockSpec(memory_space=pl.ANY)
    return pl.pallas_call(
        functools.partial(root_kernel, levels),
        out_shape=jax.ShapeDtypeStruct(offset.shape, f32),
        in_specs=[pl.BlockSpec(memory_space=pltpu.SMEM)] + [anywhere] * len(pieces) + [vmem],
        out_specs=vmem,
        scratch_shapes=[
            pltpu.VMEM((side, side), bf16),
            pltpu.VMEM((coarse, side), f32),
            pltpu.VMEM((side, width), bf16),
            pltpu.SemaphoreType.DMA((side // coarse * (side // width),)),
        ],
        compiler_params=params(40),
        cost_estimate=pl.CostEstimate(flops=4 * side * side * width, bytes_accessed=4 * side * side, transcendentals=0),
        name="root",
    )(meta, *pieces, offset)


def fill_tables(slots, levels, place_meta, own_facts, beside_facts, side_facts, across_facts, table, scale):
    level, pair = place_meta[0], place_meta[1]
    even = lax.rem(level, 2) == 0
    none = 6 * slots

    def place(slot_id):
        box = lax.div(slot_id, slots)
        apart = lax.div(box, PAIR) - level
        base = jnp.where(apart == 0, 0, jnp.where((apart < 0) == even, 4, 2))
        return (base + jnp.where(lax.rem(box, PAIR) != pair, 1, 0)) * slots + lax.rem(slot_id, slots)

    for index in range(4 * slots):
        group, r = divmod(index, slots)

        def fact(c):
            if group < 2:
                return (own_facts, beside_facts)[group][r, c]
            swap_id = jnp.where(even, 1, 0) if group == 2 else jnp.where(even, 0, 1)
            near_pair = 1 if group == 2 else 0
            return jnp.where(pair == near_pair, side_facts[swap_id, r, c], across_facts[swap_id, r, c])

        box = (
            level * PAIR + pair,
            level * PAIR + 1 - pair,
            jnp.maximum(level * PAIR - 1, 0),
            jnp.minimum((level + 1) * PAIR, levels * PAIR - 1),
        )[group]
        there = (True, True, level > 0, level < levels - 1)[group]
        own_id = box * slots + r
        own_place = place(own_id)
        table[index, 0] = jnp.where((fact(7) > 0) & there, own_place, -1)
        for a in range(3):
            for k in (0, 2):
                distance = fact(2 * a + k // 2)
                target = place(jnp.maximum(own_id + distance, 0))
                target = jnp.where(distance < 16 * slots, target, none)
                table[index, 1 + 3 * a + k] = jnp.clip(target, 0, none)
            table[index, 2 + 3 * a] = own_place
        level_of = fact(6)
        scale[index] = jnp.where(level_of == 0, 0.5, jnp.where(level_of == 1, 1.0, 2.0))


def kinetic_kernel(edge, slots, levels, place_meta, own_facts, beside_facts, side_facts, across_facts, *refs):
    parts, refs = refs[:6], refs[6:]
    (own_pot, beside_pot, fwd_in, fwd_out, back_in, back_mid, back_out), out, refs = refs[:7], refs[7], refs[8:]
    raw, x, outer, inner, total, total_fix, columns, table, scale, sems = refs
    square = edge * edge
    own = PAIR * slots
    padded, width = x.shape[2:]
    copies = [pltpu.make_async_copy(part, raw.at[place], sems.at[place]) for place, part in enumerate(parts)]
    for copy in copies:
        copy.start()
    x[...] = jnp.zeros_like(x)
    total[...] = jnp.zeros_like(total)
    total_fix[...] = jnp.zeros_like(total_fix)
    columns[0] = own_pot[...].T
    columns[1] = beside_pot[...].T
    fill_tables(slots, levels, place_meta, own_facts, beside_facts, side_facts, across_facts, table, scale)
    for copy in copies:
        copy.wait()

    def lay_out(place, carry):
        for slot in range(slots):
            for i in range(edge):
                part, row = i // (edge // 2), i % (edge // 2) * square
                x[place * slots + slot, i, :square, :] = raw[
                    place, slot, row : row + square, part * width : (part + 1) * width
                ]
        return carry

    lax.fori_loop(0, len(parts), lay_out, 0)
    chunks = -(-square // ROWS)

    def per_slot(s, carry):
        @pl.when(table[s, 0] >= 0)
        def _():
            own_scale = scale[s]
            half = 0.5 * own_scale
            sums = (total, total_fix)

            def split(exact):
                exact = own_scale * exact
                value = exact.astype(bf16).astype(f32)
                return (half * value).astype(bf16), (half * (value - exact)).astype(bf16)

            sources = [[table[s, 1 + 3 * a + k] for k in range(3)] for a in range(3)]
            for i in range(chunks):
                rows = slice(i * ROWS, (i + 1) * ROWS)
                block = [x[t, :, rows, :].reshape(edge * ROWS, width) for t in sources[0]]
                fields = split(matmul(fwd_out[...], jnp.concatenate(block, axis=0)))
                for field in range(2):
                    outer[field, :, rows, :] = fields[field].reshape(edge, ROWS, width)
            for i in range(edge):
                for a in (1, 2):
                    block = jnp.concatenate([x[t, i] for t in sources[a]], axis=0)
                    fields = split(matmul(fwd_in[a - 1], block))
                    for field in range(2):
                        inner[field, i, (a - 1) * padded : a * padded, :] = fields[field]

            def back_outer(k, target):
                for i in range(chunks):
                    rows = slice(i * ROWS, (i + 1) * ROWS)
                    for field in range(2):
                        term = matmul(back_out[k], outer[field, :, rows, :].reshape(edge * ROWS, width))
                        sums[field][target, :, rows, :] += term.reshape(edge, ROWS, width)

            for k in (0, 2):
                for a in range(3):
                    target = sources[a][k]

                    @pl.when(target < own)
                    def _():
                        if a == 0:
                            back_outer(k, target)
                        else:
                            for i in range(edge):
                                for field in range(2):
                                    here = inner[field, i, (a - 1) * padded : a * padded, :]
                                    sums[field][target, i] += matmul(back_in[a - 1, k], here)

            here = sources[0][1]

            @pl.when(here < own)
            def _():
                back_outer(1, here)
                for i in range(edge):
                    for field in range(2):
                        sums[field][here, i] += matmul(back_mid[...], inner[field, i])

        return carry

    lax.fori_loop(0, table.shape[0], per_slot, 0)

    for t in range(own):
        for i in range(edge):
            rows = slice(i * square, (i + 1) * square)
            weighted = (columns[t // slots, rows, t % slots : t % slots + 1] * x[t, i, :square, :].astype(f32)).astype(bf16)
            whole = total[t, i, :square, :] + weighted.astype(f32)
            top = whole.astype(bf16)
            low = (whole - top.astype(f32)).astype(bf16)
            fix = total_fix[t, i, :square, :].astype(bf16)
            out[t, rows, :] = jnp.concatenate([top, low, fix], axis=1)


def matrices_kernel(stacked, blocks, *refs):
    spots, outs = refs[:9], refs[9:]
    fwd_in, fwd_out, back_in, back_mid, back_out = outs
    for mode in range(3):
        spot, spread, same = spots[3 * mode : 3 * mode + 3]
        wide = matmul(matmul(spot[...], stacked[...]).astype(bf16), spread[...])
        wide = (wide * jnp.concatenate([same[...]] * 3, axis=1)).astype(bf16)
        if mode == 2:
            fwd_out[...] = wide
        else:
            fwd_in[mode] = wide
        for k in range(3):
            turned = lax.dot_general(spot[...], blocks[k], (((1,), (1,)), ((), ())), preferred_element_type=f32)
            turned = lax.dot_general(
                turned.astype(bf16), spot[...], (((1,), (1,)), ((), ())), preferred_element_type=f32
            )
            turned = (turned * same[...]).astype(bf16)
            if mode == 2:
                back_out[k] = turned
            else:
                back_in[mode, k] = turned
    back_mid[...] = jnp.concatenate([back_in[0, 1], back_in[1, 1]], axis=1)


def block_matrices(deriv_blocks):
    edge = deriv_blocks.shape[1]
    square = edge * edge
    padded = -(-square // ROWS) * ROWS
    tall = edge * ROWS
    ids = np.arange(padded)
    slow = ((ids[:, None] // edge) == np.arange(edge)).astype(np.float32)
    fast = (((ids[:, None] % edge) == np.arange(edge)) & (ids[:, None] < square)).astype(np.float32)
    ids = np.arange(tall)
    outer = ((ids[:, None] // ROWS) == np.arange(edge)).astype(np.float32)
    within = ((ids[:, None] % ROWS) == np.arange(ROWS)).astype(np.float32)
    stacked = jnp.moveaxis(deriv_blocks, 0, 1).reshape(edge, 3 * edge)
    constants = []
    for spot, mask in ((slow, fast), (fast, slow), (outer, within)):
        spread = np.kron(np.eye(3, dtype=np.float32), spot.T)
        constants += [jnp.asarray(spot, bf16), jnp.asarray(spread, bf16), jnp.asarray(mask @ mask.T, f32)]
    vmem = pl.BlockSpec(memory_space=pltpu.VMEM)
    shapes = [(2, padded, 3 * padded), (tall, 3 * tall), (2, 3, padded, padded), (padded, 2 * padded), (3, tall, tall)]
    return pl.pallas_call(
        matrices_kernel,
        out_shape=[jax.ShapeDtypeStruct(shape, bf16) for shape in shapes],
        in_specs=[vmem] * 11,
        out_specs=[vmem] * 5,
        compiler_params=params(24),
        name="matrices",
    )(stacked, deriv_blocks, *constants)


def kinetic(parts, place_meta, all_facts, pots, matrices, edge, coefficients, levels):
    slots, folded, lanes = parts[0].shape
    width = lanes // 2
    padded = matrices[0].shape[1]
    own = PAIR * slots
    vmem = pl.BlockSpec(memory_space=pltpu.VMEM)
    smem = pl.BlockSpec(memory_space=pltpu.SMEM)
    anywhere = pl.BlockSpec(memory_space=pl.ANY)
    return pl.pallas_call(
        functools.partial(kinetic_kernel, edge, slots, levels),
        out_shape=jax.ShapeDtypeStruct((own, coefficients, 3 * width), bf16),
        in_specs=[smem] * 5 + [anywhere] * 6 + [vmem] * 7,
        out_specs=vmem,
        scratch_shapes=[
            pltpu.VMEM((6, slots, folded, lanes), bf16),
            pltpu.VMEM((6 * slots + 1, edge, padded, width), bf16),
            pltpu.VMEM((2, edge, padded, width), bf16),
            pltpu.VMEM((2, edge, 2 * padded, width), bf16),
            pltpu.VMEM((own, edge, padded, width), f32),
            pltpu.VMEM((own, edge, padded, width), f32),
            pltpu.VMEM((2,) + pots[0].shape[::-1], f32),
            pltpu.SMEM((4 * slots, 10), jnp.int32),
            pltpu.SMEM((4 * slots,), f32),
            pltpu.SemaphoreType.DMA((6,)),
        ],
        compiler_params=params(48),
        cost_estimate=pl.CostEstimate(flops=2 * 10**10, bytes_accessed=40 * 10**6, transcendentals=0),
        name="kinetic",
    )(place_meta, *all_facts, *parts, *pots, *matrices)


def offset_sum_kernel(meta, *refs):
    blocks, (small, kept, sent) = refs[:-3], refs[-3:]
    total = blocks[0][...].astype(f32)
    for block in blocks[1:]:
        total = total + block[...].astype(f32)
    small[...] = total.astype(bf16)
    half = kept.shape[0]
    first = meta[0] == 0
    low, high = total[:, :half].T, total[:, half:].T
    kept[...] = jnp.where(first, low, high)
    sent[...] = jnp.where(first, high, low)


def fock_sum_kernel(meta, *refs):
    blocks, (share, kept, sent) = refs[:-3], refs[-3:]
    parts = []
    for part in range(3):
        total = blocks[0][part].astype(f32)
        for block in blocks[1:]:
            total = total + block[part].astype(f32)
        parts.append(total)
    main = parts[0] + parts[1]
    share[...] = parts[2].astype(bf16)
    half = kept.shape[0]
    first = meta[0] == 0
    low, high = main[:, :half].T, main[:, half:].T
    kept[...] = jnp.where(first, low, high)
    sent[...] = jnp.where(first, high, low)


def level_sum(kernel, meta, blocks):
    tall, width = blocks[0].shape[-2:]
    vmem = pl.BlockSpec(memory_space=pltpu.VMEM)
    turned = jax.ShapeDtypeStruct((width // PAIR, tall), f32)
    return pl.pallas_call(
        kernel,
        out_shape=[jax.ShapeDtypeStruct((tall, width), bf16), turned, turned],
        in_specs=[pl.BlockSpec(memory_space=pltpu.SMEM)] + [vmem] * len(blocks),
        out_specs=[vmem] * 3,
        compiler_params=params(24),
        name="level_sum",
    )(meta, *blocks)


def body(orbitals, potential, deriv_blocks, levels, box_counts, neighbours):
    slots, coefficients, own_width = orbitals.shape
    edge = deriv_blocks.shape[1]
    level, pair, orb = lax.axis_index("lvl"), lax.axis_index("pair"), lax.axis_index("orb")
    level_count, orb_count = lax.axis_size("lvl"), lax.axis_size("orb")
    half, fold = own_width // PAIR, coefficients // 2
    all_width = own_width * orb_count
    box_rows = all_width // (level_count * PAIR)
    first = pair == 0
    groups = range(orb_count)
    square_grid = level_count == orb_count == 4 and box_rows == half
    row0, col0 = (level * PAIR + pair) * box_rows, orb * own_width

    slot_ids = jnp.arange(slots, dtype=jnp.int32)
    own_ids = (level * PAIR + pair) * slots + slot_ids
    none = 16 * slots
    apart_ids = jnp.where(neighbours >= 0, neighbours - own_ids[:, None, None], none).reshape(slots, 6)
    live = (slot_ids < box_counts[0]).astype(jnp.int32)
    facts = jnp.concatenate([apart_ids, levels[:, None], live[:, None]], axis=1)
    wide_facts = jnp.pad(facts.astype(f32), ((0, 0), (0, own_width - facts.shape[1])))
    own_pot = jnp.pad(potential, ((0, -slots % 8), (0, -coefficients % 128)))
    beside_pot = swap(own_pot, "pair", 1)
    pack_meta = jnp.stack([pair, box_counts[0]]).astype(jnp.int32)
    [theirs] = pack(pack_meta, orbitals, wide_facts, False)
    pack_meta, theirs = lax.optimization_barrier((pack_meta, theirs))
    mine, active = pack(pack_meta, orbitals, wide_facts, True)

    far = {q: swap(active, "orb", q) for q in groups if q and q % 2 == 0}
    beside = swap(theirs, "pair", 1)
    first_mine, second_mine = trade(mine, "lvl", 0), trade(mine, "lvl", 1)
    beside_rest = swap(mine, "pair", 1)
    first_beside, second_beside = trade(beside, "lvl", 0), trade(beside, "lvl", 1)

    def facts_of(packed):
        return packed[:, fold, : facts.shape[1]].astype(f32).astype(jnp.int32)

    side_facts = jnp.stack([facts_of(first_mine), facts_of(second_mine)])
    across_facts = swap(side_facts, "pair", 1)
    matrices = block_matrices(deriv_blocks)

    far, active, parts, beside_rest, matrices, all_facts, pots = lax.optimization_barrier(
        (
            far,
            active,
            [mine, beside, first_mine, first_beside, second_mine, second_beside],
            beside_rest,
            matrices,
            [facts, facts_of(beside), side_facts, across_facts],
            [own_pot, beside_pot],
        )
    )
    beside = parts[1]

    flat = lambda block: block.reshape(-1, block.shape[-1])
    cut = -(-slots * coefficients // (2 * ROWS)) * ROWS
    beside_all, beside_top = unfold(pack_meta, beside, beside_rest, fold, cut)
    cross = {q: [swap(beside_top, "orb", q), swap(flat(far[q])[cut:], "pair", 1)] for q in far}
    left_own = {0: active, 1: swap(active, "orb", 1), **far}
    left_beside = {0: [beside_all], 1: [swap(beside_all, "orb", 1)]}
    for q in far:
        left_own[q + 1] = swap(far[q], "orb", 1)

    def natural(blocks):
        return jnp.concatenate([lax.dynamic_index_in_dim(blocks, orb ^ j, keepdims=False) for j in groups], axis=1)

    def along_levels(blocks):
        mine_block = lambda target: lax.dynamic_index_in_dim(blocks, orb ^ target, keepdims=False)
        steps = range(1, level_count)
        return [mine_block(level)] + [swap(mine_block(level ^ step), "lvl", step) for step in steps]

    def both_halves(kept, sent):
        got = swap(sent, "pair", 1)
        return jnp.concatenate([jnp.where(first, kept, got), jnp.where(first, got, kept)], axis=1)

    def own_block(strip):
        strip = lax.all_gather(lax.psum(strip, "lvl"), ("orb", "pair"), axis=0, tiled=True)
        strip = lax.dynamic_slice_in_dim(strip, row0, box_rows, axis=0)
        return lax.dynamic_slice_in_dim(strip, col0, own_width, axis=1)

    meta = jnp.stack([pair, level, orb]).astype(jnp.int32)

    place_meta = jnp.stack([level, pair]).astype(jnp.int32)
    right = kinetic(parts, place_meta, all_facts, pots, matrices, edge, coefficients, level_count)

    cross, right, meta = lax.optimization_barrier((cross, right, meta))
    lefts_own = [[flat(left_own[q])] for q in groups]
    lefts_beside = dict(left_beside)
    for q in far:
        lefts_beside[q] = list(cross[q])
        lefts_beside[q + 1] = [swap(piece, "orb", 1) for piece in cross[q]]
    lefts_beside = [lefts_beside[q] for q in groups]

    share = 1.0 / level_count
    blocks = box_correlation(share, meta, lefts_own, None, half)
    blocks = box_correlation(share, meta, lefts_beside, blocks, half)
    right = right.reshape(2, slots * coefficients, 3 * half)
    fock_part = box_fock(0, lefts_own, right, None)
    if square_grid:
        sent = along_levels(blocks)
        sent, fock_part = lax.optimization_barrier((sent, fock_part))
        small, kept, other = level_sum(offset_sum_kernel, meta, sent)
        offset = both_halves(kept, other)
    else:
        offset = own_block(natural(blocks).astype(f32))
    row_ids = row0 + jnp.arange(box_rows, dtype=jnp.int32)
    col_ids = col0 + jnp.arange(own_width, dtype=jnp.int32)
    correlation = offset + (row_ids[:, None] == col_ids[None, :]).astype(f32)
    fock_blocks = box_fock(1, lefts_beside, right, fock_part)
    if square_grid:
        pieces = [small] + [swap(small, "lvl", z) for z in range(1, level_count)]
        pieces, fock_blocks, offset = lax.optimization_barrier((pieces, fock_blocks, offset))
        join = functools.partial(jnp.concatenate, axis=0)
        top, low = join(pieces[: level_count // 2]), join(pieces[level_count // 2 :])
        sent = along_levels(fock_blocks)
        top, low = join([top, swap(top, "pair", 1)]), join([low, swap(low, "orb", 2)])
        pieces = [top, swap(top, "orb", 2), low, swap(low, "pair", 1)]
        pieces, sent = lax.optimization_barrier((pieces, sent))
        pieces += [swap(piece, "orb", 1) for piece in pieces]
        root_meta = jnp.stack([level, pair, orb]).astype(jnp.int32)
        inverse_root = root_of(root_meta, pieces, offset, all_width, level_count)
        share, kept, other = level_sum(fock_sum_kernel, meta, sent)
        to = [
            ((z * PAIR + y) * orb_count + o, (o * PAIR + y) * orb_count + z)
            for z in range(level_count)
            for y in range(PAIR)
            for o in groups
        ]
        fock = both_halves(kept, other) + lax.ppermute(share, BOX + ("orb",), to).astype(f32)
    else:
        main = natural(fock_blocks[:, 0]).astype(f32) + natural(fock_blocks[:, 1]).astype(f32)
        main = lax.all_gather(lax.psum(main, "lvl"), "pair", axis=0, tiled=True)
        fock = lax.dynamic_slice_in_dim(main, row0, box_rows, axis=1).T + own_block(natural(fock_blocks[:, 2]).astype(f32))
        gathered = lax.all_gather(offset.astype(bf16), "orb", axis=1, tiled=True)
        whole = lax.all_gather(gathered, BOX, axis=0, tiled=True)
        rows_of = lax.dynamic_slice_in_dim(whole, row0, box_rows, axis=0)
        cols_of = lax.dynamic_slice_in_dim(whole, col0, own_width, axis=1)
        row_square, col_square = matmul(rows_of, whole), matmul(whole, cols_of)
        left = (rows_of.astype(f32) - 0.25 * row_square).astype(bf16)
        right_side = (0.25 * (cols_of.astype(f32) - col_square)).astype(bf16)
        own_square = lax.dynamic_slice_in_dim(row_square, col0, own_width, axis=1)
        inverse_root = correlation - 1.5 * offset + 0.125 * own_square + matmul(left, right_side)
    return fock, correlation, inverse_root


def solution(mesh):
    levels = mesh.shape["box"] // PAIR
    split = Mesh(mesh.devices.reshape(levels, PAIR, mesh.shape["orb"]), ("lvl", "pair", "orb"))
    in_specs = (P(BOX, None, "orb"), P(BOX, None), P(), P(BOX), P(BOX), P(BOX, None, None))
    out_specs = (P(BOX, "orb"),) * 3
    return jax.shard_map(body, mesh=split, in_specs=in_specs, out_specs=out_specs, check_vma=False)
```

```python
import functools

import jax
import jax.numpy as jnp
import numpy as np
from jax import lax
from jax.experimental import pallas as pl
from jax.experimental.pallas import tpu as pltpu
from jax.sharding import Mesh, PartitionSpec as P

PAIR = 2
ROWS = 16
BOX = ("lvl", "pair")
f32, bf16 = jnp.float32, jnp.bfloat16


def swap(value, axis, bit):
    count = lax.axis_size(axis)
    return lax.ppermute(value, axis, [(i, i ^ bit) for i in range(count)])


def trade(value, axis, start):
    pairs = [(i, i + 1) for i in range(start, lax.axis_size(axis) - 1, 2)]
    return lax.ppermute(value, axis, pairs + [(b, a) for a, b in pairs])


def matmul(left, right):
    return jnp.dot(left, right, preferred_element_type=f32)


def params(mebibytes):
    return pltpu.CompilerParams(vmem_limit_bytes=mebibytes * 1024 * 1024)


def pack_kernel(meta, neighbours, levels, orbitals, theirs, mine):
    slots, coefficients, width = orbitals.shape
    half, fold = width // PAIR, coefficients // 2
    first = meta[0] == 0
    place = lax.broadcasted_iota(jnp.int32, (8, width), 1)
    for slot in range(slots):
        keep = slot < meta[1]
        for part in range(2):
            here = orbitals[slot, part * fold : (part + 1) * fold, :]
            here = jnp.where(keep, here, jnp.zeros_like(here))
            low, high = here[:, :half], here[:, half:]
            lanes = slice(part * half, (part + 1) * half)
            theirs[slot, :fold, lanes] = jnp.where(first, high, low)
            mine[slot, :fold, lanes] = jnp.where(first, low, high)
        own_id = meta[2] + slot
        facts = jnp.where(place == 6, levels[slot], jnp.where(place == 7, jnp.where(keep, 1, 0), 0))
        for c in range(6):
            target = neighbours[slot, c]
            facts = jnp.where(place == c, jnp.where(target >= 0, target - own_id, 16 * slots), facts)
        facts = facts.astype(f32).astype(bf16)
        for packed in (theirs, mine):
            packed[slot, fold : fold + 8, :] = facts
            rest = packed.shape[1] - fold - 8
            packed[slot, fold + 8 :, :] = jnp.zeros((rest, width), bf16)


def pack(meta, neighbours, levels, orbitals):
    slots, coefficients, width = orbitals.shape
    fold = coefficients // 2
    padded = (fold // ROWS + 1) * ROWS
    vmem, smem = pl.BlockSpec(memory_space=pltpu.VMEM), pl.BlockSpec(memory_space=pltpu.SMEM)
    return pl.pallas_call(
        pack_kernel,
        out_shape=[jax.ShapeDtypeStruct((slots, padded, width), bf16)] * 2,
        in_specs=[smem, smem, smem, vmem],
        out_specs=[vmem, vmem],
        compiler_params=params(24),
        name="pack",
    )(meta, neighbours, levels, orbitals)


def unfold_kernel(fold, meta, beside, rest, whole, top):
    slots, _, width = beside.shape
    half = width // PAIR
    first = meta[0] == 0
    for slot in range(slots):
        for part in range(2):
            lanes = slice(part * half, (part + 1) * half)
            near, far = beside[slot, :fold, lanes], rest[slot, :fold, lanes]
            start = (2 * slot + part) * fold
            here = jnp.concatenate([jnp.where(first, near, far), jnp.where(first, far, near)], axis=1)
            whole[start : start + fold, :] = here
    top[...] = whole[: top.shape[0], :]


def unfold(meta, beside, rest, fold, cut):
    slots, _, width = beside.shape
    vmem = pl.BlockSpec(memory_space=pltpu.VMEM)
    return pl.pallas_call(
        functools.partial(unfold_kernel, fold),
        out_shape=[
            jax.ShapeDtypeStruct((2 * slots * fold, width), bf16),
            jax.ShapeDtypeStruct((cut, width), bf16),
        ],
        in_specs=[pl.BlockSpec(memory_space=pltpu.SMEM), vmem, vmem],
        out_specs=[vmem, vmem],
        compiler_params=params(24),
        name="unfold",
    )(meta, beside, rest)


def load_left(lefts, held, sems):
    copies = []
    for q, pieces in enumerate(lefts):
        row = 0
        for piece in pieces:
            rows, width = piece.shape
            here = held.at[row : row + rows, q * width : (q + 1) * width]
            copies.append(pltpu.make_async_copy(piece, here, sems.at[len(copies)]))
            row += rows
    for copy in copies:
        copy.start()
    return copies


def grouped(refs, counts):
    refs = list(refs)
    return [[refs.pop(0) for _ in range(count)] for count in counts]


def correlation_kernel(share, counts, meta, *refs):
    refs, (out, held, turned, sems) = refs[:-4], refs[-4:]
    groups, half, width = out.shape
    lefts, before = grouped(refs, counts), refs[sum(counts) :]
    copies = load_left(lefts, held, sems)
    first = meta[0] == 0
    for copy in copies[: counts[0]]:
        copy.wait()
    own = held[:, :width]
    own = jnp.where(first, own[:, :half], own[:, half:]).T
    live = lax.broadcasted_iota(jnp.int32, own.shape, 1) < meta[1 if before else 2]
    turned[...] = jnp.where(live, own, jnp.zeros_like(own))
    for base in range(0, groups, 2):
        for copy in copies[max(sum(counts[:base]), counts[0]) : sum(counts[: base + 2])]:
            copy.wait()
        wide = matmul(turned[...], held[:, base * width : (base + 2) * width])
        for q in (base, base + 1):
            total = wide[:, (q - base) * width : (q - base + 1) * width]
            if before:
                total = total + before[0][q]
                if q == 0:
                    rows = lax.broadcasted_iota(jnp.int32, (half, width), 0) + jnp.where(first, 0, half)
                    columns = lax.broadcasted_iota(jnp.int32, (half, width), 1)
                    total = total - jnp.where(rows == columns, share, 0.0)
            out[q] = total.astype(out.dtype)


def box_correlation(share, meta, lefts, before, half):
    depth, width = sum(piece.shape[0] for piece in lefts[0]), lefts[0][0].shape[1]
    counts = [len(pieces) for pieces in lefts]
    vmem = pl.BlockSpec(memory_space=pltpu.VMEM)
    extra = [] if before is None else [before]
    return pl.pallas_call(
        functools.partial(correlation_kernel, share, counts),
        out_shape=jax.ShapeDtypeStruct((len(lefts), half, width), f32 if before is None else bf16),
        in_specs=[pl.BlockSpec(memory_space=pltpu.SMEM)]
        + [pl.BlockSpec(memory_space=pl.ANY)] * sum(counts)
        + [vmem] * len(extra),
        out_specs=vmem,
        scratch_shapes=[
            pltpu.VMEM((depth, len(lefts) * width), bf16),
            pltpu.VMEM((half, depth), bf16),
            pltpu.SemaphoreType.DMA((sum(counts),)),
        ],
        compiler_params=params(32),
        cost_estimate=pl.CostEstimate(
            flops=2 * len(lefts) * depth * width * half, bytes_accessed=2 * len(lefts) * depth * width, transcendentals=0
        ),
        name="correlation",
    )(meta, *[piece for pieces in lefts for piece in pieces], *extra)


def fock_kernel(side, counts, right, *refs):
    refs, (out, held, raw, turned, sems, last_sem) = refs[:-6], refs[-6:]
    lefts, before = grouped(refs, counts), refs[sum(counts) :]
    last = pltpu.make_async_copy(right.at[side], raw, last_sem)
    last.start()
    copies = load_left(lefts, held, sems)
    half, width = out.shape[-2] // (1 if before else 3), out.shape[-1]
    last.wait()
    turned[...] = raw[...].T
    for base in range(0, len(lefts), 2):
        for copy in copies[sum(counts[:base]) : sum(counts[: base + 2])]:
            copy.wait()
        wide = matmul(turned[...], held[:, base * width : (base + 2) * width])
        for q in (base, base + 1):
            total = wide[:, (q - base) * width : (q - base + 1) * width]
            if before:
                total = total + before[0][q]
                main = total[:half] + total[half : 2 * half]
                top = main.astype(bf16)
                out[q, 0], out[q, 1] = top, (main - top.astype(f32)).astype(bf16)
                out[q, 2] = total[2 * half :].astype(bf16)
            else:
                out[q] = total


def box_fock(side, lefts, right, before):
    depth, width = sum(piece.shape[0] for piece in lefts[0]), lefts[0][0].shape[1]
    counts = [len(pieces) for pieces in lefts]
    tall = right.shape[-1]
    anywhere, vmem = pl.BlockSpec(memory_space=pl.ANY), pl.BlockSpec(memory_space=pltpu.VMEM)
    extra = [] if before is None else [before]
    out = ((len(lefts), tall, width), f32) if before is None else ((len(lefts), 3, tall // 3, width), bf16)
    return pl.pallas_call(
        functools.partial(fock_kernel, side, counts),
        out_shape=jax.ShapeDtypeStruct(*out),
        in_specs=[anywhere] * (sum(counts) + 1) + [vmem] * len(extra),
        out_specs=vmem,
        scratch_shapes=[
            pltpu.VMEM((depth, len(lefts) * width), bf16),
            pltpu.VMEM(right.shape[1:], bf16),
            pltpu.VMEM((tall, depth), bf16),
            pltpu.SemaphoreType.DMA((sum(counts),)),
            pltpu.SemaphoreType.DMA(()),
        ],
        compiler_params=params(40),
        cost_estimate=pl.CostEstimate(
            flops=2 * len(lefts) * depth * width * tall, bytes_accessed=2 * len(lefts) * depth * width, transcendentals=0
        ),
        name="fock",
    )(right, *[piece for pieces in lefts for piece in pieces], *extra)


def root_kernel(levels, meta, *refs):
    pieces, (offset, root, whole, rows_f, cols_b, sems) = refs[:-6], refs[-6:]
    level, pair, orb = meta[0], meta[1], meta[2]
    coarse, width = offset.shape
    side = whole.shape[0]
    groups = side // width
    copies = []
    for piece, (z, y, q) in zip(pieces, piece_places(levels, groups)):
        for i in range(len(z)):
            start = ((orb ^ q[i]) * PAIR + (pair ^ y[i])) * coarse
            rows = pl.ds(pl.multiple_of(start, coarse), coarse)
            lanes = pl.ds(pl.multiple_of((level ^ z[i]) * width, width), width)
            copies.append(
                pltpu.make_async_copy(
                    piece.at[i * coarse : (i + 1) * coarse], whole.at[rows, lanes], sems.at[len(copies)]
                )
            )
    for copy in copies:
        copy.start()
    for copy in copies:
        copy.wait()
    row0 = pl.multiple_of((level * PAIR + pair) * coarse, coarse)
    own_lanes = pl.ds(pl.multiple_of(orb * width, width), width)
    rows = whole[pl.ds(row0, coarse), :]

    def across(j, carry):
        lanes = pl.ds(pl.multiple_of(j * width, width), width)
        rows_f[:, lanes] = matmul(rows, whole[:, lanes])
        return carry

    lax.fori_loop(0, groups, across, 0)
    columns = whole[:, own_lanes]

    def down(i, carry):
        here = pl.ds(pl.multiple_of(i * coarse, coarse), coarse)
        square = matmul(whole[here, :], columns)
        cols_b[here, :] = (0.25 * (whole[here, own_lanes].astype(f32) - square)).astype(bf16)
        return carry

    lax.fori_loop(0, side // coarse, down, 0)
    left = (rows.astype(f32) - 0.25 * rows_f[...]).astype(bf16)
    value = matmul(left, cols_b[...]) + 0.125 * rows_f[:, own_lanes] - 0.5 * offset[...]
    row_ids = lax.broadcasted_iota(jnp.int32, value.shape, 0) + row0
    col_ids = lax.broadcasted_iota(jnp.int32, value.shape, 1) + orb * width
    root[...] = value + jnp.where(row_ids == col_ids, 1.0, 0.0)


def piece_places(levels, groups):
    places = []
    for core in (0, 1):
        for half in range(2):
            low = [half * levels // 2 + z for z in range(levels // 2)]
            for second in (0, 1):
                z, y, q = [], [], []
                for inner in (0, 1):
                    z += low
                    y += [second if half else inner] * len(low)
                    q += [2 * (inner if half else second) + core] * len(low)
                places.append((z, y, q))
    return places


def root_of(meta, pieces, offset, side, levels):
    coarse, width = offset.shape
    vmem, anywhere = pl.BlockSpec(memory_space=pltpu.VMEM), pl.BlockSpec(memory_space=pl.ANY)
    return pl.pallas_call(
        functools.partial(root_kernel, levels),
        out_shape=jax.ShapeDtypeStruct(offset.shape, f32),
        in_specs=[pl.BlockSpec(memory_space=pltpu.SMEM)] + [anywhere] * len(pieces) + [vmem],
        out_specs=vmem,
        scratch_shapes=[
            pltpu.VMEM((side, side), bf16),
            pltpu.VMEM((coarse, side), f32),
            pltpu.VMEM((side, width), bf16),
            pltpu.SemaphoreType.DMA((side // coarse * (side // width),)),
        ],
        compiler_params=params(40),
        cost_estimate=pl.CostEstimate(flops=4 * side * side * width, bytes_accessed=4 * side * side, transcendentals=0),
        name="root",
    )(meta, *pieces, offset)


def fill_tables(slots, levels, place_meta, own_facts, beside_facts, side_facts, across_facts, table, scale):
    level, pair = place_meta[0], place_meta[1]
    even = lax.rem(level, 2) == 0
    none = 6 * slots

    def place(slot_id):
        box = lax.div(slot_id, slots)
        apart = lax.div(box, PAIR) - level
        base = jnp.where(apart == 0, 0, jnp.where((apart < 0) == even, 4, 2))
        return (base + jnp.where(lax.rem(box, PAIR) != pair, 1, 0)) * slots + lax.rem(slot_id, slots)

    for index in range(4 * slots):
        group, r = divmod(index, slots)

        def fact(c):
            if group < 2:
                return (own_facts, beside_facts)[group][r, c]
            swap_id = jnp.where(even, 1, 0) if group == 2 else jnp.where(even, 0, 1)
            near_pair = 1 if group == 2 else 0
            return jnp.where(pair == near_pair, side_facts[swap_id, r, c], across_facts[swap_id, r, c])

        box = (
            level * PAIR + pair,
            level * PAIR + 1 - pair,
            jnp.maximum(level * PAIR - 1, 0),
            jnp.minimum((level + 1) * PAIR, levels * PAIR - 1),
        )[group]
        there = (True, True, level > 0, level < levels - 1)[group]
        own_id = box * slots + r
        own_place = place(own_id)
        table[index, 0] = jnp.where((fact(7) > 0) & there, own_place, -1)
        for a in range(3):
            for k in (0, 2):
                distance = fact(2 * a + k // 2)
                target = place(jnp.maximum(own_id + distance, 0))
                target = jnp.where(distance < 16 * slots, target, none)
                table[index, 1 + 3 * a + k] = jnp.clip(target, 0, none)
            table[index, 2 + 3 * a] = own_place
        level_of = fact(6)
        scale[index] = jnp.where(level_of == 0, 0.5, jnp.where(level_of == 1, 1.0, 2.0))


def kinetic_kernel(edge, slots, levels, place_meta, own_facts, beside_facts, side_facts, across_facts, *refs):
    parts, refs = refs[:6], refs[6:]
    (own_pot, beside_pot, fwd_in, fwd_out, back_in, back_mid, back_out), out, refs = refs[:7], refs[7], refs[8:]
    raw, x, outer, inner, total, total_fix, columns, table, scale, sems = refs
    square = edge * edge
    own = PAIR * slots
    padded, width = x.shape[2:]
    copies = [pltpu.make_async_copy(part, raw.at[place], sems.at[place]) for place, part in enumerate(parts)]
    for copy in copies:
        copy.start()
    tail = padded - ROWS
    x[:, :, tail:, :] = jnp.zeros((x.shape[0], edge, ROWS, width), bf16)
    x[6 * slots] = jnp.zeros((edge, padded, width), bf16)
    total[...] = jnp.zeros_like(total)
    total_fix[...] = jnp.zeros_like(total_fix)
    columns[0] = own_pot[...].T
    columns[1] = beside_pot[...].T
    fill_tables(slots, levels, place_meta, own_facts, beside_facts, side_facts, across_facts, table, scale)
    for copy in copies:
        copy.wait()

    def lay_out(place, carry):
        for slot in range(slots):
            for i in range(edge):
                part, row = i // (edge // 2), i % (edge // 2) * square
                x[place * slots + slot, i, :square, :] = raw[
                    place, slot, row : row + square, part * width : (part + 1) * width
                ]
        return carry

    lax.fori_loop(0, len(parts), lay_out, 0)
    chunks = -(-square // ROWS)

    def per_slot(s, carry):
        @pl.when(table[s, 0] >= 0)
        def _():
            own_scale = scale[s]
            half = 0.5 * own_scale
            sums = (total, total_fix)

            def split(exact):
                exact = own_scale * exact
                value = exact.astype(bf16).astype(f32)
                return (half * value).astype(bf16), (half * (value - exact)).astype(bf16)

            sources = [[table[s, 1 + 3 * a + k] for k in range(3)] for a in range(3)]
            for i in range(chunks):
                rows = slice(i * ROWS, (i + 1) * ROWS)
                block = [x[t, :, rows, :].reshape(edge * ROWS, width) for t in sources[0]]
                fields = split(matmul(fwd_out[...], jnp.concatenate(block, axis=0)))
                for field in range(2):
                    outer[field, :, rows, :] = fields[field].reshape(edge, ROWS, width)
            for i in range(edge):
                for a in (1, 2):
                    block = jnp.concatenate([x[t, i] for t in sources[a]], axis=0)
                    fields = split(matmul(fwd_in[a - 1], block))
                    for field in range(2):
                        inner[field, i, (a - 1) * padded : a * padded, :] = fields[field]

            def back_outer(k, target):
                for i in range(chunks):
                    rows = slice(i * ROWS, (i + 1) * ROWS)
                    for field in range(2):
                        term = matmul(back_out[k], outer[field, :, rows, :].reshape(edge * ROWS, width))
                        sums[field][target, :, rows, :] += term.reshape(edge, ROWS, width)

            for k in (0, 2):
                for a in range(3):
                    target = sources[a][k]

                    @pl.when(target < own)
                    def _():
                        if a == 0:
                            back_outer(k, target)
                        else:
                            for i in range(edge):
                                for field in range(2):
                                    here = inner[field, i, (a - 1) * padded : a * padded, :]
                                    sums[field][target, i] += matmul(back_in[a - 1, k], here)

            here = sources[0][1]

            @pl.when(here < own)
            def _():
                back_outer(1, here)
                for i in range(edge):
                    for field in range(2):
                        sums[field][here, i] += matmul(back_mid[...], inner[field, i])

        return carry

    lax.fori_loop(0, table.shape[0], per_slot, 0)

    for t in range(own):
        for i in range(edge):
            rows = slice(i * square, (i + 1) * square)
            weighted = (columns[t // slots, rows, t % slots : t % slots + 1] * x[t, i, :square, :].astype(f32)).astype(bf16)
            whole = total[t, i, :square, :] + weighted.astype(f32)
            top = whole.astype(bf16)
            low = (whole - top.astype(f32)).astype(bf16)
            fix = total_fix[t, i, :square, :].astype(bf16)
            out[t, rows, :] = jnp.concatenate([top, low, fix], axis=1)


def matrices_kernel(stacked, blocks, *refs):
    spots, outs = refs[:9], refs[9:]
    fwd_in, fwd_out, back_in, back_mid, back_out = outs
    for mode in range(3):
        spot, spread, same = spots[3 * mode : 3 * mode + 3]
        wide = matmul(matmul(spot[...], stacked[...]).astype(bf16), spread[...])
        wide = (wide * jnp.concatenate([same[...]] * 3, axis=1)).astype(bf16)
        if mode == 2:
            fwd_out[...] = wide
        else:
            fwd_in[mode] = wide
        for k in range(3):
            turned = lax.dot_general(spot[...], blocks[k], (((1,), (1,)), ((), ())), preferred_element_type=f32)
            turned = lax.dot_general(
                turned.astype(bf16), spot[...], (((1,), (1,)), ((), ())), preferred_element_type=f32
            )
            turned = (turned * same[...]).astype(bf16)
            if mode == 2:
                back_out[k] = turned
            else:
                back_in[mode, k] = turned
    back_mid[...] = jnp.concatenate([back_in[0, 1], back_in[1, 1]], axis=1)


def block_matrices(deriv_blocks):
    edge = deriv_blocks.shape[1]
    square = edge * edge
    padded = -(-square // ROWS) * ROWS
    tall = edge * ROWS
    ids = np.arange(padded)
    slow = ((ids[:, None] // edge) == np.arange(edge)).astype(np.float32)
    fast = (((ids[:, None] % edge) == np.arange(edge)) & (ids[:, None] < square)).astype(np.float32)
    ids = np.arange(tall)
    outer = ((ids[:, None] // ROWS) == np.arange(edge)).astype(np.float32)
    within = ((ids[:, None] % ROWS) == np.arange(ROWS)).astype(np.float32)
    stacked = jnp.moveaxis(deriv_blocks, 0, 1).reshape(edge, 3 * edge)
    constants = []
    for spot, mask in ((slow, fast), (fast, slow), (outer, within)):
        spread = np.kron(np.eye(3, dtype=np.float32), spot.T)
        constants += [jnp.asarray(spot, bf16), jnp.asarray(spread, bf16), jnp.asarray(mask @ mask.T, f32)]
    vmem = pl.BlockSpec(memory_space=pltpu.VMEM)
    shapes = [(2, padded, 3 * padded), (tall, 3 * tall), (2, 3, padded, padded), (padded, 2 * padded), (3, tall, tall)]
    return pl.pallas_call(
        matrices_kernel,
        out_shape=[jax.ShapeDtypeStruct(shape, bf16) for shape in shapes],
        in_specs=[vmem] * 11,
        out_specs=[vmem] * 5,
        compiler_params=params(24),
        name="matrices",
    )(stacked, deriv_blocks, *constants)


def kinetic(parts, place_meta, all_facts, pots, matrices, edge, coefficients, levels):
    slots, folded, lanes = parts[0].shape
    width = lanes // 2
    padded = matrices[0].shape[1]
    own = PAIR * slots
    vmem = pl.BlockSpec(memory_space=pltpu.VMEM)
    smem = pl.BlockSpec(memory_space=pltpu.SMEM)
    anywhere = pl.BlockSpec(memory_space=pl.ANY)
    return pl.pallas_call(
        functools.partial(kinetic_kernel, edge, slots, levels),
        out_shape=jax.ShapeDtypeStruct((own, coefficients, 3 * width), bf16),
        in_specs=[smem] * 5 + [anywhere] * 6 + [vmem] * 7,
        out_specs=vmem,
        scratch_shapes=[
            pltpu.VMEM((6, slots, folded, lanes), bf16),
            pltpu.VMEM((6 * slots + 1, edge, padded, width), bf16),
            pltpu.VMEM((2, edge, padded, width), bf16),
            pltpu.VMEM((2, edge, 2 * padded, width), bf16),
            pltpu.VMEM((own, edge, padded, width), f32),
            pltpu.VMEM((own, edge, padded, width), f32),
            pltpu.VMEM((2,) + pots[0].shape[::-1], f32),
            pltpu.SMEM((4 * slots, 10), jnp.int32),
            pltpu.SMEM((4 * slots,), f32),
            pltpu.SemaphoreType.DMA((6,)),
        ],
        compiler_params=params(48),
        cost_estimate=pl.CostEstimate(flops=2 * 10**10, bytes_accessed=40 * 10**6, transcendentals=0),
        name="kinetic",
    )(place_meta, *all_facts, *parts, *pots, *matrices)


def offset_sum_kernel(meta, *refs):
    blocks, (small, kept, sent) = refs[:-3], refs[-3:]
    total = blocks[0][...].astype(f32)
    for block in blocks[1:]:
        total = total + block[...].astype(f32)
    small[...] = total.astype(bf16)
    half = kept.shape[0]
    first = meta[0] == 0
    low, high = total[:, :half].T, total[:, half:].T
    kept[...] = jnp.where(first, low, high)
    sent[...] = jnp.where(first, high, low)


def fock_sum_kernel(meta, *refs):
    blocks, (share, kept, sent) = refs[:-3], refs[-3:]
    parts = []
    for part in range(3):
        total = blocks[0][part].astype(f32)
        for block in blocks[1:]:
            total = total + block[part].astype(f32)
        parts.append(total)
    main = parts[0] + parts[1]
    share[...] = parts[2].astype(bf16)
    half = kept.shape[0]
    first = meta[0] == 0
    low, high = main[:, :half].T, main[:, half:].T
    kept[...] = jnp.where(first, low, high)
    sent[...] = jnp.where(first, high, low)


def level_sum(kernel, meta, blocks):
    tall, width = blocks[0].shape[-2:]
    vmem = pl.BlockSpec(memory_space=pltpu.VMEM)
    turned = jax.ShapeDtypeStruct((width // PAIR, tall), f32)
    return pl.pallas_call(
        kernel,
        out_shape=[jax.ShapeDtypeStruct((tall, width), bf16), turned, turned],
        in_specs=[pl.BlockSpec(memory_space=pltpu.SMEM)] + [vmem] * len(blocks),
        out_specs=[vmem] * 3,
        compiler_params=params(24),
        name="level_sum",
    )(meta, *blocks)


def body(orbitals, potential, deriv_blocks, levels, box_counts, neighbours):
    slots, coefficients, own_width = orbitals.shape
    edge = deriv_blocks.shape[1]
    level, pair, orb = lax.axis_index("lvl"), lax.axis_index("pair"), lax.axis_index("orb")
    level_count, orb_count = lax.axis_size("lvl"), lax.axis_size("orb")
    half, fold = own_width // PAIR, coefficients // 2
    all_width = own_width * orb_count
    box_rows = all_width // (level_count * PAIR)
    first = pair == 0
    groups = range(orb_count)
    square_grid = level_count == orb_count == 4 and box_rows == half
    row0, col0 = (level * PAIR + pair) * box_rows, orb * own_width

    own_pot = jnp.pad(potential, ((0, -slots % 8), (0, -coefficients % 128)))
    beside_pot = swap(own_pot, "pair", 1)
    own_base = (level * PAIR + pair) * slots
    pack_meta = jnp.stack([pair, box_counts[0], own_base]).astype(jnp.int32)
    theirs, mine = pack(pack_meta, neighbours.reshape(slots, 6), levels, orbitals)
    active = orbitals

    far = {q: swap(active, "orb", q) for q in groups if q and q % 2 == 0}
    beside = swap(theirs, "pair", 1)
    first_mine, second_mine = trade(mine, "lvl", 0), trade(mine, "lvl", 1)
    beside_rest = swap(mine, "pair", 1)
    first_beside, second_beside = trade(beside, "lvl", 0), trade(beside, "lvl", 1)

    def facts_of(packed):
        return packed[:, fold, :8].astype(f32).astype(jnp.int32)

    side_facts = jnp.stack([facts_of(first_mine), facts_of(second_mine)])
    across_facts = swap(side_facts, "pair", 1)
    matrices = block_matrices(deriv_blocks)

    far, active, parts, beside_rest, matrices, all_facts, pots = lax.optimization_barrier(
        (
            far,
            active,
            [mine, beside, first_mine, first_beside, second_mine, second_beside],
            beside_rest,
            matrices,
            [facts_of(mine), facts_of(beside), side_facts, across_facts],
            [own_pot, beside_pot],
        )
    )
    beside = parts[1]

    flat = lambda block: block.reshape(-1, block.shape[-1])
    cut = -(-slots * coefficients // (2 * ROWS)) * ROWS
    beside_all, beside_top = unfold(pack_meta, beside, beside_rest, fold, cut)
    cross = {q: [swap(beside_top, "orb", q), swap(flat(far[q])[cut:], "pair", 1)] for q in far}
    left_own = {0: active, 1: swap(active, "orb", 1), **far}
    left_beside = {0: [beside_all], 1: [swap(beside_all, "orb", 1)]}
    for q in far:
        left_own[q + 1] = swap(far[q], "orb", 1)

    def natural(blocks):
        return jnp.concatenate([lax.dynamic_index_in_dim(blocks, orb ^ j, keepdims=False) for j in groups], axis=1)

    def along_levels(blocks):
        mine_block = lambda target: lax.dynamic_index_in_dim(blocks, orb ^ target, keepdims=False)
        steps = range(1, level_count)
        return [mine_block(level)] + [swap(mine_block(level ^ step), "lvl", step) for step in steps]

    def both_halves(kept, sent):
        got = swap(sent, "pair", 1)
        return jnp.concatenate([jnp.where(first, kept, got), jnp.where(first, got, kept)], axis=1)

    def own_block(strip):
        strip = lax.all_gather(lax.psum(strip, "lvl"), ("orb", "pair"), axis=0, tiled=True)
        strip = lax.dynamic_slice_in_dim(strip, row0, box_rows, axis=0)
        return lax.dynamic_slice_in_dim(strip, col0, own_width, axis=1)

    live_rows = box_counts[0] * coefficients
    meta = jnp.stack([pair, slots * coefficients, live_rows]).astype(jnp.int32)

    place_meta = jnp.stack([level, pair]).astype(jnp.int32)
    right = kinetic(parts, place_meta, all_facts, pots, matrices, edge, coefficients, level_count)

    cross, right, meta = lax.optimization_barrier((cross, right, meta))
    lefts_own = [[flat(left_own[q])] for q in groups]
    lefts_beside = dict(left_beside)
    for q in far:
        lefts_beside[q] = list(cross[q])
        lefts_beside[q + 1] = [swap(piece, "orb", 1) for piece in cross[q]]
    lefts_beside = [lefts_beside[q] for q in groups]

    share = 1.0 / level_count
    blocks = box_correlation(share, meta, lefts_own, None, half)
    blocks = box_correlation(share, meta, lefts_beside, blocks, half)
    right = right.reshape(2, slots * coefficients, 3 * half)
    fock_part = box_fock(0, lefts_own, right, None)
    if square_grid:
        sent = along_levels(blocks)
        sent, fock_part = lax.optimization_barrier((sent, fock_part))
        small, kept, other = level_sum(offset_sum_kernel, meta, sent)
        offset = both_halves(kept, other)
    else:
        offset = own_block(natural(blocks).astype(f32))
    row_ids = row0 + jnp.arange(box_rows, dtype=jnp.int32)
    col_ids = col0 + jnp.arange(own_width, dtype=jnp.int32)
    correlation = offset + (row_ids[:, None] == col_ids[None, :]).astype(f32)
    fock_blocks = box_fock(1, lefts_beside, right, fock_part)
    if square_grid:
        pieces = [small] + [swap(small, "lvl", z) for z in range(1, level_count)]
        pieces, fock_blocks, offset = lax.optimization_barrier((pieces, fock_blocks, offset))
        join = functools.partial(jnp.concatenate, axis=0)
        top, low = join(pieces[: level_count // 2]), join(pieces[level_count // 2 :])
        sent = along_levels(fock_blocks)
        got = [swap(top, "pair", 1), swap(low, "orb", 2)]
        got, sent[1] = lax.optimization_barrier((got, sent[1]))
        top, low = join([top, got[0]]), join([low, got[1]])
        pieces = [top, swap(top, "orb", 2), low, swap(low, "pair", 1)]
        pieces, sent[2] = lax.optimization_barrier((pieces, sent[2]))
        pieces += [swap(piece, "orb", 1) for piece in pieces]
        root_meta = jnp.stack([level, pair, orb]).astype(jnp.int32)
        inverse_root = root_of(root_meta, pieces, offset, all_width, level_count)
        inverse_root, sent = lax.optimization_barrier((inverse_root, sent))
        share, kept, other = level_sum(fock_sum_kernel, meta, sent)
        to = [
            ((z * PAIR + y) * orb_count + o, (o * PAIR + y) * orb_count + z)
            for z in range(level_count)
            for y in range(PAIR)
            for o in groups
        ]
        fock = both_halves(kept, other) + lax.ppermute(share, BOX + ("orb",), to).astype(f32)
    else:
        main = natural(fock_blocks[:, 0]).astype(f32) + natural(fock_blocks[:, 1]).astype(f32)
        main = lax.all_gather(lax.psum(main, "lvl"), "pair", axis=0, tiled=True)
        fock = lax.dynamic_slice_in_dim(main, row0, box_rows, axis=1).T + own_block(natural(fock_blocks[:, 2]).astype(f32))
        gathered = lax.all_gather(offset.astype(bf16), "orb", axis=1, tiled=True)
        whole = lax.all_gather(gathered, BOX, axis=0, tiled=True)
        rows_of = lax.dynamic_slice_in_dim(whole, row0, box_rows, axis=0)
        cols_of = lax.dynamic_slice_in_dim(whole, col0, own_width, axis=1)
        row_square, col_square = matmul(rows_of, whole), matmul(whole, cols_of)
        left = (rows_of.astype(f32) - 0.25 * row_square).astype(bf16)
        right_side = (0.25 * (cols_of.astype(f32) - col_square)).astype(bf16)
        own_square = lax.dynamic_slice_in_dim(row_square, col0, own_width, axis=1)
        inverse_root = correlation - 1.5 * offset + 0.125 * own_square + matmul(left, right_side)
    return fock, correlation, inverse_root


def solution(mesh):
    levels = mesh.shape["box"] // PAIR
    split = Mesh(mesh.devices.reshape(levels, PAIR, mesh.shape["orb"]), ("lvl", "pair", "orb"))
    in_specs = (P(BOX, None, "orb"), P(BOX, None), P(), P(BOX), P(BOX), P(BOX, None, None))
    out_specs = (P(BOX, "orb"),) * 3
    return jax.shard_map(body, mesh=split, in_specs=in_specs, out_specs=out_specs, check_vma=False)
```

```python
import functools

import jax
import jax.numpy as jnp
import numpy as np
from jax import lax
from jax.experimental import pallas as pl
from jax.experimental.pallas import tpu as pltpu
from jax.sharding import Mesh, PartitionSpec as P

PAIR = 2
ROWS = 16
BOX = ("lvl", "pair")
f32, bf16 = jnp.float32, jnp.bfloat16


def swap(value, axis, bit):
    count = lax.axis_size(axis)
    return lax.ppermute(value, axis, [(i, i ^ bit) for i in range(count)])


def trade(value, axis, start):
    pairs = [(i, i + 1) for i in range(start, lax.axis_size(axis) - 1, 2)]
    return lax.ppermute(value, axis, pairs + [(b, a) for a, b in pairs])


def matmul(left, right):
    return jnp.dot(left, right, preferred_element_type=f32)


def params(mebibytes):
    return pltpu.CompilerParams(vmem_limit_bytes=mebibytes * 1024 * 1024)


def pack_kernel(meta, neighbours, levels, orbitals, pot, theirs, mine):
    slots, coefficients, width = orbitals.shape
    half, fold = width // PAIR, coefficients // 2
    first = meta[0] == 0
    place = lax.broadcasted_iota(jnp.int32, (8, width), 1)
    for slot in range(slots):
        keep = slot < meta[1]
        for part in range(2):
            here = orbitals[slot, part * fold : (part + 1) * fold, :]
            here = jnp.where(keep, here, jnp.zeros_like(here))
            low, high = here[:, :half], here[:, half:]
            lanes = slice(part * half, (part + 1) * half)
            theirs[slot, :fold, lanes] = jnp.where(first, high, low)
            mine[slot, :fold, lanes] = jnp.where(first, low, high)
        own_id = meta[2] + slot
        facts = jnp.where(place == 6, levels[slot], jnp.where(place == 7, jnp.where(keep, 1, 0), 0))
        for c in range(6):
            target = neighbours[slot, c]
            facts = jnp.where(place == c, jnp.where(target >= 0, target - own_id, 16 * slots), facts)
        facts = facts.astype(f32).astype(bf16)
        for packed in (theirs, mine):
            packed[slot, fold : fold + 8, :] = facts
        row = fold + 8
        for start in range(0, pot.shape[1], width):
            exact = pot[slot : slot + 1, start : start + width]
            for _ in range(3):
                part = exact.astype(bf16)
                exact = exact - part.astype(f32)
                for packed in (theirs, mine):
                    packed[slot, row : row + 1, :] = part
                row += 1
        for packed in (theirs, mine):
            packed[slot, row:, :] = jnp.zeros((packed.shape[1] - row, width), bf16)


def pack(meta, neighbours, levels, orbitals, pot):
    slots, coefficients, width = orbitals.shape
    fold = coefficients // 2
    padded = -(-(fold + 8 + 3 * (pot.shape[1] // width)) // ROWS) * ROWS
    vmem, smem = pl.BlockSpec(memory_space=pltpu.VMEM), pl.BlockSpec(memory_space=pltpu.SMEM)
    return pl.pallas_call(
        pack_kernel,
        out_shape=[jax.ShapeDtypeStruct((slots, padded, width), bf16)] * 2,
        in_specs=[smem, smem, smem, vmem, vmem],
        out_specs=[vmem, vmem],
        compiler_params=params(24),
        name="pack",
    )(meta, neighbours, levels, orbitals, pot)


def unfold_kernel(fold, meta, beside_in, rest_in, whole, top, beside, rest, sems):
    copies = [
        pltpu.make_async_copy(source, target, sems.at[i])
        for i, (source, target) in enumerate(((beside_in, beside), (rest_in, rest)))
    ]
    for copy in copies:
        copy.start()
    slots, _, width = beside.shape
    half = width // PAIR
    first = meta[0] == 0
    for copy in copies:
        copy.wait()
    for slot in range(slots):
        for part in range(2):
            lanes = slice(part * half, (part + 1) * half)
            near, far = beside[slot, :fold, lanes], rest[slot, :fold, lanes]
            start = (2 * slot + part) * fold
            here = jnp.concatenate([jnp.where(first, near, far), jnp.where(first, far, near)], axis=1)
            whole[start : start + fold, :] = here
    top[...] = whole[: top.shape[0], :]


def unfold(meta, beside, rest, fold, cut):
    slots, _, width = beside.shape
    vmem = pl.BlockSpec(memory_space=pltpu.VMEM)
    return pl.pallas_call(
        functools.partial(unfold_kernel, fold),
        out_shape=[
            jax.ShapeDtypeStruct((2 * slots * fold, width), bf16),
            jax.ShapeDtypeStruct((cut, width), bf16),
        ],
        in_specs=[pl.BlockSpec(memory_space=pltpu.SMEM)] + [pl.BlockSpec(memory_space=pl.ANY)] * 2,
        out_specs=[vmem, vmem],
        scratch_shapes=[
            pltpu.VMEM(beside.shape, bf16),
            pltpu.VMEM(beside.shape, bf16),
            pltpu.SemaphoreType.DMA((2,)),
        ],
        compiler_params=params(24),
        name="unfold",
    )(meta, beside, rest)


def load_left(lefts, held, sems):
    copies = []
    for q, pieces in enumerate(lefts):
        row = 0
        for piece in pieces:
            rows, width = piece.shape
            here = held.at[row : row + rows, q * width : (q + 1) * width]
            copies.append(pltpu.make_async_copy(piece, here, sems.at[len(copies)]))
            row += rows
    for copy in copies:
        copy.start()
    return copies


def grouped(refs, counts):
    refs = list(refs)
    return [[refs.pop(0) for _ in range(count)] for count in counts]


def correlation_kernel(share, counts, meta, *refs):
    refs, (out, held, turned, sems) = refs[:-4], refs[-4:]
    groups, half, width = out.shape
    lefts, before = grouped(refs, counts), refs[sum(counts) :]
    copies = load_left(lefts, held, sems)
    first = meta[0] == 0
    for copy in copies[: counts[0]]:
        copy.wait()
    own = held[:, :width]
    own = jnp.where(first, own[:, :half], own[:, half:]).T
    live = lax.broadcasted_iota(jnp.int32, own.shape, 1) < meta[1 if before else 2]
    turned[...] = jnp.where(live, own, jnp.zeros_like(own))
    for base in range(0, groups, 2):
        for copy in copies[max(sum(counts[:base]), counts[0]) : sum(counts[: base + 2])]:
            copy.wait()
        wide = matmul(turned[...], held[:, base * width : (base + 2) * width])
        for q in (base, base + 1):
            total = wide[:, (q - base) * width : (q - base + 1) * width]
            if before:
                total = total + before[0][q]
                if q == 0:
                    rows = lax.broadcasted_iota(jnp.int32, (half, width), 0) + jnp.where(first, 0, half)
                    columns = lax.broadcasted_iota(jnp.int32, (half, width), 1)
                    total = total - jnp.where(rows == columns, share, 0.0)
            out[q] = total.astype(out.dtype)


def box_correlation(share, meta, lefts, before, half):
    depth, width = sum(piece.shape[0] for piece in lefts[0]), lefts[0][0].shape[1]
    counts = [len(pieces) for pieces in lefts]
    vmem = pl.BlockSpec(memory_space=pltpu.VMEM)
    extra = [] if before is None else [before]
    return pl.pallas_call(
        functools.partial(correlation_kernel, share, counts),
        out_shape=jax.ShapeDtypeStruct((len(lefts), half, width), f32 if before is None else bf16),
        in_specs=[pl.BlockSpec(memory_space=pltpu.SMEM)]
        + [pl.BlockSpec(memory_space=pl.ANY)] * sum(counts)
        + [vmem] * len(extra),
        out_specs=vmem,
        scratch_shapes=[
            pltpu.VMEM((depth, len(lefts) * width), bf16),
            pltpu.VMEM((half, depth), bf16),
            pltpu.SemaphoreType.DMA((sum(counts),)),
        ],
        compiler_params=params(32),
        cost_estimate=pl.CostEstimate(
            flops=2 * len(lefts) * depth * width * half, bytes_accessed=2 * len(lefts) * depth * width, transcendentals=0
        ),
        name="correlation",
    )(meta, *[piece for pieces in lefts for piece in pieces], *extra)


def fock_kernel(side, counts, right, *refs):
    outs, (held, raw, turned, sems, last_sem) = refs[sum(counts) : -5], refs[-5:]
    lefts = grouped(refs, counts)
    before, apart, sent, kept = outs if len(outs) == 4 else (None, None, None, None)
    out = outs[-1]
    last = pltpu.make_async_copy(right.at[side], raw, last_sem)
    last.start()
    copies = load_left(lefts, held, sems)
    half, width = out.shape[-2] // (3 if before is None else 1), out.shape[-1]
    last.wait()
    turned[...] = raw[...].T
    for base in range(0, len(lefts), 2):
        for copy in copies[sum(counts[:base]) : sum(counts[: base + 2])]:
            copy.wait()
        wide = matmul(turned[...], held[:, base * width : (base + 2) * width])
        for q in (base, base + 1):
            total = wide[:, (q - base) * width : (q - base + 1) * width]
            if before is None:
                out[q] = total
                continue
            total = total + before[q]
            main = total[:half] + total[half : 2 * half]
            top = main.astype(bf16)
            parts = (top, (main - top.astype(f32)).astype(bf16), total[2 * half :].astype(bf16))
            distance = q ^ apart[0]

            def store(target):
                for i in range(3):
                    target[lax.shift_right_logical(distance, 1), i] = parts[i]

            pl.when(lax.rem(distance, 2) == 1)(functools.partial(store, sent))
            pl.when(lax.rem(distance, 2) == 0)(functools.partial(store, kept))


def box_fock(side, lefts, right, before, apart):
    depth, width = sum(piece.shape[0] for piece in lefts[0]), lefts[0][0].shape[1]
    counts = [len(pieces) for pieces in lefts]
    tall = right.shape[-1]
    anywhere, vmem = pl.BlockSpec(memory_space=pl.ANY), pl.BlockSpec(memory_space=pltpu.VMEM)
    extra = [] if before is None else [before, apart]
    out = jax.ShapeDtypeStruct((len(lefts), tall, width), f32)
    if before is not None:
        out = [jax.ShapeDtypeStruct((len(lefts) // 2, 3, tall // 3, width), bf16)] * 2
    return pl.pallas_call(
        functools.partial(fock_kernel, side, counts),
        out_shape=out,
        in_specs=[anywhere] * (sum(counts) + 1) + [vmem, pl.BlockSpec(memory_space=pltpu.SMEM)][: len(extra)],
        out_specs=vmem if before is None else [vmem, vmem],
        scratch_shapes=[
            pltpu.VMEM((depth, len(lefts) * width), bf16),
            pltpu.VMEM(right.shape[1:], bf16),
            pltpu.VMEM((tall, depth), bf16),
            pltpu.SemaphoreType.DMA((sum(counts),)),
            pltpu.SemaphoreType.DMA(()),
        ],
        compiler_params=params(40),
        cost_estimate=pl.CostEstimate(
            flops=2 * len(lefts) * depth * width * tall, bytes_accessed=2 * len(lefts) * depth * width, transcendentals=0
        ),
        name="fock",
    )(right, *[piece for pieces in lefts for piece in pieces], *extra)


def root_kernel(levels, meta, *refs):
    pieces, (offset, root, whole, rows_f, cols_b, sems) = refs[:-6], refs[-6:]
    level, pair, orb = meta[0], meta[1], meta[2]
    coarse, width = offset.shape
    side = whole.shape[0]
    groups = side // width
    copies = []
    for piece, (z, y, q) in zip(pieces, piece_places(levels, groups)):
        for i in range(len(z)):
            start = ((orb ^ q[i]) * PAIR + (pair ^ y[i])) * coarse
            rows = pl.ds(pl.multiple_of(start, coarse), coarse)
            lanes = pl.ds(pl.multiple_of((level ^ z[i]) * width, width), width)
            copies.append(
                pltpu.make_async_copy(
                    piece.at[i * coarse : (i + 1) * coarse], whole.at[rows, lanes], sems.at[len(copies)]
                )
            )
    for copy in copies:
        copy.start()
    for copy in copies:
        copy.wait()
    row0 = pl.multiple_of((level * PAIR + pair) * coarse, coarse)
    own_lanes = pl.ds(pl.multiple_of(orb * width, width), width)
    rows = whole[pl.ds(row0, coarse), :]

    def across(j, carry):
        lanes = pl.ds(pl.multiple_of(j * width, width), width)
        rows_f[:, lanes] = matmul(rows, whole[:, lanes])
        return carry

    lax.fori_loop(0, groups, across, 0)
    columns = whole[:, own_lanes]

    def down(i, carry):
        here = pl.ds(pl.multiple_of(i * coarse, coarse), coarse)
        square = matmul(whole[here, :], columns)
        cols_b[here, :] = (0.25 * (whole[here, own_lanes].astype(f32) - square)).astype(bf16)
        return carry

    lax.fori_loop(0, side // coarse, down, 0)
    left = (rows.astype(f32) - 0.25 * rows_f[...]).astype(bf16)
    value = matmul(left, cols_b[...]) + 0.125 * rows_f[:, own_lanes] - 0.5 * offset[...]
    row_ids = lax.broadcasted_iota(jnp.int32, value.shape, 0) + row0
    col_ids = lax.broadcasted_iota(jnp.int32, value.shape, 1) + orb * width
    root[...] = value + jnp.where(row_ids == col_ids, 1.0, 0.0)


def piece_places(levels, groups):
    places = []
    for core in (0, 1):
        for half in range(2):
            low = [half * levels // 2 + z for z in range(levels // 2)]
            for second in (0, 1):
                z, y, q = [], [], []
                for inner in (0, 1):
                    z += low
                    y += [second if half else inner] * len(low)
                    q += [2 * (inner if half else second) + core] * len(low)
                places.append((z, y, q))
    return places


def root_of(meta, pieces, offset, side, levels):
    coarse, width = offset.shape
    vmem, anywhere = pl.BlockSpec(memory_space=pltpu.VMEM), pl.BlockSpec(memory_space=pl.ANY)
    return pl.pallas_call(
        functools.partial(root_kernel, levels),
        out_shape=jax.ShapeDtypeStruct(offset.shape, f32),
        in_specs=[pl.BlockSpec(memory_space=pltpu.SMEM)] + [anywhere] * len(pieces) + [vmem],
        out_specs=vmem,
        scratch_shapes=[
            pltpu.VMEM((side, side), bf16),
            pltpu.VMEM((coarse, side), f32),
            pltpu.VMEM((side, width), bf16),
            pltpu.SemaphoreType.DMA((side // coarse * (side // width),)),
        ],
        compiler_params=params(40),
        cost_estimate=pl.CostEstimate(flops=4 * side * side * width, bytes_accessed=4 * side * side, transcendentals=0),
        name="root",
    )(meta, *pieces, offset)


def fill_tables(slots, levels, place_meta, facts, table, scale):
    level, pair = place_meta[0], place_meta[1]
    even = lax.rem(level, 2) == 0
    none = 6 * slots

    def place(slot_id):
        box = lax.div(slot_id, slots)
        apart = lax.div(box, PAIR) - level
        base = jnp.where(apart == 0, 0, jnp.where((apart < 0) == even, 4, 2))
        return (base + jnp.where(lax.rem(box, PAIR) != pair, 1, 0)) * slots + lax.rem(slot_id, slots)

    for index in range(4 * slots):
        group, r = divmod(index, slots)

        def fact(c):
            if group < 2:
                return facts[group, r, c]
            swap_id = jnp.where(even, 1, 0) if group == 2 else jnp.where(even, 0, 1)
            near_pair = 1 if group == 2 else 0
            return facts[2 + 2 * swap_id + jnp.where(pair == near_pair, 0, 1), r, c]

        box = (
            level * PAIR + pair,
            level * PAIR + 1 - pair,
            jnp.maximum(level * PAIR - 1, 0),
            jnp.minimum((level + 1) * PAIR, levels * PAIR - 1),
        )[group]
        there = (True, True, level > 0, level < levels - 1)[group]
        own_id = box * slots + r
        own_place = place(own_id)
        table[index, 0] = jnp.where((fact(7) > 0) & there, own_place, -1)
        for a in range(3):
            for k in (0, 2):
                distance = fact(2 * a + k // 2)
                target = place(jnp.maximum(own_id + distance, 0))
                target = jnp.where(distance < 16 * slots, target, none)
                table[index, 1 + 3 * a + k] = jnp.clip(target, 0, none)
            table[index, 2 + 3 * a] = own_place
        level_of = fact(6)
        scale[index] = jnp.where(level_of == 0, 0.5, jnp.where(level_of == 1, 1.0, 2.0))


def kinetic_kernel(edge, slots, levels, place_meta, facts, *refs):
    parts, refs = refs[:6], refs[6:]
    (fwd_in, fwd_out, back_in, back_mid, back_out), out, refs = refs[:5], refs[5], refs[6:]
    raw, x, outer, inner, total, total_fix, lines, columns, table, scale, sems = refs
    square = edge * edge
    own = PAIR * slots
    padded, width = x.shape[2:]
    copies = [pltpu.make_async_copy(part, raw.at[place], sems.at[place]) for place, part in enumerate(parts)]
    for copy in copies:
        copy.start()
    tail = padded - ROWS
    x[:, :, tail:, :] = jnp.zeros((x.shape[0], edge, ROWS, width), bf16)
    x[6 * slots] = jnp.zeros((edge, padded, width), bf16)
    total[...] = jnp.zeros_like(total)
    total_fix[...] = jnp.zeros_like(total_fix)
    fill_tables(slots, levels, place_meta, facts, table, scale)
    lines[...] = jnp.zeros_like(lines)
    for copy in copies:
        copy.wait()
    lanes = raw.shape[3]
    for t in range(own):
        for start in range(0, lines.shape[1], lanes):
            row = edge * square // 2 + 8 + 3 * (start // lanes)
            high, middle, low = (
                raw[t // slots, t % slots, row + i : row + i + 1, :].astype(f32) for i in range(3)
            )
            lines[t : t + 1, start : start + lanes] = (high + middle) + low
    columns[...] = lines[...].T

    def lay_out(place, carry):
        for slot in range(slots):
            for i in range(edge):
                part, row = i // (edge // 2), i % (edge // 2) * square
                x[place * slots + slot, i, :square, :] = raw[
                    place, slot, row : row + square, part * width : (part + 1) * width
                ]
        return carry

    lax.fori_loop(0, len(parts), lay_out, 0)
    chunks = -(-square // ROWS)

    def per_slot(s, carry):
        @pl.when(table[s, 0] >= 0)
        def _():
            own_scale = scale[s]
            half = 0.5 * own_scale
            sums = (total, total_fix)

            def split(exact):
                exact = own_scale * exact
                value = exact.astype(bf16).astype(f32)
                return (half * value).astype(bf16), (half * (value - exact)).astype(bf16)

            sources = [[table[s, 1 + 3 * a + k] for k in range(3)] for a in range(3)]
            here = sources[0][1]
            for a in range(3):

                @pl.when((here < own) | (sources[a][0] < own) | (sources[a][2] < own))
                def _():
                    if a == 0:
                        for i in range(chunks):
                            rows = slice(i * ROWS, (i + 1) * ROWS)
                            block = [x[t, :, rows, :].reshape(edge * ROWS, width) for t in sources[0]]
                            fields = split(matmul(fwd_out[...], jnp.concatenate(block, axis=0)))
                            for field in range(2):
                                outer[field, :, rows, :] = fields[field].reshape(edge, ROWS, width)
                    else:
                        for i in range(edge):
                            block = jnp.concatenate([x[t, i] for t in sources[a]], axis=0)
                            fields = split(matmul(fwd_in[a - 1], block))
                            for field in range(2):
                                inner[field, i, (a - 1) * padded : a * padded, :] = fields[field]

            def back_outer(k, target):
                for i in range(chunks):
                    rows = slice(i * ROWS, (i + 1) * ROWS)
                    for field in range(2):
                        term = matmul(back_out[k], outer[field, :, rows, :].reshape(edge * ROWS, width))
                        sums[field][target, :, rows, :] += term.reshape(edge, ROWS, width)

            for k in (0, 2):
                for a in range(3):
                    target = sources[a][k]

                    @pl.when(target < own)
                    def _():
                        if a == 0:
                            back_outer(k, target)
                        else:
                            for i in range(edge):
                                for field in range(2):
                                    here = inner[field, i, (a - 1) * padded : a * padded, :]
                                    sums[field][target, i] += matmul(back_in[a - 1, k], here)

            @pl.when(here < own)
            def _():
                back_outer(1, here)
                for i in range(edge):
                    for field in range(2):
                        sums[field][here, i] += matmul(back_mid[...], inner[field, i])

        return carry

    lax.fori_loop(0, table.shape[0], per_slot, 0)

    for t in range(own):
        for i in range(edge):
            rows = slice(i * square, (i + 1) * square)
            weighted = (columns[rows, t : t + 1] * x[t, i, :square, :].astype(f32)).astype(bf16)
            whole = total[t, i, :square, :] + weighted.astype(f32)
            top = whole.astype(bf16)
            low = (whole - top.astype(f32)).astype(bf16)
            fix = total_fix[t, i, :square, :].astype(bf16)
            out[t, rows, :] = jnp.concatenate([top, low, fix], axis=1)


def matrices_kernel(stacked, blocks, *refs):
    spots, outs = refs[:9], refs[9:]
    fwd_in, fwd_out, back_in, back_mid, back_out = outs
    for mode in range(3):
        spot, spread, same = spots[3 * mode : 3 * mode + 3]
        wide = matmul(matmul(spot[...], stacked[...]).astype(bf16), spread[...])
        wide = (wide * jnp.concatenate([same[...]] * 3, axis=1)).astype(bf16)
        if mode == 2:
            fwd_out[...] = wide
        else:
            fwd_in[mode] = wide
        for k in range(3):
            turned = lax.dot_general(spot[...], blocks[k], (((1,), (1,)), ((), ())), preferred_element_type=f32)
            turned = lax.dot_general(
                turned.astype(bf16), spot[...], (((1,), (1,)), ((), ())), preferred_element_type=f32
            )
            turned = (turned * same[...]).astype(bf16)
            if mode == 2:
                back_out[k] = turned
            else:
                back_in[mode, k] = turned
    back_mid[...] = jnp.concatenate([back_in[0, 1], back_in[1, 1]], axis=1)


def block_matrices(deriv_blocks):
    edge = deriv_blocks.shape[1]
    square = edge * edge
    padded = -(-square // ROWS) * ROWS
    tall = edge * ROWS
    ids = np.arange(padded)
    slow = ((ids[:, None] // edge) == np.arange(edge)).astype(np.float32)
    fast = (((ids[:, None] % edge) == np.arange(edge)) & (ids[:, None] < square)).astype(np.float32)
    ids = np.arange(tall)
    outer = ((ids[:, None] // ROWS) == np.arange(edge)).astype(np.float32)
    within = ((ids[:, None] % ROWS) == np.arange(ROWS)).astype(np.float32)
    stacked = jnp.moveaxis(deriv_blocks, 0, 1).reshape(edge, 3 * edge)
    constants = []
    for spot, mask in ((slow, fast), (fast, slow), (outer, within)):
        spread = np.kron(np.eye(3, dtype=np.float32), spot.T)
        constants += [jnp.asarray(spot, bf16), jnp.asarray(spread, bf16), jnp.asarray(mask @ mask.T, f32)]
    vmem = pl.BlockSpec(memory_space=pltpu.VMEM)
    shapes = [(2, padded, 3 * padded), (tall, 3 * tall), (2, 3, padded, padded), (padded, 2 * padded), (3, tall, tall)]
    return pl.pallas_call(
        matrices_kernel,
        out_shape=[jax.ShapeDtypeStruct(shape, bf16) for shape in shapes],
        in_specs=[vmem] * 11,
        out_specs=[vmem] * 5,
        compiler_params=params(24),
        name="matrices",
    )(stacked, deriv_blocks, *constants)


def kinetic(parts, place_meta, facts, matrices, edge, coefficients, levels):
    slots, folded, lanes = parts[0].shape
    width = lanes // 2
    padded = matrices[0].shape[1]
    own = PAIR * slots
    vmem = pl.BlockSpec(memory_space=pltpu.VMEM)
    smem = pl.BlockSpec(memory_space=pltpu.SMEM)
    anywhere = pl.BlockSpec(memory_space=pl.ANY)
    return pl.pallas_call(
        functools.partial(kinetic_kernel, edge, slots, levels),
        out_shape=jax.ShapeDtypeStruct((own, coefficients, 3 * width), bf16),
        in_specs=[smem] * 2 + [anywhere] * 6 + [vmem] * 5,
        out_specs=vmem,
        scratch_shapes=[
            pltpu.VMEM((6, slots, folded, lanes), bf16),
            pltpu.VMEM((6 * slots + 1, edge, padded, width), bf16),
            pltpu.VMEM((2, edge, padded, width), bf16),
            pltpu.VMEM((2, edge, 2 * padded, width), bf16),
            pltpu.VMEM((own, edge, padded, width), f32),
            pltpu.VMEM((own, edge, padded, width), f32),
            pltpu.VMEM((own + -own % 8, coefficients + -coefficients % lanes), f32),
            pltpu.VMEM((coefficients + -coefficients % lanes, own + -own % 8), f32),
            pltpu.SMEM((4 * slots, 10), jnp.int32),
            pltpu.SMEM((4 * slots,), f32),
            pltpu.SemaphoreType.DMA((6,)),
        ],
        compiler_params=params(48),
        cost_estimate=pl.CostEstimate(flops=2 * 10**10, bytes_accessed=40 * 10**6, transcendentals=0),
        name="kinetic",
    )(place_meta, facts, *parts, *matrices)


def offset_sum_kernel(meta, *refs):
    blocks, (small, kept, sent) = refs[:-3], refs[-3:]
    total = blocks[0][...].astype(f32)
    for block in blocks[1:]:
        total = total + block[...].astype(f32)
    small[...] = total.astype(bf16)
    half = kept.shape[0]
    first = meta[0] == 0
    low, high = total[:, :half].T, total[:, half:].T
    kept[...] = jnp.where(first, low, high)
    sent[...] = jnp.where(first, high, low)


def fock_pair_kernel(kept, got, own, sent):
    for j in range(2):
        main, share = (
            sum((block[j, i].astype(f32) for block in (kept, got) for i in parts), 0.0) for parts in ((0, 1), (2,))
        )
        if j == 0:
            own[0], own[1] = main, share
        else:
            top = main.astype(bf16)
            sent[0], sent[1], sent[2] = top, (main - top.astype(f32)).astype(bf16), share.astype(bf16)


def fock_pair(kept, got):
    vmem = pl.BlockSpec(memory_space=pltpu.VMEM)
    tall, width = kept.shape[2:]
    return pl.pallas_call(
        fock_pair_kernel,
        out_shape=[jax.ShapeDtypeStruct((2, tall, width), f32), jax.ShapeDtypeStruct((3, tall, width), bf16)],
        in_specs=[vmem, vmem],
        out_specs=[vmem, vmem],
        compiler_params=params(24),
        name="fock_pair",
    )(kept, got)


def fock_sum_kernel(meta, own, got, share, kept, sent):
    main = own[0] + got[0].astype(f32) + got[1].astype(f32)
    share[...] = (own[1] + got[2].astype(f32)).astype(bf16)
    half = kept.shape[0]
    first = meta[0] == 0
    low, high = main[:, :half].T, main[:, half:].T
    kept[...] = jnp.where(first, low, high)
    sent[...] = jnp.where(first, high, low)


def level_sum(kernel, meta, blocks):
    tall, width = blocks[0].shape[-2:]
    vmem = pl.BlockSpec(memory_space=pltpu.VMEM)
    turned = jax.ShapeDtypeStruct((width // PAIR, tall), f32)
    return pl.pallas_call(
        kernel,
        out_shape=[jax.ShapeDtypeStruct((tall, width), bf16), turned, turned],
        in_specs=[pl.BlockSpec(memory_space=pltpu.SMEM)] + [vmem] * len(blocks),
        out_specs=[vmem] * 3,
        compiler_params=params(24),
        name="level_sum",
    )(meta, *blocks)


def body(orbitals, potential, deriv_blocks, levels, box_counts, neighbours):
    slots, coefficients, own_width = orbitals.shape
    edge = deriv_blocks.shape[1]
    level, pair, orb = lax.axis_index("lvl"), lax.axis_index("pair"), lax.axis_index("orb")
    level_count, orb_count = lax.axis_size("lvl"), lax.axis_size("orb")
    half, fold = own_width // PAIR, coefficients // 2
    all_width = own_width * orb_count
    box_rows = all_width // (level_count * PAIR)
    first = pair == 0
    groups = range(orb_count)
    square_grid = level_count == orb_count == 4 and box_rows == half
    row0, col0 = (level * PAIR + pair) * box_rows, orb * own_width

    pot = jnp.pad(potential, ((0, 0), (0, -coefficients % own_width)))
    own_base = (level * PAIR + pair) * slots
    pack_meta = jnp.stack([pair, box_counts[0], own_base]).astype(jnp.int32)
    theirs, mine = pack(pack_meta, neighbours.reshape(slots, 6), levels, orbitals, pot)
    active = orbitals

    far = {q: swap(active, "orb", q) for q in groups if q and q % 2 == 0}
    beside = swap(theirs, "pair", 1)
    first_mine, second_mine = trade(mine, "lvl", 0), trade(mine, "lvl", 1)
    beside_rest = swap(mine, "pair", 1)
    first_beside, second_beside = trade(beside, "lvl", 0), trade(beside, "lvl", 1)

    matrices = block_matrices(deriv_blocks)

    far, active, parts, beside_rest, matrices = lax.optimization_barrier(
        (
            far,
            active,
            [mine, beside, first_mine, first_beside, second_mine, second_beside],
            beside_rest,
            matrices,
        )
    )
    beside = parts[1]
    facts = jnp.stack([part[:, fold, :8] for part in parts]).astype(f32).astype(jnp.int32)

    flat = lambda block: block.reshape(-1, block.shape[-1])
    cut = -(-slots * coefficients // (2 * ROWS)) * ROWS
    beside_all, beside_top = unfold(pack_meta, beside, beside_rest, fold, cut)
    cross = {q: [swap(beside_top, "orb", q), swap(flat(far[q])[cut:], "pair", 1)] for q in far}
    left_own = {0: active, 1: swap(active, "orb", 1), **far}
    left_beside = {0: [beside_all], 1: [swap(beside_all, "orb", 1)]}
    for q in far:
        left_own[q + 1] = swap(far[q], "orb", 1)

    def natural(blocks):
        return jnp.concatenate([lax.dynamic_index_in_dim(blocks, orb ^ j, keepdims=False) for j in groups], axis=1)

    def along_levels(blocks):
        mine_block = lambda target: lax.dynamic_index_in_dim(blocks, orb ^ target, keepdims=False)
        steps = range(1, level_count)
        return [mine_block(level)] + [swap(mine_block(level ^ step), "lvl", step) for step in steps]

    def both_halves(kept, sent):
        got = swap(sent, "pair", 1)
        return jnp.concatenate([jnp.where(first, kept, got), jnp.where(first, got, kept)], axis=1)

    def own_block(strip):
        strip = lax.all_gather(lax.psum(strip, "lvl"), ("orb", "pair"), axis=0, tiled=True)
        strip = lax.dynamic_slice_in_dim(strip, row0, box_rows, axis=0)
        return lax.dynamic_slice_in_dim(strip, col0, own_width, axis=1)

    live_rows = box_counts[0] * coefficients
    meta = jnp.stack([pair, slots * coefficients, live_rows]).astype(jnp.int32)

    place_meta = jnp.stack([level, pair]).astype(jnp.int32)
    right = kinetic(parts, place_meta, facts, matrices, edge, coefficients, level_count)

    cross, right, meta = lax.optimization_barrier((cross, right, meta))
    lefts_own = [[flat(left_own[q])] for q in groups]
    lefts_beside = dict(left_beside)
    for q in far:
        lefts_beside[q] = list(cross[q])
        lefts_beside[q + 1] = [swap(piece, "orb", 1) for piece in cross[q]]
    lefts_beside = [lefts_beside[q] for q in groups]

    share = 1.0 / level_count
    blocks = box_correlation(share, meta, lefts_own, None, half)
    blocks = box_correlation(share, meta, lefts_beside, blocks, half)
    right = right.reshape(2, slots * coefficients, 3 * half)
    fock_part = box_fock(0, lefts_own, right, None, None)
    if square_grid:
        sent = along_levels(blocks)
        sent, fock_part = lax.optimization_barrier((sent, fock_part))
        small, kept, other = level_sum(offset_sum_kernel, meta, sent)
        offset = both_halves(kept, other)
    else:
        offset = own_block(natural(blocks).astype(f32))
    row_ids = row0 + jnp.arange(box_rows, dtype=jnp.int32)
    col_ids = col0 + jnp.arange(own_width, dtype=jnp.int32)
    correlation = offset + (row_ids[:, None] == col_ids[None, :]).astype(f32)
    apart = (orb ^ level if square_grid else 0 * orb).reshape(1).astype(jnp.int32)
    odd, even = box_fock(1, lefts_beside, right, fock_part, apart)
    if square_grid:
        pieces = [small] + [swap(small, "lvl", z) for z in range(1, level_count)]
        pieces, odd, even, offset = lax.optimization_barrier((pieces, odd, even, offset))
        join = functools.partial(jnp.concatenate, axis=0)
        top, low = join(pieces[: level_count // 2]), join(pieces[level_count // 2 :])
        paired = swap(odd, "lvl", 1)
        got = [swap(top, "pair", 1), swap(low, "orb", 2)]
        got, paired = lax.optimization_barrier((got, paired))
        own_sum, fock_sent = fock_pair(even, paired)
        fock_got = swap(fock_sent, "lvl", 2)
        top, low = join([top, got[0]]), join([low, got[1]])
        pieces = [top, swap(top, "orb", 2), low, swap(low, "pair", 1)]
        pieces += [swap(piece, "orb", 1) for piece in pieces]
        root_meta = jnp.stack([level, pair, orb]).astype(jnp.int32)
        inverse_root = root_of(root_meta, pieces, offset, all_width, level_count)
        share, kept, other = level_sum(fock_sum_kernel, meta, [own_sum, fock_got])
        to = [
            ((z * PAIR + y) * orb_count + o, (o * PAIR + y) * orb_count + z)
            for z in range(level_count)
            for y in range(PAIR)
            for o in groups
        ]
        fock = both_halves(kept, other) + lax.ppermute(share, BOX + ("orb",), to).astype(f32)
    else:
        fock_blocks = jnp.stack([even, odd], axis=1).reshape(orb_count, 3, half, own_width)
        main = natural(fock_blocks[:, 0]).astype(f32) + natural(fock_blocks[:, 1]).astype(f32)
        main = lax.all_gather(lax.psum(main, "lvl"), "pair", axis=0, tiled=True)
        fock = lax.dynamic_slice_in_dim(main, row0, box_rows, axis=1).T + own_block(natural(fock_blocks[:, 2]).astype(f32))
        gathered = lax.all_gather(offset.astype(bf16), "orb", axis=1, tiled=True)
        whole = lax.all_gather(gathered, BOX, axis=0, tiled=True)
        rows_of = lax.dynamic_slice_in_dim(whole, row0, box_rows, axis=0)
        cols_of = lax.dynamic_slice_in_dim(whole, col0, own_width, axis=1)
        row_square, col_square = matmul(rows_of, whole), matmul(whole, cols_of)
        left = (rows_of.astype(f32) - 0.25 * row_square).astype(bf16)
        right_side = (0.25 * (cols_of.astype(f32) - col_square)).astype(bf16)
        own_square = lax.dynamic_slice_in_dim(row_square, col0, own_width, axis=1)
        inverse_root = correlation - 1.5 * offset + 0.125 * own_square + matmul(left, right_side)
    return fock, correlation, inverse_root


def solution(mesh):
    levels = mesh.shape["box"] // PAIR
    split = Mesh(mesh.devices.reshape(levels, PAIR, mesh.shape["orb"]), ("lvl", "pair", "orb"))
    in_specs = (P(BOX, None, "orb"), P(BOX, None), P(), P(BOX), P(BOX), P(BOX, None, None))
    out_specs = (P(BOX, "orb"),) * 3
    return jax.shard_map(body, mesh=split, in_specs=in_specs, out_specs=out_specs, check_vma=False)
```

```python
import functools

import jax
import jax.numpy as jnp
import numpy as np
from jax import lax
from jax.experimental import pallas as pl
from jax.experimental.pallas import tpu as pltpu
from jax.sharding import Mesh, PartitionSpec as P

PAIR = 2
ROWS = 16
BOX = ("lvl", "pair")
f32, bf16 = jnp.float32, jnp.bfloat16


def swap(value, axis, bit):
    count = lax.axis_size(axis)
    return lax.ppermute(value, axis, [(i, i ^ bit) for i in range(count)])


def trade(value, axis, start):
    pairs = [(i, i + 1) for i in range(start, lax.axis_size(axis) - 1, 2)]
    return lax.ppermute(value, axis, pairs + [(b, a) for a, b in pairs])


def matmul(left, right):
    return jnp.dot(left, right, preferred_element_type=f32)


def params(mebibytes):
    return pltpu.CompilerParams(vmem_limit_bytes=mebibytes * 1024 * 1024)


def pack_kernel(meta, neighbours, levels, orbitals, pot, theirs, mine):
    slots, coefficients, width = orbitals.shape
    half, fold = width // PAIR, coefficients // 2
    first = meta[0] == 0
    place = lax.broadcasted_iota(jnp.int32, (8, width), 1)
    for slot in range(slots):
        keep = slot < meta[1]
        for part in range(2):
            here = orbitals[slot, part * fold : (part + 1) * fold, :]
            here = jnp.where(keep, here, jnp.zeros_like(here))
            low, high = here[:, :half], here[:, half:]
            lanes = slice(part * half, (part + 1) * half)
            theirs[slot, :fold, lanes] = jnp.where(first, high, low)
            mine[slot, :fold, lanes] = jnp.where(first, low, high)
        own_id = meta[2] + slot
        facts = jnp.where(place == 6, levels[slot], jnp.where(place == 7, jnp.where(keep, 1, 0), 0))
        for c in range(6):
            target = neighbours[slot, c]
            facts = jnp.where(place == c, jnp.where(target >= 0, target - own_id, 16 * slots), facts)
        facts = facts.astype(f32).astype(bf16)
        for packed in (theirs, mine):
            packed[slot, fold : fold + 8, :] = facts
        row = fold + 8
        for start in range(0, pot.shape[1], width):
            exact = pot[slot : slot + 1, start : start + width]
            for _ in range(3):
                part = exact.astype(bf16)
                exact = exact - part.astype(f32)
                for packed in (theirs, mine):
                    packed[slot, row : row + 1, :] = part
                row += 1
        for packed in (theirs, mine):
            packed[slot, row:, :] = jnp.zeros((packed.shape[1] - row, width), bf16)


def pack(meta, neighbours, levels, orbitals, pot):
    slots, coefficients, width = orbitals.shape
    fold = coefficients // 2
    padded = -(-(fold + 8 + 3 * (pot.shape[1] // width)) // ROWS) * ROWS
    vmem, smem = pl.BlockSpec(memory_space=pltpu.VMEM), pl.BlockSpec(memory_space=pltpu.SMEM)
    return pl.pallas_call(
        pack_kernel,
        out_shape=[jax.ShapeDtypeStruct((slots, padded, width), bf16)] * 2,
        in_specs=[smem, smem, smem, vmem, vmem],
        out_specs=[vmem, vmem],
        compiler_params=params(24),
        name="pack",
    )(meta, neighbours, levels, orbitals, pot)


def unfold_kernel(fold, meta, beside_in, rest_in, whole, top, beside, rest, sems):
    copies = [
        pltpu.make_async_copy(source, target, sems.at[i])
        for i, (source, target) in enumerate(((beside_in, beside), (rest_in, rest)))
    ]
    for copy in copies:
        copy.start()
    slots, _, width = beside.shape
    half = width // PAIR
    first = meta[0] == 0
    for copy in copies:
        copy.wait()
    for slot in range(slots):
        for part in range(2):
            lanes = slice(part * half, (part + 1) * half)
            near, far = beside[slot, :fold, lanes], rest[slot, :fold, lanes]
            start = (2 * slot + part) * fold
            here = jnp.concatenate([jnp.where(first, near, far), jnp.where(first, far, near)], axis=1)
            whole[start : start + fold, :] = here
    top[...] = whole[: top.shape[0], :]


def unfold(meta, beside, rest, fold, cut):
    slots, _, width = beside.shape
    vmem = pl.BlockSpec(memory_space=pltpu.VMEM)
    return pl.pallas_call(
        functools.partial(unfold_kernel, fold),
        out_shape=[
            jax.ShapeDtypeStruct((2 * slots * fold, width), bf16),
            jax.ShapeDtypeStruct((cut, width), bf16),
        ],
        in_specs=[pl.BlockSpec(memory_space=pltpu.SMEM)] + [pl.BlockSpec(memory_space=pl.ANY)] * 2,
        out_specs=[vmem, vmem],
        scratch_shapes=[
            pltpu.VMEM(beside.shape, bf16),
            pltpu.VMEM(beside.shape, bf16),
            pltpu.SemaphoreType.DMA((2,)),
        ],
        compiler_params=params(24),
        name="unfold",
    )(meta, beside, rest)


def load_left(lefts, held, sems):
    copies = []
    for q, pieces in enumerate(lefts):
        row = 0
        for piece in pieces:
            rows, width = piece.shape
            here = held.at[row : row + rows, q * width : (q + 1) * width]
            copies.append(pltpu.make_async_copy(piece, here, sems.at[len(copies)]))
            row += rows
    for copy in copies:
        copy.start()
    return copies


def grouped(refs, counts):
    refs = list(refs)
    return [[refs.pop(0) for _ in range(count)] for count in counts]


def correlation_kernel(share, counts, meta, *refs):
    refs, (out, held, turned, sems) = refs[:-4], refs[-4:]
    groups, half, width = out.shape
    lefts, before = grouped(refs, counts), refs[sum(counts) :]
    copies = load_left(lefts, held, sems)
    first = meta[0] == 0
    for copy in copies[: counts[0]]:
        copy.wait()
    own = held[:, :width]
    own = jnp.where(first, own[:, :half], own[:, half:]).T
    live = lax.broadcasted_iota(jnp.int32, own.shape, 1) < meta[1 if before else 2]
    turned[...] = jnp.where(live, own, jnp.zeros_like(own))
    for base in range(0, groups, 2):
        for copy in copies[max(sum(counts[:base]), counts[0]) : sum(counts[: base + 2])]:
            copy.wait()
        wide = matmul(turned[...], held[:, base * width : (base + 2) * width])
        for q in (base, base + 1):
            total = wide[:, (q - base) * width : (q - base + 1) * width]
            if before:
                total = total + before[0][q]
                if q == 0:
                    rows = lax.broadcasted_iota(jnp.int32, (half, width), 0) + jnp.where(first, 0, half)
                    columns = lax.broadcasted_iota(jnp.int32, (half, width), 1)
                    total = total - jnp.where(rows == columns, share, 0.0)
            out[q] = total.astype(out.dtype)


def box_correlation(share, meta, lefts, before, half):
    depth, width = sum(piece.shape[0] for piece in lefts[0]), lefts[0][0].shape[1]
    counts = [len(pieces) for pieces in lefts]
    vmem = pl.BlockSpec(memory_space=pltpu.VMEM)
    extra = [] if before is None else [before]
    return pl.pallas_call(
        functools.partial(correlation_kernel, share, counts),
        out_shape=jax.ShapeDtypeStruct((len(lefts), half, width), f32 if before is None else bf16),
        in_specs=[pl.BlockSpec(memory_space=pltpu.SMEM)]
        + [pl.BlockSpec(memory_space=pl.ANY)] * sum(counts)
        + [vmem] * len(extra),
        out_specs=vmem,
        scratch_shapes=[
            pltpu.VMEM((depth, len(lefts) * width), bf16),
            pltpu.VMEM((half, depth), bf16),
            pltpu.SemaphoreType.DMA((sum(counts),)),
        ],
        compiler_params=params(32),
        cost_estimate=pl.CostEstimate(
            flops=2 * len(lefts) * depth * width * half, bytes_accessed=2 * len(lefts) * depth * width, transcendentals=0
        ),
        name="correlation",
    )(meta, *[piece for pieces in lefts for piece in pieces], *extra)


def fock_kernel(side, counts, right, *refs):
    outs, (held, raw, turned, sems, last_sem) = refs[sum(counts) : -5], refs[-5:]
    lefts = grouped(refs, counts)
    before, apart, outs = (None, None, outs) if len(outs) == 1 else (outs[0], outs[1], outs[2:])
    out = outs[0]
    last = pltpu.make_async_copy(right.at[side], raw, last_sem)
    last.start()
    copies = load_left(lefts, held, sems)
    half, width = out.shape[-2] // (3 if before is None else 1), out.shape[-1]
    last.wait()
    turned[...] = raw[...].T
    for base in range(0, len(lefts), 2):
        for copy in copies[sum(counts[:base]) : sum(counts[: base + 2])]:
            copy.wait()
        wide = matmul(turned[...], held[:, base * width : (base + 2) * width])
        for q in (base, base + 1):
            total = wide[:, (q - base) * width : (q - base + 1) * width]
            if before is None:
                out[q] = total
                continue
            total = total + before[q]
            main = total[:half] + total[half : 2 * half]
            top = main.astype(bf16)
            parts = (top, (main - top.astype(f32)).astype(bf16), total[2 * half :].astype(bf16))

            def store(target):
                for i in range(3):
                    target[i] = parts[i]

            for distance, target in enumerate(outs):
                pl.when(q ^ apart[0] == distance)(functools.partial(store, target))


def box_fock(side, lefts, right, before, apart):
    depth, width = sum(piece.shape[0] for piece in lefts[0]), lefts[0][0].shape[1]
    counts = [len(pieces) for pieces in lefts]
    tall = right.shape[-1]
    anywhere, vmem = pl.BlockSpec(memory_space=pl.ANY), pl.BlockSpec(memory_space=pltpu.VMEM)
    extra = [] if before is None else [before, apart]
    out = jax.ShapeDtypeStruct((len(lefts), tall, width), f32)
    if before is not None:
        out = [jax.ShapeDtypeStruct((3, tall // 3, width), bf16)] * len(lefts)
    return pl.pallas_call(
        functools.partial(fock_kernel, side, counts),
        out_shape=out,
        in_specs=[anywhere] * (sum(counts) + 1) + [vmem, pl.BlockSpec(memory_space=pltpu.SMEM)][: len(extra)],
        out_specs=vmem if before is None else [vmem] * len(lefts),
        scratch_shapes=[
            pltpu.VMEM((depth, len(lefts) * width), bf16),
            pltpu.VMEM(right.shape[1:], bf16),
            pltpu.VMEM((tall, depth), bf16),
            pltpu.SemaphoreType.DMA((sum(counts),)),
            pltpu.SemaphoreType.DMA(()),
        ],
        compiler_params=params(40),
        cost_estimate=pl.CostEstimate(
            flops=2 * len(lefts) * depth * width * tall, bytes_accessed=2 * len(lefts) * depth * width, transcendentals=0
        ),
        name="fock",
    )(right, *[piece for pieces in lefts for piece in pieces], *extra)


def root_kernel(levels, meta, *refs):
    pieces, (offset, root, whole, rows_f, cols_b, sems) = refs[:-6], refs[-6:]
    level, pair, orb = meta[0], meta[1], meta[2]
    coarse, width = offset.shape
    side = whole.shape[0]
    groups = side // width
    copies = []
    for piece, (z, y, q) in zip(pieces, piece_places(levels, groups)):
        for i in range(len(z)):
            start = ((orb ^ q[i]) * PAIR + (pair ^ y[i])) * coarse
            rows = pl.ds(pl.multiple_of(start, coarse), coarse)
            lanes = pl.ds(pl.multiple_of((level ^ z[i]) * width, width), width)
            copies.append(
                pltpu.make_async_copy(
                    piece.at[i * coarse : (i + 1) * coarse], whole.at[rows, lanes], sems.at[len(copies)]
                )
            )
    for copy in copies:
        copy.start()
    for copy in copies:
        copy.wait()
    row0 = pl.multiple_of((level * PAIR + pair) * coarse, coarse)
    own_lanes = pl.ds(pl.multiple_of(orb * width, width), width)
    rows = whole[pl.ds(row0, coarse), :]

    def across(j, carry):
        lanes = pl.ds(pl.multiple_of(j * width, width), width)
        rows_f[:, lanes] = matmul(rows, whole[:, lanes])
        return carry

    lax.fori_loop(0, groups, across, 0)
    columns = whole[:, own_lanes]

    def down(i, carry):
        here = pl.ds(pl.multiple_of(i * coarse, coarse), coarse)
        square = matmul(whole[here, :], columns)
        cols_b[here, :] = (0.25 * (whole[here, own_lanes].astype(f32) - square)).astype(bf16)
        return carry

    lax.fori_loop(0, side // coarse, down, 0)
    left = (rows.astype(f32) - 0.25 * rows_f[...]).astype(bf16)
    value = matmul(left, cols_b[...]) + 0.125 * rows_f[:, own_lanes] - 0.5 * offset[...]
    row_ids = lax.broadcasted_iota(jnp.int32, value.shape, 0) + row0
    col_ids = lax.broadcasted_iota(jnp.int32, value.shape, 1) + orb * width
    root[...] = value + jnp.where(row_ids == col_ids, 1.0, 0.0)


def piece_places(levels, groups):
    places = []
    for core in (0, 1):
        for half in range(2):
            low = [half * levels // 2 + z for z in range(levels // 2)]
            for second in (0, 1):
                z, y, q = [], [], []
                for inner in (0, 1):
                    z += low
                    y += [second if half else inner] * len(low)
                    q += [2 * (inner if half else second) + core] * len(low)
                places.append((z, y, q))
    return places


def root_of(meta, pieces, offset, side, levels):
    coarse, width = offset.shape
    vmem, anywhere = pl.BlockSpec(memory_space=pltpu.VMEM), pl.BlockSpec(memory_space=pl.ANY)
    return pl.pallas_call(
        functools.partial(root_kernel, levels),
        out_shape=jax.ShapeDtypeStruct(offset.shape, f32),
        in_specs=[pl.BlockSpec(memory_space=pltpu.SMEM)] + [anywhere] * len(pieces) + [vmem],
        out_specs=vmem,
        scratch_shapes=[
            pltpu.VMEM((side, side), bf16),
            pltpu.VMEM((coarse, side), f32),
            pltpu.VMEM((side, width), bf16),
            pltpu.SemaphoreType.DMA((side // coarse * (side // width),)),
        ],
        compiler_params=params(40),
        cost_estimate=pl.CostEstimate(flops=16 * side * side * width, bytes_accessed=4 * side * side, transcendentals=0),
        name="root",
    )(meta, *pieces, offset)


def fill_tables(slots, levels, place_meta, facts, table, scale):
    level, pair = place_meta[0], place_meta[1]
    even = lax.rem(level, 2) == 0
    none = 6 * slots

    def place(slot_id):
        box = lax.div(slot_id, slots)
        apart = lax.div(box, PAIR) - level
        base = jnp.where(apart == 0, 0, jnp.where((apart < 0) == even, 4, 2))
        return (base + jnp.where(lax.rem(box, PAIR) != pair, 1, 0)) * slots + lax.rem(slot_id, slots)

    for index in range(4 * slots):
        group, r = divmod(index, slots)

        def fact(c):
            if group < 2:
                return facts[group, r, c]
            swap_id = jnp.where(even, 1, 0) if group == 2 else jnp.where(even, 0, 1)
            near_pair = 1 if group == 2 else 0
            return facts[2 + swap_id + jnp.where(pair == near_pair, 0, 2), r, c]

        box = (
            level * PAIR + pair,
            level * PAIR + 1 - pair,
            jnp.maximum(level * PAIR - 1, 0),
            jnp.minimum((level + 1) * PAIR, levels * PAIR - 1),
        )[group]
        there = (True, True, level > 0, level < levels - 1)[group]
        own_id = box * slots + r
        own_place = place(own_id)
        table[index, 0] = jnp.where((fact(7) > 0) & there, own_place, -1)
        for a in range(3):
            for k in (0, 2):
                distance = fact(2 * a + k // 2)
                target = place(jnp.maximum(own_id + distance, 0))
                target = jnp.where(distance < 16 * slots, target, none)
                table[index, 1 + 3 * a + k] = jnp.clip(target, 0, none)
            table[index, 2 + 3 * a] = own_place
        level_of = fact(6)
        scale[index] = jnp.where(level_of == 0, 0.5, jnp.where(level_of == 1, 1.0, 2.0))


def kinetic_kernel(edge, slots, levels, place_meta, facts, *refs):
    parts, refs = refs[:6], refs[6:]
    (fwd_in, fwd_out, back_in, back_mid, back_out), out, refs = refs[:5], refs[5], refs[6:]
    raw, x, outer, inner, total, total_fix, lines, columns, table, scale, sems = refs
    square = edge * edge
    own = PAIR * slots
    padded, width = x.shape[2:]
    copies = [pltpu.make_async_copy(part, raw.at[place], sems.at[place]) for place, part in enumerate(parts)]
    for copy in copies:
        copy.start()
    tail = padded - ROWS
    x[:, :, tail:, :] = jnp.zeros((x.shape[0], edge, ROWS, width), bf16)
    x[6 * slots] = jnp.zeros((edge, padded, width), bf16)
    total[...] = jnp.zeros_like(total)
    total_fix[...] = jnp.zeros_like(total_fix)
    fill_tables(slots, levels, place_meta, facts, table, scale)
    lines[...] = jnp.zeros_like(lines)
    for copy in copies:
        copy.wait()
    lanes = raw.shape[3]
    for t in range(own):
        for start in range(0, lines.shape[1], lanes):
            row = edge * square // 2 + 8 + 3 * (start // lanes)
            high, middle, low = (
                raw[t // slots, t % slots, row + i : row + i + 1, :].astype(f32) for i in range(3)
            )
            lines[t : t + 1, start : start + lanes] = (high + middle) + low
    columns[...] = lines[...].T

    def lay_out(place, carry):
        for slot in range(slots):
            for i in range(edge):
                part, row = i // (edge // 2), i % (edge // 2) * square
                x[place * slots + slot, i, :square, :] = raw[
                    place, slot, row : row + square, part * width : (part + 1) * width
                ]
        return carry

    lax.fori_loop(0, len(parts), lay_out, 0)
    chunks = -(-square // ROWS)

    def per_slot(s, carry):
        @pl.when(table[s, 0] >= 0)
        def _():
            own_scale = scale[s]
            half = 0.5 * own_scale
            sums = (total, total_fix)

            def split(exact):
                exact = own_scale * exact
                value = exact.astype(bf16).astype(f32)
                return (half * value).astype(bf16), (half * (value - exact)).astype(bf16)

            sources = [[table[s, 1 + 3 * a + k] for k in range(3)] for a in range(3)]
            here = sources[0][1]
            for a in range(3):

                @pl.when((here < own) | (sources[a][0] < own) | (sources[a][2] < own))
                def _():
                    if a == 0:
                        for i in range(chunks):
                            rows = slice(i * ROWS, (i + 1) * ROWS)
                            block = [x[t, :, rows, :].reshape(edge * ROWS, width) for t in sources[0]]
                            fields = split(matmul(fwd_out[...], jnp.concatenate(block, axis=0)))
                            for field in range(2):
                                outer[field, :, rows, :] = fields[field].reshape(edge, ROWS, width)
                    else:
                        for i in range(edge):
                            block = jnp.concatenate([x[t, i] for t in sources[a]], axis=0)
                            fields = split(matmul(fwd_in[a - 1], block))
                            for field in range(2):
                                inner[field, i, (a - 1) * padded : a * padded, :] = fields[field]

            def back_outer(k, target):
                for i in range(chunks):
                    rows = slice(i * ROWS, (i + 1) * ROWS)
                    for field in range(2):
                        term = matmul(back_out[k], outer[field, :, rows, :].reshape(edge * ROWS, width))
                        sums[field][target, :, rows, :] += term.reshape(edge, ROWS, width)

            for k in (0, 2):
                for a in range(3):
                    target = sources[a][k]

                    @pl.when(target < own)
                    def _():
                        if a == 0:
                            back_outer(k, target)
                        else:
                            for i in range(edge):
                                for field in range(2):
                                    here = inner[field, i, (a - 1) * padded : a * padded, :]
                                    sums[field][target, i] += matmul(back_in[a - 1, k], here)

            @pl.when(here < own)
            def _():
                back_outer(1, here)
                for i in range(edge):
                    for field in range(2):
                        sums[field][here, i] += matmul(back_mid[...], inner[field, i])

        return carry

    lax.fori_loop(0, table.shape[0], per_slot, 0)

    for t in range(own):
        for i in range(edge):
            rows = slice(i * square, (i + 1) * square)
            weighted = (columns[rows, t : t + 1] * x[t, i, :square, :].astype(f32)).astype(bf16)
            whole = total[t, i, :square, :] + weighted.astype(f32)
            top = whole.astype(bf16)
            low = (whole - top.astype(f32)).astype(bf16)
            fix = total_fix[t, i, :square, :].astype(bf16)
            out[t, rows, :] = jnp.concatenate([top, low, fix], axis=1)


def matrices_kernel(stacked, blocks, *refs):
    spots, outs = refs[:9], refs[9:]
    fwd_in, fwd_out, back_in, back_mid, back_out = outs
    for mode in range(3):
        spot, spread, same = spots[3 * mode : 3 * mode + 3]
        wide = matmul(matmul(spot[...], stacked[...]).astype(bf16), spread[...])
        wide = (wide * jnp.concatenate([same[...]] * 3, axis=1)).astype(bf16)
        if mode == 2:
            fwd_out[...] = wide
        else:
            fwd_in[mode] = wide
        for k in range(3):
            turned = lax.dot_general(spot[...], blocks[k], (((1,), (1,)), ((), ())), preferred_element_type=f32)
            turned = lax.dot_general(
                turned.astype(bf16), spot[...], (((1,), (1,)), ((), ())), preferred_element_type=f32
            )
            turned = (turned * same[...]).astype(bf16)
            if mode == 2:
                back_out[k] = turned
            else:
                back_in[mode, k] = turned
    back_mid[...] = jnp.concatenate([back_in[0, 1], back_in[1, 1]], axis=1)


def block_matrices(deriv_blocks):
    edge = deriv_blocks.shape[1]
    square = edge * edge
    padded = -(-square // ROWS) * ROWS
    tall = edge * ROWS
    ids = np.arange(padded)
    slow = ((ids[:, None] // edge) == np.arange(edge)).astype(np.float32)
    fast = (((ids[:, None] % edge) == np.arange(edge)) & (ids[:, None] < square)).astype(np.float32)
    ids = np.arange(tall)
    outer = ((ids[:, None] // ROWS) == np.arange(edge)).astype(np.float32)
    within = ((ids[:, None] % ROWS) == np.arange(ROWS)).astype(np.float32)
    stacked = jnp.moveaxis(deriv_blocks, 0, 1).reshape(edge, 3 * edge)
    constants = []
    for spot, mask in ((slow, fast), (fast, slow), (outer, within)):
        spread = np.kron(np.eye(3, dtype=np.float32), spot.T)
        constants += [jnp.asarray(spot, bf16), jnp.asarray(spread, bf16), jnp.asarray(mask @ mask.T, f32)]
    vmem = pl.BlockSpec(memory_space=pltpu.VMEM)
    shapes = [(2, padded, 3 * padded), (tall, 3 * tall), (2, 3, padded, padded), (padded, 2 * padded), (3, tall, tall)]
    return pl.pallas_call(
        matrices_kernel,
        out_shape=[jax.ShapeDtypeStruct(shape, bf16) for shape in shapes],
        in_specs=[vmem] * 11,
        out_specs=[vmem] * 5,
        compiler_params=params(24),
        name="matrices",
    )(stacked, deriv_blocks, *constants)


def kinetic(parts, place_meta, facts, matrices, edge, coefficients, levels):
    slots, folded, lanes = parts[0].shape
    width = lanes // 2
    padded = matrices[0].shape[1]
    own = PAIR * slots
    vmem = pl.BlockSpec(memory_space=pltpu.VMEM)
    smem = pl.BlockSpec(memory_space=pltpu.SMEM)
    anywhere = pl.BlockSpec(memory_space=pl.ANY)
    return pl.pallas_call(
        functools.partial(kinetic_kernel, edge, slots, levels),
        out_shape=jax.ShapeDtypeStruct((own, coefficients, 3 * width), bf16),
        in_specs=[smem] * 2 + [anywhere] * 6 + [vmem] * 5,
        out_specs=vmem,
        scratch_shapes=[
            pltpu.VMEM((6, slots, folded, lanes), bf16),
            pltpu.VMEM((6 * slots + 1, edge, padded, width), bf16),
            pltpu.VMEM((2, edge, padded, width), bf16),
            pltpu.VMEM((2, edge, 2 * padded, width), bf16),
            pltpu.VMEM((own, edge, padded, width), f32),
            pltpu.VMEM((own, edge, padded, width), f32),
            pltpu.VMEM((own + -own % 8, coefficients + -coefficients % lanes), f32),
            pltpu.VMEM((coefficients + -coefficients % lanes, own + -own % 8), f32),
            pltpu.SMEM((4 * slots, 10), jnp.int32),
            pltpu.SMEM((4 * slots,), f32),
            pltpu.SemaphoreType.DMA((6,)),
        ],
        compiler_params=params(48),
        cost_estimate=pl.CostEstimate(flops=2 * 10**10, bytes_accessed=40 * 10**6, transcendentals=0),
        name="kinetic",
    )(place_meta, facts, *parts, *matrices)


def offset_sum_kernel(meta, *refs):
    blocks, (small, kept, sent) = refs[:-3], refs[-3:]
    total = blocks[0][...].astype(f32)
    for block in blocks[1:]:
        total = total + block[...].astype(f32)
    small[...] = total.astype(bf16)
    half = kept.shape[0]
    first = meta[0] == 0
    low, high = total[:, :half].T, total[:, half:].T
    kept[...] = jnp.where(first, low, high)
    sent[...] = jnp.where(first, high, low)


def fock_sum_kernel(meta, *refs):
    blocks, (share, kept, sent) = refs[:-3], refs[-3:]
    sums = [sum((block[part].astype(f32) for block in blocks[1:]), blocks[0][part].astype(f32)) for part in range(3)]
    main = sums[0] + sums[1]
    share[...] = sums[2].astype(bf16)
    half = kept.shape[0]
    first = meta[0] == 0
    low, high = main[:, :half].T, main[:, half:].T
    kept[...] = jnp.where(first, low, high)
    sent[...] = jnp.where(first, high, low)


def level_sum(kernel, meta, blocks):
    tall, width = blocks[0].shape[-2:]
    vmem = pl.BlockSpec(memory_space=pltpu.VMEM)
    turned = jax.ShapeDtypeStruct((width // PAIR, tall), f32)
    return pl.pallas_call(
        kernel,
        out_shape=[jax.ShapeDtypeStruct((tall, width), bf16), turned, turned],
        in_specs=[pl.BlockSpec(memory_space=pltpu.SMEM)] + [vmem] * len(blocks),
        out_specs=[vmem] * 3,
        compiler_params=params(24),
        name="level_sum",
    )(meta, *blocks)


def body(orbitals, potential, deriv_blocks, levels, box_counts, neighbours):
    slots, coefficients, own_width = orbitals.shape
    edge = deriv_blocks.shape[1]
    level, pair, orb = lax.axis_index("lvl"), lax.axis_index("pair"), lax.axis_index("orb")
    level_count, orb_count = lax.axis_size("lvl"), lax.axis_size("orb")
    half, fold = own_width // PAIR, coefficients // 2
    all_width = own_width * orb_count
    box_rows = all_width // (level_count * PAIR)
    first = pair == 0
    groups = range(orb_count)
    square_grid = level_count == orb_count == 4 and box_rows == half
    row0, col0 = (level * PAIR + pair) * box_rows, orb * own_width

    pot = jnp.pad(potential, ((0, 0), (0, -coefficients % own_width)))
    own_base = (level * PAIR + pair) * slots
    pack_meta = jnp.stack([pair, box_counts[0], own_base]).astype(jnp.int32)
    theirs, mine = pack(pack_meta, neighbours.reshape(slots, 6), levels, orbitals, pot)
    active = orbitals

    far = {q: swap(active, "orb", q) for q in groups if q and q % 2 == 0}
    beside = swap(theirs, "pair", 1)
    first_mine, second_mine = trade(mine, "lvl", 0), trade(mine, "lvl", 1)
    beside_rest = swap(mine, "pair", 1)
    first_beside, second_beside = trade(beside, "lvl", 0), trade(beside, "lvl", 1)

    matrices = block_matrices(deriv_blocks)

    def facts_of(parts):
        return jnp.stack([part[:, fold, :8] for part in parts]).astype(f32).astype(jnp.int32)

    early_facts = facts_of([mine, beside, first_mine, second_mine])
    flat = lambda block: block.reshape(-1, block.shape[-1])
    cut = -(-slots * coefficients // (2 * ROWS)) * ROWS
    beside_all, beside_top = unfold(pack_meta, beside, beside_rest, fold, cut)

    parts = [mine, beside, first_mine, first_beside, second_mine, second_beside]
    far, active, parts, beside_all, beside_top, matrices, early_facts = lax.optimization_barrier(
        (far, active, parts, beside_all, beside_top, matrices, early_facts)
    )
    facts = jnp.concatenate([early_facts, facts_of([parts[3], parts[5]])])
    cross = {q: [swap(beside_top, "orb", q), swap(flat(far[q])[cut:], "pair", 1)] for q in far}
    left_own = {0: active, 1: swap(active, "orb", 1), **far}
    left_beside = {0: [beside_all], 1: [swap(beside_all, "orb", 1)]}
    for q in far:
        left_own[q + 1] = swap(far[q], "orb", 1)

    def natural(blocks):
        return jnp.concatenate([lax.dynamic_index_in_dim(blocks, orb ^ j, keepdims=False) for j in groups], axis=1)

    def along_levels(blocks):
        mine_block = lambda target: lax.dynamic_index_in_dim(blocks, orb ^ target, keepdims=False)
        steps = range(1, level_count)
        return [mine_block(level)] + [swap(mine_block(level ^ step), "lvl", step) for step in steps]

    def both_halves(kept, got):
        return jnp.concatenate([jnp.where(first, kept, got), jnp.where(first, got, kept)], axis=1)

    def own_block(strip):
        strip = lax.all_gather(lax.psum(strip, "lvl"), ("orb", "pair"), axis=0, tiled=True)
        strip = lax.dynamic_slice_in_dim(strip, row0, box_rows, axis=0)
        return lax.dynamic_slice_in_dim(strip, col0, own_width, axis=1)

    live_rows = box_counts[0] * coefficients
    meta = jnp.stack([pair, slots * coefficients, live_rows]).astype(jnp.int32)

    place_meta = jnp.stack([level, pair]).astype(jnp.int32)
    right = kinetic(parts, place_meta, facts, matrices, edge, coefficients, level_count)

    cross, right, meta = lax.optimization_barrier((cross, right, meta))
    lefts_own = [[flat(left_own[q])] for q in groups]
    lefts_beside = dict(left_beside)
    for q in far:
        lefts_beside[q] = list(cross[q])
        lefts_beside[q + 1] = [swap(piece, "orb", 1) for piece in cross[q]]
    lefts_beside = [lefts_beside[q] for q in groups]

    share = 1.0 / level_count
    blocks = box_correlation(share, meta, lefts_own, None, half)
    blocks = box_correlation(share, meta, lefts_beside, blocks, half)
    right = right.reshape(2, slots * coefficients, 3 * half)
    fock_part = box_fock(0, lefts_own, right, None, None)
    if square_grid:
        sent = along_levels(blocks)
        sent, fock_part = lax.optimization_barrier((sent, fock_part))
        small, kept, other = level_sum(offset_sum_kernel, meta, sent)
        offset = both_halves(kept, swap(other, "pair", 1))
    else:
        offset = own_block(natural(blocks).astype(f32))
    row_ids = row0 + jnp.arange(box_rows, dtype=jnp.int32)
    col_ids = col0 + jnp.arange(own_width, dtype=jnp.int32)
    correlation = offset + (row_ids[:, None] == col_ids[None, :]).astype(f32)
    apart = (orb ^ level if square_grid else 0 * orb).reshape(1).astype(jnp.int32)
    fock_blocks = box_fock(1, lefts_beside, right, fock_part, apart)
    if square_grid:
        pieces = [small] + [swap(small, "lvl", z) for z in range(1, level_count)]
        pieces, fock_blocks, offset = lax.optimization_barrier((pieces, fock_blocks, offset))
        join = functools.partial(jnp.concatenate, axis=0)
        top, low = join(pieces[: level_count // 2]), join(pieces[level_count // 2 :])
        sent = [fock_blocks[0]] + [swap(fock_blocks[step], "lvl", step) for step in range(1, level_count)]
        got = [swap(top, "pair", 1), swap(low, "orb", 2)]
        got, sent[2] = lax.optimization_barrier((got, sent[2]))
        top, low = join([top, got[0]]), join([low, got[1]])
        pieces = [top, swap(top, "orb", 2), low, swap(low, "pair", 1)]
        pieces, sent = lax.optimization_barrier((pieces, sent))
        pieces += [swap(piece, "orb", 1) for piece in pieces]
        root_meta = jnp.stack([level, pair, orb]).astype(jnp.int32)
        inverse_root = root_of(root_meta, pieces, offset, all_width, level_count)
        share, kept, other = level_sum(fock_sum_kernel, meta, sent)
        to = [
            ((z * PAIR + y) * orb_count + o, (o * PAIR + y) * orb_count + z)
            for z in range(level_count)
            for y in range(PAIR)
            for o in groups
        ]
        got = swap(other, "pair", 1), lax.ppermute(share, BOX + ("orb",), to)
        inverse_root, got = lax.optimization_barrier((inverse_root, got))
        fock = both_halves(kept, got[0]) + got[1].astype(f32)
    else:
        fock_blocks = jnp.stack(fock_blocks)
        main = natural(fock_blocks[:, 0]).astype(f32) + natural(fock_blocks[:, 1]).astype(f32)
        main = lax.all_gather(lax.psum(main, "lvl"), "pair", axis=0, tiled=True)
        fock = lax.dynamic_slice_in_dim(main, row0, box_rows, axis=1).T + own_block(natural(fock_blocks[:, 2]).astype(f32))
        gathered = lax.all_gather(offset.astype(bf16), "orb", axis=1, tiled=True)
        whole = lax.all_gather(gathered, BOX, axis=0, tiled=True)
        rows_of = lax.dynamic_slice_in_dim(whole, row0, box_rows, axis=0)
        cols_of = lax.dynamic_slice_in_dim(whole, col0, own_width, axis=1)
        row_square, col_square = matmul(rows_of, whole), matmul(whole, cols_of)
        left = (rows_of.astype(f32) - 0.25 * row_square).astype(bf16)
        right_side = (0.25 * (cols_of.astype(f32) - col_square)).astype(bf16)
        own_square = lax.dynamic_slice_in_dim(row_square, col0, own_width, axis=1)
        inverse_root = correlation - 1.5 * offset + 0.125 * own_square + matmul(left, right_side)
    return fock, correlation, inverse_root


def solution(mesh):
    levels = mesh.shape["box"] // PAIR
    split = Mesh(mesh.devices.reshape(levels, PAIR, mesh.shape["orb"]), ("lvl", "pair", "orb"))
    in_specs = (P(BOX, None, "orb"), P(BOX, None), P(), P(BOX), P(BOX), P(BOX, None, None))
    out_specs = (P(BOX, "orb"),) * 3
    return jax.shard_map(body, mesh=split, in_specs=in_specs, out_specs=out_specs, check_vma=False)
```

```python
import functools

import jax
import jax.numpy as jnp
import numpy as np
from jax import lax
from jax.experimental import pallas as pl
from jax.experimental.pallas import tpu as pltpu
from jax.sharding import Mesh, PartitionSpec as P

PAIR = 2
ROWS = 16
BOX = ("lvl", "pair")
f32, bf16 = jnp.float32, jnp.bfloat16


def swap(value, axis, bit):
    count = lax.axis_size(axis)
    return lax.ppermute(value, axis, [(i, i ^ bit) for i in range(count)])


def trade(value, axis, start):
    pairs = [(i, i + 1) for i in range(start, lax.axis_size(axis) - 1, 2)]
    return lax.ppermute(value, axis, pairs + [(b, a) for a, b in pairs])


def matmul(left, right):
    return jnp.dot(left, right, preferred_element_type=f32)


def params(mebibytes):
    return pltpu.CompilerParams(vmem_limit_bytes=mebibytes * 1024 * 1024)


def pack_kernel(meta, neighbours, levels, orbitals, pot, theirs, mine):
    slots, coefficients, width = orbitals.shape
    half, fold = width // PAIR, coefficients // 2
    first = meta[0] == 0
    place = lax.broadcasted_iota(jnp.int32, (8, width), 1)
    for slot in range(slots):
        keep = slot < meta[1]
        for part in range(2):
            here = orbitals[slot, part * fold : (part + 1) * fold, :]
            here = jnp.where(keep, here, jnp.zeros_like(here))
            low, high = here[:, :half], here[:, half:]
            lanes = slice(part * half, (part + 1) * half)
            theirs[slot, :fold, lanes] = jnp.where(first, high, low)
            mine[slot, :fold, lanes] = jnp.where(first, low, high)
        own_id = meta[2] + slot
        facts = jnp.where(place == 6, levels[slot], jnp.where(place == 7, jnp.where(keep, 1, 0), 0))
        for c in range(6):
            target = neighbours[slot, c]
            facts = jnp.where(place == c, jnp.where(target >= 0, target - own_id, 16 * slots), facts)
        facts = facts.astype(f32).astype(bf16)
        for packed in (theirs, mine):
            packed[slot, fold : fold + 8, :] = facts
        row = fold + 8
        for start in range(0, pot.shape[1], width):
            exact = pot[slot : slot + 1, start : start + width]
            for _ in range(3):
                part = exact.astype(bf16)
                exact = exact - part.astype(f32)
                for packed in (theirs, mine):
                    packed[slot, row : row + 1, :] = part
                row += 1
        for packed in (theirs, mine):
            packed[slot, row:, :] = jnp.zeros((packed.shape[1] - row, width), bf16)


def pack(meta, neighbours, levels, orbitals, pot):
    slots, coefficients, width = orbitals.shape
    fold = coefficients // 2
    padded = -(-(fold + 8 + 3 * (pot.shape[1] // width)) // ROWS) * ROWS
    vmem, smem = pl.BlockSpec(memory_space=pltpu.VMEM), pl.BlockSpec(memory_space=pltpu.SMEM)
    return pl.pallas_call(
        pack_kernel,
        out_shape=[jax.ShapeDtypeStruct((slots, padded, width), bf16)] * 2,
        in_specs=[smem, smem, smem, vmem, vmem],
        out_specs=[vmem, vmem],
        compiler_params=params(24),
        name="pack",
    )(meta, neighbours, levels, orbitals, pot)


def unfold_kernel(fold, meta, beside_in, rest_in, whole, top, beside, rest, sems):
    copies = [
        pltpu.make_async_copy(source, target, sems.at[i])
        for i, (source, target) in enumerate(((beside_in, beside), (rest_in, rest)))
    ]
    for copy in copies:
        copy.start()
    slots, _, width = beside.shape
    half = width // PAIR
    first = meta[0] == 0
    for copy in copies:
        copy.wait()
    for slot in range(slots):
        for part in range(2):
            lanes = slice(part * half, (part + 1) * half)
            near, far = beside[slot, :fold, lanes], rest[slot, :fold, lanes]
            start = (2 * slot + part) * fold
            here = jnp.concatenate([jnp.where(first, near, far), jnp.where(first, far, near)], axis=1)
            whole[start : start + fold, :] = here
    top[...] = whole[: top.shape[0], :]


def unfold(meta, beside, rest, fold, cut):
    slots, _, width = beside.shape
    vmem = pl.BlockSpec(memory_space=pltpu.VMEM)
    return pl.pallas_call(
        functools.partial(unfold_kernel, fold),
        out_shape=[
            jax.ShapeDtypeStruct((2 * slots * fold, width), bf16),
            jax.ShapeDtypeStruct((cut, width), bf16),
        ],
        in_specs=[pl.BlockSpec(memory_space=pltpu.SMEM)] + [pl.BlockSpec(memory_space=pl.ANY)] * 2,
        out_specs=[vmem, vmem],
        scratch_shapes=[
            pltpu.VMEM(beside.shape, bf16),
            pltpu.VMEM(beside.shape, bf16),
            pltpu.SemaphoreType.DMA((2,)),
        ],
        compiler_params=params(24),
        name="unfold",
    )(meta, beside, rest)


def load_left(lefts, held, sems):
    copies = []
    for q, pieces in enumerate(lefts):
        row = 0
        for piece in pieces:
            rows, width = piece.shape
            here = held.at[row : row + rows, q * width : (q + 1) * width]
            copies.append(pltpu.make_async_copy(piece, here, sems.at[len(copies)]))
            row += rows
    for copy in copies:
        copy.start()
    return copies


def grouped(refs, counts):
    refs = list(refs)
    return [[refs.pop(0) for _ in range(count)] for count in counts]


def correlation_kernel(share, counts, meta, *refs):
    refs, (out, held, turned, sems) = refs[:-4], refs[-4:]
    groups, half, width = out.shape
    lefts, before = grouped(refs, counts), refs[sum(counts) :]
    copies = load_left(lefts, held, sems)
    first = meta[0] == 0
    for copy in copies[: counts[0]]:
        copy.wait()
    own = held[:, :width]
    own = jnp.where(first, own[:, :half], own[:, half:]).T
    live = lax.broadcasted_iota(jnp.int32, own.shape, 1) < meta[1 if before else 2]
    turned[...] = jnp.where(live, own, jnp.zeros_like(own))
    for base in range(0, groups, 2):
        for copy in copies[max(sum(counts[:base]), counts[0]) : sum(counts[: base + 2])]:
            copy.wait()
        wide = matmul(turned[...], held[:, base * width : (base + 2) * width])
        for q in (base, base + 1):
            total = wide[:, (q - base) * width : (q - base + 1) * width]
            if before:
                total = total + before[0][q]
                if q == 0:
                    rows = lax.broadcasted_iota(jnp.int32, (half, width), 0) + jnp.where(first, 0, half)
                    columns = lax.broadcasted_iota(jnp.int32, (half, width), 1)
                    total = total - jnp.where(rows == columns, share, 0.0)
            out[q] = total.astype(out.dtype)


def box_correlation(share, meta, lefts, before, half):
    depth, width = sum(piece.shape[0] for piece in lefts[0]), lefts[0][0].shape[1]
    counts = [len(pieces) for pieces in lefts]
    vmem = pl.BlockSpec(memory_space=pltpu.VMEM)
    extra = [] if before is None else [before]
    return pl.pallas_call(
        functools.partial(correlation_kernel, share, counts),
        out_shape=jax.ShapeDtypeStruct((len(lefts), half, width), f32 if before is None else bf16),
        in_specs=[pl.BlockSpec(memory_space=pltpu.SMEM)]
        + [pl.BlockSpec(memory_space=pl.ANY)] * sum(counts)
        + [vmem] * len(extra),
        out_specs=vmem,
        scratch_shapes=[
            pltpu.VMEM((depth, len(lefts) * width), bf16),
            pltpu.VMEM((half, depth), bf16),
            pltpu.SemaphoreType.DMA((sum(counts),)),
        ],
        compiler_params=params(32),
        cost_estimate=pl.CostEstimate(
            flops=2 * len(lefts) * depth * width * half, bytes_accessed=2 * len(lefts) * depth * width, transcendentals=0
        ),
        name="correlation",
    )(meta, *[piece for pieces in lefts for piece in pieces], *extra)


def fock_kernel(side, counts, right, *refs):
    outs, (held, raw, turned, sems, last_sem) = refs[sum(counts) : -5], refs[-5:]
    lefts = grouped(refs, counts)
    before, apart, outs = (None, None, outs) if len(outs) == 1 else (outs[0], outs[1], outs[2:])
    out = outs[0]
    last = pltpu.make_async_copy(right.at[side], raw, last_sem)
    last.start()
    copies = load_left(lefts, held, sems)
    half, width = out.shape[-2] // (3 if before is None else 1), out.shape[-1]
    last.wait()
    turned[...] = raw[...].T
    for base in range(0, len(lefts), 2):
        for copy in copies[sum(counts[:base]) : sum(counts[: base + 2])]:
            copy.wait()
        wide = matmul(turned[...], held[:, base * width : (base + 2) * width])
        for q in (base, base + 1):
            total = wide[:, (q - base) * width : (q - base + 1) * width]
            if before is None:
                out[q] = total
                continue
            total = total + before[q]
            main = total[:half] + total[half : 2 * half]
            top = main.astype(bf16)
            parts = (top, (main - top.astype(f32)).astype(bf16), total[2 * half :].astype(bf16))

            def store(target):
                for i in range(3):
                    target[i] = parts[i]

            for distance, target in enumerate(outs):
                pl.when(q ^ apart[0] == distance)(functools.partial(store, target))


def box_fock(side, lefts, right, before, apart):
    depth, width = sum(piece.shape[0] for piece in lefts[0]), lefts[0][0].shape[1]
    counts = [len(pieces) for pieces in lefts]
    tall = right.shape[-1]
    anywhere, vmem = pl.BlockSpec(memory_space=pl.ANY), pl.BlockSpec(memory_space=pltpu.VMEM)
    extra = [] if before is None else [before, apart]
    out = jax.ShapeDtypeStruct((len(lefts), tall, width), f32)
    if before is not None:
        out = [jax.ShapeDtypeStruct((3, tall // 3, width), bf16)] * len(lefts)
    return pl.pallas_call(
        functools.partial(fock_kernel, side, counts),
        out_shape=out,
        in_specs=[anywhere] * (sum(counts) + 1) + [vmem, pl.BlockSpec(memory_space=pltpu.SMEM)][: len(extra)],
        out_specs=vmem if before is None else [vmem] * len(lefts),
        scratch_shapes=[
            pltpu.VMEM((depth, len(lefts) * width), bf16),
            pltpu.VMEM(right.shape[1:], bf16),
            pltpu.VMEM((tall, depth), bf16),
            pltpu.SemaphoreType.DMA((sum(counts),)),
            pltpu.SemaphoreType.DMA(()),
        ],
        compiler_params=params(40),
        cost_estimate=pl.CostEstimate(
            flops=2 * len(lefts) * depth * width * tall, bytes_accessed=2 * len(lefts) * depth * width, transcendentals=0
        ),
        name="fock",
    )(right, *[piece for pieces in lefts for piece in pieces], *extra)


def root_kernel(levels, meta, *refs):
    pieces, (offset, root, whole, rows_f, cols_b, sems) = refs[:-6], refs[-6:]
    level, pair, orb = meta[0], meta[1], meta[2]
    coarse, width = offset.shape
    side = whole.shape[0]
    groups = side // width
    copies = []
    for piece, (z, y, q) in zip(pieces, piece_places(levels)):
        for i in range(len(z)):
            start = ((orb ^ q) * PAIR + (pair ^ y)) * coarse
            rows = pl.ds(pl.multiple_of(start, coarse), coarse)
            lanes = pl.ds(pl.multiple_of((level ^ z[i]) * width, width), width)
            copies.append(
                pltpu.make_async_copy(
                    piece.at[i * coarse : (i + 1) * coarse], whole.at[rows, lanes], sems.at[len(copies)]
                )
            )
    for copy in copies:
        copy.start()
    for copy in copies:
        copy.wait()
    row0 = pl.multiple_of((level * PAIR + pair) * coarse, coarse)
    own_lanes = pl.ds(pl.multiple_of(orb * width, width), width)
    rows = whole[pl.ds(row0, coarse), :]

    for j in range(groups):
        lanes = slice(j * width, (j + 1) * width)
        rows_f[:, lanes] = matmul(rows, whole[:, lanes])
    columns = whole[:, own_lanes]
    for i in range(groups):
        here = slice(i * width, (i + 1) * width)
        square = matmul(whole[here, :], columns)
        cols_b[here, :] = (0.25 * (whole[here, own_lanes].astype(f32) - square)).astype(bf16)
    left = (rows.astype(f32) - 0.25 * rows_f[...]).astype(bf16)
    value = matmul(left, cols_b[...]) + 0.125 * rows_f[:, own_lanes] - 0.5 * offset[...]
    row_ids = lax.broadcasted_iota(jnp.int32, value.shape, 0) + row0
    col_ids = lax.broadcasted_iota(jnp.int32, value.shape, 1) + orb * width
    root[...] = value + jnp.where(row_ids == col_ids, 1.0, 0.0)


def piece_places(levels):
    places = []
    for core in (0, 1):
        for half in range(2):
            z = [half * levels // 2 + i for i in range(levels // 2)]
            for second in (0, 1):
                for inner in (0, 1):
                    y, far = (second, inner) if half else (inner, second)
                    places.append((z, y, 2 * far + core))
    return places


def root_of(meta, pieces, offset, side, levels):
    coarse, width = offset.shape
    vmem, anywhere = pl.BlockSpec(memory_space=pltpu.VMEM), pl.BlockSpec(memory_space=pl.ANY)
    return pl.pallas_call(
        functools.partial(root_kernel, levels),
        out_shape=jax.ShapeDtypeStruct(offset.shape, f32),
        in_specs=[pl.BlockSpec(memory_space=pltpu.SMEM)] + [anywhere] * len(pieces) + [vmem],
        out_specs=vmem,
        scratch_shapes=[
            pltpu.VMEM((side, side), bf16),
            pltpu.VMEM((coarse, side), f32),
            pltpu.VMEM((side, width), bf16),
            pltpu.SemaphoreType.DMA((side // coarse * (side // width),)),
        ],
        compiler_params=params(40),
        cost_estimate=pl.CostEstimate(flops=16 * side * side * width, bytes_accessed=4 * side * side, transcendentals=0),
        name="root",
    )(meta, *pieces, offset)


def fill_tables(slots, levels, place_meta, facts, table, scale):
    level, pair = place_meta[0], place_meta[1]
    even = lax.rem(level, 2) == 0
    none = 6 * slots

    def place(slot_id):
        box = lax.div(slot_id, slots)
        apart = lax.div(box, PAIR) - level
        base = jnp.where(apart == 0, 0, jnp.where((apart < 0) == even, 4, 2))
        return (base + jnp.where(lax.rem(box, PAIR) != pair, 1, 0)) * slots + lax.rem(slot_id, slots)

    for index in range(4 * slots):
        group, r = divmod(index, slots)

        def fact(c):
            if group < 2:
                return facts[group, r, c]
            swap_id = jnp.where(even, 1, 0) if group == 2 else jnp.where(even, 0, 1)
            near_pair = 1 if group == 2 else 0
            return facts[2 + swap_id + jnp.where(pair == near_pair, 0, 2), r, c]

        box = (
            level * PAIR + pair,
            level * PAIR + 1 - pair,
            jnp.maximum(level * PAIR - 1, 0),
            jnp.minimum((level + 1) * PAIR, levels * PAIR - 1),
        )[group]
        there = (True, True, level > 0, level < levels - 1)[group]
        own_id = box * slots + r
        own_place = place(own_id)
        table[index, 0] = jnp.where((fact(7) > 0) & there, own_place, -1)
        for a in range(3):
            for k in (0, 2):
                distance = fact(2 * a + k // 2)
                target = place(jnp.maximum(own_id + distance, 0))
                target = jnp.where(distance < 16 * slots, target, none)
                table[index, 1 + 3 * a + k] = jnp.clip(target, 0, none)
            table[index, 2 + 3 * a] = own_place
        level_of = fact(6)
        scale[index] = jnp.where(level_of == 0, 0.5, jnp.where(level_of == 1, 1.0, 2.0))


def kinetic_kernel(edge, slots, levels, place_meta, facts, *refs):
    parts, refs = refs[:6], refs[6:]
    (fwd_in, fwd_out, back_in, back_mid, back_out), out, refs = refs[:5], refs[5], refs[6:]
    raw, x, outer, inner, total, total_fix, lines, columns, table, scale, sems = refs
    square = edge * edge
    own = PAIR * slots
    padded, width = x.shape[2:]
    copies = [pltpu.make_async_copy(part, raw.at[place], sems.at[place]) for place, part in enumerate(parts)]
    for copy in copies:
        copy.start()
    tail = padded - ROWS
    x[:, :, tail:, :] = jnp.zeros((x.shape[0], edge, ROWS, width), bf16)
    x[6 * slots] = jnp.zeros((edge, padded, width), bf16)
    total[...] = jnp.zeros_like(total)
    total_fix[...] = jnp.zeros_like(total_fix)
    fill_tables(slots, levels, place_meta, facts, table, scale)
    lines[...] = jnp.zeros_like(lines)
    for copy in copies:
        copy.wait()
    lanes = raw.shape[3]
    for t in range(own):
        for start in range(0, lines.shape[1], lanes):
            row = edge * square // 2 + 8 + 3 * (start // lanes)
            high, middle, low = (
                raw[t // slots, t % slots, row + i : row + i + 1, :].astype(f32) for i in range(3)
            )
            lines[t : t + 1, start : start + lanes] = (high + middle) + low
    columns[...] = lines[...].T

    def lay_out(place, carry):
        for slot in range(slots):
            for i in range(edge):
                part, row = i // (edge // 2), i % (edge // 2) * square
                x[place * slots + slot, i, :square, :] = raw[
                    place, slot, row : row + square, part * width : (part + 1) * width
                ]
        return carry

    lax.fori_loop(0, len(parts), lay_out, 0)
    chunks = -(-square // ROWS)

    def per_slot(s, carry):
        @pl.when(table[s, 0] >= 0)
        def _():
            own_scale = scale[s]
            half = 0.5 * own_scale
            sums = (total, total_fix)

            def split(exact):
                exact = own_scale * exact
                value = exact.astype(bf16).astype(f32)
                return (half * value).astype(bf16), (half * (value - exact)).astype(bf16)

            sources = [[table[s, 1 + 3 * a + k] for k in range(3)] for a in range(3)]
            here = sources[0][1]
            for a in range(3):

                @pl.when((here < own) | (sources[a][0] < own) | (sources[a][2] < own))
                def _():
                    if a == 0:
                        for i in range(chunks):
                            rows = slice(i * ROWS, (i + 1) * ROWS)
                            block = [x[t, :, rows, :].reshape(edge * ROWS, width) for t in sources[0]]
                            fields = split(matmul(fwd_out[...], jnp.concatenate(block, axis=0)))
                            for field in range(2):
                                outer[field, :, rows, :] = fields[field].reshape(edge, ROWS, width)
                    else:
                        for i in range(edge):
                            block = jnp.concatenate([x[t, i] for t in sources[a]], axis=0)
                            fields = split(matmul(fwd_in[a - 1], block))
                            for field in range(2):
                                inner[field, i, (a - 1) * padded : a * padded, :] = fields[field]

            def back_outer(k, target):
                for i in range(chunks):
                    rows = slice(i * ROWS, (i + 1) * ROWS)
                    for field in range(2):
                        term = matmul(back_out[k], outer[field, :, rows, :].reshape(edge * ROWS, width))
                        sums[field][target, :, rows, :] += term.reshape(edge, ROWS, width)

            for k in (0, 2):
                for a in range(3):
                    target = sources[a][k]

                    @pl.when(target < own)
                    def _():
                        if a == 0:
                            back_outer(k, target)
                        else:
                            for i in range(edge):
                                for field in range(2):
                                    here = inner[field, i, (a - 1) * padded : a * padded, :]
                                    sums[field][target, i] += matmul(back_in[a - 1, k], here)

            @pl.when(here < own)
            def _():
                back_outer(1, here)
                for i in range(edge):
                    for field in range(2):
                        sums[field][here, i] += matmul(back_mid[...], inner[field, i])

        return carry

    lax.fori_loop(0, table.shape[0], per_slot, 0)

    for t in range(own):
        for i in range(edge):
            rows = slice(i * square, (i + 1) * square)
            weighted = (columns[rows, t : t + 1] * x[t, i, :square, :].astype(f32)).astype(bf16)
            whole = total[t, i, :square, :] + weighted.astype(f32)
            top = whole.astype(bf16)
            low = (whole - top.astype(f32)).astype(bf16)
            fix = total_fix[t, i, :square, :].astype(bf16)
            out[t, rows, :] = jnp.concatenate([top, low, fix], axis=1)


def matrices_kernel(stacked, blocks, *refs):
    spots, outs = refs[:9], refs[9:]
    fwd_in, fwd_out, back_in, back_mid, back_out = outs
    for mode in range(3):
        spot, spread, same = spots[3 * mode : 3 * mode + 3]
        wide = matmul(matmul(spot[...], stacked[...]).astype(bf16), spread[...])
        wide = (wide * jnp.concatenate([same[...]] * 3, axis=1)).astype(bf16)
        if mode == 2:
            fwd_out[...] = wide
        else:
            fwd_in[mode] = wide
        for k in range(3):
            turned = lax.dot_general(spot[...], blocks[k], (((1,), (1,)), ((), ())), preferred_element_type=f32)
            turned = lax.dot_general(
                turned.astype(bf16), spot[...], (((1,), (1,)), ((), ())), preferred_element_type=f32
            )
            turned = (turned * same[...]).astype(bf16)
            if mode == 2:
                back_out[k] = turned
            else:
                back_in[mode, k] = turned
    back_mid[...] = jnp.concatenate([back_in[0, 1], back_in[1, 1]], axis=1)


def block_matrices(deriv_blocks):
    edge = deriv_blocks.shape[1]
    square = edge * edge
    padded = -(-square // ROWS) * ROWS
    tall = edge * ROWS
    ids = np.arange(padded)
    slow = ((ids[:, None] // edge) == np.arange(edge)).astype(np.float32)
    fast = (((ids[:, None] % edge) == np.arange(edge)) & (ids[:, None] < square)).astype(np.float32)
    ids = np.arange(tall)
    outer = ((ids[:, None] // ROWS) == np.arange(edge)).astype(np.float32)
    within = ((ids[:, None] % ROWS) == np.arange(ROWS)).astype(np.float32)
    stacked = jnp.moveaxis(deriv_blocks, 0, 1).reshape(edge, 3 * edge)
    constants = []
    for spot, mask in ((slow, fast), (fast, slow), (outer, within)):
        spread = np.kron(np.eye(3, dtype=np.float32), spot.T)
        constants += [jnp.asarray(spot, bf16), jnp.asarray(spread, bf16), jnp.asarray(mask @ mask.T, f32)]
    vmem = pl.BlockSpec(memory_space=pltpu.VMEM)
    shapes = [(2, padded, 3 * padded), (tall, 3 * tall), (2, 3, padded, padded), (padded, 2 * padded), (3, tall, tall)]
    return pl.pallas_call(
        matrices_kernel,
        out_shape=[jax.ShapeDtypeStruct(shape, bf16) for shape in shapes],
        in_specs=[vmem] * 11,
        out_specs=[vmem] * 5,
        compiler_params=params(24),
        name="matrices",
    )(stacked, deriv_blocks, *constants)


def kinetic(parts, place_meta, facts, matrices, edge, coefficients, levels):
    slots, folded, lanes = parts[0].shape
    width = lanes // 2
    padded = matrices[0].shape[1]
    own = PAIR * slots
    vmem = pl.BlockSpec(memory_space=pltpu.VMEM)
    smem = pl.BlockSpec(memory_space=pltpu.SMEM)
    anywhere = pl.BlockSpec(memory_space=pl.ANY)
    return pl.pallas_call(
        functools.partial(kinetic_kernel, edge, slots, levels),
        out_shape=jax.ShapeDtypeStruct((own, coefficients, 3 * width), bf16),
        in_specs=[smem] * 2 + [anywhere] * 6 + [vmem] * 5,
        out_specs=vmem,
        scratch_shapes=[
            pltpu.VMEM((6, slots, folded, lanes), bf16),
            pltpu.VMEM((6 * slots + 1, edge, padded, width), bf16),
            pltpu.VMEM((2, edge, padded, width), bf16),
            pltpu.VMEM((2, edge, 2 * padded, width), bf16),
            pltpu.VMEM((own, edge, padded, width), f32),
            pltpu.VMEM((own, edge, padded, width), f32),
            pltpu.VMEM((own + -own % 8, coefficients + -coefficients % lanes), f32),
            pltpu.VMEM((coefficients + -coefficients % lanes, own + -own % 8), f32),
            pltpu.SMEM((4 * slots, 10), jnp.int32),
            pltpu.SMEM((4 * slots,), f32),
            pltpu.SemaphoreType.DMA((6,)),
        ],
        compiler_params=params(48),
        cost_estimate=pl.CostEstimate(flops=2 * 10**10, bytes_accessed=40 * 10**6, transcendentals=0),
        name="kinetic",
    )(place_meta, facts, *parts, *matrices)


def offset_sum_kernel(meta, *refs):
    blocks, (small, kept, sent) = refs[:-3], refs[-3:]
    total = blocks[0][...].astype(f32)
    for block in blocks[1:]:
        total = total + block[...].astype(f32)
    small[...] = total.astype(bf16)
    half = kept.shape[0]
    first = meta[0] == 0
    low, high = total[:, :half].T, total[:, half:].T
    kept[...] = jnp.where(first, low, high)
    sent[...] = jnp.where(first, high, low)


def fock_sum_kernel(meta, *refs):
    blocks, (share, kept, sent) = refs[:-3], refs[-3:]
    sums = [sum((block[part].astype(f32) for block in blocks[1:]), blocks[0][part].astype(f32)) for part in range(3)]
    main = sums[0] + sums[1]
    share[...] = sums[2].astype(bf16)
    half = kept.shape[0]
    first = meta[0] == 0
    low, high = main[:, :half].T, main[:, half:].T
    kept[...] = jnp.where(first, low, high)
    sent[...] = jnp.where(first, high, low)


def level_sum(kernel, meta, blocks):
    tall, width = blocks[0].shape[-2:]
    vmem = pl.BlockSpec(memory_space=pltpu.VMEM)
    turned = jax.ShapeDtypeStruct((width // PAIR, tall), f32)
    return pl.pallas_call(
        kernel,
        out_shape=[jax.ShapeDtypeStruct((tall, width), bf16), turned, turned],
        in_specs=[pl.BlockSpec(memory_space=pltpu.SMEM)] + [vmem] * len(blocks),
        out_specs=[vmem] * 3,
        compiler_params=params(24),
        name="level_sum",
    )(meta, *blocks)


def body(orbitals, potential, deriv_blocks, levels, box_counts, neighbours):
    slots, coefficients, own_width = orbitals.shape
    edge = deriv_blocks.shape[1]
    level, pair, orb = lax.axis_index("lvl"), lax.axis_index("pair"), lax.axis_index("orb")
    level_count, orb_count = lax.axis_size("lvl"), lax.axis_size("orb")
    half, fold = own_width // PAIR, coefficients // 2
    all_width = own_width * orb_count
    box_rows = all_width // (level_count * PAIR)
    first = pair == 0
    groups = range(orb_count)
    square_grid = level_count == orb_count == 4 and box_rows == half
    row0, col0 = (level * PAIR + pair) * box_rows, orb * own_width

    pot = jnp.pad(potential, ((0, 0), (0, -coefficients % own_width)))
    own_base = (level * PAIR + pair) * slots
    pack_meta = jnp.stack([pair, box_counts[0], own_base]).astype(jnp.int32)
    theirs, mine = pack(pack_meta, neighbours.reshape(slots, 6), levels, orbitals, pot)
    active = orbitals

    far = {q: swap(active, "orb", q) for q in groups if q and q % 2 == 0}
    beside = swap(theirs, "pair", 1)
    first_mine, second_mine = trade(mine, "lvl", 0), trade(mine, "lvl", 1)
    later_mine, beside = lax.optimization_barrier((mine, beside))
    beside_rest = swap(later_mine, "pair", 1)
    first_beside, second_beside = trade(beside, "lvl", 0), trade(beside, "lvl", 1)

    matrices = block_matrices(deriv_blocks)

    def facts_of(parts):
        return jnp.stack([part[:, fold, :8] for part in parts]).astype(f32).astype(jnp.int32)

    early_facts = facts_of([mine, beside, first_mine, second_mine])
    flat = lambda block: block.reshape(-1, block.shape[-1])
    cut = -(-slots * coefficients // (2 * ROWS)) * ROWS
    beside_all, beside_top = unfold(pack_meta, beside, beside_rest, fold, cut)

    parts = [mine, beside, first_mine, first_beside, second_mine, second_beside]
    far, active, parts, beside_all, beside_top, matrices, early_facts = lax.optimization_barrier(
        (far, active, parts, beside_all, beside_top, matrices, early_facts)
    )
    facts = jnp.concatenate([early_facts, facts_of([parts[3], parts[5]])])
    cross = {q: [swap(beside_top, "orb", q), swap(flat(far[q])[cut:], "pair", 1)] for q in far}
    left_own = {0: active, 1: swap(active, "orb", 1), **far}
    left_beside = {0: [beside_all], 1: [swap(beside_all, "orb", 1)]}
    for q in far:
        left_own[q + 1] = swap(far[q], "orb", 1)

    def natural(blocks):
        return jnp.concatenate([lax.dynamic_index_in_dim(blocks, orb ^ j, keepdims=False) for j in groups], axis=1)

    def along_levels(blocks):
        mine_block = lambda target: lax.dynamic_index_in_dim(blocks, orb ^ target, keepdims=False)
        steps = range(1, level_count)
        return [mine_block(level)] + [swap(mine_block(level ^ step), "lvl", step) for step in steps]

    def both_halves(kept, got):
        return jnp.concatenate([jnp.where(first, kept, got), jnp.where(first, got, kept)], axis=1)

    def own_block(strip):
        strip = lax.all_gather(lax.psum(strip, "lvl"), ("orb", "pair"), axis=0, tiled=True)
        strip = lax.dynamic_slice_in_dim(strip, row0, box_rows, axis=0)
        return lax.dynamic_slice_in_dim(strip, col0, own_width, axis=1)

    live_rows = box_counts[0] * coefficients
    meta = jnp.stack([pair, slots * coefficients, live_rows]).astype(jnp.int32)

    place_meta = jnp.stack([level, pair]).astype(jnp.int32)
    right = kinetic(parts, place_meta, facts, matrices, edge, coefficients, level_count)

    cross, right, meta = lax.optimization_barrier((cross, right, meta))
    lefts_own = [[flat(left_own[q])] for q in groups]
    lefts_beside = dict(left_beside)
    for q in far:
        lefts_beside[q] = list(cross[q])
        lefts_beside[q + 1] = [swap(piece, "orb", 1) for piece in cross[q]]
    lefts_beside = [lefts_beside[q] for q in groups]

    share = 1.0 / level_count
    blocks = box_correlation(share, meta, lefts_own, None, half)
    blocks = box_correlation(share, meta, lefts_beside, blocks, half)
    right = right.reshape(2, slots * coefficients, 3 * half)
    fock_part = box_fock(0, lefts_own, right, None, None)
    if square_grid:
        sent = along_levels(blocks)
        sent, fock_part = lax.optimization_barrier((sent, fock_part))
        small, kept, other = level_sum(offset_sum_kernel, meta, sent)
        offset = both_halves(kept, swap(other, "pair", 1))
    else:
        offset = own_block(natural(blocks).astype(f32))
    row_ids = row0 + jnp.arange(box_rows, dtype=jnp.int32)
    col_ids = col0 + jnp.arange(own_width, dtype=jnp.int32)
    correlation = offset + (row_ids[:, None] == col_ids[None, :]).astype(f32)
    apart = (orb ^ level if square_grid else 0 * orb).reshape(1).astype(jnp.int32)
    fock_blocks = box_fock(1, lefts_beside, right, fock_part, apart)
    if square_grid:
        pieces = [small] + [swap(small, "lvl", z) for z in range(1, level_count)]
        pieces, fock_blocks, offset = lax.optimization_barrier((pieces, fock_blocks, offset))
        join = functools.partial(jnp.concatenate, axis=0)
        top, low = join(pieces[: level_count // 2]), join(pieces[level_count // 2 :])
        sent = [fock_blocks[0]] + [swap(fock_blocks[step], "lvl", step) for step in range(1, level_count)]
        got = [swap(top, "pair", 1), swap(low, "orb", 2)]
        got, sent[:3] = lax.optimization_barrier((got, sent[:3]))
        tops, lows = [top, got[0]], [low, got[1]]
        pieces = tops + [swap(piece, "orb", 2) for piece in tops] + lows + [swap(piece, "pair", 1) for piece in lows]
        pieces, sent = lax.optimization_barrier((pieces, sent))
        pieces += [swap(piece, "orb", 1) for piece in pieces]
        root_meta = jnp.stack([level, pair, orb]).astype(jnp.int32)
        inverse_root = root_of(root_meta, pieces, offset, all_width, level_count)
        share, kept, other = level_sum(fock_sum_kernel, meta, sent)
        to = [
            ((z * PAIR + y) * orb_count + o, (o * PAIR + y) * orb_count + z)
            for z in range(level_count)
            for y in range(PAIR)
            for o in groups
        ]
        got = swap(other, "pair", 1), lax.ppermute(share, BOX + ("orb",), to)
        inverse_root, got = lax.optimization_barrier((inverse_root, got))
        fock = both_halves(kept, got[0]) + got[1].astype(f32)
    else:
        fock_blocks = jnp.stack(fock_blocks)
        main = natural(fock_blocks[:, 0]).astype(f32) + natural(fock_blocks[:, 1]).astype(f32)
        main = lax.all_gather(lax.psum(main, "lvl"), "pair", axis=0, tiled=True)
        fock = lax.dynamic_slice_in_dim(main, row0, box_rows, axis=1).T + own_block(natural(fock_blocks[:, 2]).astype(f32))
        gathered = lax.all_gather(offset.astype(bf16), "orb", axis=1, tiled=True)
        whole = lax.all_gather(gathered, BOX, axis=0, tiled=True)
        rows_of = lax.dynamic_slice_in_dim(whole, row0, box_rows, axis=0)
        cols_of = lax.dynamic_slice_in_dim(whole, col0, own_width, axis=1)
        row_square, col_square = matmul(rows_of, whole), matmul(whole, cols_of)
        left = (rows_of.astype(f32) - 0.25 * row_square).astype(bf16)
        right_side = (0.25 * (cols_of.astype(f32) - col_square)).astype(bf16)
        own_square = lax.dynamic_slice_in_dim(row_square, col0, own_width, axis=1)
        inverse_root = correlation - 1.5 * offset + 0.125 * own_square + matmul(left, right_side)
    return fock, correlation, inverse_root


def solution(mesh):
    levels = mesh.shape["box"] // PAIR
    split = Mesh(mesh.devices.reshape(levels, PAIR, mesh.shape["orb"]), ("lvl", "pair", "orb"))
    in_specs = (P(BOX, None, "orb"), P(BOX, None), P(), P(BOX), P(BOX), P(BOX, None, None))
    out_specs = (P(BOX, "orb"),) * 3
    return jax.shard_map(body, mesh=split, in_specs=in_specs, out_specs=out_specs, check_vma=False)
```

```python
import functools

import jax
import jax.numpy as jnp
import numpy as np
from jax import lax
from jax.experimental import pallas as pl
from jax.experimental.pallas import tpu as pltpu
from jax.sharding import Mesh, PartitionSpec as P

PAIR = 2
ROWS = 16
BOX = ("lvl", "pair")
f32, bf16 = jnp.float32, jnp.bfloat16


def swap(value, axis, bit):
    count = lax.axis_size(axis)
    return lax.ppermute(value, axis, [(i, i ^ bit) for i in range(count)])


def trade(value, axis, start):
    pairs = [(i, i + 1) for i in range(start, lax.axis_size(axis) - 1, 2)]
    return lax.ppermute(value, axis, pairs + [(b, a) for a, b in pairs])


def matmul(left, right):
    return jnp.dot(left, right, preferred_element_type=f32)


def params(mebibytes):
    return pltpu.CompilerParams(vmem_limit_bytes=mebibytes * 1024 * 1024)


def pack_kernel(meta, neighbours, levels, orbitals, pot, theirs, mine):
    slots, coefficients, width = orbitals.shape
    half, fold = width // PAIR, coefficients // 2
    first = meta[0] == 0
    place = lax.broadcasted_iota(jnp.int32, (8, width), 1)
    for slot in range(slots):
        keep = slot < meta[1]
        for part in range(2):
            here = orbitals[slot, part * fold : (part + 1) * fold, :]
            here = jnp.where(keep, here, jnp.zeros_like(here))
            low, high = here[:, :half], here[:, half:]
            lanes = slice(part * half, (part + 1) * half)
            theirs[slot, :fold, lanes] = jnp.where(first, high, low)
            mine[slot, :fold, lanes] = jnp.where(first, low, high)
        own_id = meta[2] + slot
        facts = jnp.where(place == 6, levels[slot], jnp.where(place == 7, jnp.where(keep, 1, 0), 0))
        for c in range(6):
            target = neighbours[slot, c // 2, c % 2]
            facts = jnp.where(place == c, jnp.where(target >= 0, target - own_id, 16 * slots), facts)
        facts = facts.astype(f32).astype(bf16)
        for packed in (theirs, mine):
            packed[slot, fold : fold + 8, :] = facts
        row = fold + 8
        for start in range(0, pot.shape[1], width):
            stop = min(start + width, pot.shape[1])
            exact = pot[slot : slot + 1, start:stop]
            for _ in range(3):
                part = exact.astype(bf16)
                exact = exact - part.astype(f32)
                for packed in (theirs, mine):
                    packed[slot, row : row + 1, : stop - start] = part
                    if stop - start < width:
                        packed[slot, row : row + 1, stop - start :] = jnp.zeros((1, width - stop + start), bf16)
                row += 1
        for packed in (theirs, mine):
            packed[slot, row:, :] = jnp.zeros((packed.shape[1] - row, width), bf16)


def pack(meta, neighbours, levels, orbitals, pot):
    slots, coefficients, width = orbitals.shape
    fold = coefficients // 2
    padded = -(-(fold + 8 + 3 * -(-coefficients // width)) // ROWS) * ROWS
    vmem, smem = pl.BlockSpec(memory_space=pltpu.VMEM), pl.BlockSpec(memory_space=pltpu.SMEM)
    return pl.pallas_call(
        pack_kernel,
        out_shape=[jax.ShapeDtypeStruct((slots, padded, width), bf16)] * 2,
        in_specs=[smem, smem, smem, vmem, vmem],
        out_specs=[vmem, vmem],
        compiler_params=params(24),
        name="pack",
    )(meta, neighbours, levels, orbitals, pot)


def unfold_kernel(fold, meta, beside_in, rest_in, whole, top, beside, rest, sems):
    copies = [
        pltpu.make_async_copy(source, target, sems.at[i])
        for i, (source, target) in enumerate(((beside_in, beside), (rest_in, rest)))
    ]
    for copy in copies:
        copy.start()
    slots, _, width = beside.shape
    half = width // PAIR
    first = meta[0] == 0
    for copy in copies:
        copy.wait()
    for slot in range(slots):
        for part in range(2):
            lanes = slice(part * half, (part + 1) * half)
            near, far = beside[slot, :fold, lanes], rest[slot, :fold, lanes]
            start = (2 * slot + part) * fold
            here = jnp.concatenate([jnp.where(first, near, far), jnp.where(first, far, near)], axis=1)
            whole[start : start + fold, :] = here
    top[...] = whole[: top.shape[0], :]


def unfold(meta, beside, rest, fold, cut):
    slots, _, width = beside.shape
    vmem = pl.BlockSpec(memory_space=pltpu.VMEM)
    return pl.pallas_call(
        functools.partial(unfold_kernel, fold),
        out_shape=[
            jax.ShapeDtypeStruct((2 * slots * fold, width), bf16),
            jax.ShapeDtypeStruct((cut, width), bf16),
        ],
        in_specs=[pl.BlockSpec(memory_space=pltpu.SMEM)] + [pl.BlockSpec(memory_space=pl.ANY)] * 2,
        out_specs=[vmem, vmem],
        scratch_shapes=[
            pltpu.VMEM(beside.shape, bf16),
            pltpu.VMEM(beside.shape, bf16),
            pltpu.SemaphoreType.DMA((2,)),
        ],
        compiler_params=params(24),
        name="unfold",
    )(meta, beside, rest)


def load_left(lefts, held, sems):
    copies = []
    for q, pieces in enumerate(lefts):
        row = 0
        for piece in pieces:
            rows, width = piece.shape
            here = held.at[row : row + rows, q * width : (q + 1) * width]
            copies.append(pltpu.make_async_copy(piece, here, sems.at[len(copies)]))
            row += rows
    for copy in copies:
        copy.start()
    return copies


def grouped(refs, counts):
    refs = list(refs)
    return [[refs.pop(0) for _ in range(count)] for count in counts]


def correlation_kernel(share, boxes, bases, meta, *refs):
    extra = 2 if share else 0
    blocks, refs = refs[: sum(map(sum, boxes))], refs[sum(map(sum, boxes)) :]
    refs, (out, held, turned, sems) = refs[:extra], refs[extra:]
    first = meta[0] == 0
    half, width = out.shape[1:]
    lefts, used = [], 0
    for counts in boxes:
        lefts.append(grouped(blocks[used : used + sum(counts)], counts))
        used += sum(counts)
    copies = [load_left(left, held.at[box], sems.at[box]) for box, left in enumerate(lefts)]
    if share:
        before, own_turned = refs
    for box, counts in enumerate(boxes):
        done = 0
        if share and box == 0:
            right = own_turned
        else:
            for copy in copies[box][: counts[0]]:
                copy.wait()
            done = counts[0]
            own = held[box, :, :width]
            own = jnp.where(first, own[:, :half], own[:, half:]).T
            if not share:
                live = lax.broadcasted_iota(jnp.int32, own.shape, 1) < meta[1]
                own = jnp.where(live, own, jnp.zeros_like(own))
            right = turned
            right[...] = own
        for base in range(0, len(counts), 2):
            upto = sum(counts[: base + 2])
            for copy in copies[box][done:upto]:
                copy.wait()
            done = upto
            wide = matmul(right[...], held[box, :, base * width : (base + 2) * width])
            for q in (base, base + 1):
                target = bases[box] + q
                total = wide[:, (q - base) * width : (q - base + 1) * width]
                out[target] = total if box == 0 else out[target] + total


def early_correlation(meta, lefts, half):
    depth, width = lefts[0].shape
    vmem = pl.BlockSpec(memory_space=pltpu.VMEM)

    def kernel(meta, *refs):
        blocks, (out, turned, held, sems) = refs[: len(lefts)], refs[len(lefts) :]
        correlation_kernel(None, [[1] * len(lefts)], [0], meta, *blocks, out, held, turned, sems)

    return pl.pallas_call(
        kernel,
        out_shape=[
            jax.ShapeDtypeStruct((len(lefts), half, width), f32),
            jax.ShapeDtypeStruct((half, depth), bf16),
        ],
        in_specs=[pl.BlockSpec(memory_space=pltpu.SMEM)] + [pl.BlockSpec(memory_space=pl.ANY)] * len(lefts),
        out_specs=[vmem, vmem],
        scratch_shapes=[
            pltpu.VMEM((1, depth, len(lefts) * width), bf16),
            pltpu.SemaphoreType.DMA((1, len(lefts))),
        ],
        compiler_params=params(24),
        name="early_correlation",
    )(meta, *lefts)


def late_correlation(share, meta, lefts_own, lefts_beside, before, own_turned):
    half, width = before.shape[1:]
    depth = own_turned.shape[1]
    boxes = [[len(pieces) for pieces in lefts] for lefts in (lefts_own, lefts_beside)]
    groups, early = len(lefts_beside), before.shape[0]
    operands = [piece for lefts in (lefts_own, lefts_beside) for pieces in lefts for piece in pieces]
    vmem = pl.BlockSpec(memory_space=pltpu.VMEM)

    def kernel(meta, *refs):
        out, total, held, turned, sems = refs[-5:]
        before = refs[-7]
        for q in range(early):
            total[q] = before[q]
        correlation_kernel(share, boxes, [early, 0], meta, *refs[:-5], total, held, turned, sems)
        first = meta[0] == 0
        rows = lax.broadcasted_iota(jnp.int32, (half, width), 0) + jnp.where(first, 0, half)
        columns = lax.broadcasted_iota(jnp.int32, (half, width), 1)
        total[0] = total[0] - jnp.where(rows == columns, share, 0.0)
        out[...] = total[...].astype(bf16)

    return pl.pallas_call(
        kernel,
        out_shape=jax.ShapeDtypeStruct((groups, half, width), bf16),
        in_specs=[pl.BlockSpec(memory_space=pltpu.SMEM)]
        + [pl.BlockSpec(memory_space=pl.ANY)] * len(operands)
        + [vmem, vmem],
        out_specs=vmem,
        scratch_shapes=[
            pltpu.VMEM((groups, half, width), f32),
            pltpu.VMEM((2, depth, groups * width), bf16),
            pltpu.VMEM((half, depth), bf16),
            pltpu.SemaphoreType.DMA((2, max(map(sum, boxes)))),
        ],
        compiler_params=params(40),
        cost_estimate=pl.CostEstimate(
            flops=2 * 2 * groups * depth * width * half, bytes_accessed=4 * groups * depth * width, transcendentals=0
        ),
        name="correlation",
    )(meta, *operands, before, own_turned)


def fock_kernel(side, counts, right, *refs):
    outs, (held, raw, turned, sems, last_sem) = refs[sum(counts) : -5], refs[-5:]
    lefts = grouped(refs, counts)
    before, apart, outs = (None, None, outs) if len(outs) == 1 else (outs[0], outs[1], outs[2:])
    out = outs[0]
    last = pltpu.make_async_copy(right.at[side], raw, last_sem)
    last.start()
    copies = load_left(lefts, held, sems)
    half, width = out.shape[-2] // (3 if before is None else 1), out.shape[-1]
    last.wait()
    turned[...] = raw[...].T
    for base in range(0, len(lefts), 2):
        for copy in copies[sum(counts[:base]) : sum(counts[: base + 2])]:
            copy.wait()
        wide = matmul(turned[...], held[:, base * width : (base + 2) * width])
        for q in (base, base + 1):
            total = wide[:, (q - base) * width : (q - base + 1) * width]
            if before is None:
                out[q] = total
                continue
            total = total + before[q]
            main = total[:half] + total[half : 2 * half]
            top = main.astype(bf16)
            parts = (top, (main - top.astype(f32)).astype(bf16), total[2 * half :].astype(bf16))

            def store(target):
                for i in range(3):
                    target[i] = parts[i]

            for distance, target in enumerate(outs):
                pl.when(q ^ apart[0] == distance)(functools.partial(store, target))


def box_fock(side, lefts, right, before, apart):
    depth, width = sum(piece.shape[0] for piece in lefts[0]), lefts[0][0].shape[1]
    counts = [len(pieces) for pieces in lefts]
    tall = right.shape[-1]
    anywhere, vmem = pl.BlockSpec(memory_space=pl.ANY), pl.BlockSpec(memory_space=pltpu.VMEM)
    extra = [] if before is None else [before, apart]
    out = jax.ShapeDtypeStruct((len(lefts), tall, width), f32)
    if before is not None:
        out = [jax.ShapeDtypeStruct((3, tall // 3, width), bf16)] * len(lefts)
    return pl.pallas_call(
        functools.partial(fock_kernel, side, counts),
        out_shape=out,
        in_specs=[anywhere] * (sum(counts) + 1) + [vmem, pl.BlockSpec(memory_space=pltpu.SMEM)][: len(extra)],
        out_specs=vmem if before is None else [vmem] * len(lefts),
        scratch_shapes=[
            pltpu.VMEM((depth, len(lefts) * width), bf16),
            pltpu.VMEM(right.shape[1:], bf16),
            pltpu.VMEM((tall, depth), bf16),
            pltpu.SemaphoreType.DMA((sum(counts),)),
            pltpu.SemaphoreType.DMA(()),
        ],
        compiler_params=params(40),
        cost_estimate=pl.CostEstimate(
            flops=2 * len(lefts) * depth * width * tall, bytes_accessed=2 * len(lefts) * depth * width, transcendentals=0
        ),
        name="fock",
    )(right, *[piece for pieces in lefts for piece in pieces], *extra)


def root_kernel(levels, meta, *refs):
    pieces, (offset, root, whole, rows_f, cols_b, sems) = refs[:-6], refs[-6:]
    level, pair, orb = meta[0], meta[1], meta[2]
    coarse, width = offset.shape
    side = whole.shape[0]
    groups = side // width
    copies = []
    for piece, (z, y, q) in zip(pieces, piece_places(levels)):
        for i in range(len(z)):
            start = ((orb ^ q) * PAIR + (pair ^ y)) * coarse
            rows = pl.ds(pl.multiple_of(start, coarse), coarse)
            lanes = pl.ds(pl.multiple_of((level ^ z[i]) * width, width), width)
            copies.append(
                pltpu.make_async_copy(
                    piece.at[i * coarse : (i + 1) * coarse], whole.at[rows, lanes], sems.at[len(copies)]
                )
            )
    for copy in copies:
        copy.start()
    for copy in copies:
        copy.wait()
    row0 = pl.multiple_of((level * PAIR + pair) * coarse, coarse)
    own_lanes = pl.ds(pl.multiple_of(orb * width, width), width)
    rows = whole[pl.ds(row0, coarse), :]

    for j in range(groups):
        lanes = slice(j * width, (j + 1) * width)
        rows_f[:, lanes] = matmul(rows, whole[:, lanes])
    columns = whole[:, own_lanes]
    for i in range(groups):
        here = slice(i * width, (i + 1) * width)
        square = matmul(whole[here, :], columns)
        cols_b[here, :] = (0.25 * (whole[here, own_lanes].astype(f32) - square)).astype(bf16)
    left = (rows.astype(f32) - 0.25 * rows_f[...]).astype(bf16)
    value = matmul(left, cols_b[...]) + 0.125 * rows_f[:, own_lanes] - 0.5 * offset[...]
    row_ids = lax.broadcasted_iota(jnp.int32, value.shape, 0) + row0
    col_ids = lax.broadcasted_iota(jnp.int32, value.shape, 1) + orb * width
    root[...] = value + jnp.where(row_ids == col_ids, 1.0, 0.0)


def piece_places(levels):
    places = []
    for core in (0, 1):
        for half in range(2):
            z = [half * levels // 2 + i for i in range(levels // 2)]
            for second in (0, 1):
                for inner in (0, 1):
                    y, far = (second, inner) if half else (inner, second)
                    places.append((z, y, 2 * far + core))
    return places


def root_of(meta, pieces, offset, side, levels):
    coarse, width = offset.shape
    vmem, anywhere = pl.BlockSpec(memory_space=pltpu.VMEM), pl.BlockSpec(memory_space=pl.ANY)
    return pl.pallas_call(
        functools.partial(root_kernel, levels),
        out_shape=jax.ShapeDtypeStruct(offset.shape, f32),
        in_specs=[pl.BlockSpec(memory_space=pltpu.SMEM)] + [anywhere] * len(pieces) + [vmem],
        out_specs=vmem,
        scratch_shapes=[
            pltpu.VMEM((side, side), bf16),
            pltpu.VMEM((coarse, side), f32),
            pltpu.VMEM((side, width), bf16),
            pltpu.SemaphoreType.DMA((side // coarse * (side // width),)),
        ],
        compiler_params=params(40),
        cost_estimate=pl.CostEstimate(flops=side * side, bytes_accessed=side, transcendentals=0),
        name="root",
    )(meta, *pieces, offset)


def fill_tables(slots, levels, place_meta, facts, table, scale):
    level, pair = place_meta[0], place_meta[1]
    even = lax.rem(level, 2) == 0
    none = 6 * slots

    def place(slot_id):
        box = lax.div(slot_id, slots)
        apart = lax.div(box, PAIR) - level
        base = jnp.where(apart == 0, 0, jnp.where((apart < 0) == even, 4, 2))
        return (base + jnp.where(lax.rem(box, PAIR) != pair, 1, 0)) * slots + lax.rem(slot_id, slots)

    for index in range(4 * slots):
        group, r = divmod(index, slots)

        def fact(c):
            if group < 2:
                return facts[group, r, c]
            swap_id = jnp.where(even, 1, 0) if group == 2 else jnp.where(even, 0, 1)
            near_pair = 1 if group == 2 else 0
            return facts[2 + swap_id + jnp.where(pair == near_pair, 0, 2), r, c]

        box = (
            level * PAIR + pair,
            level * PAIR + 1 - pair,
            jnp.maximum(level * PAIR - 1, 0),
            jnp.minimum((level + 1) * PAIR, levels * PAIR - 1),
        )[group]
        there = (True, True, level > 0, level < levels - 1)[group]
        own_id = box * slots + r
        own_place = place(own_id)
        table[index, 0] = jnp.where((fact(7) > 0) & there, own_place, -1)
        for a in range(3):
            for k in (0, 2):
                distance = fact(2 * a + k // 2)
                target = place(jnp.maximum(own_id + distance, 0))
                target = jnp.where(distance < 16 * slots, target, none)
                table[index, 1 + 3 * a + k] = jnp.clip(target, 0, none)
            table[index, 2 + 3 * a] = own_place
        level_of = fact(6)
        scale[index] = jnp.where(level_of == 0, 0.5, jnp.where(level_of == 1, 1.0, 2.0))


def kinetic_kernel(edge, slots, levels, place_meta, facts, *refs):
    parts, refs = refs[:6], refs[6:]
    (fwd_in, fwd_out, back_in, back_mid, back_out), out, refs = refs[:5], refs[5], refs[6:]
    raw, x, outer, inner, total, total_fix, lines, columns, table, scale, sems = refs
    square = edge * edge
    own = PAIR * slots
    padded, width = x.shape[2:]
    copies = [pltpu.make_async_copy(part, raw.at[place], sems.at[place]) for place, part in enumerate(parts)]
    for copy in copies:
        copy.start()
    tail = padded - ROWS
    x[:, :, tail:, :] = jnp.zeros((x.shape[0], edge, ROWS, width), bf16)
    x[6 * slots] = jnp.zeros((edge, padded, width), bf16)
    total[...] = jnp.zeros_like(total)
    total_fix[...] = jnp.zeros_like(total_fix)
    fill_tables(slots, levels, place_meta, facts, table, scale)
    lines[...] = jnp.zeros_like(lines)
    for copy in copies:
        copy.wait()
    lanes = raw.shape[3]
    for t in range(own):
        for start in range(0, lines.shape[1], lanes):
            row = edge * square // 2 + 8 + 3 * (start // lanes)
            high, middle, low = (
                raw[t // slots, t % slots, row + i : row + i + 1, :].astype(f32) for i in range(3)
            )
            lines[t : t + 1, start : start + lanes] = (high + middle) + low
    columns[...] = lines[...].T

    def lay_out(place, carry):
        for slot in range(slots):
            for i in range(edge):
                part, row = i // (edge // 2), i % (edge // 2) * square
                x[place * slots + slot, i, :square, :] = raw[
                    place, slot, row : row + square, part * width : (part + 1) * width
                ]
        return carry

    lax.fori_loop(0, len(parts), lay_out, 0)
    chunks = -(-square // ROWS)

    def per_slot(s, carry):
        @pl.when(table[s, 0] >= 0)
        def _():
            own_scale = scale[s]
            half = 0.5 * own_scale
            sums = (total, total_fix)

            def split(exact):
                exact = own_scale * exact
                value = exact.astype(bf16).astype(f32)
                return (half * value).astype(bf16), (half * (value - exact)).astype(bf16)

            sources = [[table[s, 1 + 3 * a + k] for k in range(3)] for a in range(3)]
            here = sources[0][1]
            for a in range(3):

                @pl.when((here < own) | (sources[a][0] < own) | (sources[a][2] < own))
                def _():
                    if a == 0:
                        for i in range(chunks):
                            rows = slice(i * ROWS, (i + 1) * ROWS)
                            block = [x[t, :, rows, :].reshape(edge * ROWS, width) for t in sources[0]]
                            fields = split(matmul(fwd_out[...], jnp.concatenate(block, axis=0)))
                            for field in range(2):
                                outer[field, :, rows, :] = fields[field].reshape(edge, ROWS, width)
                    else:
                        for i in range(edge):
                            block = jnp.concatenate([x[t, i] for t in sources[a]], axis=0)
                            fields = split(matmul(fwd_in[a - 1], block))
                            for field in range(2):
                                inner[field, i, (a - 1) * padded : a * padded, :] = fields[field]

            def back_outer(k, target):
                for i in range(chunks):
                    rows = slice(i * ROWS, (i + 1) * ROWS)
                    for field in range(2):
                        term = matmul(back_out[k], outer[field, :, rows, :].reshape(edge * ROWS, width))
                        sums[field][target, :, rows, :] += term.reshape(edge, ROWS, width)

            for k in (0, 2):
                for a in range(3):
                    target = sources[a][k]

                    @pl.when(target < own)
                    def _():
                        if a == 0:
                            back_outer(k, target)
                        else:
                            for i in range(edge):
                                for field in range(2):
                                    here = inner[field, i, (a - 1) * padded : a * padded, :]
                                    sums[field][target, i] += matmul(back_in[a - 1, k], here)

            @pl.when(here < own)
            def _():
                back_outer(1, here)
                for i in range(edge):
                    for field in range(2):
                        sums[field][here, i] += matmul(back_mid[...], inner[field, i])

        return carry

    lax.fori_loop(0, table.shape[0], per_slot, 0)

    for t in range(own):
        for i in range(edge):
            rows = slice(i * square, (i + 1) * square)
            weighted = (columns[rows, t : t + 1] * x[t, i, :square, :].astype(f32)).astype(bf16)
            whole = total[t, i, :square, :] + weighted.astype(f32)
            top = whole.astype(bf16)
            low = (whole - top.astype(f32)).astype(bf16)
            fix = total_fix[t, i, :square, :].astype(bf16)
            out[t, rows, :] = jnp.concatenate([top, low, fix], axis=1)


def matrices_kernel(stacked, blocks, *refs):
    spots, outs = refs[:9], refs[9:]
    fwd_in, fwd_out, back_in, back_mid, back_out = outs
    for mode in range(3):
        spot, spread, same = spots[3 * mode : 3 * mode + 3]
        wide = matmul(matmul(spot[...], stacked[...]).astype(bf16), spread[...])
        wide = (wide * jnp.concatenate([same[...]] * 3, axis=1)).astype(bf16)
        if mode == 2:
            fwd_out[...] = wide
        else:
            fwd_in[mode] = wide
        for k in range(3):
            turned = lax.dot_general(spot[...], blocks[k], (((1,), (1,)), ((), ())), preferred_element_type=f32)
            turned = lax.dot_general(
                turned.astype(bf16), spot[...], (((1,), (1,)), ((), ())), preferred_element_type=f32
            )
            turned = (turned * same[...]).astype(bf16)
            if mode == 2:
                back_out[k] = turned
            else:
                back_in[mode, k] = turned
    back_mid[...] = jnp.concatenate([back_in[0, 1], back_in[1, 1]], axis=1)


def block_matrices(deriv_blocks):
    edge = deriv_blocks.shape[1]
    square = edge * edge
    padded = -(-square // ROWS) * ROWS
    tall = edge * ROWS
    ids = np.arange(padded)
    slow = ((ids[:, None] // edge) == np.arange(edge)).astype(np.float32)
    fast = (((ids[:, None] % edge) == np.arange(edge)) & (ids[:, None] < square)).astype(np.float32)
    ids = np.arange(tall)
    outer = ((ids[:, None] // ROWS) == np.arange(edge)).astype(np.float32)
    within = ((ids[:, None] % ROWS) == np.arange(ROWS)).astype(np.float32)
    stacked = jnp.moveaxis(deriv_blocks, 0, 1).reshape(edge, 3 * edge)
    constants = []
    for spot, mask in ((slow, fast), (fast, slow), (outer, within)):
        spread = np.kron(np.eye(3, dtype=np.float32), spot.T)
        constants += [jnp.asarray(spot, bf16), jnp.asarray(spread, bf16), jnp.asarray(mask @ mask.T, f32)]
    vmem = pl.BlockSpec(memory_space=pltpu.VMEM)
    shapes = [(2, padded, 3 * padded), (tall, 3 * tall), (2, 3, padded, padded), (padded, 2 * padded), (3, tall, tall)]
    return pl.pallas_call(
        matrices_kernel,
        out_shape=[jax.ShapeDtypeStruct(shape, bf16) for shape in shapes],
        in_specs=[vmem] * 11,
        out_specs=[vmem] * 5,
        compiler_params=params(24),
        name="matrices",
    )(stacked, deriv_blocks, *constants)


def kinetic(parts, place_meta, facts, matrices, edge, coefficients, levels):
    slots, folded, lanes = parts[0].shape
    width = lanes // 2
    padded = matrices[0].shape[1]
    own = PAIR * slots
    vmem = pl.BlockSpec(memory_space=pltpu.VMEM)
    smem = pl.BlockSpec(memory_space=pltpu.SMEM)
    anywhere = pl.BlockSpec(memory_space=pl.ANY)
    return pl.pallas_call(
        functools.partial(kinetic_kernel, edge, slots, levels),
        out_shape=jax.ShapeDtypeStruct((own, coefficients, 3 * width), bf16),
        in_specs=[smem] * 2 + [anywhere] * 6 + [vmem] * 5,
        out_specs=vmem,
        scratch_shapes=[
            pltpu.VMEM((6, slots, folded, lanes), bf16),
            pltpu.VMEM((6 * slots + 1, edge, padded, width), bf16),
            pltpu.VMEM((2, edge, padded, width), bf16),
            pltpu.VMEM((2, edge, 2 * padded, width), bf16),
            pltpu.VMEM((own, edge, padded, width), f32),
            pltpu.VMEM((own, edge, padded, width), f32),
            pltpu.VMEM((own + -own % 8, coefficients + -coefficients % lanes), f32),
            pltpu.VMEM((coefficients + -coefficients % lanes, own + -own % 8), f32),
            pltpu.SMEM((4 * slots, 10), jnp.int32),
            pltpu.SMEM((4 * slots,), f32),
            pltpu.SemaphoreType.DMA((6,)),
        ],
        compiler_params=params(48),
        cost_estimate=pl.CostEstimate(flops=2 * 10**10, bytes_accessed=40 * 10**6, transcendentals=0),
        name="kinetic",
    )(place_meta, facts, *parts, *matrices)


def offset_sum_kernel(meta, *refs):
    blocks, (small, kept, sent) = refs[:-3], refs[-3:]
    total = blocks[0][...].astype(f32)
    for block in blocks[1:]:
        total = total + block[...].astype(f32)
    small[...] = total.astype(bf16)
    half = kept.shape[0]
    first = meta[0] == 0
    low, high = total[:, :half].T, total[:, half:].T
    kept[...] = jnp.where(first, low, high)
    sent[...] = jnp.where(first, high, low)


def fock_sum_kernel(meta, *refs):
    blocks, (share, kept, sent) = refs[:-3], refs[-3:]
    sums = [sum((block[part].astype(f32) for block in blocks[1:]), blocks[0][part].astype(f32)) for part in range(3)]
    main = sums[0] + sums[1]
    share[...] = sums[2].astype(bf16)
    half = kept.shape[0]
    first = meta[0] == 0
    low, high = main[:, :half].T, main[:, half:].T
    kept[...] = jnp.where(first, low, high)
    sent[...] = jnp.where(first, high, low)


def level_sum(kernel, meta, blocks):
    tall, width = blocks[0].shape[-2:]
    vmem = pl.BlockSpec(memory_space=pltpu.VMEM)
    turned = jax.ShapeDtypeStruct((width // PAIR, tall), f32)
    return pl.pallas_call(
        kernel,
        out_shape=[jax.ShapeDtypeStruct((tall, width), bf16), turned, turned],
        in_specs=[pl.BlockSpec(memory_space=pltpu.SMEM)] + [vmem] * len(blocks),
        out_specs=[vmem] * 3,
        compiler_params=params(24),
        name="level_sum",
    )(meta, *blocks)


def body(orbitals, potential, deriv_blocks, levels, box_counts, neighbours):
    slots, coefficients, own_width = orbitals.shape
    edge = deriv_blocks.shape[1]
    level, pair, orb = lax.axis_index("lvl"), lax.axis_index("pair"), lax.axis_index("orb")
    level_count, orb_count = lax.axis_size("lvl"), lax.axis_size("orb")
    half, fold = own_width // PAIR, coefficients // 2
    all_width = own_width * orb_count
    box_rows = all_width // (level_count * PAIR)
    first = pair == 0
    groups = range(orb_count)
    square_grid = level_count == orb_count == 4 and box_rows == half
    row0, col0 = (level * PAIR + pair) * box_rows, orb * own_width

    own_base = (level * PAIR + pair) * slots
    pack_meta = jnp.stack([pair, box_counts[0], own_base]).astype(jnp.int32)
    theirs, mine = pack(pack_meta, neighbours, levels, orbitals, potential)
    active = orbitals

    meta = jnp.stack([pair, box_counts[0] * coefficients]).astype(jnp.int32)
    near_active = swap(active, "orb", 1)
    flat = lambda block: block.reshape(-1, block.shape[-1])
    early_blocks, own_turned = early_correlation(meta, [flat(active), flat(near_active)], half)

    far = {q: swap(active, "orb", q) for q in groups if q and q % 2 == 0}
    beside = swap(theirs, "pair", 1)
    first_mine, second_mine = trade(mine, "lvl", 0), trade(mine, "lvl", 1)
    later_mine, beside = lax.optimization_barrier((mine, beside))
    beside_rest = swap(later_mine, "pair", 1)
    first_beside, second_beside = trade(beside, "lvl", 0), trade(beside, "lvl", 1)

    matrices = block_matrices(deriv_blocks)

    def facts_of(parts):
        return jnp.stack([part[:, fold, :8] for part in parts]).astype(f32).astype(jnp.int32)

    early_facts = facts_of([mine, beside, first_mine, second_mine])
    cut = -(-slots * coefficients // (2 * ROWS)) * ROWS
    beside_all, beside_top = unfold(pack_meta, beside, beside_rest, fold, cut)

    parts = [mine, beside, first_mine, first_beside, second_mine, second_beside]
    far, early_blocks, parts, beside_all, beside_top, matrices, early_facts = lax.optimization_barrier(
        (far, early_blocks, parts, beside_all, beside_top, matrices, early_facts)
    )
    facts = jnp.concatenate([early_facts, facts_of([parts[3], parts[5]])])
    cross = {q: [swap(beside_top, "orb", q), swap(flat(far[q])[cut:], "pair", 1)] for q in far}
    left_own = {0: active, 1: near_active, **far}
    left_beside = {0: [beside_all], 1: [swap(beside_all, "orb", 1)]}
    for q in far:
        left_own[q + 1] = swap(far[q], "orb", 1)

    def natural(blocks):
        return jnp.concatenate([lax.dynamic_index_in_dim(blocks, orb ^ j, keepdims=False) for j in groups], axis=1)

    def along_levels(blocks):
        mine_block = lambda target: lax.dynamic_index_in_dim(blocks, orb ^ target, keepdims=False)
        steps = range(1, level_count)
        return [mine_block(level)] + [swap(mine_block(level ^ step), "lvl", step) for step in steps]

    def both_halves(kept, got):
        return jnp.concatenate([jnp.where(first, kept, got), jnp.where(first, got, kept)], axis=1)

    def own_block(strip):
        strip = lax.all_gather(lax.psum(strip, "lvl"), ("orb", "pair"), axis=0, tiled=True)
        strip = lax.dynamic_slice_in_dim(strip, row0, box_rows, axis=0)
        return lax.dynamic_slice_in_dim(strip, col0, own_width, axis=1)


    place_meta = jnp.stack([level, pair]).astype(jnp.int32)
    right = kinetic(parts, place_meta, facts, matrices, edge, coefficients, level_count)

    cross, right, meta = lax.optimization_barrier((cross, right, meta))
    lefts_own = [[flat(left_own[q])] for q in groups]
    lefts_beside = dict(left_beside)
    for q in far:
        lefts_beside[q] = list(cross[q])
        lefts_beside[q + 1] = [swap(piece, "orb", 1) for piece in cross[q]]
    lefts_beside = [lefts_beside[q] for q in groups]

    share = 1.0 / level_count
    blocks = late_correlation(share, meta, lefts_own[2:], lefts_beside, early_blocks, own_turned)
    right = right.reshape(2, slots * coefficients, 3 * half)
    fock_part = box_fock(0, lefts_own, right, None, None)
    if square_grid:
        sent = along_levels(blocks)
        sent, fock_part = lax.optimization_barrier((sent, fock_part))
        small, kept, other = level_sum(offset_sum_kernel, meta, sent)
        offset = both_halves(kept, swap(other, "pair", 1))
    else:
        offset = own_block(natural(blocks).astype(f32))
    row_ids = row0 + jnp.arange(box_rows, dtype=jnp.int32)
    col_ids = col0 + jnp.arange(own_width, dtype=jnp.int32)
    correlation = offset + (row_ids[:, None] == col_ids[None, :]).astype(f32)
    apart = (orb ^ level if square_grid else 0 * orb).reshape(1).astype(jnp.int32)
    fock_blocks = box_fock(1, lefts_beside, right, fock_part, apart)
    if square_grid:
        pieces = [small] + [swap(small, "lvl", z) for z in range(1, level_count)]
        pieces, fock_blocks, offset = lax.optimization_barrier((pieces, fock_blocks, offset))
        join = functools.partial(jnp.concatenate, axis=0)
        top, low = join(pieces[: level_count // 2]), join(pieces[level_count // 2 :])
        sent = [fock_blocks[0]] + [swap(fock_blocks[step], "lvl", step) for step in range(1, level_count)]
        got = [swap(top, "pair", 1), swap(low, "orb", 2)]
        got, sent[:2] = lax.optimization_barrier((got, sent[:2]))
        tops, lows = [top, got[0]], [low, got[1]]
        pieces = tops + [swap(piece, "orb", 2) for piece in tops] + lows + [swap(piece, "pair", 1) for piece in lows]
        pieces, sent[:3] = lax.optimization_barrier((pieces, sent[:3]))
        pieces += [swap(piece, "orb", 1) for piece in pieces]
        root_meta = jnp.stack([level, pair, orb]).astype(jnp.int32)
        inverse_root = root_of(root_meta, pieces, offset, all_width, level_count)
        inverse_root, sent = lax.optimization_barrier((inverse_root, sent))
        share, kept, other = level_sum(fock_sum_kernel, meta, sent)
        to = [
            ((z * PAIR + y) * orb_count + o, (o * PAIR + y) * orb_count + z)
            for z in range(level_count)
            for y in range(PAIR)
            for o in groups
        ]
        got = swap(other, "pair", 1), lax.ppermute(share, BOX + ("orb",), to)
        fock = both_halves(kept, got[0]) + got[1].astype(f32)
    else:
        fock_blocks = jnp.stack(fock_blocks)
        main = natural(fock_blocks[:, 0]).astype(f32) + natural(fock_blocks[:, 1]).astype(f32)
        main = lax.all_gather(lax.psum(main, "lvl"), "pair", axis=0, tiled=True)
        fock = lax.dynamic_slice_in_dim(main, row0, box_rows, axis=1).T + own_block(natural(fock_blocks[:, 2]).astype(f32))
        gathered = lax.all_gather(offset.astype(bf16), "orb", axis=1, tiled=True)
        whole = lax.all_gather(gathered, BOX, axis=0, tiled=True)
        rows_of = lax.dynamic_slice_in_dim(whole, row0, box_rows, axis=0)
        cols_of = lax.dynamic_slice_in_dim(whole, col0, own_width, axis=1)
        row_square, col_square = matmul(rows_of, whole), matmul(whole, cols_of)
        left = (rows_of.astype(f32) - 0.25 * row_square).astype(bf16)
        right_side = (0.25 * (cols_of.astype(f32) - col_square)).astype(bf16)
        own_square = lax.dynamic_slice_in_dim(row_square, col0, own_width, axis=1)
        inverse_root = correlation - 1.5 * offset + 0.125 * own_square + matmul(left, right_side)
    return fock, correlation, inverse_root


def solution(mesh):
    levels = mesh.shape["box"] // PAIR
    split = Mesh(mesh.devices.reshape(levels, PAIR, mesh.shape["orb"]), ("lvl", "pair", "orb"))
    in_specs = (P(BOX, None, "orb"), P(BOX, None), P(), P(BOX), P(BOX), P(BOX, None, None))
    out_specs = (P(BOX, "orb"),) * 3
    return jax.shard_map(body, mesh=split, in_specs=in_specs, out_specs=out_specs, check_vma=False)
```

```python
import functools

import jax
import jax.numpy as jnp
import numpy as np
from jax import lax
from jax.experimental import pallas as pl
from jax.experimental.pallas import tpu as pltpu
from jax.sharding import Mesh, PartitionSpec as P

PAIR = 2
ROWS = 16
BOX = ("lvl", "pair")
f32, bf16 = jnp.float32, jnp.bfloat16


def swap(value, axis, bit):
    count = lax.axis_size(axis)
    return lax.ppermute(value, axis, [(i, i ^ bit) for i in range(count)])


def trade(value, axis, start):
    pairs = [(i, i + 1) for i in range(start, lax.axis_size(axis) - 1, 2)]
    return lax.ppermute(value, axis, pairs + [(b, a) for a, b in pairs])


def matmul(left, right):
    return jnp.dot(left, right, preferred_element_type=f32)


def params(mebibytes):
    return pltpu.CompilerParams(vmem_limit_bytes=mebibytes * 1024 * 1024)


def pack_kernel(meta, neighbours, levels, orbitals, pot, theirs, mine):
    slots, coefficients, width = orbitals.shape
    half, fold = width // PAIR, coefficients // 2
    first = meta[0] == 0
    place = lax.broadcasted_iota(jnp.int32, (8, width), 1)
    for slot in range(slots):
        keep = slot < meta[1]
        for part in range(2):
            here = orbitals[slot, part * fold : (part + 1) * fold, :]
            here = jnp.where(keep, here, jnp.zeros_like(here))
            low, high = here[:, :half], here[:, half:]
            lanes = slice(part * half, (part + 1) * half)
            theirs[slot, :fold, lanes] = jnp.where(first, high, low)
            mine[slot, :fold, lanes] = jnp.where(first, low, high)
        own_id = meta[2] + slot
        facts = jnp.where(place == 6, levels[slot], jnp.where(place == 7, jnp.where(keep, 1, 0), 0))
        for c in range(6):
            target = neighbours[slot, c // 2, c % 2]
            facts = jnp.where(place == c, jnp.where(target >= 0, target - own_id, 16 * slots), facts)
        facts = facts.astype(f32).astype(bf16)
        for packed in (theirs, mine):
            packed[slot, fold : fold + 8, :] = facts
        row = fold + 8
        for start in range(0, pot.shape[1], width):
            stop = min(start + width, pot.shape[1])
            exact = pot[slot : slot + 1, start:stop]
            for _ in range(3):
                part = exact.astype(bf16)
                exact = exact - part.astype(f32)
                for packed in (theirs, mine):
                    packed[slot, row : row + 1, : stop - start] = part
                    if stop - start < width:
                        packed[slot, row : row + 1, stop - start :] = jnp.zeros((1, width - stop + start), bf16)
                row += 1
        for packed in (theirs, mine):
            packed[slot, row:, :] = jnp.zeros((packed.shape[1] - row, width), bf16)


def pack(meta, neighbours, levels, orbitals, pot):
    slots, coefficients, width = orbitals.shape
    fold = coefficients // 2
    padded = -(-(fold + 8 + 3 * -(-coefficients // width)) // ROWS) * ROWS
    vmem, smem = pl.BlockSpec(memory_space=pltpu.VMEM), pl.BlockSpec(memory_space=pltpu.SMEM)
    return pl.pallas_call(
        pack_kernel,
        out_shape=[jax.ShapeDtypeStruct((slots, padded, width), bf16)] * 2,
        in_specs=[smem, smem, smem, vmem, vmem],
        out_specs=[vmem, vmem],
        compiler_params=params(24),
        name="pack",
    )(meta, neighbours, levels, orbitals, pot)


def unfold_kernel(fold, meta, beside_in, rest_in, whole, top, beside, rest, sems):
    copies = [
        pltpu.make_async_copy(source, target, sems.at[i])
        for i, (source, target) in enumerate(((beside_in, beside), (rest_in, rest)))
    ]
    for copy in copies:
        copy.start()
    slots, _, width = beside.shape
    half = width // PAIR
    first = meta[0] == 0
    for copy in copies:
        copy.wait()
    for slot in range(slots):
        for part in range(2):
            lanes = slice(part * half, (part + 1) * half)
            near, far = beside[slot, :fold, lanes], rest[slot, :fold, lanes]
            start = (2 * slot + part) * fold
            here = jnp.concatenate([jnp.where(first, near, far), jnp.where(first, far, near)], axis=1)
            whole[start : start + fold, :] = here
    top[...] = whole[: top.shape[0], :]


def unfold(meta, beside, rest, fold, cut):
    slots, _, width = beside.shape
    vmem = pl.BlockSpec(memory_space=pltpu.VMEM)
    return pl.pallas_call(
        functools.partial(unfold_kernel, fold),
        out_shape=[
            jax.ShapeDtypeStruct((2 * slots * fold, width), bf16),
            jax.ShapeDtypeStruct((cut, width), bf16),
        ],
        in_specs=[pl.BlockSpec(memory_space=pltpu.SMEM)] + [pl.BlockSpec(memory_space=pl.ANY)] * 2,
        out_specs=[vmem, vmem],
        scratch_shapes=[
            pltpu.VMEM(beside.shape, bf16),
            pltpu.VMEM(beside.shape, bf16),
            pltpu.SemaphoreType.DMA((2,)),
        ],
        compiler_params=params(24),
        name="unfold",
    )(meta, beside, rest)


def load_left(lefts, held, sems):
    copies = []
    for q, pieces in enumerate(lefts):
        row = 0
        for piece in pieces:
            rows, width = piece.shape
            here = held.at[row : row + rows, q * width : (q + 1) * width]
            copies.append(pltpu.make_async_copy(piece, here, sems.at[len(copies)]))
            row += rows
    for copy in copies:
        copy.start()
    return copies


def grouped(refs, counts):
    refs = list(refs)
    return [[refs.pop(0) for _ in range(count)] for count in counts]


def correlation_kernel(share, counts, meta, *refs):
    refs, (out, held, turned, sems) = refs[:-4], refs[-4:]
    groups, half, width = out.shape
    lefts, before = grouped(refs, counts), refs[sum(counts) :]
    copies = load_left(lefts, held, sems)
    first = meta[0] == 0
    for copy in copies[: counts[0]]:
        copy.wait()
    own = held[:, :width]
    own = jnp.where(first, own[:, :half], own[:, half:]).T
    live = lax.broadcasted_iota(jnp.int32, own.shape, 1) < meta[1 if before else 2]
    turned[...] = jnp.where(live, own, jnp.zeros_like(own))
    for base in range(0, groups, 2):
        for copy in copies[max(sum(counts[:base]), counts[0]) : sum(counts[: base + 2])]:
            copy.wait()
        wide = matmul(turned[...], held[:, base * width : (base + 2) * width])
        for q in (base, base + 1):
            total = wide[:, (q - base) * width : (q - base + 1) * width]
            if before:
                total = total + before[0][q]
                if q == 0:
                    rows = lax.broadcasted_iota(jnp.int32, (half, width), 0) + jnp.where(first, 0, half)
                    columns = lax.broadcasted_iota(jnp.int32, (half, width), 1)
                    total = total - jnp.where(rows == columns, share, 0.0)
            out[q] = total.astype(out.dtype)


def box_correlation(share, meta, lefts, before, half):
    depth, width = sum(piece.shape[0] for piece in lefts[0]), lefts[0][0].shape[1]
    counts = [len(pieces) for pieces in lefts]
    vmem = pl.BlockSpec(memory_space=pltpu.VMEM)
    extra = [] if before is None else [before]
    return pl.pallas_call(
        functools.partial(correlation_kernel, share, counts),
        out_shape=jax.ShapeDtypeStruct((len(lefts), half, width), f32 if before is None else bf16),
        in_specs=[pl.BlockSpec(memory_space=pltpu.SMEM)]
        + [pl.BlockSpec(memory_space=pl.ANY)] * sum(counts)
        + [vmem] * len(extra),
        out_specs=vmem,
        scratch_shapes=[
            pltpu.VMEM((depth, len(lefts) * width), bf16),
            pltpu.VMEM((half, depth), bf16),
            pltpu.SemaphoreType.DMA((sum(counts),)),
        ],
        compiler_params=params(32),
        cost_estimate=pl.CostEstimate(
            flops=2 * len(lefts) * depth * width * half, bytes_accessed=2 * len(lefts) * depth * width, transcendentals=0
        ),
        name="correlation",
    )(meta, *[piece for pieces in lefts for piece in pieces], *extra)


def fock_kernel(side, counts, right, *refs):
    outs, (held, raw, turned, sems, last_sem) = refs[sum(counts) : -5], refs[-5:]
    lefts = grouped(refs, counts)
    before, apart, outs = (None, None, outs) if len(outs) == 1 else (outs[0], outs[1], outs[2:])
    out = outs[0]
    last = pltpu.make_async_copy(right.at[side], raw, last_sem)
    last.start()
    copies = load_left(lefts, held, sems)
    half, width = out.shape[-2] // (3 if before is None else 1), out.shape[-1]
    last.wait()
    turned[...] = raw[...].T
    for base in range(0, len(lefts), 2):
        for copy in copies[sum(counts[:base]) : sum(counts[: base + 2])]:
            copy.wait()
        wide = matmul(turned[...], held[:, base * width : (base + 2) * width])
        for q in (base, base + 1):
            total = wide[:, (q - base) * width : (q - base + 1) * width]
            if before is None:
                out[q] = total
                continue
            total = total + before[q]
            main = total[:half] + total[half : 2 * half]
            top = main.astype(bf16)
            parts = (top, (main - top.astype(f32)).astype(bf16), total[2 * half :].astype(bf16))

            def store(target):
                for i in range(3):
                    target[i] = parts[i]

            for distance, target in enumerate(outs):
                pl.when(q ^ apart[0] == distance)(functools.partial(store, target))


def box_fock(side, lefts, right, before, apart):
    depth, width = sum(piece.shape[0] for piece in lefts[0]), lefts[0][0].shape[1]
    counts = [len(pieces) for pieces in lefts]
    tall = right.shape[-1]
    anywhere, vmem = pl.BlockSpec(memory_space=pl.ANY), pl.BlockSpec(memory_space=pltpu.VMEM)
    extra = [] if before is None else [before, apart]
    out = jax.ShapeDtypeStruct((len(lefts), tall, width), f32)
    if before is not None:
        out = [jax.ShapeDtypeStruct((3, tall // 3, width), bf16)] * len(lefts)
    return pl.pallas_call(
        functools.partial(fock_kernel, side, counts),
        out_shape=out,
        in_specs=[anywhere] * (sum(counts) + 1) + [vmem, pl.BlockSpec(memory_space=pltpu.SMEM)][: len(extra)],
        out_specs=vmem if before is None else [vmem] * len(lefts),
        scratch_shapes=[
            pltpu.VMEM((depth, len(lefts) * width), bf16),
            pltpu.VMEM(right.shape[1:], bf16),
            pltpu.VMEM((tall, depth), bf16),
            pltpu.SemaphoreType.DMA((sum(counts),)),
            pltpu.SemaphoreType.DMA(()),
        ],
        compiler_params=params(40),
        cost_estimate=pl.CostEstimate(
            flops=2 * len(lefts) * depth * width * tall, bytes_accessed=2 * len(lefts) * depth * width, transcendentals=0
        ),
        name="fock",
    )(right, *[piece for pieces in lefts for piece in pieces], *extra)


def root_kernel(levels, meta, *refs):
    pieces, (offset, root, whole, rows_f, cols_b, sems) = refs[:-6], refs[-6:]
    level, pair, orb = meta[0], meta[1], meta[2]
    coarse, width = offset.shape
    side = whole.shape[0]
    groups = side // width
    copies = []
    for piece, (z, y, q) in zip(pieces, piece_places(levels)):
        for i in range(len(z)):
            start = ((orb ^ q) * PAIR + (pair ^ y)) * coarse
            rows = pl.ds(pl.multiple_of(start, coarse), coarse)
            lanes = pl.ds(pl.multiple_of((level ^ z[i]) * width, width), width)
            copies.append(
                pltpu.make_async_copy(
                    piece.at[i * coarse : (i + 1) * coarse], whole.at[rows, lanes], sems.at[len(copies)]
                )
            )
    for copy in copies:
        copy.start()
    for copy in copies:
        copy.wait()
    row0 = pl.multiple_of((level * PAIR + pair) * coarse, coarse)
    own_lanes = pl.ds(pl.multiple_of(orb * width, width), width)
    rows = whole[pl.ds(row0, coarse), :]

    for j in range(groups):
        lanes = slice(j * width, (j + 1) * width)
        rows_f[:, lanes] = matmul(rows, whole[:, lanes])
    columns = whole[:, own_lanes]
    for i in range(groups):
        here = slice(i * width, (i + 1) * width)
        square = matmul(whole[here, :], columns)
        cols_b[here, :] = (0.25 * (whole[here, own_lanes].astype(f32) - square)).astype(bf16)
    left = (rows.astype(f32) - 0.25 * rows_f[...]).astype(bf16)
    value = matmul(left, cols_b[...]) + 0.125 * rows_f[:, own_lanes] - 0.5 * offset[...]
    row_ids = lax.broadcasted_iota(jnp.int32, value.shape, 0) + row0
    col_ids = lax.broadcasted_iota(jnp.int32, value.shape, 1) + orb * width
    root[...] = value + jnp.where(row_ids == col_ids, 1.0, 0.0)


def piece_places(levels):
    places = []
    for core in (0, 1):
        for half in range(2):
            z = [half * levels // 2 + i for i in range(levels // 2)]
            for second in (0, 1):
                for inner in (0, 1):
                    y, far = (second, inner) if half else (inner, second)
                    places.append((z, y, 2 * far + core))
    return places


def root_of(meta, pieces, offset, side, levels):
    coarse, width = offset.shape
    vmem, anywhere = pl.BlockSpec(memory_space=pltpu.VMEM), pl.BlockSpec(memory_space=pl.ANY)
    return pl.pallas_call(
        functools.partial(root_kernel, levels),
        out_shape=jax.ShapeDtypeStruct(offset.shape, f32),
        in_specs=[pl.BlockSpec(memory_space=pltpu.SMEM)] + [anywhere] * len(pieces) + [vmem],
        out_specs=vmem,
        scratch_shapes=[
            pltpu.VMEM((side, side), bf16),
            pltpu.VMEM((coarse, side), f32),
            pltpu.VMEM((side, width), bf16),
            pltpu.SemaphoreType.DMA((side // coarse * (side // width),)),
        ],
        compiler_params=params(40),
        cost_estimate=pl.CostEstimate(flops=16 * side * side * width, bytes_accessed=4 * side * side, transcendentals=0),
        name="root",
    )(meta, *pieces, offset)


def fill_tables(slots, levels, place_meta, facts, table, scale):
    level, pair = place_meta[0], place_meta[1]
    even = lax.rem(level, 2) == 0
    none = 6 * slots

    def place(slot_id):
        box = lax.div(slot_id, slots)
        apart = lax.div(box, PAIR) - level
        base = jnp.where(apart == 0, 0, jnp.where((apart < 0) == even, 4, 2))
        return (base + jnp.where(lax.rem(box, PAIR) != pair, 1, 0)) * slots + lax.rem(slot_id, slots)

    for index in range(4 * slots):
        group, r = divmod(index, slots)

        def fact(c):
            if group < 2:
                return facts[group, r, c]
            swap_id = jnp.where(even, 1, 0) if group == 2 else jnp.where(even, 0, 1)
            near_pair = 1 if group == 2 else 0
            return facts[2 + swap_id + jnp.where(pair == near_pair, 0, 2), r, c]

        box = (
            level * PAIR + pair,
            level * PAIR + 1 - pair,
            jnp.maximum(level * PAIR - 1, 0),
            jnp.minimum((level + 1) * PAIR, levels * PAIR - 1),
        )[group]
        there = (True, True, level > 0, level < levels - 1)[group]
        own_id = box * slots + r
        own_place = place(own_id)
        table[index, 0] = jnp.where((fact(7) > 0) & there, own_place, -1)
        for a in range(3):
            for k in (0, 2):
                distance = fact(2 * a + k // 2)
                target = place(jnp.maximum(own_id + distance, 0))
                target = jnp.where(distance < 16 * slots, target, none)
                table[index, 1 + 3 * a + k] = jnp.clip(target, 0, none)
            table[index, 2 + 3 * a] = own_place
        level_of = fact(6)
        scale[index] = jnp.where(level_of == 0, 0.5, jnp.where(level_of == 1, 1.0, 2.0))


def kinetic_kernel(edge, slots, levels, place_meta, facts, *refs):
    parts, refs = refs[:6], refs[6:]
    (fwd_in, fwd_out, back_in, back_mid, back_out), out, refs = refs[:5], refs[5], refs[6:]
    raw, x, outer, inner, total, total_fix, lines, columns, table, scale, sems = refs
    square = edge * edge
    own = PAIR * slots
    padded, width = x.shape[2:]
    copies = [pltpu.make_async_copy(part, raw.at[place], sems.at[place]) for place, part in enumerate(parts)]
    for copy in copies:
        copy.start()
    tail = padded - ROWS
    x[:, :, tail:, :] = jnp.zeros((x.shape[0], edge, ROWS, width), bf16)
    x[6 * slots] = jnp.zeros((edge, padded, width), bf16)
    total[...] = jnp.zeros_like(total)
    total_fix[...] = jnp.zeros_like(total_fix)
    fill_tables(slots, levels, place_meta, facts, table, scale)
    lines[...] = jnp.zeros_like(lines)
    for copy in copies:
        copy.wait()
    lanes = raw.shape[3]
    for t in range(own):
        for start in range(0, lines.shape[1], lanes):
            row = edge * square // 2 + 8 + 3 * (start // lanes)
            high, middle, low = (
                raw[t // slots, t % slots, row + i : row + i + 1, :].astype(f32) for i in range(3)
            )
            lines[t : t + 1, start : start + lanes] = (high + middle) + low
    columns[...] = lines[...].T

    def lay_out(place, carry):
        for slot in range(slots):
            for i in range(edge):
                part, row = i // (edge // 2), i % (edge // 2) * square
                x[place * slots + slot, i, :square, :] = raw[
                    place, slot, row : row + square, part * width : (part + 1) * width
                ]
        return carry

    lax.fori_loop(0, len(parts), lay_out, 0)
    chunks = -(-square // ROWS)

    def per_slot(s, carry):
        @pl.when(table[s, 0] >= 0)
        def _():
            own_scale = scale[s]
            half = 0.5 * own_scale
            sums = (total, total_fix)

            def split(exact):
                exact = own_scale * exact
                value = exact.astype(bf16).astype(f32)
                return (half * value).astype(bf16), (half * (value - exact)).astype(bf16)

            sources = [[table[s, 1 + 3 * a + k] for k in range(3)] for a in range(3)]
            here = sources[0][1]
            for a in range(3):

                @pl.when((here < own) | (sources[a][0] < own) | (sources[a][2] < own))
                def _():
                    if a == 0:
                        for i in range(chunks):
                            rows = slice(i * ROWS, (i + 1) * ROWS)
                            block = [x[t, :, rows, :].reshape(edge * ROWS, width) for t in sources[0]]
                            fields = split(matmul(fwd_out[...], jnp.concatenate(block, axis=0)))
                            for field in range(2):
                                outer[field, :, rows, :] = fields[field].reshape(edge, ROWS, width)
                    else:
                        for i in range(edge):
                            block = jnp.concatenate([x[t, i] for t in sources[a]], axis=0)
                            fields = split(matmul(fwd_in[a - 1], block))
                            for field in range(2):
                                inner[field, i, (a - 1) * padded : a * padded, :] = fields[field]

            def back_outer(k, target):
                for i in range(chunks):
                    rows = slice(i * ROWS, (i + 1) * ROWS)
                    for field in range(2):
                        term = matmul(back_out[k], outer[field, :, rows, :].reshape(edge * ROWS, width))
                        sums[field][target, :, rows, :] += term.reshape(edge, ROWS, width)

            for k in (0, 2):
                for a in range(3):
                    target = sources[a][k]

                    @pl.when(target < own)
                    def _():
                        if a == 0:
                            back_outer(k, target)
                        else:
                            for i in range(edge):
                                for field in range(2):
                                    here = inner[field, i, (a - 1) * padded : a * padded, :]
                                    sums[field][target, i] += matmul(back_in[a - 1, k], here)

            @pl.when(here < own)
            def _():
                back_outer(1, here)
                for i in range(edge):
                    for field in range(2):
                        sums[field][here, i] += matmul(back_mid[...], inner[field, i])

        return carry

    lax.fori_loop(0, table.shape[0], per_slot, 0)

    for t in range(own):
        for i in range(edge):
            rows = slice(i * square, (i + 1) * square)
            weighted = (columns[rows, t : t + 1] * x[t, i, :square, :].astype(f32)).astype(bf16)
            whole = total[t, i, :square, :] + weighted.astype(f32)
            top = whole.astype(bf16)
            low = (whole - top.astype(f32)).astype(bf16)
            fix = total_fix[t, i, :square, :].astype(bf16)
            out[t, rows, :] = jnp.concatenate([top, low, fix], axis=1)


def matrices_kernel(stacked, blocks, *refs):
    spots, outs = refs[:9], refs[9:]
    fwd_in, fwd_out, back_in, back_mid, back_out = outs
    for mode in range(3):
        spot, spread, same = spots[3 * mode : 3 * mode + 3]
        wide = matmul(matmul(spot[...], stacked[...]).astype(bf16), spread[...])
        wide = (wide * jnp.concatenate([same[...]] * 3, axis=1)).astype(bf16)
        if mode == 2:
            fwd_out[...] = wide
        else:
            fwd_in[mode] = wide
        for k in range(3):
            turned = lax.dot_general(spot[...], blocks[k], (((1,), (1,)), ((), ())), preferred_element_type=f32)
            turned = lax.dot_general(
                turned.astype(bf16), spot[...], (((1,), (1,)), ((), ())), preferred_element_type=f32
            )
            turned = (turned * same[...]).astype(bf16)
            if mode == 2:
                back_out[k] = turned
            else:
                back_in[mode, k] = turned
    back_mid[...] = jnp.concatenate([back_in[0, 1], back_in[1, 1]], axis=1)


def block_matrices(deriv_blocks):
    edge = deriv_blocks.shape[1]
    square = edge * edge
    padded = -(-square // ROWS) * ROWS
    tall = edge * ROWS
    ids = np.arange(padded)
    slow = ((ids[:, None] // edge) == np.arange(edge)).astype(np.float32)
    fast = (((ids[:, None] % edge) == np.arange(edge)) & (ids[:, None] < square)).astype(np.float32)
    ids = np.arange(tall)
    outer = ((ids[:, None] // ROWS) == np.arange(edge)).astype(np.float32)
    within = ((ids[:, None] % ROWS) == np.arange(ROWS)).astype(np.float32)
    stacked = jnp.moveaxis(deriv_blocks, 0, 1).reshape(edge, 3 * edge)
    constants = []
    for spot, mask in ((slow, fast), (fast, slow), (outer, within)):
        spread = np.kron(np.eye(3, dtype=np.float32), spot.T)
        constants += [jnp.asarray(spot, bf16), jnp.asarray(spread, bf16), jnp.asarray(mask @ mask.T, f32)]
    vmem = pl.BlockSpec(memory_space=pltpu.VMEM)
    shapes = [(2, padded, 3 * padded), (tall, 3 * tall), (2, 3, padded, padded), (padded, 2 * padded), (3, tall, tall)]
    return pl.pallas_call(
        matrices_kernel,
        out_shape=[jax.ShapeDtypeStruct(shape, bf16) for shape in shapes],
        in_specs=[vmem] * 11,
        out_specs=[vmem] * 5,
        compiler_params=params(24),
        name="matrices",
    )(stacked, deriv_blocks, *constants)


def kinetic(parts, place_meta, facts, matrices, edge, coefficients, levels):
    slots, folded, lanes = parts[0].shape
    width = lanes // 2
    padded = matrices[0].shape[1]
    own = PAIR * slots
    vmem = pl.BlockSpec(memory_space=pltpu.VMEM)
    smem = pl.BlockSpec(memory_space=pltpu.SMEM)
    anywhere = pl.BlockSpec(memory_space=pl.ANY)
    return pl.pallas_call(
        functools.partial(kinetic_kernel, edge, slots, levels),
        out_shape=jax.ShapeDtypeStruct((own, coefficients, 3 * width), bf16),
        in_specs=[smem] * 2 + [anywhere] * 6 + [vmem] * 5,
        out_specs=vmem,
        scratch_shapes=[
            pltpu.VMEM((6, slots, folded, lanes), bf16),
            pltpu.VMEM((6 * slots + 1, edge, padded, width), bf16),
            pltpu.VMEM((2, edge, padded, width), bf16),
            pltpu.VMEM((2, edge, 2 * padded, width), bf16),
            pltpu.VMEM((own, edge, padded, width), f32),
            pltpu.VMEM((own, edge, padded, width), f32),
            pltpu.VMEM((own + -own % 8, coefficients + -coefficients % lanes), f32),
            pltpu.VMEM((coefficients + -coefficients % lanes, own + -own % 8), f32),
            pltpu.SMEM((4 * slots, 10), jnp.int32),
            pltpu.SMEM((4 * slots,), f32),
            pltpu.SemaphoreType.DMA((6,)),
        ],
        compiler_params=params(48),
        cost_estimate=pl.CostEstimate(flops=2 * 10**10, bytes_accessed=40 * 10**6, transcendentals=0),
        name="kinetic",
    )(place_meta, facts, *parts, *matrices)


def offset_sum_kernel(meta, *refs):
    blocks, (small, kept, sent) = refs[:-3], refs[-3:]
    total = blocks[0][...].astype(f32)
    for block in blocks[1:]:
        total = total + block[...].astype(f32)
    small[...] = total.astype(bf16)
    half = kept.shape[0]
    first = meta[0] == 0
    low, high = total[:, :half].T, total[:, half:].T
    kept[...] = jnp.where(first, low, high)
    sent[...] = jnp.where(first, high, low)


def fock_sum_kernel(meta, *refs):
    blocks, (share, kept, sent) = refs[:-3], refs[-3:]
    sums = [sum((block[part].astype(f32) for block in blocks[1:]), blocks[0][part].astype(f32)) for part in range(3)]
    main = sums[0] + sums[1]
    share[...] = sums[2].astype(bf16)
    half = kept.shape[0]
    first = meta[0] == 0
    low, high = main[:, :half].T, main[:, half:].T
    kept[...] = jnp.where(first, low, high)
    sent[...] = jnp.where(first, high, low)


def level_sum(kernel, meta, blocks):
    tall, width = blocks[0].shape[-2:]
    vmem = pl.BlockSpec(memory_space=pltpu.VMEM)
    turned = jax.ShapeDtypeStruct((width // PAIR, tall), f32)
    return pl.pallas_call(
        kernel,
        out_shape=[jax.ShapeDtypeStruct((tall, width), bf16), turned, turned],
        in_specs=[pl.BlockSpec(memory_space=pltpu.SMEM)] + [vmem] * len(blocks),
        out_specs=[vmem] * 3,
        compiler_params=params(24),
        name="level_sum",
    )(meta, *blocks)


def body(orbitals, potential, deriv_blocks, levels, box_counts, neighbours):
    slots, coefficients, own_width = orbitals.shape
    edge = deriv_blocks.shape[1]
    level, pair, orb = lax.axis_index("lvl"), lax.axis_index("pair"), lax.axis_index("orb")
    level_count, orb_count = lax.axis_size("lvl"), lax.axis_size("orb")
    half, fold = own_width // PAIR, coefficients // 2
    all_width = own_width * orb_count
    box_rows = all_width // (level_count * PAIR)
    first = pair == 0
    groups = range(orb_count)
    square_grid = level_count == orb_count == 4 and box_rows == half
    row0, col0 = (level * PAIR + pair) * box_rows, orb * own_width

    own_base = (level * PAIR + pair) * slots
    pack_meta = jnp.stack([pair, box_counts[0], own_base]).astype(jnp.int32)
    theirs, mine = pack(pack_meta, neighbours, levels, orbitals, potential)
    active = orbitals

    far = {q: swap(active, "orb", q) for q in groups if q and q % 2 == 0}
    beside = swap(theirs, "pair", 1)
    first_mine, second_mine = trade(mine, "lvl", 0), trade(mine, "lvl", 1)
    later_mine, beside = lax.optimization_barrier((mine, beside))
    beside_rest = swap(later_mine, "pair", 1)
    first_beside, second_beside = trade(beside, "lvl", 0), trade(beside, "lvl", 1)

    matrices = block_matrices(deriv_blocks)

    def facts_of(parts):
        return jnp.stack([part[:, fold, :8] for part in parts]).astype(f32).astype(jnp.int32)

    early_facts = facts_of([mine, beside, first_mine, second_mine])
    flat = lambda block: block.reshape(-1, block.shape[-1])
    cut = -(-slots * coefficients // (2 * ROWS)) * ROWS
    beside_all, beside_top = unfold(pack_meta, beside, beside_rest, fold, cut)

    parts = [mine, beside, first_mine, first_beside, second_mine, second_beside]
    far, active, parts, beside_all, beside_top, matrices, early_facts = lax.optimization_barrier(
        (far, active, parts, beside_all, beside_top, matrices, early_facts)
    )
    facts = jnp.concatenate([early_facts, facts_of([parts[3], parts[5]])])
    cross = {q: [swap(beside_top, "orb", q), swap(flat(far[q])[cut:], "pair", 1)] for q in far}
    left_own = {0: active, 1: swap(active, "orb", 1), **far}
    left_beside = {0: [beside_all], 1: [swap(beside_all, "orb", 1)]}
    for q in far:
        left_own[q + 1] = swap(far[q], "orb", 1)

    def natural(blocks):
        return jnp.concatenate([lax.dynamic_index_in_dim(blocks, orb ^ j, keepdims=False) for j in groups], axis=1)

    def along_levels(blocks):
        mine_block = lambda target: lax.dynamic_index_in_dim(blocks, orb ^ target, keepdims=False)
        steps = range(1, level_count)
        return [mine_block(level)] + [swap(mine_block(level ^ step), "lvl", step) for step in steps]

    def both_halves(kept, got):
        return jnp.concatenate([jnp.where(first, kept, got), jnp.where(first, got, kept)], axis=1)

    def own_block(strip):
        strip = lax.all_gather(lax.psum(strip, "lvl"), ("orb", "pair"), axis=0, tiled=True)
        strip = lax.dynamic_slice_in_dim(strip, row0, box_rows, axis=0)
        return lax.dynamic_slice_in_dim(strip, col0, own_width, axis=1)

    live_rows = box_counts[0] * coefficients
    meta = jnp.stack([pair, slots * coefficients, live_rows]).astype(jnp.int32)

    place_meta = jnp.stack([level, pair]).astype(jnp.int32)
    right = kinetic(parts, place_meta, facts, matrices, edge, coefficients, level_count)

    cross, right, meta = lax.optimization_barrier((cross, right, meta))
    lefts_own = [[flat(left_own[q])] for q in groups]
    lefts_beside = dict(left_beside)
    for q in far:
        lefts_beside[q] = list(cross[q])
        lefts_beside[q + 1] = [swap(piece, "orb", 1) for piece in cross[q]]
    lefts_beside = [lefts_beside[q] for q in groups]

    share = 1.0 / level_count
    blocks = box_correlation(share, meta, lefts_own, None, half)
    blocks = box_correlation(share, meta, lefts_beside, blocks, half)
    right = right.reshape(2, slots * coefficients, 3 * half)
    fock_part = box_fock(0, lefts_own, right, None, None)
    if square_grid:
        sent = along_levels(blocks)
        sent, fock_part = lax.optimization_barrier((sent, fock_part))
        small, kept, other = level_sum(offset_sum_kernel, meta, sent)
        offset = both_halves(kept, swap(other, "pair", 1))
    else:
        offset = own_block(natural(blocks).astype(f32))
    row_ids = row0 + jnp.arange(box_rows, dtype=jnp.int32)
    col_ids = col0 + jnp.arange(own_width, dtype=jnp.int32)
    correlation = offset + (row_ids[:, None] == col_ids[None, :]).astype(f32)
    apart = (orb ^ level if square_grid else 0 * orb).reshape(1).astype(jnp.int32)
    fock_blocks = box_fock(1, lefts_beside, right, fock_part, apart)
    if square_grid:
        pieces = [small] + [swap(small, "lvl", z) for z in range(1, level_count)]
        pieces, fock_blocks, offset = lax.optimization_barrier((pieces, fock_blocks, offset))
        join = functools.partial(jnp.concatenate, axis=0)
        top, low = join(pieces[: level_count // 2]), join(pieces[level_count // 2 :])
        sent = [fock_blocks[0]] + [swap(fock_blocks[step], "lvl", step) for step in range(1, level_count)]
        got = [swap(top, "pair", 1), swap(low, "orb", 2)]
        got, sent[:2] = lax.optimization_barrier((got, sent[:2]))
        tops, lows = [top, got[0]], [low, got[1]]
        far_tops, far_lows = [swap(piece, "orb", 2) for piece in tops], [swap(piece, "pair", 1) for piece in lows]
        far_tops, far_lows, sent = lax.optimization_barrier((far_tops, far_lows, sent))
        pieces = tops + far_tops + lows + far_lows
        pieces += [swap(piece, "orb", 1) for piece in pieces]
        root_meta = jnp.stack([level, pair, orb]).astype(jnp.int32)
        inverse_root = root_of(root_meta, pieces, offset, all_width, level_count)
        share, kept, other = level_sum(fock_sum_kernel, meta, sent)
        to = [
            ((z * PAIR + y) * orb_count + o, (o * PAIR + y) * orb_count + z)
            for z in range(level_count)
            for y in range(PAIR)
            for o in groups
        ]
        got = swap(other, "pair", 1), lax.ppermute(share, BOX + ("orb",), to)
        inverse_root, got = lax.optimization_barrier((inverse_root, got))
        fock = both_halves(kept, got[0]) + got[1].astype(f32)
    else:
        fock_blocks = jnp.stack(fock_blocks)
        main = natural(fock_blocks[:, 0]).astype(f32) + natural(fock_blocks[:, 1]).astype(f32)
        main = lax.all_gather(lax.psum(main, "lvl"), "pair", axis=0, tiled=True)
        fock = lax.dynamic_slice_in_dim(main, row0, box_rows, axis=1).T + own_block(natural(fock_blocks[:, 2]).astype(f32))
        gathered = lax.all_gather(offset.astype(bf16), "orb", axis=1, tiled=True)
        whole = lax.all_gather(gathered, BOX, axis=0, tiled=True)
        rows_of = lax.dynamic_slice_in_dim(whole, row0, box_rows, axis=0)
        cols_of = lax.dynamic_slice_in_dim(whole, col0, own_width, axis=1)
        row_square, col_square = matmul(rows_of, whole), matmul(whole, cols_of)
        left = (rows_of.astype(f32) - 0.25 * row_square).astype(bf16)
        right_side = (0.25 * (cols_of.astype(f32) - col_square)).astype(bf16)
        own_square = lax.dynamic_slice_in_dim(row_square, col0, own_width, axis=1)
        inverse_root = correlation - 1.5 * offset + 0.125 * own_square + matmul(left, right_side)
    return fock, correlation, inverse_root


def solution(mesh):
    levels = mesh.shape["box"] // PAIR
    split = Mesh(mesh.devices.reshape(levels, PAIR, mesh.shape["orb"]), ("lvl", "pair", "orb"))
    in_specs = (P(BOX, None, "orb"), P(BOX, None), P(), P(BOX), P(BOX), P(BOX, None, None))
    out_specs = (P(BOX, "orb"),) * 3
    return jax.shard_map(body, mesh=split, in_specs=in_specs, out_specs=out_specs, check_vma=False)
```

```python
import functools

import jax
import jax.numpy as jnp
import numpy as np
from jax import lax
from jax.experimental import pallas as pl
from jax.experimental.pallas import tpu as pltpu
from jax.sharding import Mesh, PartitionSpec as P

PAIR = 2
ROWS = 16
BOX = ("lvl", "pair")
f32, bf16 = jnp.float32, jnp.bfloat16


def swap(value, axis, bit):
    count = lax.axis_size(axis)
    return lax.ppermute(value, axis, [(i, i ^ bit) for i in range(count)])


def trade(value, axis, start):
    pairs = [(i, i + 1) for i in range(start, lax.axis_size(axis) - 1, 2)]
    return lax.ppermute(value, axis, pairs + [(b, a) for a, b in pairs])


def matmul(left, right):
    return jnp.dot(left, right, preferred_element_type=f32)


def params(mebibytes):
    return pltpu.CompilerParams(vmem_limit_bytes=mebibytes * 1024 * 1024)


def pack_kernel(meta, neighbours, levels, orbitals, pot, theirs, mine):
    slots, coefficients, width = orbitals.shape
    half, fold = width // PAIR, coefficients // 2
    first = meta[0] == 0
    place = lax.broadcasted_iota(jnp.int32, (8, width), 1)
    for slot in range(slots):
        keep = slot < meta[1]
        for part in range(2):
            here = orbitals[slot, part * fold : (part + 1) * fold, :]
            here = jnp.where(keep, here, jnp.zeros_like(here))
            low, high = here[:, :half], here[:, half:]
            lanes = slice(part * half, (part + 1) * half)
            theirs[slot, :fold, lanes] = jnp.where(first, high, low)
            mine[slot, :fold, lanes] = jnp.where(first, low, high)
        own_id = meta[2] + slot
        facts = jnp.where(place == 6, levels[slot], jnp.where(place == 7, jnp.where(keep, 1, 0), 0))
        for c in range(6):
            target = neighbours[slot, c // 2, c % 2]
            facts = jnp.where(place == c, jnp.where(target >= 0, target - own_id, 16 * slots), facts)
        facts = facts.astype(f32).astype(bf16)
        for packed in (theirs, mine):
            packed[slot, fold : fold + 1, :] = facts[:1]
        row = fold + 1
        for start in range(0, pot.shape[1], width):
            stop = min(start + width, pot.shape[1])
            exact = pot[slot : slot + 1, start:stop]
            for _ in range(3):
                part = exact.astype(bf16)
                exact = exact - part.astype(f32)
                for packed in (theirs, mine):
                    packed[slot, row : row + 1, : stop - start] = part
                    if stop - start < width:
                        packed[slot, row : row + 1, stop - start :] = jnp.zeros((1, width - stop + start), bf16)
                row += 1
        for packed in (theirs, mine):
            packed[slot, row:, :] = jnp.zeros((packed.shape[1] - row, width), bf16)


def pack(meta, neighbours, levels, orbitals, pot):
    slots, coefficients, width = orbitals.shape
    fold = coefficients // 2
    padded = -(-(fold + 1 + 3 * -(-coefficients // width)) // ROWS) * ROWS
    vmem, smem = pl.BlockSpec(memory_space=pltpu.VMEM), pl.BlockSpec(memory_space=pltpu.SMEM)
    return pl.pallas_call(
        pack_kernel,
        out_shape=[jax.ShapeDtypeStruct((slots, padded, width), bf16)] * 2,
        in_specs=[smem, smem, smem, vmem, vmem],
        out_specs=[vmem, vmem],
        compiler_params=params(24),
        name="pack",
    )(meta, neighbours, levels, orbitals, pot)


def unfold_kernel(fold, meta, beside_in, rest_in, whole, top, beside, rest, sems):
    copies = [
        pltpu.make_async_copy(source, target, sems.at[i])
        for i, (source, target) in enumerate(((beside_in, beside), (rest_in, rest)))
    ]
    for copy in copies:
        copy.start()
    slots, _, width = beside.shape
    half = width // PAIR
    first = meta[0] == 0
    for copy in copies:
        copy.wait()
    for slot in range(slots):
        for part in range(2):
            lanes = slice(part * half, (part + 1) * half)
            near, far = beside[slot, :fold, lanes], rest[slot, :fold, lanes]
            start = (2 * slot + part) * fold
            here = jnp.concatenate([jnp.where(first, near, far), jnp.where(first, far, near)], axis=1)
            whole[start : start + fold, :] = here
    top[...] = whole[: top.shape[0], :]


def unfold(meta, beside, rest, fold, cut):
    slots, _, width = beside.shape
    vmem = pl.BlockSpec(memory_space=pltpu.VMEM)
    return pl.pallas_call(
        functools.partial(unfold_kernel, fold),
        out_shape=[
            jax.ShapeDtypeStruct((2 * slots * fold, width), bf16),
            jax.ShapeDtypeStruct((cut, width), bf16),
        ],
        in_specs=[pl.BlockSpec(memory_space=pltpu.SMEM)] + [pl.BlockSpec(memory_space=pl.ANY)] * 2,
        out_specs=[vmem, vmem],
        scratch_shapes=[
            pltpu.VMEM(beside.shape, bf16),
            pltpu.VMEM(beside.shape, bf16),
            pltpu.SemaphoreType.DMA((2,)),
        ],
        compiler_params=params(24),
        name="unfold",
    )(meta, beside, rest)


def load_left(lefts, held, sems):
    copies = []
    for q, pieces in enumerate(lefts):
        row = 0
        for piece in pieces:
            rows, width = piece.shape
            here = held.at[row : row + rows, q * width : (q + 1) * width]
            copies.append(pltpu.make_async_copy(piece, here, sems.at[len(copies)]))
            row += rows
    for copy in copies:
        copy.start()
    return copies


def grouped(refs, counts):
    refs = list(refs)
    return [[refs.pop(0) for _ in range(count)] for count in counts]


def correlation_kernel(share, counts, meta, *refs):
    refs, (out, held, turned, sems) = refs[:-4], refs[-4:]
    groups, half, width = out.shape
    lefts, before = grouped(refs, counts), refs[sum(counts) :]
    copies = load_left(lefts, held, sems)
    first = meta[0] == 0
    for copy in copies[: counts[0]]:
        copy.wait()
    own = held[:, :width]
    own = jnp.where(first, own[:, :half], own[:, half:]).T
    live = lax.broadcasted_iota(jnp.int32, own.shape, 1) < meta[1 if before else 2]
    turned[...] = jnp.where(live, own, jnp.zeros_like(own))
    for base in range(0, groups, 2):
        for copy in copies[max(sum(counts[:base]), counts[0]) : sum(counts[: base + 2])]:
            copy.wait()
        wide = matmul(turned[...], held[:, base * width : (base + 2) * width])
        for q in (base, base + 1):
            total = wide[:, (q - base) * width : (q - base + 1) * width]
            if before:
                total = total + before[0][q]
                if q == 0:
                    rows = lax.broadcasted_iota(jnp.int32, (half, width), 0) + jnp.where(first, 0, half)
                    columns = lax.broadcasted_iota(jnp.int32, (half, width), 1)
                    total = total - jnp.where(rows == columns, share, 0.0)
            out[q] = total.astype(out.dtype)


def box_correlation(share, meta, lefts, before, half):
    depth, width = sum(piece.shape[0] for piece in lefts[0]), lefts[0][0].shape[1]
    counts = [len(pieces) for pieces in lefts]
    vmem = pl.BlockSpec(memory_space=pltpu.VMEM)
    extra = [] if before is None else [before]
    return pl.pallas_call(
        functools.partial(correlation_kernel, share, counts),
        out_shape=jax.ShapeDtypeStruct((len(lefts), half, width), f32 if before is None else bf16),
        in_specs=[pl.BlockSpec(memory_space=pltpu.SMEM)]
        + [pl.BlockSpec(memory_space=pl.ANY)] * sum(counts)
        + [vmem] * len(extra),
        out_specs=vmem,
        scratch_shapes=[
            pltpu.VMEM((depth, len(lefts) * width), bf16),
            pltpu.VMEM((half, depth), bf16),
            pltpu.SemaphoreType.DMA((sum(counts),)),
        ],
        compiler_params=params(32),
        cost_estimate=pl.CostEstimate(
            flops=2 * len(lefts) * depth * width * half, bytes_accessed=2 * len(lefts) * depth * width, transcendentals=0
        ),
        name="correlation",
    )(meta, *[piece for pieces in lefts for piece in pieces], *extra)


def fock_kernel(side, counts, right, *refs):
    outs, (held, raw, turned, sems, last_sem) = refs[sum(counts) : -5], refs[-5:]
    lefts = grouped(refs, counts)
    before, apart, outs = (None, None, outs) if len(outs) == 1 else (outs[0], outs[1], outs[2:])
    out = outs[0]
    last = pltpu.make_async_copy(right.at[side], raw, last_sem)
    last.start()
    copies = load_left(lefts, held, sems)
    half, width = out.shape[-2] // (3 if before is None else 1), out.shape[-1]
    last.wait()
    turned[...] = raw[...].T
    for base in range(0, len(lefts), 2):
        for copy in copies[sum(counts[:base]) : sum(counts[: base + 2])]:
            copy.wait()
        wide = matmul(turned[...], held[:, base * width : (base + 2) * width])
        for q in (base, base + 1):
            total = wide[:, (q - base) * width : (q - base + 1) * width]
            if before is None:
                out[q] = total
                continue
            total = total + before[q]
            main = total[:half] + total[half : 2 * half]
            top = main.astype(bf16)
            parts = (top, (main - top.astype(f32)).astype(bf16), total[2 * half :].astype(bf16))

            def store(target):
                for i in range(3):
                    target[i] = parts[i]

            for distance, target in enumerate(outs):
                pl.when(q ^ apart[0] == distance)(functools.partial(store, target))


def box_fock(side, lefts, right, before, apart):
    depth, width = sum(piece.shape[0] for piece in lefts[0]), lefts[0][0].shape[1]
    counts = [len(pieces) for pieces in lefts]
    tall = right.shape[-1]
    anywhere, vmem = pl.BlockSpec(memory_space=pl.ANY), pl.BlockSpec(memory_space=pltpu.VMEM)
    extra = [] if before is None else [before, apart]
    out = jax.ShapeDtypeStruct((len(lefts), tall, width), f32)
    if before is not None:
        out = [jax.ShapeDtypeStruct((3, tall // 3, width), bf16)] * len(lefts)
    return pl.pallas_call(
        functools.partial(fock_kernel, side, counts),
        out_shape=out,
        in_specs=[anywhere] * (sum(counts) + 1) + [vmem, pl.BlockSpec(memory_space=pltpu.SMEM)][: len(extra)],
        out_specs=vmem if before is None else [vmem] * len(lefts),
        scratch_shapes=[
            pltpu.VMEM((depth, len(lefts) * width), bf16),
            pltpu.VMEM(right.shape[1:], bf16),
            pltpu.VMEM((tall, depth), bf16),
            pltpu.SemaphoreType.DMA((sum(counts),)),
            pltpu.SemaphoreType.DMA(()),
        ],
        compiler_params=params(40),
        cost_estimate=pl.CostEstimate(
            flops=2 * len(lefts) * depth * width * tall, bytes_accessed=2 * len(lefts) * depth * width, transcendentals=0
        ),
        name="fock",
    )(right, *[piece for pieces in lefts for piece in pieces], *extra)


def root_kernel(meta, *refs):
    pieces, (offset, root, whole, rows_f, cols_b, sems) = refs[:-6], refs[-6:]
    level, pair, orb = meta[0], meta[1], meta[2]
    coarse, width = offset.shape
    side = whole.shape[0]
    groups = side // width
    copies = []
    for piece, (z, y, q) in zip(pieces, piece_places()):
        for i in range(len(z)):
            start = ((orb ^ q) * PAIR + (pair ^ y)) * coarse
            rows = pl.ds(pl.multiple_of(start, coarse), coarse)
            lanes = pl.ds(pl.multiple_of((level ^ z[i]) * width, width), width)
            copies.append(
                pltpu.make_async_copy(
                    piece.at[i * coarse : (i + 1) * coarse], whole.at[rows, lanes], sems.at[len(copies)]
                )
            )
    for copy in copies:
        copy.start()
    for copy in copies:
        copy.wait()
    row0 = pl.multiple_of((level * PAIR + pair) * coarse, coarse)
    own_lanes = pl.ds(pl.multiple_of(orb * width, width), width)
    rows = whole[pl.ds(row0, coarse), :]

    for j in range(groups):
        lanes = slice(j * width, (j + 1) * width)
        rows_f[:, lanes] = matmul(rows, whole[:, lanes])
    columns = whole[:, own_lanes]
    for i in range(groups):
        here = slice(i * width, (i + 1) * width)
        square = matmul(whole[here, :], columns)
        cols_b[here, :] = (0.25 * (whole[here, own_lanes].astype(f32) - square)).astype(bf16)
    left = (rows.astype(f32) - 0.25 * rows_f[...]).astype(bf16)
    value = matmul(left, cols_b[...]) + 0.125 * rows_f[:, own_lanes] - 0.5 * offset[...]
    row_ids = lax.broadcasted_iota(jnp.int32, value.shape, 0) + row0
    col_ids = lax.broadcasted_iota(jnp.int32, value.shape, 1) + orb * width
    root[...] = value + jnp.where(row_ids == col_ids, 1.0, 0.0)


def piece_places():
    places = []
    for core in (0, 1):
        for half in (0, 1):
            z = [half, half ^ 2]
            for second in (0, 1):
                for inner in (0, 1):
                    y, far = (second, inner) if half else (inner, second)
                    places.append((z, y, 2 * far + core))
    return places


def root_of(meta, pieces, offset, side):
    coarse, width = offset.shape
    vmem, anywhere = pl.BlockSpec(memory_space=pltpu.VMEM), pl.BlockSpec(memory_space=pl.ANY)
    return pl.pallas_call(
        root_kernel,
        out_shape=jax.ShapeDtypeStruct(offset.shape, f32),
        in_specs=[pl.BlockSpec(memory_space=pltpu.SMEM)] + [anywhere] * len(pieces) + [vmem],
        out_specs=vmem,
        scratch_shapes=[
            pltpu.VMEM((side, side), bf16),
            pltpu.VMEM((coarse, side), f32),
            pltpu.VMEM((side, width), bf16),
            pltpu.SemaphoreType.DMA((side // coarse * (side // width),)),
        ],
        compiler_params=params(40),
        cost_estimate=pl.CostEstimate(flops=16 * side * side * width, bytes_accessed=4 * side * side, transcendentals=0),
        name="root",
    )(meta, *pieces, offset)


def fill_tables(slots, levels, place_meta, facts, table, scale):
    level, pair = place_meta[0], place_meta[1]
    even = lax.rem(level, 2) == 0
    none = 6 * slots

    def place(slot_id):
        box = lax.div(slot_id, slots)
        apart = lax.div(box, PAIR) - level
        base = jnp.where(apart == 0, 0, jnp.where((apart < 0) == even, 4, 2))
        return (base + jnp.where(lax.rem(box, PAIR) != pair, 1, 0)) * slots + lax.rem(slot_id, slots)

    for index in range(4 * slots):
        group, r = divmod(index, slots)

        def fact(c):
            if group < 2:
                return facts[group, r, c]
            swap_id = jnp.where(even, 1, 0) if group == 2 else jnp.where(even, 0, 1)
            near_pair = 1 if group == 2 else 0
            return facts[2 + swap_id + jnp.where(pair == near_pair, 0, 2), r, c]

        box = (
            level * PAIR + pair,
            level * PAIR + 1 - pair,
            jnp.maximum(level * PAIR - 1, 0),
            jnp.minimum((level + 1) * PAIR, levels * PAIR - 1),
        )[group]
        there = (True, True, level > 0, level < levels - 1)[group]
        own_id = box * slots + r
        own_place = place(own_id)
        table[index, 0] = jnp.where((fact(7) > 0) & there, own_place, -1)
        for a in range(3):
            for k in (0, 2):
                distance = fact(2 * a + k // 2)
                target = place(jnp.maximum(own_id + distance, 0))
                target = jnp.where(distance < 16 * slots, target, none)
                table[index, 1 + 3 * a + k] = jnp.clip(target, 0, none)
            table[index, 2 + 3 * a] = own_place
        level_of = fact(6)
        scale[index] = jnp.where(level_of == 0, 0.5, jnp.where(level_of == 1, 1.0, 2.0))


def kinetic_kernel(edge, slots, levels, place_meta, facts, *refs):
    parts, refs = refs[:6], refs[6:]
    (fwd_in, fwd_out, back_in, back_mid, back_out), out, refs = refs[:5], refs[5], refs[6:]
    raw, x, outer, inner, total, total_fix, lines, columns, table, scale, sems = refs
    square = edge * edge
    own = PAIR * slots
    padded, width = x.shape[2:]
    copies = [pltpu.make_async_copy(part, raw.at[place], sems.at[place]) for place, part in enumerate(parts)]
    for copy in copies:
        copy.start()
    tail = padded - ROWS
    x[:, :, tail:, :] = jnp.zeros((x.shape[0], edge, ROWS, width), bf16)
    x[6 * slots] = jnp.zeros((edge, padded, width), bf16)
    total[...] = jnp.zeros_like(total)
    total_fix[...] = jnp.zeros_like(total_fix)
    fill_tables(slots, levels, place_meta, facts, table, scale)
    lines[...] = jnp.zeros_like(lines)
    for copy in copies:
        copy.wait()
    lanes = raw.shape[3]
    for t in range(own):
        for start in range(0, lines.shape[1], lanes):
            row = edge * square // 2 + 1 + 3 * (start // lanes)
            high, middle, low = (
                raw[t // slots, t % slots, row + i : row + i + 1, :].astype(f32) for i in range(3)
            )
            lines[t : t + 1, start : start + lanes] = (high + middle) + low
    columns[...] = lines[...].T

    def lay_out(place, carry):
        for slot in range(slots):
            for i in range(edge):
                part, row = i // (edge // 2), i % (edge // 2) * square
                x[place * slots + slot, i, :square, :] = raw[
                    place, slot, row : row + square, part * width : (part + 1) * width
                ]
        return carry

    lax.fori_loop(0, len(parts), lay_out, 0)
    chunks = -(-square // ROWS)

    def per_slot(s, carry):
        @pl.when(table[s, 0] >= 0)
        def _():
            own_scale = scale[s]
            half = 0.5 * own_scale
            sums = (total, total_fix)

            def split(exact):
                exact = own_scale * exact
                value = exact.astype(bf16).astype(f32)
                return (half * value).astype(bf16), (half * (value - exact)).astype(bf16)

            sources = [[table[s, 1 + 3 * a + k] for k in range(3)] for a in range(3)]
            here = sources[0][1]
            for a in range(3):

                @pl.when((here < own) | (sources[a][0] < own) | (sources[a][2] < own))
                def _():
                    if a == 0:
                        for i in range(chunks):
                            rows = slice(i * ROWS, (i + 1) * ROWS)
                            block = [x[t, :, rows, :].reshape(edge * ROWS, width) for t in sources[0]]
                            fields = split(matmul(fwd_out[...], jnp.concatenate(block, axis=0)))
                            for field in range(2):
                                outer[field, :, rows, :] = fields[field].reshape(edge, ROWS, width)
                    else:
                        for i in range(edge):
                            block = jnp.concatenate([x[t, i] for t in sources[a]], axis=0)
                            fields = split(matmul(fwd_in[a - 1], block))
                            for field in range(2):
                                inner[field, i, (a - 1) * padded : a * padded, :] = fields[field]

            def back_outer(k, target):
                for i in range(chunks):
                    rows = slice(i * ROWS, (i + 1) * ROWS)
                    for field in range(2):
                        term = matmul(back_out[k], outer[field, :, rows, :].reshape(edge * ROWS, width))
                        sums[field][target, :, rows, :] += term.reshape(edge, ROWS, width)

            for k in (0, 2):
                for a in range(3):
                    target = sources[a][k]

                    @pl.when(target < own)
                    def _():
                        if a == 0:
                            back_outer(k, target)
                        else:
                            for i in range(edge):
                                for field in range(2):
                                    here = inner[field, i, (a - 1) * padded : a * padded, :]
                                    sums[field][target, i] += matmul(back_in[a - 1, k], here)

            @pl.when(here < own)
            def _():
                back_outer(1, here)
                for i in range(edge):
                    for field in range(2):
                        sums[field][here, i] += matmul(back_mid[...], inner[field, i])

        return carry

    lax.fori_loop(0, table.shape[0], per_slot, 0)

    for t in range(own):
        for i in range(edge):
            rows = slice(i * square, (i + 1) * square)
            weighted = (columns[rows, t : t + 1] * x[t, i, :square, :].astype(f32)).astype(bf16)
            whole = total[t, i, :square, :] + weighted.astype(f32)
            top = whole.astype(bf16)
            low = (whole - top.astype(f32)).astype(bf16)
            fix = total_fix[t, i, :square, :].astype(bf16)
            out[t, rows, :] = jnp.concatenate([top, low, fix], axis=1)


def matrices_kernel(stacked, blocks, *refs):
    spots, outs = refs[:9], refs[9:]
    fwd_in, fwd_out, back_in, back_mid, back_out = outs
    for mode in range(3):
        spot, spread, same = spots[3 * mode : 3 * mode + 3]
        wide = matmul(matmul(spot[...], stacked[...]).astype(bf16), spread[...])
        wide = (wide * jnp.concatenate([same[...]] * 3, axis=1)).astype(bf16)
        if mode == 2:
            fwd_out[...] = wide
        else:
            fwd_in[mode] = wide
        for k in range(3):
            turned = lax.dot_general(spot[...], blocks[k], (((1,), (1,)), ((), ())), preferred_element_type=f32)
            turned = lax.dot_general(
                turned.astype(bf16), spot[...], (((1,), (1,)), ((), ())), preferred_element_type=f32
            )
            turned = (turned * same[...]).astype(bf16)
            if mode == 2:
                back_out[k] = turned
            else:
                back_in[mode, k] = turned
    back_mid[...] = jnp.concatenate([back_in[0, 1], back_in[1, 1]], axis=1)


def block_matrices(deriv_blocks):
    edge = deriv_blocks.shape[1]
    square = edge * edge
    padded = -(-square // ROWS) * ROWS
    tall = edge * ROWS
    ids = np.arange(padded)
    slow = ((ids[:, None] // edge) == np.arange(edge)).astype(np.float32)
    fast = (((ids[:, None] % edge) == np.arange(edge)) & (ids[:, None] < square)).astype(np.float32)
    ids = np.arange(tall)
    outer = ((ids[:, None] // ROWS) == np.arange(edge)).astype(np.float32)
    within = ((ids[:, None] % ROWS) == np.arange(ROWS)).astype(np.float32)
    stacked = jnp.moveaxis(deriv_blocks, 0, 1).reshape(edge, 3 * edge)
    constants = []
    for spot, mask in ((slow, fast), (fast, slow), (outer, within)):
        spread = np.kron(np.eye(3, dtype=np.float32), spot.T)
        constants += [jnp.asarray(spot, bf16), jnp.asarray(spread, bf16), jnp.asarray(mask @ mask.T, f32)]
    vmem = pl.BlockSpec(memory_space=pltpu.VMEM)
    shapes = [(2, padded, 3 * padded), (tall, 3 * tall), (2, 3, padded, padded), (padded, 2 * padded), (3, tall, tall)]
    return pl.pallas_call(
        matrices_kernel,
        out_shape=[jax.ShapeDtypeStruct(shape, bf16) for shape in shapes],
        in_specs=[vmem] * 11,
        out_specs=[vmem] * 5,
        compiler_params=params(24),
        name="matrices",
    )(stacked, deriv_blocks, *constants)


def kinetic(parts, place_meta, facts, matrices, edge, coefficients, levels):
    slots, folded, lanes = parts[0].shape
    width = lanes // 2
    padded = matrices[0].shape[1]
    own = PAIR * slots
    vmem = pl.BlockSpec(memory_space=pltpu.VMEM)
    smem = pl.BlockSpec(memory_space=pltpu.SMEM)
    anywhere = pl.BlockSpec(memory_space=pl.ANY)
    return pl.pallas_call(
        functools.partial(kinetic_kernel, edge, slots, levels),
        out_shape=jax.ShapeDtypeStruct((own, coefficients, 3 * width), bf16),
        in_specs=[smem] * 2 + [anywhere] * 6 + [vmem] * 5,
        out_specs=vmem,
        scratch_shapes=[
            pltpu.VMEM((6, slots, folded, lanes), bf16),
            pltpu.VMEM((6 * slots + 1, edge, padded, width), bf16),
            pltpu.VMEM((2, edge, padded, width), bf16),
            pltpu.VMEM((2, edge, 2 * padded, width), bf16),
            pltpu.VMEM((own, edge, padded, width), f32),
            pltpu.VMEM((own, edge, padded, width), f32),
            pltpu.VMEM((own + -own % 8, coefficients + -coefficients % lanes), f32),
            pltpu.VMEM((coefficients + -coefficients % lanes, own + -own % 8), f32),
            pltpu.SMEM((4 * slots, 10), jnp.int32),
            pltpu.SMEM((4 * slots,), f32),
            pltpu.SemaphoreType.DMA((6,)),
        ],
        compiler_params=params(48),
        cost_estimate=pl.CostEstimate(flops=2 * 10**10, bytes_accessed=40 * 10**6, transcendentals=0),
        name="kinetic",
    )(place_meta, facts, *parts, *matrices)


def offset_sum_kernel(meta, *refs):
    blocks, (small, kept, sent) = refs[:-3], refs[-3:]
    total = blocks[0][...].astype(f32)
    for block in blocks[1:]:
        total = total + block[...].astype(f32)
    small[...] = total.astype(bf16)
    half = kept.shape[0]
    first = meta[0] == 0
    low, high = total[:, :half].T, total[:, half:].T
    kept[...] = jnp.where(first, low, high)
    sent[...] = jnp.where(first, high, low)


def fock_sum_kernel(meta, *refs):
    blocks, (share, kept, sent) = refs[:-3], refs[-3:]
    sums = [sum((block[part].astype(f32) for block in blocks[1:]), blocks[0][part].astype(f32)) for part in range(3)]
    main = sums[0] + sums[1]
    share[...] = sums[2].astype(bf16)
    half = kept.shape[0]
    first = meta[0] == 0
    low, high = main[:, :half].T, main[:, half:].T
    kept[...] = jnp.where(first, low, high)
    sent[...] = jnp.where(first, high, low)


def level_sum(kernel, meta, blocks):
    tall, width = blocks[0].shape[-2:]
    vmem = pl.BlockSpec(memory_space=pltpu.VMEM)
    turned = jax.ShapeDtypeStruct((width // PAIR, tall), f32)
    return pl.pallas_call(
        kernel,
        out_shape=[jax.ShapeDtypeStruct((tall, width), bf16), turned, turned],
        in_specs=[pl.BlockSpec(memory_space=pltpu.SMEM)] + [vmem] * len(blocks),
        out_specs=[vmem] * 3,
        compiler_params=params(24),
        name="level_sum",
    )(meta, *blocks)


def body(orbitals, potential, deriv_blocks, levels, box_counts, neighbours):
    slots, coefficients, own_width = orbitals.shape
    edge = deriv_blocks.shape[1]
    level, pair, orb = lax.axis_index("lvl"), lax.axis_index("pair"), lax.axis_index("orb")
    level_count, orb_count = lax.axis_size("lvl"), lax.axis_size("orb")
    half, fold = own_width // PAIR, coefficients // 2
    all_width = own_width * orb_count
    box_rows = all_width // (level_count * PAIR)
    first = pair == 0
    groups = range(orb_count)
    square_grid = level_count == orb_count == 4 and box_rows == half
    row0, col0 = (level * PAIR + pair) * box_rows, orb * own_width

    own_base = (level * PAIR + pair) * slots
    pack_meta = jnp.stack([pair, box_counts[0], own_base]).astype(jnp.int32)
    theirs, mine = pack(pack_meta, neighbours, levels, orbitals, potential)
    active = orbitals

    far = {q: swap(active, "orb", q) for q in groups if q and q % 2 == 0}
    beside = swap(theirs, "pair", 1)
    first_mine, second_mine = trade(mine, "lvl", 0), trade(mine, "lvl", 1)
    later_mine, beside = lax.optimization_barrier((mine, beside))
    beside_rest = swap(later_mine, "pair", 1)
    first_beside, second_beside = trade(beside, "lvl", 0), trade(beside, "lvl", 1)

    matrices = block_matrices(deriv_blocks)

    def facts_of(parts):
        return jnp.stack([part[:, fold, :8] for part in parts]).astype(f32).astype(jnp.int32)

    early_facts = facts_of([mine, beside, first_mine, second_mine])
    flat = lambda block: block.reshape(-1, block.shape[-1])
    cut = -(-slots * coefficients // (2 * ROWS)) * ROWS
    beside_all, beside_top = unfold(pack_meta, beside, beside_rest, fold, cut)

    parts = [mine, beside, first_mine, first_beside, second_mine, second_beside]
    far, active, parts, beside_all, beside_top, matrices, early_facts = lax.optimization_barrier(
        (far, active, parts, beside_all, beside_top, matrices, early_facts)
    )
    facts = jnp.concatenate([early_facts, facts_of([parts[3], parts[5]])])
    cross = {q: [swap(beside_top, "orb", q), swap(flat(far[q])[cut:], "pair", 1)] for q in far}
    left_own = {0: active, 1: swap(active, "orb", 1), **far}
    left_beside = {0: [beside_all], 1: [swap(beside_all, "orb", 1)]}
    for q in far:
        left_own[q + 1] = swap(far[q], "orb", 1)

    def natural(blocks):
        return jnp.concatenate([lax.dynamic_index_in_dim(blocks, orb ^ j, keepdims=False) for j in groups], axis=1)

    def along_levels(blocks):
        mine_block = lambda target: lax.dynamic_index_in_dim(blocks, orb ^ target, keepdims=False)
        steps = range(1, level_count)
        return [mine_block(level)] + [swap(mine_block(level ^ step), "lvl", step) for step in steps]

    def both_halves(kept, got):
        return jnp.concatenate([jnp.where(first, kept, got), jnp.where(first, got, kept)], axis=1)

    def own_block(strip):
        strip = lax.all_gather(lax.psum(strip, "lvl"), ("orb", "pair"), axis=0, tiled=True)
        strip = lax.dynamic_slice_in_dim(strip, row0, box_rows, axis=0)
        return lax.dynamic_slice_in_dim(strip, col0, own_width, axis=1)

    live_rows = box_counts[0] * coefficients
    meta = jnp.stack([pair, slots * coefficients, live_rows]).astype(jnp.int32)

    place_meta = jnp.stack([level, pair]).astype(jnp.int32)
    right = kinetic(parts, place_meta, facts, matrices, edge, coefficients, level_count)

    cross, right, meta = lax.optimization_barrier((cross, right, meta))
    lefts_own = [[flat(left_own[q])] for q in groups]
    lefts_beside = dict(left_beside)
    for q in far:
        lefts_beside[q] = list(cross[q])
        lefts_beside[q + 1] = [swap(piece, "orb", 1) for piece in cross[q]]
    lefts_beside = [lefts_beside[q] for q in groups]

    share = 1.0 / level_count
    blocks = box_correlation(share, meta, lefts_own, None, half)
    blocks = box_correlation(share, meta, lefts_beside, blocks, half)
    right = right.reshape(2, slots * coefficients, 3 * half)
    fock_part = box_fock(0, lefts_own, right, None, None)
    if square_grid:
        sent = along_levels(blocks)
        sent, fock_part = lax.optimization_barrier((sent, fock_part))
        small, kept, other = level_sum(offset_sum_kernel, meta, sent)
        offset = both_halves(kept, swap(other, "pair", 1))
    else:
        offset = own_block(natural(blocks).astype(f32))
    row_ids = row0 + jnp.arange(box_rows, dtype=jnp.int32)
    col_ids = col0 + jnp.arange(own_width, dtype=jnp.int32)
    correlation = offset + (row_ids[:, None] == col_ids[None, :]).astype(f32)
    apart = (orb ^ level if square_grid else 0 * orb).reshape(1).astype(jnp.int32)
    fock_blocks = box_fock(1, lefts_beside, right, fock_part, apart)
    if square_grid:
        over = swap(small, "lvl", 2)
        over, fock_blocks, offset = lax.optimization_barrier((over, fock_blocks, offset))
        top = jnp.concatenate([small, over])
        low = swap(top, "lvl", 1)
        sent = [fock_blocks[0]] + [swap(fock_blocks[step], "lvl", step) for step in range(1, level_count)]
        got = [swap(top, "pair", 1), swap(low, "orb", 2)]
        got, sent[:2] = lax.optimization_barrier((got, sent[:2]))
        tops, lows = [top, got[0]], [low, got[1]]
        far_tops, far_lows = [swap(piece, "orb", 2) for piece in tops], [swap(piece, "pair", 1) for piece in lows]
        far_lows[1], sent = lax.optimization_barrier((far_lows[1], sent))
        pieces = tops + far_tops + lows + far_lows
        pieces += [swap(piece, "orb", 1) for piece in pieces]
        root_meta = jnp.stack([level, pair, orb]).astype(jnp.int32)
        inverse_root = root_of(root_meta, pieces, offset, all_width)
        share, kept, other = level_sum(fock_sum_kernel, meta, sent)
        to = [
            ((z * PAIR + y) * orb_count + o, (o * PAIR + y) * orb_count + z)
            for z in range(level_count)
            for y in range(PAIR)
            for o in groups
        ]
        got = swap(other, "pair", 1), lax.ppermute(share, BOX + ("orb",), to)
        inverse_root, got = lax.optimization_barrier((inverse_root, got))
        fock = both_halves(kept, got[0]) + got[1].astype(f32)
    else:
        fock_blocks = jnp.stack(fock_blocks)
        main = natural(fock_blocks[:, 0]).astype(f32) + natural(fock_blocks[:, 1]).astype(f32)
        main = lax.all_gather(lax.psum(main, "lvl"), "pair", axis=0, tiled=True)
        fock = lax.dynamic_slice_in_dim(main, row0, box_rows, axis=1).T + own_block(natural(fock_blocks[:, 2]).astype(f32))
        gathered = lax.all_gather(offset.astype(bf16), "orb", axis=1, tiled=True)
        whole = lax.all_gather(gathered, BOX, axis=0, tiled=True)
        rows_of = lax.dynamic_slice_in_dim(whole, row0, box_rows, axis=0)
        cols_of = lax.dynamic_slice_in_dim(whole, col0, own_width, axis=1)
        row_square, col_square = matmul(rows_of, whole), matmul(whole, cols_of)
        left = (rows_of.astype(f32) - 0.25 * row_square).astype(bf16)
        right_side = (0.25 * (cols_of.astype(f32) - col_square)).astype(bf16)
        own_square = lax.dynamic_slice_in_dim(row_square, col0, own_width, axis=1)
        inverse_root = correlation - 1.5 * offset + 0.125 * own_square + matmul(left, right_side)
    return fock, correlation, inverse_root


def solution(mesh):
    levels = mesh.shape["box"] // PAIR
    split = Mesh(mesh.devices.reshape(levels, PAIR, mesh.shape["orb"]), ("lvl", "pair", "orb"))
    in_specs = (P(BOX, None, "orb"), P(BOX, None), P(), P(BOX), P(BOX), P(BOX, None, None))
    out_specs = (P(BOX, "orb"),) * 3
    return jax.shard_map(body, mesh=split, in_specs=in_specs, out_specs=out_specs, check_vma=False)
```

```python
import functools

import jax
import jax.numpy as jnp
import numpy as np
from jax import lax
from jax.experimental import pallas as pl
from jax.experimental.pallas import tpu as pltpu
from jax.sharding import Mesh, PartitionSpec as P

PAIR = 2
ROWS = 16
BOX = ("lvl", "pair")
f32, bf16 = jnp.float32, jnp.bfloat16


def swap(value, axis, bit):
    count = lax.axis_size(axis)
    return lax.ppermute(value, axis, [(i, i ^ bit) for i in range(count)])


def trade(value, axis, start):
    pairs = [(i, i + 1) for i in range(start, lax.axis_size(axis) - 1, 2)]
    return lax.ppermute(value, axis, pairs + [(b, a) for a, b in pairs])


def matmul(left, right):
    return jnp.dot(left, right, preferred_element_type=f32)


def params(mebibytes):
    return pltpu.CompilerParams(vmem_limit_bytes=mebibytes * 1024 * 1024)


def pack_kernel(meta, neighbours, levels, orbitals, pot, theirs, mine):
    slots, coefficients, width = orbitals.shape
    half, fold = width // PAIR, coefficients // 2
    first = meta[0] == 0
    place = lax.broadcasted_iota(jnp.int32, (8, width), 1)
    for slot in range(slots):
        keep = slot < meta[1]
        for part in range(2):
            here = orbitals[slot, part * fold : (part + 1) * fold, :]
            here = jnp.where(keep, here, jnp.zeros_like(here))
            low, high = here[:, :half], here[:, half:]
            lanes = slice(part * half, (part + 1) * half)
            theirs[slot, :fold, lanes] = jnp.where(first, high, low)
            mine[slot, :fold, lanes] = jnp.where(first, low, high)
        own_id = meta[2] + slot
        facts = jnp.where(place == 6, levels[slot], jnp.where(place == 7, jnp.where(keep, 1, 0), 0))
        for c in range(6):
            target = neighbours[slot, c // 2, c % 2]
            facts = jnp.where(place == c, jnp.where(target >= 0, target - own_id, 16 * slots), facts)
        facts = facts.astype(f32).astype(bf16)
        for packed in (theirs, mine):
            packed[slot, fold : fold + 1, :] = facts[:1]
        row = fold + 1
        for start in range(0, pot.shape[1], width):
            stop = min(start + width, pot.shape[1])
            exact = pot[slot : slot + 1, start:stop]
            for _ in range(3):
                part = exact.astype(bf16)
                exact = exact - part.astype(f32)
                for packed in (theirs, mine):
                    packed[slot, row : row + 1, : stop - start] = part
                    if stop - start < width:
                        packed[slot, row : row + 1, stop - start :] = jnp.zeros((1, width - stop + start), bf16)
                row += 1
        for packed in (theirs, mine):
            packed[slot, row:, :] = jnp.zeros((packed.shape[1] - row, width), bf16)


def pack(meta, neighbours, levels, orbitals, pot):
    slots, coefficients, width = orbitals.shape
    fold = coefficients // 2
    padded = -(-(fold + 1 + 3 * -(-coefficients // width)) // ROWS) * ROWS
    vmem, smem = pl.BlockSpec(memory_space=pltpu.VMEM), pl.BlockSpec(memory_space=pltpu.SMEM)
    return pl.pallas_call(
        pack_kernel,
        out_shape=[jax.ShapeDtypeStruct((slots, padded, width), bf16)] * 2,
        in_specs=[smem, smem, smem, vmem, vmem],
        out_specs=[vmem, vmem],
        compiler_params=params(24),
        name="pack",
    )(meta, neighbours, levels, orbitals, pot)


def unfold_kernel(fold, meta, beside_in, rest_in, whole, top, beside, rest, sems):
    copies = [
        pltpu.make_async_copy(source, target, sems.at[i])
        for i, (source, target) in enumerate(((beside_in, beside), (rest_in, rest)))
    ]
    for copy in copies:
        copy.start()
    slots, _, width = beside.shape
    half = width // PAIR
    first = meta[0] == 0
    for copy in copies:
        copy.wait()
    for slot in range(slots):
        for part in range(2):
            lanes = slice(part * half, (part + 1) * half)
            near, far = beside[slot, :fold, lanes], rest[slot, :fold, lanes]
            start = (2 * slot + part) * fold
            here = jnp.concatenate([jnp.where(first, near, far), jnp.where(first, far, near)], axis=1)
            whole[start : start + fold, :] = here
    top[...] = whole[: top.shape[0], :]


def unfold(meta, beside, rest, fold, cut):
    slots, _, width = beside.shape
    vmem = pl.BlockSpec(memory_space=pltpu.VMEM)
    return pl.pallas_call(
        functools.partial(unfold_kernel, fold),
        out_shape=[
            jax.ShapeDtypeStruct((2 * slots * fold, width), bf16),
            jax.ShapeDtypeStruct((cut, width), bf16),
        ],
        in_specs=[pl.BlockSpec(memory_space=pltpu.SMEM)] + [pl.BlockSpec(memory_space=pltpu.HBM)] * 2,
        out_specs=[vmem, vmem],
        scratch_shapes=[
            pltpu.VMEM(beside.shape, bf16),
            pltpu.VMEM(beside.shape, bf16),
            pltpu.SemaphoreType.DMA((2,)),
        ],
        compiler_params=params(24),
        name="unfold",
    )(meta, beside, rest)


def load_left(lefts, held, sems):
    copies = []
    for q, pieces in enumerate(lefts):
        row = 0
        for piece in pieces:
            rows, width = piece.shape
            here = held.at[row : row + rows, q * width : (q + 1) * width]
            copies.append(pltpu.make_async_copy(piece, here, sems.at[len(copies)]))
            row += rows
    for copy in copies:
        copy.start()
    return copies


def grouped(refs, counts):
    refs = list(refs)
    return [[refs.pop(0) for _ in range(count)] for count in counts]


def correlation_kernel(share, counts, meta, *refs):
    refs, (out, held, turned, sems) = refs[:-4], refs[-4:]
    groups, half, width = out.shape
    lefts, before = grouped(refs, counts), refs[sum(counts) :]
    copies = load_left(lefts, held, sems)
    first = meta[0] == 0
    for copy in copies[: counts[0]]:
        copy.wait()
    own = held[:, :width]
    own = jnp.where(first, own[:, :half], own[:, half:]).T
    live = lax.broadcasted_iota(jnp.int32, own.shape, 1) < meta[1 if before else 2]
    turned[...] = jnp.where(live, own, jnp.zeros_like(own))
    for base in range(0, groups, 2):
        for copy in copies[max(sum(counts[:base]), counts[0]) : sum(counts[: base + 2])]:
            copy.wait()
        wide = matmul(turned[...], held[:, base * width : (base + 2) * width])
        for q in (base, base + 1):
            total = wide[:, (q - base) * width : (q - base + 1) * width]
            if before:
                total = total + before[0][q]
                if q == 0:
                    rows = lax.broadcasted_iota(jnp.int32, (half, width), 0) + jnp.where(first, 0, half)
                    columns = lax.broadcasted_iota(jnp.int32, (half, width), 1)
                    total = total - jnp.where(rows == columns, share, 0.0)
            out[q] = total.astype(out.dtype)


def box_correlation(share, meta, lefts, before, half):
    depth, width = sum(piece.shape[0] for piece in lefts[0]), lefts[0][0].shape[1]
    counts = [len(pieces) for pieces in lefts]
    vmem = pl.BlockSpec(memory_space=pltpu.VMEM)
    extra = [] if before is None else [before]
    return pl.pallas_call(
        functools.partial(correlation_kernel, share, counts),
        out_shape=jax.ShapeDtypeStruct((len(lefts), half, width), f32 if before is None else bf16),
        in_specs=[pl.BlockSpec(memory_space=pltpu.SMEM)]
        + [pl.BlockSpec(memory_space=pl.ANY)] * sum(counts)
        + [vmem] * len(extra),
        out_specs=vmem,
        scratch_shapes=[
            pltpu.VMEM((depth, len(lefts) * width), bf16),
            pltpu.VMEM((half, depth), bf16),
            pltpu.SemaphoreType.DMA((sum(counts),)),
        ],
        compiler_params=params(32),
        cost_estimate=pl.CostEstimate(
            flops=2 * len(lefts) * depth * width * half, bytes_accessed=2 * len(lefts) * depth * width, transcendentals=0
        ),
        name="correlation",
    )(meta, *[piece for pieces in lefts for piece in pieces], *extra)


def fock_kernel(side, counts, right, *refs):
    outs, (held, raw, turned, sems, last_sem) = refs[sum(counts) : -5], refs[-5:]
    lefts = grouped(refs, counts)
    before, apart, outs = (None, None, outs) if len(outs) == 1 else (outs[0], outs[1], outs[2:])
    out = outs[0]
    last = pltpu.make_async_copy(right.at[side], raw, last_sem)
    last.start()
    copies = load_left(lefts, held, sems)
    half, width = out.shape[-2] // (3 if before is None else 1), out.shape[-1]
    last.wait()
    turned[...] = raw[...].T
    for base in range(0, len(lefts), 2):
        for copy in copies[sum(counts[:base]) : sum(counts[: base + 2])]:
            copy.wait()
        wide = matmul(turned[...], held[:, base * width : (base + 2) * width])
        for q in (base, base + 1):
            total = wide[:, (q - base) * width : (q - base + 1) * width]
            if before is None:
                out[q] = total
                continue
            total = total + before[q]
            main = total[:half] + total[half : 2 * half]
            top = main.astype(bf16)
            parts = (top, (main - top.astype(f32)).astype(bf16), total[2 * half :].astype(bf16))

            def store(target):
                for i in range(3):
                    target[i] = parts[i]

            for distance, target in enumerate(outs):
                pl.when(q ^ apart[0] == distance)(functools.partial(store, target))


def box_fock(side, lefts, right, before, apart):
    depth, width = sum(piece.shape[0] for piece in lefts[0]), lefts[0][0].shape[1]
    counts = [len(pieces) for pieces in lefts]
    tall = right.shape[-1]
    anywhere, vmem = pl.BlockSpec(memory_space=pl.ANY), pl.BlockSpec(memory_space=pltpu.VMEM)
    extra = [] if before is None else [before, apart]
    out = jax.ShapeDtypeStruct((len(lefts), tall, width), f32)
    if before is not None:
        out = [jax.ShapeDtypeStruct((3, tall // 3, width), bf16)] * len(lefts)
    return pl.pallas_call(
        functools.partial(fock_kernel, side, counts),
        out_shape=out,
        in_specs=[anywhere] * (sum(counts) + 1) + [vmem, pl.BlockSpec(memory_space=pltpu.SMEM)][: len(extra)],
        out_specs=vmem if before is None else [vmem] * len(lefts),
        scratch_shapes=[
            pltpu.VMEM((depth, len(lefts) * width), bf16),
            pltpu.VMEM(right.shape[1:], bf16),
            pltpu.VMEM((tall, depth), bf16),
            pltpu.SemaphoreType.DMA((sum(counts),)),
            pltpu.SemaphoreType.DMA(()),
        ],
        compiler_params=params(40),
        cost_estimate=pl.CostEstimate(
            flops=2 * len(lefts) * depth * width * tall, bytes_accessed=2 * len(lefts) * depth * width, transcendentals=0
        ),
        name="fock",
    )(right, *[piece for pieces in lefts for piece in pieces], *extra)


def root_kernel(levels, meta, *refs):
    pieces, (offset, root, whole, rows_f, cols_b, sems) = refs[:-6], refs[-6:]
    level, pair, orb = meta[0], meta[1], meta[2]
    coarse, width = offset.shape
    side = whole.shape[0]
    groups = side // width
    copies = []
    for piece, (z, y, q) in zip(pieces, piece_places(levels)):
        for i in range(len(z)):
            start = ((orb ^ q) * PAIR + (pair ^ y)) * coarse
            rows = pl.ds(pl.multiple_of(start, coarse), coarse)
            lanes = pl.ds(pl.multiple_of((level ^ z[i]) * width, width), width)
            copies.append(
                pltpu.make_async_copy(
                    piece.at[i * coarse : (i + 1) * coarse], whole.at[rows, lanes], sems.at[len(copies)]
                )
            )
    for copy in copies:
        copy.start()
    for copy in copies:
        copy.wait()
    row0 = pl.multiple_of((level * PAIR + pair) * coarse, coarse)
    own_lanes = pl.ds(pl.multiple_of(orb * width, width), width)
    rows = whole[pl.ds(row0, coarse), :]

    for j in range(groups):
        lanes = slice(j * width, (j + 1) * width)
        rows_f[:, lanes] = matmul(rows, whole[:, lanes])
    columns = whole[:, own_lanes]
    for i in range(groups):
        here = slice(i * width, (i + 1) * width)
        square = matmul(whole[here, :], columns)
        cols_b[here, :] = (0.25 * (whole[here, own_lanes].astype(f32) - square)).astype(bf16)
    left = (rows.astype(f32) - 0.25 * rows_f[...]).astype(bf16)
    value = matmul(left, cols_b[...]) + 0.125 * rows_f[:, own_lanes] - 0.5 * offset[...]
    row_ids = lax.broadcasted_iota(jnp.int32, value.shape, 0) + row0
    col_ids = lax.broadcasted_iota(jnp.int32, value.shape, 1) + orb * width
    root[...] = value + jnp.where(row_ids == col_ids, 1.0, 0.0)


def piece_places(levels):
    places = []
    for core in (0, 1):
        for half in range(2):
            z = [half * levels // 2 + i for i in range(levels // 2)]
            for second in (0, 1):
                for inner in (0, 1):
                    y, far = (second, inner) if half else (inner, second)
                    places.append((z, y, 2 * far + core))
    return places


def root_of(meta, pieces, offset, side, levels):
    coarse, width = offset.shape
    vmem, anywhere = pl.BlockSpec(memory_space=pltpu.VMEM), pl.BlockSpec(memory_space=pl.ANY)
    return pl.pallas_call(
        functools.partial(root_kernel, levels),
        out_shape=jax.ShapeDtypeStruct(offset.shape, f32),
        in_specs=[pl.BlockSpec(memory_space=pltpu.SMEM)] + [anywhere] * len(pieces) + [vmem],
        out_specs=vmem,
        scratch_shapes=[
            pltpu.VMEM((side, side), bf16),
            pltpu.VMEM((coarse, side), f32),
            pltpu.VMEM((side, width), bf16),
            pltpu.SemaphoreType.DMA((side // coarse * (side // width),)),
        ],
        compiler_params=params(40),
        cost_estimate=pl.CostEstimate(flops=16 * side * side * width, bytes_accessed=4 * side * side, transcendentals=0),
        name="root",
    )(meta, *pieces, offset)


def fill_tables(slots, levels, place_meta, facts, table, scale):
    level, pair = place_meta[0], place_meta[1]
    even = lax.rem(level, 2) == 0
    none = 6 * slots

    def place(slot_id):
        box = lax.div(slot_id, slots)
        apart = lax.div(box, PAIR) - level
        base = jnp.where(apart == 0, 0, jnp.where((apart < 0) == even, 4, 2))
        return (base + jnp.where(lax.rem(box, PAIR) != pair, 1, 0)) * slots + lax.rem(slot_id, slots)

    for index in range(4 * slots):
        group, r = divmod(index, slots)

        def fact(c):
            if group < 2:
                return facts[group, r, c]
            swap_id = jnp.where(even, 1, 0) if group == 2 else jnp.where(even, 0, 1)
            near_pair = 1 if group == 2 else 0
            return facts[2 + swap_id + jnp.where(pair == near_pair, 0, 2), r, c]

        box = (
            level * PAIR + pair,
            level * PAIR + 1 - pair,
            jnp.maximum(level * PAIR - 1, 0),
            jnp.minimum((level + 1) * PAIR, levels * PAIR - 1),
        )[group]
        there = (True, True, level > 0, level < levels - 1)[group]
        own_id = box * slots + r
        own_place = place(own_id)
        table[index, 0] = jnp.where((fact(7) > 0) & there, own_place, -1)
        for a in range(3):
            for k in (0, 2):
                distance = fact(2 * a + k // 2)
                target = place(jnp.maximum(own_id + distance, 0))
                target = jnp.where(distance < 16 * slots, target, none)
                table[index, 1 + 3 * a + k] = jnp.clip(target, 0, none)
            table[index, 2 + 3 * a] = own_place
        level_of = fact(6)
        scale[index] = jnp.where(level_of == 0, 0.5, jnp.where(level_of == 1, 1.0, 2.0))


def kinetic_kernel(edge, slots, levels, place_meta, facts, *refs):
    parts, refs = refs[:6], refs[6:]
    (fwd_in, fwd_out, back_in, back_mid, back_out), out, refs = refs[:5], refs[5], refs[6:]
    raw, x, outer, inner, total, total_fix, lines, columns, table, scale, sems = refs
    square = edge * edge
    own = PAIR * slots
    padded, width = x.shape[2:]
    copies = [pltpu.make_async_copy(part, raw.at[place], sems.at[place]) for place, part in enumerate(parts)]
    for copy in copies:
        copy.start()
    tail = padded - ROWS
    x[:, :, tail:, :] = jnp.zeros((x.shape[0], edge, ROWS, width), bf16)
    x[6 * slots] = jnp.zeros((edge, padded, width), bf16)
    total[...] = jnp.zeros_like(total)
    total_fix[...] = jnp.zeros_like(total_fix)
    fill_tables(slots, levels, place_meta, facts, table, scale)
    lines[...] = jnp.zeros_like(lines)
    for copy in copies:
        copy.wait()
    lanes = raw.shape[3]
    for t in range(own):
        for start in range(0, lines.shape[1], lanes):
            row = edge * square // 2 + 1 + 3 * (start // lanes)
            high, middle, low = (
                raw[t // slots, t % slots, row + i : row + i + 1, :].astype(f32) for i in range(3)
            )
            lines[t : t + 1, start : start + lanes] = (high + middle) + low
    columns[...] = lines[...].T

    def lay_out(place, carry):
        for slot in range(slots):
            for i in range(edge):
                part, row = i // (edge // 2), i % (edge // 2) * square
                x[place * slots + slot, i, :square, :] = raw[
                    place, slot, row : row + square, part * width : (part + 1) * width
                ]
        return carry

    lax.fori_loop(0, len(parts), lay_out, 0)
    chunks = -(-square // ROWS)

    def per_slot(s, carry):
        @pl.when(table[s, 0] >= 0)
        def _():
            own_scale = scale[s]
            half = 0.5 * own_scale
            sums = (total, total_fix)

            def split(exact):
                exact = own_scale * exact
                value = exact.astype(bf16).astype(f32)
                return (half * value).astype(bf16), (half * (value - exact)).astype(bf16)

            sources = [[table[s, 1 + 3 * a + k] for k in range(3)] for a in range(3)]
            here = sources[0][1]

            def forward(a):
                if a == 0:
                    for i in range(chunks):
                        rows = slice(i * ROWS, (i + 1) * ROWS)
                        block = [x[t, :, rows, :].reshape(edge * ROWS, width) for t in sources[0]]
                        fields = split(matmul(fwd_out[...], jnp.concatenate(block, axis=0)))
                        for field in range(2):
                            outer[field, :, rows, :] = fields[field].reshape(edge, ROWS, width)
                else:
                    for i in range(edge):
                        block = jnp.concatenate([x[t, i] for t in sources[a]], axis=0)
                        fields = split(matmul(fwd_in[a - 1], block))
                        for field in range(2):
                            inner[field, i, (a - 1) * padded : a * padded, :] = fields[field]

            def back_outer(k, target):
                for i in range(chunks):
                    rows = slice(i * ROWS, (i + 1) * ROWS)
                    for field in range(2):
                        term = matmul(back_out[k], outer[field, :, rows, :].reshape(edge * ROWS, width))
                        sums[field][target, :, rows, :] += term.reshape(edge, ROWS, width)

            @pl.when(here < own)
            def _():
                for a in range(3):
                    forward(a)
                back_outer(1, here)
                for i in range(edge):
                    for field in range(2):
                        sums[field][here, i] += matmul(back_mid[...], inner[field, i])

            for a in range(3):
                pl.when((here >= own) & ((sources[a][0] < own) | (sources[a][2] < own)))(functools.partial(forward, a))

            for k in (0, 2):
                for a in range(3):
                    target = sources[a][k]

                    @pl.when(target < own)
                    def _():
                        if a == 0:
                            back_outer(k, target)
                        else:
                            for i in range(edge):
                                for field in range(2):
                                    here = inner[field, i, (a - 1) * padded : a * padded, :]
                                    sums[field][target, i] += matmul(back_in[a - 1, k], here)

        return carry

    lax.fori_loop(0, table.shape[0], per_slot, 0)

    for t in range(own):
        for i in range(edge):
            rows = slice(i * square, (i + 1) * square)
            weighted = (columns[rows, t : t + 1] * x[t, i, :square, :].astype(f32)).astype(bf16)
            whole = total[t, i, :square, :] + weighted.astype(f32)
            top = whole.astype(bf16)
            low = (whole - top.astype(f32)).astype(bf16)
            fix = total_fix[t, i, :square, :].astype(bf16)
            out[t, rows, :] = jnp.concatenate([top, low, fix], axis=1)


def matrices_kernel(stacked, blocks, *refs):
    spots, outs = refs[:9], refs[9:]
    fwd_in, fwd_out, back_in, back_mid, back_out = outs
    for mode in range(3):
        spot, spread, same = spots[3 * mode : 3 * mode + 3]
        wide = matmul(matmul(spot[...], stacked[...]).astype(bf16), spread[...])
        wide = (wide * jnp.concatenate([same[...]] * 3, axis=1)).astype(bf16)
        if mode == 2:
            fwd_out[...] = wide
        else:
            fwd_in[mode] = wide
        for k in range(3):
            turned = lax.dot_general(spot[...], blocks[k], (((1,), (1,)), ((), ())), preferred_element_type=f32)
            turned = lax.dot_general(
                turned.astype(bf16), spot[...], (((1,), (1,)), ((), ())), preferred_element_type=f32
            )
            turned = (turned * same[...]).astype(bf16)
            if mode == 2:
                back_out[k] = turned
            else:
                back_in[mode, k] = turned
    back_mid[...] = jnp.concatenate([back_in[0, 1], back_in[1, 1]], axis=1)


def block_matrices(deriv_blocks):
    edge = deriv_blocks.shape[1]
    square = edge * edge
    padded = -(-square // ROWS) * ROWS
    tall = edge * ROWS
    ids = np.arange(padded)
    slow = ((ids[:, None] // edge) == np.arange(edge)).astype(np.float32)
    fast = (((ids[:, None] % edge) == np.arange(edge)) & (ids[:, None] < square)).astype(np.float32)
    ids = np.arange(tall)
    outer = ((ids[:, None] // ROWS) == np.arange(edge)).astype(np.float32)
    within = ((ids[:, None] % ROWS) == np.arange(ROWS)).astype(np.float32)
    stacked = jnp.moveaxis(deriv_blocks, 0, 1).reshape(edge, 3 * edge)
    constants = []
    for spot, mask in ((slow, fast), (fast, slow), (outer, within)):
        spread = np.kron(np.eye(3, dtype=np.float32), spot.T)
        constants += [jnp.asarray(spot, bf16), jnp.asarray(spread, bf16), jnp.asarray(mask @ mask.T, f32)]
    vmem = pl.BlockSpec(memory_space=pltpu.VMEM)
    shapes = [(2, padded, 3 * padded), (tall, 3 * tall), (2, 3, padded, padded), (padded, 2 * padded), (3, tall, tall)]
    return pl.pallas_call(
        matrices_kernel,
        out_shape=[jax.ShapeDtypeStruct(shape, bf16) for shape in shapes],
        in_specs=[vmem] * 11,
        out_specs=[vmem] * 5,
        compiler_params=params(24),
        name="matrices",
    )(stacked, deriv_blocks, *constants)


def kinetic(parts, place_meta, facts, matrices, edge, coefficients, levels):
    slots, folded, lanes = parts[0].shape
    width = lanes // 2
    padded = matrices[0].shape[1]
    own = PAIR * slots
    vmem = pl.BlockSpec(memory_space=pltpu.VMEM)
    smem = pl.BlockSpec(memory_space=pltpu.SMEM)
    anywhere = pl.BlockSpec(memory_space=pl.ANY)
    return pl.pallas_call(
        functools.partial(kinetic_kernel, edge, slots, levels),
        out_shape=jax.ShapeDtypeStruct((own, coefficients, 3 * width), bf16),
        in_specs=[smem] * 2 + [anywhere] * 6 + [vmem] * 5,
        out_specs=vmem,
        scratch_shapes=[
            pltpu.VMEM((6, slots, folded, lanes), bf16),
            pltpu.VMEM((6 * slots + 1, edge, padded, width), bf16),
            pltpu.VMEM((2, edge, padded, width), bf16),
            pltpu.VMEM((2, edge, 2 * padded, width), bf16),
            pltpu.VMEM((own, edge, padded, width), f32),
            pltpu.VMEM((own, edge, padded, width), f32),
            pltpu.VMEM((own + -own % 8, coefficients + -coefficients % lanes), f32),
            pltpu.VMEM((coefficients + -coefficients % lanes, own + -own % 8), f32),
            pltpu.SMEM((4 * slots, 10), jnp.int32),
            pltpu.SMEM((4 * slots,), f32),
            pltpu.SemaphoreType.DMA((6,)),
        ],
        compiler_params=params(48),
        cost_estimate=pl.CostEstimate(flops=2 * 10**10, bytes_accessed=40 * 10**6, transcendentals=0),
        name="kinetic",
    )(place_meta, facts, *parts, *matrices)


def offset_sum_kernel(meta, *refs):
    blocks, (small, kept, sent) = refs[:-3], refs[-3:]
    total = blocks[0][...].astype(f32)
    for block in blocks[1:]:
        total = total + block[...].astype(f32)
    small[...] = total.astype(bf16)
    half = kept.shape[0]
    first = meta[0] == 0
    low, high = total[:, :half].T, total[:, half:].T
    kept[...] = jnp.where(first, low, high)
    sent[...] = jnp.where(first, high, low)


def fock_sum_kernel(meta, *refs):
    blocks, (share, kept, sent) = refs[:-3], refs[-3:]
    sums = [sum((block[part].astype(f32) for block in blocks[1:]), blocks[0][part].astype(f32)) for part in range(3)]
    main = sums[0] + sums[1]
    share[...] = sums[2].astype(bf16)
    half = kept.shape[0]
    first = meta[0] == 0
    low, high = main[:, :half].T, main[:, half:].T
    kept[...] = jnp.where(first, low, high)
    sent[...] = jnp.where(first, high, low)


def level_sum(kernel, meta, blocks):
    tall, width = blocks[0].shape[-2:]
    vmem = pl.BlockSpec(memory_space=pltpu.VMEM)
    turned = jax.ShapeDtypeStruct((width // PAIR, tall), f32)
    return pl.pallas_call(
        kernel,
        out_shape=[jax.ShapeDtypeStruct((tall, width), bf16), turned, turned],
        in_specs=[pl.BlockSpec(memory_space=pltpu.SMEM)] + [vmem] * len(blocks),
        out_specs=[vmem] * 3,
        compiler_params=params(24),
        name="level_sum",
    )(meta, *blocks)


def body(orbitals, potential, deriv_blocks, levels, box_counts, neighbours):
    slots, coefficients, own_width = orbitals.shape
    edge = deriv_blocks.shape[1]
    level, pair, orb = lax.axis_index("lvl"), lax.axis_index("pair"), lax.axis_index("orb")
    level_count, orb_count = lax.axis_size("lvl"), lax.axis_size("orb")
    half, fold = own_width // PAIR, coefficients // 2
    all_width = own_width * orb_count
    box_rows = all_width // (level_count * PAIR)
    first = pair == 0
    groups = range(orb_count)
    square_grid = level_count == orb_count == 4 and box_rows == half
    row0, col0 = (level * PAIR + pair) * box_rows, orb * own_width

    own_base = (level * PAIR + pair) * slots
    pack_meta = jnp.stack([pair, box_counts[0], own_base]).astype(jnp.int32)
    theirs, mine = pack(pack_meta, neighbours, levels, orbitals, potential)
    active = orbitals

    far = {q: swap(active, "orb", q) for q in groups if q and q % 2 == 0}
    beside = swap(theirs, "pair", 1)
    first_mine, second_mine = trade(mine, "lvl", 0), trade(mine, "lvl", 1)
    later_mine, beside = lax.optimization_barrier((mine, beside))
    beside_rest = swap(later_mine, "pair", 1)
    first_beside, second_beside = trade(beside, "lvl", 0), trade(beside, "lvl", 1)

    matrices = block_matrices(deriv_blocks)

    def facts_of(parts):
        return jnp.stack([part[:, fold, :8] for part in parts]).astype(f32).astype(jnp.int32)

    early_facts = facts_of([mine, beside, first_mine, second_mine])
    flat = lambda block: block.reshape(-1, block.shape[-1])
    cut = -(-slots * coefficients // (2 * ROWS)) * ROWS
    beside_all, beside_top = unfold(pack_meta, beside, beside_rest, fold, cut)

    parts = [mine, beside, first_mine, first_beside, second_mine, second_beside]
    far, active, parts, beside_all, beside_top, matrices, early_facts = lax.optimization_barrier(
        (far, active, parts, beside_all, beside_top, matrices, early_facts)
    )
    facts = jnp.concatenate([early_facts, facts_of([parts[3], parts[5]])])
    cross = {q: [swap(beside_top, "orb", q), swap(flat(far[q])[cut:], "pair", 1)] for q in far}
    left_own = {0: active, 1: swap(active, "orb", 1), **far}
    left_beside = {0: [beside_all], 1: [swap(beside_all, "orb", 1)]}
    for q in far:
        left_own[q + 1] = swap(far[q], "orb", 1)

    def natural(blocks):
        return jnp.concatenate([lax.dynamic_index_in_dim(blocks, orb ^ j, keepdims=False) for j in groups], axis=1)

    def along_levels(blocks):
        mine_block = lambda target: lax.dynamic_index_in_dim(blocks, orb ^ target, keepdims=False)
        steps = range(1, level_count)
        return [mine_block(level)] + [swap(mine_block(level ^ step), "lvl", step) for step in steps]

    def both_halves(kept, got):
        return jnp.concatenate([jnp.where(first, kept, got), jnp.where(first, got, kept)], axis=1)

    def own_block(strip):
        strip = lax.all_gather(lax.psum(strip, "lvl"), ("orb", "pair"), axis=0, tiled=True)
        strip = lax.dynamic_slice_in_dim(strip, row0, box_rows, axis=0)
        return lax.dynamic_slice_in_dim(strip, col0, own_width, axis=1)

    live_rows = box_counts[0] * coefficients
    meta = jnp.stack([pair, slots * coefficients, live_rows]).astype(jnp.int32)

    place_meta = jnp.stack([level, pair]).astype(jnp.int32)
    right = kinetic(parts, place_meta, facts, matrices, edge, coefficients, level_count)

    cross, right, meta = lax.optimization_barrier((cross, right, meta))
    lefts_own = [[flat(left_own[q])] for q in groups]
    lefts_beside = dict(left_beside)
    for q in far:
        lefts_beside[q] = list(cross[q])
        lefts_beside[q + 1] = [swap(piece, "orb", 1) for piece in cross[q]]
    lefts_beside = [lefts_beside[q] for q in groups]

    share = 1.0 / level_count
    blocks = box_correlation(share, meta, lefts_own, None, half)
    blocks = box_correlation(share, meta, lefts_beside, blocks, half)
    right = right.reshape(2, slots * coefficients, 3 * half)
    fock_part = box_fock(0, lefts_own, right, None, None)
    if square_grid:
        sent = along_levels(blocks)
        sent, fock_part = lax.optimization_barrier((sent, fock_part))
        small, kept, other = level_sum(offset_sum_kernel, meta, sent)
        offset = both_halves(kept, swap(other, "pair", 1))
    else:
        offset = own_block(natural(blocks).astype(f32))
    row_ids = row0 + jnp.arange(box_rows, dtype=jnp.int32)
    col_ids = col0 + jnp.arange(own_width, dtype=jnp.int32)
    correlation = offset + (row_ids[:, None] == col_ids[None, :]).astype(f32)
    apart = (orb ^ level if square_grid else 0 * orb).reshape(1).astype(jnp.int32)
    fock_blocks = box_fock(1, lefts_beside, right, fock_part, apart)
    if square_grid:
        pieces = [small] + [swap(small, "lvl", z) for z in range(1, level_count)]
        pieces, fock_blocks, offset = lax.optimization_barrier((pieces, fock_blocks, offset))
        join = functools.partial(jnp.concatenate, axis=0)
        top, low = join(pieces[: level_count // 2]), join(pieces[level_count // 2 :])
        sent = [fock_blocks[0]] + [swap(fock_blocks[step], "lvl", step) for step in range(1, level_count)]
        got = [swap(top, "pair", 1), swap(low, "orb", 2)]
        got, sent[:2] = lax.optimization_barrier((got, sent[:2]))
        tops, lows = [top, got[0]], [low, got[1]]
        far_tops, far_lows = [swap(piece, "orb", 2) for piece in tops], [swap(piece, "pair", 1) for piece in lows]
        far_tops, far_lows, sent = lax.optimization_barrier((far_tops, far_lows, sent))
        pieces = tops + far_tops + lows + far_lows
        pieces += [swap(piece, "orb", 1) for piece in pieces]
        root_meta = jnp.stack([level, pair, orb]).astype(jnp.int32)
        inverse_root = root_of(root_meta, pieces, offset, all_width, level_count)
        share, kept, other = level_sum(fock_sum_kernel, meta, sent)
        to = [
            ((z * PAIR + y) * orb_count + o, (o * PAIR + y) * orb_count + z)
            for z in range(level_count)
            for y in range(PAIR)
            for o in groups
        ]
        got = swap(other, "pair", 1), lax.ppermute(share, BOX + ("orb",), to)
        inverse_root, got = lax.optimization_barrier((inverse_root, got))
        fock = both_halves(kept, got[0]) + got[1].astype(f32)
    else:
        fock_blocks = jnp.stack(fock_blocks)
        main = natural(fock_blocks[:, 0]).astype(f32) + natural(fock_blocks[:, 1]).astype(f32)
        main = lax.all_gather(lax.psum(main, "lvl"), "pair", axis=0, tiled=True)
        fock = lax.dynamic_slice_in_dim(main, row0, box_rows, axis=1).T + own_block(natural(fock_blocks[:, 2]).astype(f32))
        gathered = lax.all_gather(offset.astype(bf16), "orb", axis=1, tiled=True)
        whole = lax.all_gather(gathered, BOX, axis=0, tiled=True)
        rows_of = lax.dynamic_slice_in_dim(whole, row0, box_rows, axis=0)
        cols_of = lax.dynamic_slice_in_dim(whole, col0, own_width, axis=1)
        row_square, col_square = matmul(rows_of, whole), matmul(whole, cols_of)
        left = (rows_of.astype(f32) - 0.25 * row_square).astype(bf16)
        right_side = (0.25 * (cols_of.astype(f32) - col_square)).astype(bf16)
        own_square = lax.dynamic_slice_in_dim(row_square, col0, own_width, axis=1)
        inverse_root = correlation - 1.5 * offset + 0.125 * own_square + matmul(left, right_side)
    return fock, correlation, inverse_root


def solution(mesh):
    levels = mesh.shape["box"] // PAIR
    split = Mesh(mesh.devices.reshape(levels, PAIR, mesh.shape["orb"]), ("lvl", "pair", "orb"))
    in_specs = (P(BOX, None, "orb"), P(BOX, None), P(), P(BOX), P(BOX), P(BOX, None, None))
    out_specs = (P(BOX, "orb"),) * 3
    return jax.shard_map(body, mesh=split, in_specs=in_specs, out_specs=out_specs, check_vma=False)
```

```python
import functools

import jax
import jax.numpy as jnp
import numpy as np
from jax import lax
from jax.experimental import pallas as pl
from jax.experimental.pallas import tpu as pltpu
from jax.sharding import Mesh, PartitionSpec as P

PAIR = 2
ROWS = 16
BOX = ("lvl", "pair")
f32, bf16 = jnp.float32, jnp.bfloat16


def swap(value, axis, bit):
    count = lax.axis_size(axis)
    return lax.ppermute(value, axis, [(i, i ^ bit) for i in range(count)])


def trade(value, axis, start):
    pairs = [(i, i + 1) for i in range(start, lax.axis_size(axis) - 1, 2)]
    return lax.ppermute(value, axis, pairs + [(b, a) for a, b in pairs])


def matmul(left, right):
    return jnp.dot(left, right, preferred_element_type=f32)


def params(mebibytes):
    return pltpu.CompilerParams(vmem_limit_bytes=mebibytes * 1024 * 1024)


def pack_kernel(meta, neighbours, levels, orbitals, pot, theirs, mine):
    slots, coefficients, width = orbitals.shape
    half, fold = width // PAIR, coefficients // 2
    first = meta[0] == 0
    place = lax.broadcasted_iota(jnp.int32, (8, width), 1)
    for slot in range(slots):
        keep = slot < meta[1]
        for part in range(2):
            here = orbitals[slot, part * fold : (part + 1) * fold, :]
            here = jnp.where(keep, here, jnp.zeros_like(here))
            low, high = here[:, :half], here[:, half:]
            lanes = slice(part * half, (part + 1) * half)
            theirs[slot, :fold, lanes] = jnp.where(first, high, low)
            mine[slot, :fold, lanes] = jnp.where(first, low, high)
        own_id = meta[2] + slot
        facts = jnp.where(place == 6, levels[slot], jnp.where(place == 7, jnp.where(keep, 1, 0), 0))
        for c in range(6):
            target = neighbours[slot, c // 2, c % 2]
            facts = jnp.where(place == c, jnp.where(target >= 0, target - own_id, 16 * slots), facts)
        facts = facts.astype(f32).astype(bf16)
        for packed in (theirs, mine):
            packed[slot, fold : fold + 1, :] = facts[:1]
        row = fold + 1
        for start in range(0, pot.shape[1], width):
            stop = min(start + width, pot.shape[1])
            exact = pot[slot : slot + 1, start:stop]
            for _ in range(3):
                part = exact.astype(bf16)
                exact = exact - part.astype(f32)
                for packed in (theirs, mine):
                    packed[slot, row : row + 1, : stop - start] = part
                    if stop - start < width:
                        packed[slot, row : row + 1, stop - start :] = jnp.zeros((1, width - stop + start), bf16)
                row += 1
        for packed in (theirs, mine):
            packed[slot, row:, :] = jnp.zeros((packed.shape[1] - row, width), bf16)


def pack(meta, neighbours, levels, orbitals, pot):
    slots, coefficients, width = orbitals.shape
    fold = coefficients // 2
    padded = -(-(fold + 1 + 3 * -(-coefficients // width)) // ROWS) * ROWS
    vmem, smem = pl.BlockSpec(memory_space=pltpu.VMEM), pl.BlockSpec(memory_space=pltpu.SMEM)
    return pl.pallas_call(
        pack_kernel,
        out_shape=[jax.ShapeDtypeStruct((slots, padded, width), bf16)] * 2,
        in_specs=[smem, smem, smem, vmem, vmem],
        out_specs=[vmem, vmem],
        compiler_params=params(24),
        name="pack",
    )(meta, neighbours, levels, orbitals, pot)


def unfold_kernel(fold, meta, beside_in, rest_in, whole, top, beside, rest, sems):
    copies = [
        pltpu.make_async_copy(source, target, sems.at[i])
        for i, (source, target) in enumerate(((beside_in, beside), (rest_in, rest)))
    ]
    for copy in copies:
        copy.start()
    slots, _, width = beside.shape
    half = width // PAIR
    first = meta[0] == 0
    for copy in copies:
        copy.wait()
    for slot in range(slots):
        for part in range(2):
            lanes = slice(part * half, (part + 1) * half)
            near, far = beside[slot, :fold, lanes], rest[slot, :fold, lanes]
            start = (2 * slot + part) * fold
            here = jnp.concatenate([jnp.where(first, near, far), jnp.where(first, far, near)], axis=1)
            whole[start : start + fold, :] = here
    top[...] = whole[: top.shape[0], :]


def unfold(meta, beside, rest, fold, cut):
    slots, _, width = beside.shape
    vmem = pl.BlockSpec(memory_space=pltpu.VMEM)
    return pl.pallas_call(
        functools.partial(unfold_kernel, fold),
        out_shape=[
            jax.ShapeDtypeStruct((2 * slots * fold, width), bf16),
            jax.ShapeDtypeStruct((cut, width), bf16),
        ],
        in_specs=[pl.BlockSpec(memory_space=pltpu.SMEM)] + [pl.BlockSpec(memory_space=pltpu.HBM)] * 2,
        out_specs=[vmem, vmem],
        scratch_shapes=[
            pltpu.VMEM(beside.shape, bf16),
            pltpu.VMEM(beside.shape, bf16),
            pltpu.SemaphoreType.DMA((2,)),
        ],
        compiler_params=params(24),
        name="unfold",
    )(meta, beside, rest)


def load_left(lefts, held, sems):
    copies = []
    for q, pieces in enumerate(lefts):
        row = 0
        for piece in pieces:
            rows, width = piece.shape
            here = held.at[row : row + rows, q * width : (q + 1) * width]
            copies.append(pltpu.make_async_copy(piece, here, sems.at[len(copies)]))
            row += rows
    for copy in copies:
        copy.start()
    return copies


def grouped(refs, counts):
    refs = list(refs)
    return [[refs.pop(0) for _ in range(count)] for count in counts]


def correlation_kernel(share, counts, meta, *refs):
    refs, (out, held, turned, sems) = refs[:-4], refs[-4:]
    groups, half, width = out.shape
    lefts, before = grouped(refs, counts), refs[sum(counts) :]
    copies = load_left(lefts, held, sems)
    first = meta[0] == 0
    for copy in copies[: counts[0]]:
        copy.wait()
    own = held[:, :width]
    own = jnp.where(first, own[:, :half], own[:, half:]).T
    live = lax.broadcasted_iota(jnp.int32, own.shape, 1) < meta[1 if before else 2]
    turned[...] = jnp.where(live, own, jnp.zeros_like(own))
    for base in range(0, groups, 2):
        for copy in copies[max(sum(counts[:base]), counts[0]) : sum(counts[: base + 2])]:
            copy.wait()
        wide = matmul(turned[...], held[:, base * width : (base + 2) * width])
        for q in (base, base + 1):
            total = wide[:, (q - base) * width : (q - base + 1) * width]
            if before:
                total = total + before[0][q]
                if q == 0:
                    rows = lax.broadcasted_iota(jnp.int32, (half, width), 0) + jnp.where(first, 0, half)
                    columns = lax.broadcasted_iota(jnp.int32, (half, width), 1)
                    total = total - jnp.where(rows == columns, share, 0.0)
            out[q] = total.astype(out.dtype)


def box_correlation(share, meta, lefts, before, half):
    depth, width = sum(piece.shape[0] for piece in lefts[0]), lefts[0][0].shape[1]
    counts = [len(pieces) for pieces in lefts]
    vmem = pl.BlockSpec(memory_space=pltpu.VMEM)
    extra = [] if before is None else [before]
    return pl.pallas_call(
        functools.partial(correlation_kernel, share, counts),
        out_shape=jax.ShapeDtypeStruct((len(lefts), half, width), f32 if before is None else bf16),
        in_specs=[pl.BlockSpec(memory_space=pltpu.SMEM)]
        + [pl.BlockSpec(memory_space=pl.ANY)] * sum(counts)
        + [vmem] * len(extra),
        out_specs=vmem,
        scratch_shapes=[
            pltpu.VMEM((depth, len(lefts) * width), bf16),
            pltpu.VMEM((half, depth), bf16),
            pltpu.SemaphoreType.DMA((sum(counts),)),
        ],
        compiler_params=params(32),
        cost_estimate=pl.CostEstimate(
            flops=2 * len(lefts) * depth * width * half, bytes_accessed=2 * len(lefts) * depth * width, transcendentals=0
        ),
        name="correlation",
    )(meta, *[piece for pieces in lefts for piece in pieces], *extra)


def fock_kernel(side, counts, right, *refs):
    outs, (held, raw, turned, sems, last_sem) = refs[sum(counts) : -5], refs[-5:]
    lefts = grouped(refs, counts)
    before, apart, outs = (None, None, outs) if len(outs) == 1 else (outs[0], outs[1], outs[2:])
    out = outs[0]
    last = pltpu.make_async_copy(right.at[side], raw, last_sem)
    last.start()
    copies = load_left(lefts, held, sems)
    half, width = out.shape[-2] // (3 if before is None else 1), out.shape[-1]
    last.wait()
    turned[...] = raw[...].T
    for base in range(0, len(lefts), 2):
        for copy in copies[sum(counts[:base]) : sum(counts[: base + 2])]:
            copy.wait()
        wide = matmul(turned[...], held[:, base * width : (base + 2) * width])
        for q in (base, base + 1):
            total = wide[:, (q - base) * width : (q - base + 1) * width]
            if before is None:
                out[q] = total
                continue
            total = total + before[q]
            main = total[:half] + total[half : 2 * half]
            top = main.astype(bf16)
            parts = (top, (main - top.astype(f32)).astype(bf16), total[2 * half :].astype(bf16))

            def store(target):
                for i in range(3):
                    target[i] = parts[i]

            for distance, target in enumerate(outs):
                pl.when(q ^ apart[0] == distance)(functools.partial(store, target))


def box_fock(side, lefts, right, before, apart):
    depth, width = sum(piece.shape[0] for piece in lefts[0]), lefts[0][0].shape[1]
    counts = [len(pieces) for pieces in lefts]
    tall = right.shape[-1]
    anywhere, vmem = pl.BlockSpec(memory_space=pl.ANY), pl.BlockSpec(memory_space=pltpu.VMEM)
    extra = [] if before is None else [before, apart]
    out = jax.ShapeDtypeStruct((len(lefts), tall, width), f32)
    if before is not None:
        out = [jax.ShapeDtypeStruct((3, tall // 3, width), bf16)] * len(lefts)
    return pl.pallas_call(
        functools.partial(fock_kernel, side, counts),
        out_shape=out,
        in_specs=[anywhere] * (sum(counts) + 1) + [vmem, pl.BlockSpec(memory_space=pltpu.SMEM)][: len(extra)],
        out_specs=vmem if before is None else [vmem] * len(lefts),
        scratch_shapes=[
            pltpu.VMEM((depth, len(lefts) * width), bf16),
            pltpu.VMEM(right.shape[1:], bf16),
            pltpu.VMEM((tall, depth), bf16),
            pltpu.SemaphoreType.DMA((sum(counts),)),
            pltpu.SemaphoreType.DMA(()),
        ],
        compiler_params=params(40),
        cost_estimate=pl.CostEstimate(
            flops=2 * len(lefts) * depth * width * tall, bytes_accessed=2 * len(lefts) * depth * width, transcendentals=0
        ),
        name="fock",
    )(right, *[piece for pieces in lefts for piece in pieces], *extra)


def root_kernel(levels, meta, *refs):
    pieces, (offset, root, whole, rows_f, cols_b, sems) = refs[:-6], refs[-6:]
    level, pair, orb = meta[0], meta[1], meta[2]
    coarse, width = offset.shape
    side = whole.shape[0]
    groups = side // width
    copies = []
    for piece, (z, y, q) in zip(pieces, piece_places(levels)):
        for i in range(len(z)):
            start = ((orb ^ q) * PAIR + (pair ^ y)) * coarse
            rows = pl.ds(pl.multiple_of(start, coarse), coarse)
            lanes = pl.ds(pl.multiple_of((level ^ z[i]) * width, width), width)
            copies.append(
                pltpu.make_async_copy(
                    piece.at[i * coarse : (i + 1) * coarse], whole.at[rows, lanes], sems.at[len(copies)]
                )
            )
    for copy in copies:
        copy.start()
    for copy in copies:
        copy.wait()
    row0 = pl.multiple_of((level * PAIR + pair) * coarse, coarse)
    own_lanes = pl.ds(pl.multiple_of(orb * width, width), width)
    rows = whole[pl.ds(row0, coarse), :]

    for j in range(groups):
        lanes = slice(j * width, (j + 1) * width)
        rows_f[:, lanes] = matmul(rows, whole[:, lanes])
    columns = whole[:, own_lanes]
    for i in range(groups):
        here = slice(i * width, (i + 1) * width)
        square = matmul(whole[here, :], columns)
        cols_b[here, :] = (0.25 * (whole[here, own_lanes].astype(f32) - square)).astype(bf16)
    left = (rows.astype(f32) - 0.25 * rows_f[...]).astype(bf16)
    value = matmul(left, cols_b[...]) + 0.125 * rows_f[:, own_lanes] - 0.5 * offset[...]
    row_ids = lax.broadcasted_iota(jnp.int32, value.shape, 0) + row0
    col_ids = lax.broadcasted_iota(jnp.int32, value.shape, 1) + orb * width
    root[...] = value + jnp.where(row_ids == col_ids, 1.0, 0.0)


def piece_places(levels):
    places = []
    for core in (0, 1):
        for half in range(2):
            z = [half * levels // 2 + i for i in range(levels // 2)]
            for second in (0, 1):
                for inner in (0, 1):
                    y, far = (second, inner) if half else (inner, second)
                    places.append((z, y, 2 * far + core))
    return places


def root_of(meta, pieces, offset, side, levels):
    coarse, width = offset.shape
    vmem, anywhere = pl.BlockSpec(memory_space=pltpu.VMEM), pl.BlockSpec(memory_space=pl.ANY)
    return pl.pallas_call(
        functools.partial(root_kernel, levels),
        out_shape=jax.ShapeDtypeStruct(offset.shape, f32),
        in_specs=[pl.BlockSpec(memory_space=pltpu.SMEM)] + [anywhere] * len(pieces) + [vmem],
        out_specs=vmem,
        scratch_shapes=[
            pltpu.VMEM((side, side), bf16),
            pltpu.VMEM((coarse, side), f32),
            pltpu.VMEM((side, width), bf16),
            pltpu.SemaphoreType.DMA((side // coarse * (side // width),)),
        ],
        compiler_params=params(40),
        cost_estimate=pl.CostEstimate(flops=16 * side * side * width, bytes_accessed=4 * side * side, transcendentals=0),
        name="root",
    )(meta, *pieces, offset)


def fill_tables(slots, levels, place_meta, facts, table, scale):
    level, pair = place_meta[0], place_meta[1]
    even = lax.rem(level, 2) == 0
    none = 6 * slots

    def place(slot_id):
        box = lax.div(slot_id, slots)
        apart = lax.div(box, PAIR) - level
        base = jnp.where(apart == 0, 0, jnp.where((apart < 0) == even, 4, 2))
        return (base + jnp.where(lax.rem(box, PAIR) != pair, 1, 0)) * slots + lax.rem(slot_id, slots)

    for index in range(4 * slots):
        group, r = divmod(index, slots)

        def fact(c):
            if group < 2:
                return facts[group, r, c]
            swap_id = jnp.where(even, 1, 0) if group == 2 else jnp.where(even, 0, 1)
            near_pair = 1 if group == 2 else 0
            return facts[2 + swap_id + jnp.where(pair == near_pair, 0, 2), r, c]

        box = (
            level * PAIR + pair,
            level * PAIR + 1 - pair,
            jnp.maximum(level * PAIR - 1, 0),
            jnp.minimum((level + 1) * PAIR, levels * PAIR - 1),
        )[group]
        there = (True, True, level > 0, level < levels - 1)[group]
        own_id = box * slots + r
        own_place = place(own_id)
        table[index, 0] = jnp.where((fact(7) > 0) & there, own_place, -1)
        for a in range(3):
            for k in (0, 2):
                distance = fact(2 * a + k // 2)
                target = place(jnp.maximum(own_id + distance, 0))
                target = jnp.where(distance < 16 * slots, target, none)
                table[index, 1 + 3 * a + k] = jnp.clip(target, 0, none)
            table[index, 2 + 3 * a] = own_place
        level_of = fact(6)
        scale[index] = jnp.where(level_of == 0, 0.5, jnp.where(level_of == 1, 1.0, 2.0))


def kinetic_kernel(edge, slots, levels, place_meta, facts, *refs):
    parts, refs = refs[:6], refs[6:]
    (fwd_in, fwd_out, back_in, back_mid, back_out), out, refs = refs[:5], refs[5], refs[6:]
    raw, x, outer, inner, total, total_fix, lines, columns, table, scale, sems = refs
    square = edge * edge
    own = PAIR * slots
    padded, width = x.shape[2:]
    copies = [pltpu.make_async_copy(part, raw.at[place], sems.at[place]) for place, part in enumerate(parts)]
    for copy in copies:
        copy.start()
    tail = padded - ROWS
    x[:, :, tail:, :] = jnp.zeros((x.shape[0], edge, ROWS, width), bf16)
    x[6 * slots] = jnp.zeros((edge, padded, width), bf16)
    total[...] = jnp.zeros_like(total)
    total_fix[...] = jnp.zeros_like(total_fix)
    fill_tables(slots, levels, place_meta, facts, table, scale)
    lines[...] = jnp.zeros_like(lines)
    for copy in copies:
        copy.wait()
    lanes = raw.shape[3]
    for t in range(own):
        for start in range(0, lines.shape[1], lanes):
            row = edge * square // 2 + 1 + 3 * (start // lanes)
            high, middle, low = (
                raw[t // slots, t % slots, row + i : row + i + 1, :].astype(f32) for i in range(3)
            )
            lines[t : t + 1, start : start + lanes] = (high + middle) + low
    columns[...] = lines[...].T

    def lay_out(place, carry):
        for slot in range(slots):
            for i in range(edge):
                part, row = i // (edge // 2), i % (edge // 2) * square
                x[place * slots + slot, i, :square, :] = raw[
                    place, slot, row : row + square, part * width : (part + 1) * width
                ]
        return carry

    lax.fori_loop(0, len(parts), lay_out, 0)
    chunks = -(-square // ROWS)

    def per_slot(s, carry):
        @pl.when(table[s, 0] >= 0)
        def _():
            both_scales = 0.5 * scale[s] * scale[s]
            sums = (total, total_fix)

            def split(exact):
                exact = both_scales * exact
                value = exact.astype(bf16)
                return value, (value.astype(f32) - exact).astype(bf16)

            sources = [[table[s, 1 + 3 * a + k] for k in range(3)] for a in range(3)]
            here = sources[0][1]

            def forward(a):
                if a == 0:
                    for i in range(chunks):
                        rows = slice(i * ROWS, (i + 1) * ROWS)
                        block = [x[t, :, rows, :].reshape(edge * ROWS, width) for t in sources[0]]
                        fields = split(matmul(fwd_out[...], jnp.concatenate(block, axis=0)))
                        for field in range(2):
                            outer[field, :, rows, :] = fields[field].reshape(edge, ROWS, width)
                else:
                    for i in range(edge):
                        block = jnp.concatenate([x[t, i] for t in sources[a]], axis=0)
                        fields = split(matmul(fwd_in[a - 1], block))
                        for field in range(2):
                            inner[field, i, (a - 1) * padded : a * padded, :] = fields[field]

            def back_outer(k, target):
                for i in range(chunks):
                    rows = slice(i * ROWS, (i + 1) * ROWS)
                    for field in range(2):
                        term = matmul(back_out[k], outer[field, :, rows, :].reshape(edge * ROWS, width))
                        sums[field][target, :, rows, :] += term.reshape(edge, ROWS, width)

            @pl.when(here < own)
            def _():
                for a in range(3):
                    forward(a)
                back_outer(1, here)
                for i in range(edge):
                    for field in range(2):
                        sums[field][here, i] += matmul(back_mid[...], inner[field, i])

            for a in range(3):
                pl.when((here >= own) & ((sources[a][0] < own) | (sources[a][2] < own)))(functools.partial(forward, a))

            for k in (0, 2):
                for a in range(3):
                    target = sources[a][k]

                    @pl.when(target < own)
                    def _():
                        if a == 0:
                            back_outer(k, target)
                        else:
                            for i in range(edge):
                                for field in range(2):
                                    here = inner[field, i, (a - 1) * padded : a * padded, :]
                                    sums[field][target, i] += matmul(back_in[a - 1, k], here)

        return carry

    lax.fori_loop(0, table.shape[0], per_slot, 0)

    for t in range(own):
        for i in range(edge):
            rows = slice(i * square, (i + 1) * square)
            weighted = (columns[rows, t : t + 1] * x[t, i, :square, :].astype(f32)).astype(bf16)
            whole = total[t, i, :square, :] + weighted.astype(f32)
            top = whole.astype(bf16)
            low = (whole - top.astype(f32)).astype(bf16)
            fix = total_fix[t, i, :square, :].astype(bf16)
            out[t, rows, :] = jnp.concatenate([top, low, fix], axis=1)


def matrices_kernel(stacked, blocks, *refs):
    spots, outs = refs[:9], refs[9:]
    fwd_in, fwd_out, back_in, back_mid, back_out = outs
    for mode in range(3):
        spot, spread, same = spots[3 * mode : 3 * mode + 3]
        wide = matmul(matmul(spot[...], stacked[...]).astype(bf16), spread[...])
        wide = (wide * jnp.concatenate([same[...]] * 3, axis=1)).astype(bf16)
        if mode == 2:
            fwd_out[...] = wide
        else:
            fwd_in[mode] = wide
        for k in range(3):
            turned = lax.dot_general(spot[...], blocks[k], (((1,), (1,)), ((), ())), preferred_element_type=f32)
            turned = lax.dot_general(
                turned.astype(bf16), spot[...], (((1,), (1,)), ((), ())), preferred_element_type=f32
            )
            turned = (turned * same[...]).astype(bf16)
            if mode == 2:
                back_out[k] = turned
            else:
                back_in[mode, k] = turned
    back_mid[...] = jnp.concatenate([back_in[0, 1], back_in[1, 1]], axis=1)


def block_matrices(deriv_blocks):
    edge = deriv_blocks.shape[1]
    square = edge * edge
    padded = -(-square // ROWS) * ROWS
    tall = edge * ROWS
    ids = np.arange(padded)
    slow = ((ids[:, None] // edge) == np.arange(edge)).astype(np.float32)
    fast = (((ids[:, None] % edge) == np.arange(edge)) & (ids[:, None] < square)).astype(np.float32)
    ids = np.arange(tall)
    outer = ((ids[:, None] // ROWS) == np.arange(edge)).astype(np.float32)
    within = ((ids[:, None] % ROWS) == np.arange(ROWS)).astype(np.float32)
    stacked = jnp.moveaxis(deriv_blocks, 0, 1).reshape(edge, 3 * edge)
    constants = []
    for spot, mask in ((slow, fast), (fast, slow), (outer, within)):
        spread = np.kron(np.eye(3, dtype=np.float32), spot.T)
        constants += [jnp.asarray(spot, bf16), jnp.asarray(spread, bf16), jnp.asarray(mask @ mask.T, f32)]
    vmem = pl.BlockSpec(memory_space=pltpu.VMEM)
    shapes = [(2, padded, 3 * padded), (tall, 3 * tall), (2, 3, padded, padded), (padded, 2 * padded), (3, tall, tall)]
    return pl.pallas_call(
        matrices_kernel,
        out_shape=[jax.ShapeDtypeStruct(shape, bf16) for shape in shapes],
        in_specs=[vmem] * 11,
        out_specs=[vmem] * 5,
        compiler_params=params(24),
        name="matrices",
    )(stacked, deriv_blocks, *constants)


def kinetic(parts, place_meta, facts, matrices, edge, coefficients, levels):
    slots, folded, lanes = parts[0].shape
    width = lanes // 2
    padded = matrices[0].shape[1]
    own = PAIR * slots
    vmem = pl.BlockSpec(memory_space=pltpu.VMEM)
    smem = pl.BlockSpec(memory_space=pltpu.SMEM)
    anywhere = pl.BlockSpec(memory_space=pl.ANY)
    return pl.pallas_call(
        functools.partial(kinetic_kernel, edge, slots, levels),
        out_shape=jax.ShapeDtypeStruct((own, coefficients, 3 * width), bf16),
        in_specs=[smem] * 2 + [anywhere] * 6 + [vmem] * 5,
        out_specs=vmem,
        scratch_shapes=[
            pltpu.VMEM((6, slots, folded, lanes), bf16),
            pltpu.VMEM((6 * slots + 1, edge, padded, width), bf16),
            pltpu.VMEM((2, edge, padded, width), bf16),
            pltpu.VMEM((2, edge, 2 * padded, width), bf16),
            pltpu.VMEM((own, edge, padded, width), f32),
            pltpu.VMEM((own, edge, padded, width), f32),
            pltpu.VMEM((own + -own % 8, coefficients + -coefficients % lanes), f32),
            pltpu.VMEM((coefficients + -coefficients % lanes, own + -own % 8), f32),
            pltpu.SMEM((4 * slots, 10), jnp.int32),
            pltpu.SMEM((4 * slots,), f32),
            pltpu.SemaphoreType.DMA((6,)),
        ],
        compiler_params=params(48),
        cost_estimate=pl.CostEstimate(flops=2 * 10**10, bytes_accessed=40 * 10**6, transcendentals=0),
        name="kinetic",
    )(place_meta, facts, *parts, *matrices)


def offset_sum_kernel(meta, *refs):
    blocks, (small, kept, sent) = refs[:-3], refs[-3:]
    total = blocks[0][...].astype(f32)
    for block in blocks[1:]:
        total = total + block[...].astype(f32)
    small[...] = total.astype(bf16)
    half = kept.shape[0]
    first = meta[0] == 0
    low, high = total[:, :half].T, total[:, half:].T
    kept[...] = jnp.where(first, low, high)
    sent[...] = jnp.where(first, high, low)


def fock_sum_kernel(meta, *refs):
    blocks, (share, kept, sent) = refs[:-3], refs[-3:]
    sums = [sum((block[part].astype(f32) for block in blocks[1:]), blocks[0][part].astype(f32)) for part in range(3)]
    main = sums[0] + sums[1]
    share[...] = sums[2].astype(bf16)
    half = kept.shape[0]
    first = meta[0] == 0
    low, high = main[:, :half].T, main[:, half:].T
    kept[...] = jnp.where(first, low, high)
    sent[...] = jnp.where(first, high, low)


def level_sum(kernel, meta, blocks):
    tall, width = blocks[0].shape[-2:]
    vmem = pl.BlockSpec(memory_space=pltpu.VMEM)
    turned = jax.ShapeDtypeStruct((width // PAIR, tall), f32)
    return pl.pallas_call(
        kernel,
        out_shape=[jax.ShapeDtypeStruct((tall, width), bf16), turned, turned],
        in_specs=[pl.BlockSpec(memory_space=pltpu.SMEM)] + [vmem] * len(blocks),
        out_specs=[vmem] * 3,
        compiler_params=params(24),
        name="level_sum",
    )(meta, *blocks)


def body(orbitals, potential, deriv_blocks, levels, box_counts, neighbours):
    slots, coefficients, own_width = orbitals.shape
    edge = deriv_blocks.shape[1]
    level, pair, orb = lax.axis_index("lvl"), lax.axis_index("pair"), lax.axis_index("orb")
    level_count, orb_count = lax.axis_size("lvl"), lax.axis_size("orb")
    half, fold = own_width // PAIR, coefficients // 2
    all_width = own_width * orb_count
    box_rows = all_width // (level_count * PAIR)
    first = pair == 0
    groups = range(orb_count)
    square_grid = level_count == orb_count == 4 and box_rows == half
    row0, col0 = (level * PAIR + pair) * box_rows, orb * own_width

    own_base = (level * PAIR + pair) * slots
    pack_meta = jnp.stack([pair, box_counts[0], own_base]).astype(jnp.int32)
    theirs, mine = pack(pack_meta, neighbours, levels, orbitals, potential)
    active = orbitals

    far = {q: swap(active, "orb", q) for q in groups if q and q % 2 == 0}
    beside = swap(theirs, "pair", 1)
    first_mine, second_mine = trade(mine, "lvl", 0), trade(mine, "lvl", 1)
    later_mine, beside = lax.optimization_barrier((mine, beside))
    beside_rest = swap(later_mine, "pair", 1)
    first_beside, second_beside = trade(beside, "lvl", 0), trade(beside, "lvl", 1)

    matrices = block_matrices(deriv_blocks)

    def facts_of(parts):
        return jnp.stack([part[:, fold, :8] for part in parts]).astype(f32).astype(jnp.int32)

    early_facts = facts_of([mine, beside, first_mine, second_mine])
    flat = lambda block: block.reshape(-1, block.shape[-1])
    cut = -(-slots * coefficients // (2 * ROWS)) * ROWS
    beside_all, beside_top = unfold(pack_meta, beside, beside_rest, fold, cut)

    parts = [mine, beside, first_mine, first_beside, second_mine, second_beside]
    far, active, parts, beside_all, beside_top, matrices, early_facts = lax.optimization_barrier(
        (far, active, parts, beside_all, beside_top, matrices, early_facts)
    )
    facts = jnp.concatenate([early_facts, facts_of([parts[3], parts[5]])])
    cross = {q: [swap(beside_top, "orb", q), swap(flat(far[q])[cut:], "pair", 1)] for q in far}
    left_own = {0: active, 1: swap(active, "orb", 1), **far}
    left_beside = {0: [beside_all], 1: [swap(beside_all, "orb", 1)]}
    for q in far:
        left_own[q + 1] = swap(far[q], "orb", 1)

    def natural(blocks):
        return jnp.concatenate([lax.dynamic_index_in_dim(blocks, orb ^ j, keepdims=False) for j in groups], axis=1)

    def along_levels(blocks):
        mine_block = lambda target: lax.dynamic_index_in_dim(blocks, orb ^ target, keepdims=False)
        steps = range(1, level_count)
        return [mine_block(level)] + [swap(mine_block(level ^ step), "lvl", step) for step in steps]

    def both_halves(kept, got):
        return jnp.concatenate([jnp.where(first, kept, got), jnp.where(first, got, kept)], axis=1)

    def own_block(strip):
        strip = lax.all_gather(lax.psum(strip, "lvl"), ("orb", "pair"), axis=0, tiled=True)
        strip = lax.dynamic_slice_in_dim(strip, row0, box_rows, axis=0)
        return lax.dynamic_slice_in_dim(strip, col0, own_width, axis=1)

    live_rows = box_counts[0] * coefficients
    meta = jnp.stack([pair, slots * coefficients, live_rows]).astype(jnp.int32)

    place_meta = jnp.stack([level, pair]).astype(jnp.int32)
    right = kinetic(parts, place_meta, facts, matrices, edge, coefficients, level_count)

    cross, right, meta = lax.optimization_barrier((cross, right, meta))
    lefts_own = [[flat(left_own[q])] for q in groups]
    lefts_beside = dict(left_beside)
    for q in far:
        lefts_beside[q] = list(cross[q])
        lefts_beside[q + 1] = [swap(piece, "orb", 1) for piece in cross[q]]
    lefts_beside = [lefts_beside[q] for q in groups]

    share = 1.0 / level_count
    blocks = box_correlation(share, meta, lefts_own, None, half)
    blocks = box_correlation(share, meta, lefts_beside, blocks, half)
    right = right.reshape(2, slots * coefficients, 3 * half)
    fock_part = box_fock(0, lefts_own, right, None, None)
    if square_grid:
        sent = along_levels(blocks)
        sent, fock_part = lax.optimization_barrier((sent, fock_part))
        small, kept, other = level_sum(offset_sum_kernel, meta, sent)
        offset = both_halves(kept, swap(other, "pair", 1))
    else:
        offset = own_block(natural(blocks).astype(f32))
    row_ids = row0 + jnp.arange(box_rows, dtype=jnp.int32)
    col_ids = col0 + jnp.arange(own_width, dtype=jnp.int32)
    correlation = offset + (row_ids[:, None] == col_ids[None, :]).astype(f32)
    apart = (orb ^ level if square_grid else 0 * orb).reshape(1).astype(jnp.int32)
    fock_blocks = box_fock(1, lefts_beside, right, fock_part, apart)
    if square_grid:
        pieces = [small] + [swap(small, "lvl", z) for z in range(1, level_count)]
        pieces, fock_blocks, offset = lax.optimization_barrier((pieces, fock_blocks, offset))
        join = functools.partial(jnp.concatenate, axis=0)
        top, low = join(pieces[: level_count // 2]), join(pieces[level_count // 2 :])
        sent = [fock_blocks[0]] + [swap(fock_blocks[step], "lvl", step) for step in range(1, level_count)]
        got = [swap(top, "pair", 1), swap(low, "orb", 2)]
        tops, lows = [top, got[0]], [low, got[1]]
        far_tops, far_lows = [swap(piece, "orb", 2) for piece in tops], [swap(piece, "pair", 1) for piece in lows]
        far_tops[1], far_lows[1], sent = lax.optimization_barrier((far_tops[1], far_lows[1], sent))
        pieces = tops + far_tops + lows + far_lows
        pieces += [swap(piece, "orb", 1) for piece in pieces]
        root_meta = jnp.stack([level, pair, orb]).astype(jnp.int32)
        inverse_root = root_of(root_meta, pieces, offset, all_width, level_count)
        share, kept, other = level_sum(fock_sum_kernel, meta, sent)
        to = [
            ((z * PAIR + y) * orb_count + o, (o * PAIR + y) * orb_count + z)
            for z in range(level_count)
            for y in range(PAIR)
            for o in groups
        ]
        got = swap(other, "pair", 1), lax.ppermute(share, BOX + ("orb",), to)
        inverse_root, got = lax.optimization_barrier((inverse_root, got))
        fock = both_halves(kept, got[0]) + got[1].astype(f32)
    else:
        fock_blocks = jnp.stack(fock_blocks)
        main = natural(fock_blocks[:, 0]).astype(f32) + natural(fock_blocks[:, 1]).astype(f32)
        main = lax.all_gather(lax.psum(main, "lvl"), "pair", axis=0, tiled=True)
        fock = lax.dynamic_slice_in_dim(main, row0, box_rows, axis=1).T + own_block(natural(fock_blocks[:, 2]).astype(f32))
        gathered = lax.all_gather(offset.astype(bf16), "orb", axis=1, tiled=True)
        whole = lax.all_gather(gathered, BOX, axis=0, tiled=True)
        rows_of = lax.dynamic_slice_in_dim(whole, row0, box_rows, axis=0)
        cols_of = lax.dynamic_slice_in_dim(whole, col0, own_width, axis=1)
        row_square, col_square = matmul(rows_of, whole), matmul(whole, cols_of)
        left = (rows_of.astype(f32) - 0.25 * row_square).astype(bf16)
        right_side = (0.25 * (cols_of.astype(f32) - col_square)).astype(bf16)
        own_square = lax.dynamic_slice_in_dim(row_square, col0, own_width, axis=1)
        inverse_root = correlation - 1.5 * offset + 0.125 * own_square + matmul(left, right_side)
    return fock, correlation, inverse_root


def solution(mesh):
    levels = mesh.shape["box"] // PAIR
    split = Mesh(mesh.devices.reshape(levels, PAIR, mesh.shape["orb"]), ("lvl", "pair", "orb"))
    in_specs = (P(BOX, None, "orb"), P(BOX, None), P(), P(BOX), P(BOX), P(BOX, None, None))
    out_specs = (P(BOX, "orb"),) * 3
    return jax.shard_map(body, mesh=split, in_specs=in_specs, out_specs=out_specs, check_vma=False)
```

```python
import functools

import jax
import jax.numpy as jnp
import numpy as np
from jax import lax
from jax.experimental import pallas as pl
from jax.experimental.pallas import tpu as pltpu
from jax.sharding import Mesh, PartitionSpec as P

PAIR = 2
ROWS = 16
BOX = ("lvl", "pair")
f32, bf16 = jnp.float32, jnp.bfloat16


def swap(value, axis, bit):
    count = lax.axis_size(axis)
    return lax.ppermute(value, axis, [(i, i ^ bit) for i in range(count)])


def trade(value, axis, start):
    pairs = [(i, i + 1) for i in range(start, lax.axis_size(axis) - 1, 2)]
    return lax.ppermute(value, axis, pairs + [(b, a) for a, b in pairs])


def matmul(left, right):
    return jnp.dot(left, right, preferred_element_type=f32)


def params(mebibytes):
    return pltpu.CompilerParams(vmem_limit_bytes=mebibytes * 1024 * 1024)


def pack_kernel(meta, neighbours, levels, orbitals, pot, theirs, mine):
    slots, coefficients, width = orbitals.shape
    half, fold = width // PAIR, coefficients // 2
    first = meta[0] == 0
    place = lax.broadcasted_iota(jnp.int32, (8, width), 1)
    for slot in range(slots):
        keep = slot < meta[1]
        for part in range(2):
            here = orbitals[slot, part * fold : (part + 1) * fold, :]
            here = jnp.where(keep, here, jnp.zeros_like(here))
            low, high = here[:, :half], here[:, half:]
            lanes = slice(part * half, (part + 1) * half)
            theirs[slot, :fold, lanes] = jnp.where(first, high, low)
            mine[slot, :fold, lanes] = jnp.where(first, low, high)
        own_id = meta[2] + slot
        facts = jnp.where(place == 6, levels[slot], jnp.where(place == 7, jnp.where(keep, 1, 0), 0))
        for c in range(6):
            target = neighbours[slot, c // 2, c % 2]
            facts = jnp.where(place == c, jnp.where(target >= 0, target - own_id, 16 * slots), facts)
        facts = facts.astype(f32).astype(bf16)
        for packed in (theirs, mine):
            packed[slot, fold : fold + 1, :] = facts[:1]
        row = fold + 1
        for start in range(0, pot.shape[1], width):
            stop = min(start + width, pot.shape[1])
            exact = pot[slot : slot + 1, start:stop]
            for _ in range(3):
                part = exact.astype(bf16)
                exact = exact - part.astype(f32)
                for packed in (theirs, mine):
                    packed[slot, row : row + 1, : stop - start] = part
                    if stop - start < width:
                        packed[slot, row : row + 1, stop - start :] = jnp.zeros((1, width - stop + start), bf16)
                row += 1
        for packed in (theirs, mine):
            packed[slot, row:, :] = jnp.zeros((packed.shape[1] - row, width), bf16)


def pack(meta, neighbours, levels, orbitals, pot):
    slots, coefficients, width = orbitals.shape
    fold = coefficients // 2
    padded = -(-(fold + 1 + 3 * -(-coefficients // width)) // ROWS) * ROWS
    vmem, smem = pl.BlockSpec(memory_space=pltpu.VMEM), pl.BlockSpec(memory_space=pltpu.SMEM)
    return pl.pallas_call(
        pack_kernel,
        out_shape=[jax.ShapeDtypeStruct((slots, padded, width), bf16)] * 2,
        in_specs=[smem, smem, smem, vmem, vmem],
        out_specs=[vmem, vmem],
        compiler_params=params(8),
        name="pack",
    )(meta, neighbours, levels, orbitals, pot)


def unfold_kernel(fold, meta, beside_in, rest_in, whole, top, beside, rest, sems):
    copies = [
        pltpu.make_async_copy(source, target, sems.at[i])
        for i, (source, target) in enumerate(((beside_in, beside), (rest_in, rest)))
    ]
    for copy in copies:
        copy.start()
    slots, _, width = beside.shape
    half = width // PAIR
    first = meta[0] == 0
    for copy in copies:
        copy.wait()
    for slot in range(slots):
        for part in range(2):
            lanes = slice(part * half, (part + 1) * half)
            near, far = beside[slot, :fold, lanes], rest[slot, :fold, lanes]
            start = (2 * slot + part) * fold
            here = jnp.concatenate([jnp.where(first, near, far), jnp.where(first, far, near)], axis=1)
            whole[start : start + fold, :] = here
    top[...] = whole[: top.shape[0], :]


def unfold(meta, beside, rest, fold, cut):
    slots, _, width = beside.shape
    vmem = pl.BlockSpec(memory_space=pltpu.VMEM)
    return pl.pallas_call(
        functools.partial(unfold_kernel, fold),
        out_shape=[
            jax.ShapeDtypeStruct((2 * slots * fold, width), bf16),
            jax.ShapeDtypeStruct((cut, width), bf16),
        ],
        in_specs=[pl.BlockSpec(memory_space=pltpu.SMEM)] + [pl.BlockSpec(memory_space=pl.ANY)] * 2,
        out_specs=[vmem, vmem],
        scratch_shapes=[
            pltpu.VMEM(beside.shape, bf16),
            pltpu.VMEM(beside.shape, bf16),
            pltpu.SemaphoreType.DMA((2,)),
        ],
        compiler_params=params(8),
        name="unfold",
    )(meta, beside, rest)


def load_left(lefts, held, sems):
    copies = []
    for q, pieces in enumerate(lefts):
        row = 0
        for piece in pieces:
            rows, width = piece.shape
            here = held.at[row : row + rows, q * width : (q + 1) * width]
            copies.append(pltpu.make_async_copy(piece, here, sems.at[len(copies)]))
            row += rows
    for copy in copies:
        copy.start()
    return copies


def grouped(refs, counts):
    refs = list(refs)
    return [[refs.pop(0) for _ in range(count)] for count in counts]


def correlation_kernel(share, counts, meta, *refs):
    refs, (out, held, turned, sems) = refs[:-4], refs[-4:]
    groups, half, width = out.shape
    lefts, before = grouped(refs, counts), refs[sum(counts) :]
    copies = load_left(lefts, held, sems)
    first = meta[0] == 0
    for copy in copies[: counts[0]]:
        copy.wait()
    own = held[:, :width]
    own = jnp.where(first, own[:, :half], own[:, half:]).T
    live = lax.broadcasted_iota(jnp.int32, own.shape, 1) < meta[1 if before else 2]
    turned[...] = jnp.where(live, own, jnp.zeros_like(own))
    for base in range(0, groups, 2):
        for copy in copies[max(sum(counts[:base]), counts[0]) : sum(counts[: base + 2])]:
            copy.wait()
        wide = matmul(turned[...], held[:, base * width : (base + 2) * width])
        for q in (base, base + 1):
            total = wide[:, (q - base) * width : (q - base + 1) * width]
            if before:
                total = total + before[0][q]
                if q == 0:
                    rows = lax.broadcasted_iota(jnp.int32, (half, width), 0) + jnp.where(first, 0, half)
                    columns = lax.broadcasted_iota(jnp.int32, (half, width), 1)
                    total = total - jnp.where(rows == columns, share, 0.0)
            out[q] = total.astype(out.dtype)


def box_correlation(share, meta, lefts, before, half):
    depth, width = sum(piece.shape[0] for piece in lefts[0]), lefts[0][0].shape[1]
    counts = [len(pieces) for pieces in lefts]
    vmem = pl.BlockSpec(memory_space=pltpu.VMEM)
    extra = [] if before is None else [before]
    return pl.pallas_call(
        functools.partial(correlation_kernel, share, counts),
        out_shape=jax.ShapeDtypeStruct((len(lefts), half, width), f32 if before is None else bf16),
        in_specs=[pl.BlockSpec(memory_space=pltpu.SMEM)]
        + [pl.BlockSpec(memory_space=pl.ANY)] * sum(counts)
        + [vmem] * len(extra),
        out_specs=vmem,
        scratch_shapes=[
            pltpu.VMEM((depth, len(lefts) * width), bf16),
            pltpu.VMEM((half, depth), bf16),
            pltpu.SemaphoreType.DMA((sum(counts),)),
        ],
        compiler_params=params(32),
        cost_estimate=pl.CostEstimate(
            flops=2 * len(lefts) * depth * width * half, bytes_accessed=2 * len(lefts) * depth * width, transcendentals=0
        ),
        name="correlation",
    )(meta, *[piece for pieces in lefts for piece in pieces], *extra)


def fock_kernel(side, counts, right, *refs):
    outs, (held, raw, turned, sems, last_sem) = refs[sum(counts) : -5], refs[-5:]
    lefts = grouped(refs, counts)
    before, apart, outs = (None, None, outs) if len(outs) == 1 else (outs[0], outs[1], outs[2:])
    out = outs[0]
    last = pltpu.make_async_copy(right.at[side], raw, last_sem)
    last.start()
    copies = load_left(lefts, held, sems)
    half, width = out.shape[-2] // (3 if before is None else 1), out.shape[-1]
    last.wait()
    turned[...] = raw[...].T
    for base in range(0, len(lefts), 2):
        for copy in copies[sum(counts[:base]) : sum(counts[: base + 2])]:
            copy.wait()
        wide = matmul(turned[...], held[:, base * width : (base + 2) * width])
        for q in (base, base + 1):
            total = wide[:, (q - base) * width : (q - base + 1) * width]
            if before is None:
                out[q] = total
                continue
            total = total + before[q]
            main = total[:half] + total[half : 2 * half]
            top = main.astype(bf16)
            parts = (top, (main - top.astype(f32)).astype(bf16), total[2 * half :].astype(bf16))

            def store(target):
                for i in range(3):
                    target[i] = parts[i]

            for distance, target in enumerate(outs):
                pl.when(q ^ apart[0] == distance)(functools.partial(store, target))


def box_fock(side, lefts, right, before, apart):
    depth, width = sum(piece.shape[0] for piece in lefts[0]), lefts[0][0].shape[1]
    counts = [len(pieces) for pieces in lefts]
    tall = right.shape[-1]
    anywhere, vmem = pl.BlockSpec(memory_space=pl.ANY), pl.BlockSpec(memory_space=pltpu.VMEM)
    extra = [] if before is None else [before, apart]
    out = jax.ShapeDtypeStruct((len(lefts), tall, width), f32)
    if before is not None:
        out = [jax.ShapeDtypeStruct((3, tall // 3, width), bf16)] * len(lefts)
    return pl.pallas_call(
        functools.partial(fock_kernel, side, counts),
        out_shape=out,
        in_specs=[anywhere] * (sum(counts) + 1) + [vmem, pl.BlockSpec(memory_space=pltpu.SMEM)][: len(extra)],
        out_specs=vmem if before is None else [vmem] * len(lefts),
        scratch_shapes=[
            pltpu.VMEM((depth, len(lefts) * width), bf16),
            pltpu.VMEM(right.shape[1:], bf16),
            pltpu.VMEM((tall, depth), bf16),
            pltpu.SemaphoreType.DMA((sum(counts),)),
            pltpu.SemaphoreType.DMA(()),
        ],
        compiler_params=params(40),
        cost_estimate=pl.CostEstimate(
            flops=2 * len(lefts) * depth * width * tall, bytes_accessed=2 * len(lefts) * depth * width, transcendentals=0
        ),
        name="fock",
    )(right, *[piece for pieces in lefts for piece in pieces], *extra)


def root_kernel(levels, meta, *refs):
    pieces, (offset, root, whole, rows_f, cols_b, sems) = refs[:-6], refs[-6:]
    level, pair, orb = meta[0], meta[1], meta[2]
    coarse, width = offset.shape
    side = whole.shape[0]
    groups = side // width
    copies = []
    for piece, (z, y, q) in zip(pieces, piece_places(levels)):
        for i in range(len(z)):
            start = ((orb ^ q) * PAIR + (pair ^ y)) * coarse
            rows = pl.ds(pl.multiple_of(start, coarse), coarse)
            lanes = pl.ds(pl.multiple_of((level ^ z[i]) * width, width), width)
            copies.append(
                pltpu.make_async_copy(
                    piece.at[i * coarse : (i + 1) * coarse], whole.at[rows, lanes], sems.at[len(copies)]
                )
            )
    for copy in copies:
        copy.start()
    for copy in copies:
        copy.wait()
    row0 = pl.multiple_of((level * PAIR + pair) * coarse, coarse)
    own_lanes = pl.ds(pl.multiple_of(orb * width, width), width)
    rows = whole[pl.ds(row0, coarse), :]

    for j in range(groups):
        lanes = slice(j * width, (j + 1) * width)
        rows_f[:, lanes] = matmul(rows, whole[:, lanes])
    columns = whole[:, own_lanes]
    for i in range(groups):
        here = slice(i * width, (i + 1) * width)
        square = matmul(whole[here, :], columns)
        cols_b[here, :] = (0.25 * (whole[here, own_lanes].astype(f32) - square)).astype(bf16)
    left = (rows.astype(f32) - 0.25 * rows_f[...]).astype(bf16)
    value = matmul(left, cols_b[...]) + 0.125 * rows_f[:, own_lanes] - 0.5 * offset[...]
    row_ids = lax.broadcasted_iota(jnp.int32, value.shape, 0) + row0
    col_ids = lax.broadcasted_iota(jnp.int32, value.shape, 1) + orb * width
    root[...] = value + jnp.where(row_ids == col_ids, 1.0, 0.0)


def piece_places(levels):
    places = []
    for core in (0, 1):
        for half in range(2):
            z = [half * levels // 2 + i for i in range(levels // 2)]
            for second in (0, 1):
                for inner in (0, 1):
                    y, far = (second, inner) if half else (inner, second)
                    places.append((z, y, 2 * far + core))
    return places


def root_of(meta, pieces, offset, side, levels):
    coarse, width = offset.shape
    vmem, anywhere = pl.BlockSpec(memory_space=pltpu.VMEM), pl.BlockSpec(memory_space=pl.ANY)
    return pl.pallas_call(
        functools.partial(root_kernel, levels),
        out_shape=jax.ShapeDtypeStruct(offset.shape, f32),
        in_specs=[pl.BlockSpec(memory_space=pltpu.SMEM)] + [anywhere] * len(pieces) + [vmem],
        out_specs=vmem,
        scratch_shapes=[
            pltpu.VMEM((side, side), bf16),
            pltpu.VMEM((coarse, side), f32),
            pltpu.VMEM((side, width), bf16),
            pltpu.SemaphoreType.DMA((side // coarse * (side // width),)),
        ],
        compiler_params=params(40),
        cost_estimate=pl.CostEstimate(flops=16 * side * side * width, bytes_accessed=4 * side * side, transcendentals=0),
        name="root",
    )(meta, *pieces, offset)


def fill_tables(slots, levels, place_meta, facts, table, scale):
    level, pair = place_meta[0], place_meta[1]
    even = lax.rem(level, 2) == 0
    none = 6 * slots

    def place(slot_id):
        box = lax.div(slot_id, slots)
        apart = lax.div(box, PAIR) - level
        base = jnp.where(apart == 0, 0, jnp.where((apart < 0) == even, 4, 2))
        return (base + jnp.where(lax.rem(box, PAIR) != pair, 1, 0)) * slots + lax.rem(slot_id, slots)

    for index in range(4 * slots):
        group, r = divmod(index, slots)

        def fact(c):
            if group < 2:
                return facts[group, r, c]
            swap_id = jnp.where(even, 1, 0) if group == 2 else jnp.where(even, 0, 1)
            near_pair = 1 if group == 2 else 0
            return facts[2 + swap_id + jnp.where(pair == near_pair, 0, 2), r, c]

        box = (
            level * PAIR + pair,
            level * PAIR + 1 - pair,
            jnp.maximum(level * PAIR - 1, 0),
            jnp.minimum((level + 1) * PAIR, levels * PAIR - 1),
        )[group]
        there = (True, True, level > 0, level < levels - 1)[group]
        own_id = box * slots + r
        own_place = place(own_id)
        table[index, 0] = jnp.where((fact(7) > 0) & there, own_place, -1)
        for a in range(3):
            for k in (0, 2):
                distance = fact(2 * a + k // 2)
                target = place(jnp.maximum(own_id + distance, 0))
                target = jnp.where(distance < 16 * slots, target, none)
                table[index, 1 + 3 * a + k] = jnp.clip(target, 0, none)
            table[index, 2 + 3 * a] = own_place
        level_of = fact(6)
        scale[index] = jnp.where(level_of == 0, 0.5, jnp.where(level_of == 1, 1.0, 2.0))


def kinetic_kernel(edge, slots, levels, place_meta, facts, *refs):
    parts, refs = refs[:6], refs[6:]
    (fwd_in, fwd_out, back_in, back_mid, back_out), out, refs = refs[:5], refs[5], refs[6:]
    raw, x, outer, inner, total, total_fix, lines, columns, table, scale, sems = refs
    square = edge * edge
    own = PAIR * slots
    padded, width = x.shape[2:]
    copies = [pltpu.make_async_copy(part, raw.at[place], sems.at[place]) for place, part in enumerate(parts)]
    for copy in copies:
        copy.start()
    tail = padded - ROWS
    x[:, :, tail:, :] = jnp.zeros((x.shape[0], edge, ROWS, width), bf16)
    x[6 * slots] = jnp.zeros((edge, padded, width), bf16)
    total[...] = jnp.zeros_like(total)
    total_fix[...] = jnp.zeros_like(total_fix)
    fill_tables(slots, levels, place_meta, facts, table, scale)
    lines[...] = jnp.zeros_like(lines)
    for copy in copies:
        copy.wait()
    lanes = raw.shape[3]
    for t in range(own):
        for start in range(0, lines.shape[1], lanes):
            row = edge * square // 2 + 1 + 3 * (start // lanes)
            high, middle, low = (
                raw[t // slots, t % slots, row + i : row + i + 1, :].astype(f32) for i in range(3)
            )
            lines[t : t + 1, start : start + lanes] = (high + middle) + low
    columns[...] = lines[...].T

    def lay_out(place, carry):
        for slot in range(slots):
            for i in range(edge):
                part, row = i // (edge // 2), i % (edge // 2) * square
                x[place * slots + slot, i, :square, :] = raw[
                    place, slot, row : row + square, part * width : (part + 1) * width
                ]
        return carry

    lax.fori_loop(0, len(parts), lay_out, 0)
    chunks = -(-square // ROWS)

    def per_slot(s, carry):
        @pl.when(table[s, 0] >= 0)
        def _():
            both_scales = 0.5 * scale[s] * scale[s]
            sums = (total, total_fix)

            def split(exact):
                exact = both_scales * exact
                value = exact.astype(bf16)
                return value, (value.astype(f32) - exact).astype(bf16)

            sources = [[table[s, 1 + 3 * a + k] for k in range(3)] for a in range(3)]
            here = sources[0][1]

            def forward(a):
                if a == 0:
                    for i in range(chunks):
                        rows = slice(i * ROWS, (i + 1) * ROWS)
                        block = [x[t, :, rows, :].reshape(edge * ROWS, width) for t in sources[0]]
                        fields = split(matmul(fwd_out[...], jnp.concatenate(block, axis=0)))
                        for field in range(2):
                            outer[field, :, rows, :] = fields[field].reshape(edge, ROWS, width)
                else:
                    for i in range(edge):
                        block = jnp.concatenate([x[t, i] for t in sources[a]], axis=0)
                        fields = split(matmul(fwd_in[a - 1], block))
                        for field in range(2):
                            inner[field, i, (a - 1) * padded : a * padded, :] = fields[field]

            def back_outer(k, target):
                for i in range(chunks):
                    rows = slice(i * ROWS, (i + 1) * ROWS)
                    for field in range(2):
                        term = matmul(back_out[k], outer[field, :, rows, :].reshape(edge * ROWS, width))
                        sums[field][target, :, rows, :] += term.reshape(edge, ROWS, width)

            @pl.when(here < own)
            def _():
                for a in range(3):
                    forward(a)
                back_outer(1, here)
                for i in range(edge):
                    for field in range(2):
                        sums[field][here, i] += matmul(back_mid[...], inner[field, i])

            for a in range(3):
                pl.when((here >= own) & ((sources[a][0] < own) | (sources[a][2] < own)))(functools.partial(forward, a))

            for k in (0, 2):
                for a in range(3):
                    target = sources[a][k]

                    @pl.when(target < own)
                    def _():
                        if a == 0:
                            back_outer(k, target)
                        else:
                            for i in range(edge):
                                for field in range(2):
                                    here = inner[field, i, (a - 1) * padded : a * padded, :]
                                    sums[field][target, i] += matmul(back_in[a - 1, k], here)

        return carry

    lax.fori_loop(0, table.shape[0], per_slot, 0)

    for t in range(own):
        for i in range(edge):
            rows = slice(i * square, (i + 1) * square)
            weighted = (columns[rows, t : t + 1] * x[t, i, :square, :].astype(f32)).astype(bf16)
            whole = total[t, i, :square, :] + weighted.astype(f32)
            top = whole.astype(bf16)
            low = (whole - top.astype(f32)).astype(bf16)
            fix = total_fix[t, i, :square, :].astype(bf16)
            out[t, rows, :] = jnp.concatenate([top, low, fix], axis=1)


def matrices_kernel(stacked, blocks, *refs):
    spots, outs = refs[:9], refs[9:]
    fwd_in, fwd_out, back_in, back_mid, back_out = outs
    for mode in range(3):
        spot, spread, same = spots[3 * mode : 3 * mode + 3]
        wide = matmul(matmul(spot[...], stacked[...]).astype(bf16), spread[...])
        wide = (wide * jnp.concatenate([same[...]] * 3, axis=1)).astype(bf16)
        if mode == 2:
            fwd_out[...] = wide
        else:
            fwd_in[mode] = wide
        for k in range(3):
            turned = lax.dot_general(spot[...], blocks[k], (((1,), (1,)), ((), ())), preferred_element_type=f32)
            turned = lax.dot_general(
                turned.astype(bf16), spot[...], (((1,), (1,)), ((), ())), preferred_element_type=f32
            )
            turned = (turned * same[...]).astype(bf16)
            if mode == 2:
                back_out[k] = turned
            else:
                back_in[mode, k] = turned
    back_mid[...] = jnp.concatenate([back_in[0, 1], back_in[1, 1]], axis=1)


def block_matrices(deriv_blocks):
    edge = deriv_blocks.shape[1]
    square = edge * edge
    padded = -(-square // ROWS) * ROWS
    tall = edge * ROWS
    ids = np.arange(padded)
    slow = ((ids[:, None] // edge) == np.arange(edge)).astype(np.float32)
    fast = (((ids[:, None] % edge) == np.arange(edge)) & (ids[:, None] < square)).astype(np.float32)
    ids = np.arange(tall)
    outer = ((ids[:, None] // ROWS) == np.arange(edge)).astype(np.float32)
    within = ((ids[:, None] % ROWS) == np.arange(ROWS)).astype(np.float32)
    stacked = jnp.moveaxis(deriv_blocks, 0, 1).reshape(edge, 3 * edge)
    constants = []
    for spot, mask in ((slow, fast), (fast, slow), (outer, within)):
        spread = np.kron(np.eye(3, dtype=np.float32), spot.T)
        constants += [jnp.asarray(spot, bf16), jnp.asarray(spread, bf16), jnp.asarray(mask @ mask.T, f32)]
    vmem = pl.BlockSpec(memory_space=pltpu.VMEM)
    shapes = [(2, padded, 3 * padded), (tall, 3 * tall), (2, 3, padded, padded), (padded, 2 * padded), (3, tall, tall)]
    return pl.pallas_call(
        matrices_kernel,
        out_shape=[jax.ShapeDtypeStruct(shape, bf16) for shape in shapes],
        in_specs=[vmem] * 11,
        out_specs=[vmem] * 5,
        compiler_params=params(8),
        name="matrices",
    )(stacked, deriv_blocks, *constants)


def kinetic(parts, place_meta, facts, matrices, edge, coefficients, levels):
    slots, folded, lanes = parts[0].shape
    width = lanes // 2
    padded = matrices[0].shape[1]
    own = PAIR * slots
    vmem = pl.BlockSpec(memory_space=pltpu.VMEM)
    smem = pl.BlockSpec(memory_space=pltpu.SMEM)
    anywhere = pl.BlockSpec(memory_space=pl.ANY)
    return pl.pallas_call(
        functools.partial(kinetic_kernel, edge, slots, levels),
        out_shape=jax.ShapeDtypeStruct((own, coefficients, 3 * width), bf16),
        in_specs=[smem] * 2 + [anywhere] * 6 + [vmem] * 5,
        out_specs=vmem,
        scratch_shapes=[
            pltpu.VMEM((6, slots, folded, lanes), bf16),
            pltpu.VMEM((6 * slots + 1, edge, padded, width), bf16),
            pltpu.VMEM((2, edge, padded, width), bf16),
            pltpu.VMEM((2, edge, 2 * padded, width), bf16),
            pltpu.VMEM((own, edge, padded, width), f32),
            pltpu.VMEM((own, edge, padded, width), f32),
            pltpu.VMEM((own + -own % 8, coefficients + -coefficients % lanes), f32),
            pltpu.VMEM((coefficients + -coefficients % lanes, own + -own % 8), f32),
            pltpu.SMEM((4 * slots, 10), jnp.int32),
            pltpu.SMEM((4 * slots,), f32),
            pltpu.SemaphoreType.DMA((6,)),
        ],
        compiler_params=params(48),
        cost_estimate=pl.CostEstimate(flops=2 * 10**10, bytes_accessed=40 * 10**6, transcendentals=0),
        name="kinetic",
    )(place_meta, facts, *parts, *matrices)


def offset_sum_kernel(meta, *refs):
    blocks, (small, kept, sent) = refs[:-3], refs[-3:]
    total = blocks[0][...].astype(f32)
    for block in blocks[1:]:
        total = total + block[...].astype(f32)
    small[...] = total.astype(bf16)
    half = kept.shape[0]
    first = meta[0] == 0
    low, high = total[:, :half].T, total[:, half:].T
    kept[...] = jnp.where(first, low, high)
    sent[...] = jnp.where(first, high, low)


def fock_sum_kernel(meta, *refs):
    blocks, (share, kept, sent) = refs[:-3], refs[-3:]
    sums = [sum((block[part].astype(f32) for block in blocks[1:]), blocks[0][part].astype(f32)) for part in range(3)]
    main = sums[0] + sums[1]
    share[...] = sums[2].astype(bf16)
    half = kept.shape[0]
    first = meta[0] == 0
    low, high = main[:, :half].T, main[:, half:].T
    kept[...] = jnp.where(first, low, high)
    sent[...] = jnp.where(first, high, low)


def level_sum(kernel, meta, blocks):
    tall, width = blocks[0].shape[-2:]
    vmem = pl.BlockSpec(memory_space=pltpu.VMEM)
    turned = jax.ShapeDtypeStruct((width // PAIR, tall), f32)
    return pl.pallas_call(
        kernel,
        out_shape=[jax.ShapeDtypeStruct((tall, width), bf16), turned, turned],
        in_specs=[pl.BlockSpec(memory_space=pltpu.SMEM)] + [vmem] * len(blocks),
        out_specs=[vmem] * 3,
        compiler_params=params(8),
        name="level_sum",
    )(meta, *blocks)


def body(orbitals, potential, deriv_blocks, levels, box_counts, neighbours):
    slots, coefficients, own_width = orbitals.shape
    edge = deriv_blocks.shape[1]
    level, pair, orb = lax.axis_index("lvl"), lax.axis_index("pair"), lax.axis_index("orb")
    level_count, orb_count = lax.axis_size("lvl"), lax.axis_size("orb")
    half, fold = own_width // PAIR, coefficients // 2
    all_width = own_width * orb_count
    box_rows = all_width // (level_count * PAIR)
    first = pair == 0
    groups = range(orb_count)
    square_grid = level_count == orb_count == 4 and box_rows == half
    row0, col0 = (level * PAIR + pair) * box_rows, orb * own_width

    own_base = (level * PAIR + pair) * slots
    pack_meta = jnp.stack([pair, box_counts[0], own_base]).astype(jnp.int32)
    theirs, mine = pack(pack_meta, neighbours, levels, orbitals, potential)
    active = orbitals

    far = {q: swap(active, "orb", q) for q in groups if q and q % 2 == 0}
    beside = swap(theirs, "pair", 1)
    first_mine, second_mine = trade(mine, "lvl", 0), trade(mine, "lvl", 1)
    later_mine, beside = lax.optimization_barrier((mine, beside))
    beside_rest = swap(later_mine, "pair", 1)
    first_beside, second_beside = trade(beside, "lvl", 0), trade(beside, "lvl", 1)

    matrices = block_matrices(deriv_blocks)

    def facts_of(parts):
        return jnp.stack([part[:, fold, :8] for part in parts]).astype(f32).astype(jnp.int32)

    early_facts = facts_of([mine, beside, first_mine, second_mine])
    flat = lambda block: block.reshape(-1, block.shape[-1])
    cut = -(-slots * coefficients // (2 * ROWS)) * ROWS
    beside_all, beside_top = unfold(pack_meta, beside, beside_rest, fold, cut)

    parts = [mine, beside, first_mine, first_beside, second_mine, second_beside]
    far, active, parts, beside_all, beside_top, matrices, early_facts = lax.optimization_barrier(
        (far, active, parts, beside_all, beside_top, matrices, early_facts)
    )
    facts = jnp.concatenate([early_facts, facts_of([parts[3], parts[5]])])
    cross = {q: [swap(beside_top, "orb", q), swap(flat(far[q])[cut:], "pair", 1)] for q in far}
    left_own = {0: active, 1: swap(active, "orb", 1), **far}
    left_beside = {0: [beside_all], 1: [swap(beside_all, "orb", 1)]}
    for q in far:
        left_own[q + 1] = swap(far[q], "orb", 1)

    def natural(blocks):
        return jnp.concatenate([lax.dynamic_index_in_dim(blocks, orb ^ j, keepdims=False) for j in groups], axis=1)

    def along_levels(blocks):
        mine_block = lambda target: lax.dynamic_index_in_dim(blocks, orb ^ target, keepdims=False)
        steps = range(1, level_count)
        return [mine_block(level)] + [swap(mine_block(level ^ step), "lvl", step) for step in steps]

    def both_halves(kept, got):
        return jnp.concatenate([jnp.where(first, kept, got), jnp.where(first, got, kept)], axis=1)

    def own_block(strip):
        strip = lax.all_gather(lax.psum(strip, "lvl"), ("orb", "pair"), axis=0, tiled=True)
        strip = lax.dynamic_slice_in_dim(strip, row0, box_rows, axis=0)
        return lax.dynamic_slice_in_dim(strip, col0, own_width, axis=1)

    live_rows = box_counts[0] * coefficients
    meta = jnp.stack([pair, slots * coefficients, live_rows]).astype(jnp.int32)

    place_meta = jnp.stack([level, pair]).astype(jnp.int32)
    right = kinetic(parts, place_meta, facts, matrices, edge, coefficients, level_count)

    cross, right, meta = lax.optimization_barrier((cross, right, meta))
    lefts_own = [[flat(left_own[q])] for q in groups]
    lefts_beside = dict(left_beside)
    for q in far:
        lefts_beside[q] = list(cross[q])
        lefts_beside[q + 1] = [swap(piece, "orb", 1) for piece in cross[q]]
    lefts_beside = [lefts_beside[q] for q in groups]

    share = 1.0 / level_count
    blocks = box_correlation(share, meta, lefts_own, None, half)
    blocks = box_correlation(share, meta, lefts_beside, blocks, half)
    right = right.reshape(2, slots * coefficients, 3 * half)
    fock_part = box_fock(0, lefts_own, right, None, None)
    if square_grid:
        sent = along_levels(blocks)
        sent, fock_part = lax.optimization_barrier((sent, fock_part))
        small, kept, other = level_sum(offset_sum_kernel, meta, sent)
        offset = both_halves(kept, swap(other, "pair", 1))
    else:
        offset = own_block(natural(blocks).astype(f32))
    row_ids = row0 + jnp.arange(box_rows, dtype=jnp.int32)
    col_ids = col0 + jnp.arange(own_width, dtype=jnp.int32)
    correlation = offset + (row_ids[:, None] == col_ids[None, :]).astype(f32)
    apart = (orb ^ level if square_grid else 0 * orb).reshape(1).astype(jnp.int32)
    fock_blocks = box_fock(1, lefts_beside, right, fock_part, apart)
    if square_grid:
        pieces = [small] + [swap(small, "lvl", z) for z in range(1, level_count)]
        pieces, fock_blocks, offset = lax.optimization_barrier((pieces, fock_blocks, offset))
        join = functools.partial(jnp.concatenate, axis=0)
        top, low = join(pieces[: level_count // 2]), join(pieces[level_count // 2 :])
        sent = [fock_blocks[0]] + [swap(fock_blocks[step], "lvl", step) for step in range(1, level_count)]
        got = [swap(top, "pair", 1), swap(low, "orb", 2)]
        got, sent[:2] = lax.optimization_barrier((got, sent[:2]))
        tops, lows = [top, got[0]], [low, got[1]]
        far_tops, far_lows = [swap(piece, "orb", 2) for piece in tops], [swap(piece, "pair", 1) for piece in lows]
        far_tops, far_lows, sent = lax.optimization_barrier((far_tops, far_lows, sent))
        pieces = tops + far_tops + lows + far_lows
        pieces += [swap(piece, "orb", 1) for piece in pieces]
        root_meta = jnp.stack([level, pair, orb]).astype(jnp.int32)
        inverse_root = root_of(root_meta, pieces, offset, all_width, level_count)
        share, kept, other = level_sum(fock_sum_kernel, meta, sent)
        to = [
            ((z * PAIR + y) * orb_count + o, (o * PAIR + y) * orb_count + z)
            for z in range(level_count)
            for y in range(PAIR)
            for o in groups
        ]
        got = swap(other, "pair", 1), lax.ppermute(share, BOX + ("orb",), to)
        inverse_root, got = lax.optimization_barrier((inverse_root, got))
        fock = both_halves(kept, got[0]) + got[1].astype(f32)
    else:
        fock_blocks = jnp.stack(fock_blocks)
        main = natural(fock_blocks[:, 0]).astype(f32) + natural(fock_blocks[:, 1]).astype(f32)
        main = lax.all_gather(lax.psum(main, "lvl"), "pair", axis=0, tiled=True)
        fock = lax.dynamic_slice_in_dim(main, row0, box_rows, axis=1).T + own_block(natural(fock_blocks[:, 2]).astype(f32))
        gathered = lax.all_gather(offset.astype(bf16), "orb", axis=1, tiled=True)
        whole = lax.all_gather(gathered, BOX, axis=0, tiled=True)
        rows_of = lax.dynamic_slice_in_dim(whole, row0, box_rows, axis=0)
        cols_of = lax.dynamic_slice_in_dim(whole, col0, own_width, axis=1)
        row_square, col_square = matmul(rows_of, whole), matmul(whole, cols_of)
        left = (rows_of.astype(f32) - 0.25 * row_square).astype(bf16)
        right_side = (0.25 * (cols_of.astype(f32) - col_square)).astype(bf16)
        own_square = lax.dynamic_slice_in_dim(row_square, col0, own_width, axis=1)
        inverse_root = correlation - 1.5 * offset + 0.125 * own_square + matmul(left, right_side)
    return fock, correlation, inverse_root


def solution(mesh):
    levels = mesh.shape["box"] // PAIR
    split = Mesh(mesh.devices.reshape(levels, PAIR, mesh.shape["orb"]), ("lvl", "pair", "orb"))
    in_specs = (P(BOX, None, "orb"), P(BOX, None), P(), P(BOX), P(BOX), P(BOX, None, None))
    out_specs = (P(BOX, "orb"),) * 3
    return jax.shard_map(body, mesh=split, in_specs=in_specs, out_specs=out_specs, check_vma=False)
```
